32 devices in a mesh: row: 4 (over z), col: 8 (over y, x, core).
Axes of the slice: x: 2, y: 2, z: 4, core: 2. Of those that a mesh axis runs over, the one named last changes fastest.
Arguments:
- blocks: bfloat16 [4, 8, 128, 4096], P('row', 'col'), may hold values from -0.25 to 0.25
- block_row: int32 [4, 8, 128], P('row', 'col'), may hold values from 0 to 15
- block_col: int32 [4, 8, 128], P('row', 'col'), may hold values from 0 to 7
- counts: int32 [4, 8], P('row', 'col'), may hold values from 0 to 128, as said below
- vectors: float32 [64, 4096], P(('col', 'row')), may hold values from -6 to 6
- row_mass: float32 [64, 64], P(('row', 'col')), may hold values from 0.25 to 4
- col_mass: float32 [64, 64], P(('col', 'row')), may hold values from 0.25 to 4
Outputs:
- subspace: float32 [64, 4096], P(('col', 'row'))
The draws below stay inside these ranges and needn't reach their ends.
Inputs may be any that keep to these rules, and one draw needn't show every extreme that they name: `counts`: in every row panel one tile uses all 128 slots; every other tile uses at most 8.
All inputs are finite; a program needn't handle non-finite values.
Results may differ from the reference program's by a relative error of at most 0.0085.
Values may be sent and summed in bfloat16 or wider, within the bound.
No kernel may reach another device: no remote copies, remote signals or barrier semaphores. Data moves between devices by JAX's collectives and lax.ppermute only.
A program may use at most 64 MiB of HBM per device.

```python
import math
import jax
import jax.numpy as jnp
from jax import lax

BS = 64
K = 64
ITERS = 4
BAND = 16
BLK_DEV = 2
NB_CAP = 128
NB = 64
N_ROW = 4
N_COL = 8


def sparse_layout(key):
    rblk = BLK_DEV * N_COL
    cblk = BLK_DEV * N_ROW
    tile_r = jnp.arange(N_ROW, dtype=jnp.int32)[:, None]
    tile_c = jnp.arange(N_COL, dtype=jnp.int32)[None, :]
    home_col = (tile_r * rblk + rblk // 2) // cblk
    is_home = tile_c == home_col
    shape = (N_ROW, N_COL, NB_CAP)
    rows = jax.random.randint(jax.random.fold_in(key, 11), shape, 0, rblk).astype(jnp.int32)
    global_row = tile_r[:, :, None] * rblk + rows
    offset = jax.random.randint(jax.random.fold_in(key, 12), shape, -BAND, BAND + 1).astype(jnp.int32)
    near = jnp.clip(global_row + offset - tile_c[:, :, None] * cblk, 0, cblk - 1)
    far = jax.random.randint(jax.random.fold_in(key, 13), shape, 0, cblk).astype(jnp.int32)
    cols = jnp.where(is_home[:, :, None], near, far).astype(jnp.int32)
    sparse = jax.random.randint(jax.random.fold_in(key, 14), (N_ROW, N_COL), 0, NB_CAP // 16 + 1)
    filled = jnp.where(is_home, NB_CAP, sparse).astype(jnp.int32)
    return (rows, cols, filled)


def draw_block_row(key, part):
    return sparse_layout(key)[0]


def draw_block_col(key, part):
    return sparse_layout(key)[1]


def draw_counts(key, part):
    return sparse_layout(key)[2]


def block_scale(key, extent, shards, least, largest):
    loudness, own = 1.0, jax.random.fold_in(key, 6)
    for dim, blocks in shards:
        draws = jnp.exp(jax.random.uniform(jax.random.fold_in(own, dim), (blocks,), jnp.float32, least / len(shards), largest / len(shards)))
        loudness = loudness * jnp.repeat(draws, extent[dim] // blocks).reshape([-1 if axis == dim else 1 for axis in range(len(extent))])
    return loudness


def scatter_about(rng, dims, width, bound, shards=(), kind=jnp.bfloat16):
    loudness = block_scale(rng, dims, shards, -0.22, 0.18) if shards else 1.0
    result = jax.random.normal(rng, dims, jnp.float32) * width * loudness
    return jnp.minimum(jnp.maximum(result, -bound), bound).astype(kind)


def setup_inputs(seed: int = 0) -> dict:
    arg_keys = jax.random.split(jax.random.key(seed), 8)
    blocks = scatter_about(arg_keys[0], (N_ROW, N_COL, NB_CAP, BS * BS), (8 * BS) ** -0.5, 0.25, ((0, 4), (1, 8)))
    block_row = draw_block_row(jax.random.fold_in(arg_keys[7], 71), 0)
    block_col = draw_block_col(jax.random.fold_in(arg_keys[7], 71), 0)
    counts = draw_counts(jax.random.fold_in(arg_keys[7], 71), 0)
    vectors = scatter_about(arg_keys[4], (NB, K * BS), 1.0, 6.0, ((0, 32),), jnp.float32)
    row_mass = jnp.clip(jnp.exp(math.log(4.0) - 2.7725887 * jax.random.uniform(arg_keys[5], (NB, BS), jnp.float32) ** block_scale(arg_keys[5], (NB, BS), ((0, 32),), -0.2, 0.2)), 0.25, 4.0)
    col_mass = jnp.clip(jnp.exp(math.log(4.0) - 2.7725887 * jax.random.uniform(arg_keys[6], (NB, BS), jnp.float32) ** block_scale(arg_keys[6], (NB, BS), ((0, 32),), -0.2, 0.2)), 0.25, 4.0)
    return dict(blocks=blocks, block_row=block_row, block_col=block_col, counts=counts, vectors=vectors, row_mass=row_mass, col_mass=col_mass)


def reference(blocks, block_row, block_col, counts, vectors, row_mass, col_mass):
    rblk = BLK_DEV * N_COL
    cblk = BLK_DEV * N_ROW
    nblk = BLK_DEV * N_ROW * N_COL
    ntile = N_ROW * N_COL
    tiles = blocks.reshape(ntile, NB_CAP, BS, BS)
    rows_all = block_row.reshape(ntile, NB_CAP)
    cols_all = block_col.reshape(ntile, NB_CAP)
    live = jnp.arange(NB_CAP)[None, :] < counts.reshape(-1)[:, None]
    fwd_ids = jnp.where(live, rows_all, rblk).astype(jnp.int32)
    bwd_ids = jnp.where(live, cols_all, cblk).astype(jnp.int32)
    tile_row = (jnp.arange(ntile) // N_COL).astype(jnp.int32)
    tile_col = (jnp.arange(ntile) % N_COL).astype(jnp.int32)
    inv_col = 1.0 / jnp.sqrt(col_mass)
    current = vectors.reshape(nblk, K, BS)
    for step in range(ITERS):
        scaled = (current * inv_col[:, None, :]).astype(jnp.bfloat16)

        def fstep(carry, item):
            tile, cols, ids, rpos, cpos = item
            panel = lax.dynamic_slice_in_dim(scaled, (cpos * cblk).astype(jnp.int32), cblk, 0)
            taken = jnp.take(panel, cols, axis=0).astype(jnp.float32)
            prod = jnp.einsum('bij,bkj->bki', tile.astype(jnp.float32), taken)
            seg = jax.ops.segment_sum(prod, ids, num_segments=rblk + 1)[:rblk]
            start = (rpos * rblk).astype(jnp.int32)
            old = lax.dynamic_slice_in_dim(carry, start, rblk, 0)
            return (lax.dynamic_update_slice_in_dim(carry, old + seg, start, 0), None)
        rows_sum, unused = lax.scan(fstep, jnp.zeros((nblk, K, BS), jnp.float32), (tiles, cols_all, fwd_ids, tile_row, tile_col))
        weighted = (rows_sum * row_mass[:, None, :]).astype(jnp.bfloat16)

        def bstep(carry, item):
            tile, rows, ids, rpos, cpos = item
            panel = lax.dynamic_slice_in_dim(weighted, (rpos * rblk).astype(jnp.int32), rblk, 0)
            taken = jnp.take(panel, rows, axis=0).astype(jnp.float32)
            prod = jnp.einsum('bij,bki->bkj', tile.astype(jnp.float32), taken)
            seg = jax.ops.segment_sum(prod, ids, num_segments=cblk + 1)[:cblk]
            start = (cpos * cblk).astype(jnp.int32)
            old = lax.dynamic_slice_in_dim(carry, start, cblk, 0)
            return (lax.dynamic_update_slice_in_dim(carry, old + seg, start, 0), None)
        cols_sum, unused = lax.scan(bstep, jnp.zeros((nblk, K, BS), jnp.float32), (tiles, rows_all, bwd_ids, tile_row, tile_col))
        projected = cols_sum * inv_col[:, None, :]
        gram = jnp.einsum('bki,bli->kl', projected, projected, precision=lax.Precision.HIGHEST) / (nblk * BS)
        lower = jnp.linalg.cholesky(gram)
        inverse = lax.linalg.triangular_solve(lower, jnp.eye(K, dtype=jnp.float32), left_side=True, lower=True)
        current = jnp.einsum('kl,bli->bki', inverse, projected, precision=lax.Precision.HIGHEST)
    return current.reshape(nblk, K * BS)
```

```python
import functools

import jax
import jax.numpy as jnp
from jax import lax
from jax.experimental import pallas as pl
from jax.experimental.pallas import tpu as pltpu
from jax.sharding import PartitionSpec as P

ITERS = 4
OFF_CAP = 8
META = 16
UNROLL = 4
VMEM_LIMIT = 56 * 1024 * 1024

NT = (((1,), (1,)), ((), ()))
NN = (((1,), (0,)), ((), ()))


def dot(a, b, dims=NN):
    return lax.dot_general(a, b, dims, preferred_element_type=jnp.float32)


def split2(x):
    hi = x.astype(jnp.bfloat16)
    return hi, (x - hi.astype(jnp.float32)).astype(jnp.bfloat16)


def inverse_factor(gram):
    n = gram.shape[0]
    rows = lax.broadcasted_iota(jnp.int32, (n, n), 0)
    cols = lax.broadcasted_iota(jnp.int32, (n, n), 1)
    eye = (rows == cols).astype(jnp.float32)
    both = jnp.concatenate([gram, eye], axis=1)
    tiles = [both[8 * t : 8 * t + 8] for t in range(n // 8)]
    sub = lax.broadcasted_iota(jnp.int32, (8, 2 * n), 0)
    lane = lax.broadcasted_iota(jnp.int32, (8, 2 * n), 1)
    for j in range(n):
        t0, s0 = divmod(j, 8)
        row = tiles[t0][s0 : s0 + 1]
        step = row * (1.0 / row[:, j : j + 1])
        for t in range(t0, n // 8):
            factor = jnp.broadcast_to(tiles[t][:, j : j + 1], (8, 2 * n))
            if t == t0:
                factor = jnp.where(sub > s0, factor, 0.0)
            tiles[t] = tiles[t] - factor * step
    out = []
    for t in range(n // 8):
        pivot = jnp.sum(jnp.where(lane == sub + 8 * t, tiles[t], 0.0), axis=1, keepdims=True)
        out.append(tiles[t] * lax.rsqrt(pivot))
    return jnp.concatenate(out, axis=0)[:, n:]


def kernel(
    n_row, n_col, n_cap, total,
    meta, own, pay, out,
    lv, lw, tmp, home, emb, vs, w, wt, y, ph, rm, ic, linv,
):
    n_dev = n_row * n_col
    k = vs.shape[1]
    half = k // 2
    rpairs, cpairs = n_col, n_row
    rblk = 2 * rpairs
    part = n_cap // n_col
    off_at = half * part
    vec_at = off_at + OFF_CAP * half
    meta_at = vec_at + k
    width = cpairs * 128
    height = rblk * k

    left = lax.broadcasted_iota(jnp.int32, (rblk, 128), 1) < 64

    for r in range(n_row):
        for c in range(n_col):
            q, p = c * n_row + r, r * n_col + c
            rows = pay[q, meta_at : meta_at + META, :].astype(jnp.float32)
            rm[p] = jnp.broadcast_to(rows[0:1] + rows[1:2] + rows[2:3], (8, 128))
            ic[q] = jnp.broadcast_to(rows[3:4] + rows[4:5] + rows[5:6], (8, 128))
            vs[q] = pay[q, vec_at : vec_at + k, :]

    homes = []
    for r in range(n_row):
        h = jnp.int32(0)
        for c in range(n_col):
            h = jnp.where(meta[c * n_row + r, 2 * OFF_CAP] > OFF_CAP, c, h)
        homes.append(h)
        index = pay[h * n_row + r, meta_at : meta_at + META, :].astype(jnp.float32)
        place = index[7:8] * float(rblk) + index[6:7]
        want = lax.broadcasted_iota(jnp.int32, (2 * cpairs * rblk, n_cap), 0).astype(jnp.float32)
        select = jnp.where(want == place, 1.0, 0.0).astype(jnp.bfloat16)

        def build(m, carry, r=r, select=select):
            at = pl.multiple_of(m * part, part)
            slots = jnp.concatenate(
                [pay[c * n_row + r, pl.ds(at, part), :] for c in range(n_col)], axis=0
            )
            dense = dot(select, slots)
            for u in range(cpairs):
                a = dense[2 * u * rblk : (2 * u + 1) * rblk]
                b = dense[(2 * u + 1) * rblk : (2 * u + 2) * rblk]
                even = jnp.where(left, a, pltpu.roll(b, 64, 1))
                odd = jnp.where(left, pltpu.roll(a, 64, 1), b)
                tmp[u, pl.ds(m, rblk, stride=k), :] = even
                tmp[u, pl.ds(m + half, rblk, stride=k), :] = odd
            return carry

        lax.fori_loop(0, half, build, 0, unroll=2)

        def cut(i, carry, r=r):
            at = pl.multiple_of(i * k, k)
            for u in range(cpairs):
                hi, lo = split2(tmp[u, pl.ds(at, k), :])
                home[r, pl.ds(at, k), u * 128 : (u + 1) * 128] = hi
                home[r, pl.ds(at, k), width + u * 128 : width + (u + 1) * 128] = lo
            return carry

        lax.fori_loop(0, rblk, cut, 0, unroll=2)

    lanes = lax.broadcasted_iota(jnp.int32, (half, 128), 1)

    def device(q, n):
        count = meta[q, 2 * OFF_CAP]
        count = jnp.where(count > OFF_CAP, 0, count)
        c = q // n_row
        r = q - c * n_row

        def slot(s, n):
            br, bc = meta[q, s], meta[q, OFF_CAP + s]
            lv[n] = c * cpairs + bc // 2
            lw[n] = r * rpairs + br // 2
            side, row = bc % 2, pl.multiple_of((br % 2) * k, k)
            other = pl.multiple_of(k - row, k)
            at = pl.multiple_of(off_at + s * half, half)
            x = pay[q, pl.ds(at, half), :].astype(jnp.float32)
            rolled = pltpu.roll(x, 64, 1)
            mask = (lanes // 64) == side
            even = jnp.where(mask, jnp.where(side == 0, x, rolled), 0.0)
            odd = jnp.where(mask, jnp.where(side == 0, rolled, x), 0.0)
            block = jnp.concatenate([even, odd], axis=0).astype(jnp.bfloat16)
            emb[n, pl.ds(row, k), :] = block
            emb[n, pl.ds(other, k), :] = jnp.zeros_like(block)
            return n + 1

        return lax.fori_loop(0, count, slot, n)

    n_live = lax.fori_loop(0, n_dev, device, jnp.int32(0))
    for u in range(UNROLL - 1):
        lv[n_live + u] = 0
        lw[n_live + u] = 0
        emb[n_live + u] = jnp.zeros((128, 128), jnp.bfloat16)
    n_group = (n_live + UNROLL - 1) // UNROLL

    def iteration(it, carry):
        @pl.when(it > 0)
        def _():
            lh, ll = split2(linv[...])
            for q in range(n_dev):
                hi, lo = ph[q, :k, :], ph[q, k:, :]
                current = dot(lh, hi) + dot(ll, hi) + dot(lh, lo)
                vs[q] = (current * ic[q, 0:1, :]).astype(jnp.bfloat16)

        for r in range(n_row):
            base = homes[r] * cpairs
            vec = jnp.concatenate([vs[base + u] for u in range(cpairs)] * 2, axis=1)
            for p in range(0, rpairs, 2):
                prod = dot(vec, home[r, p * 128 : (p + 2) * 128, :], NT)
                w[r * rpairs + p] = prod[:, :128]
                w[r * rpairs + p + 1] = prod[:, 128:]

        def forward(i, carry):
            prods = [dot(vs[lv[i * UNROLL + u]], emb[i * UNROLL + u], NT) for u in range(UNROLL)]
            for u in range(UNROLL):
                p = lw[i * UNROLL + u]
                w[p] = w[p] + prods[u]
            return carry

        lax.fori_loop(0, n_group, forward, 0)
        for p in range(n_dev):
            wt[p] = (w[p] * rm[p, 0:1, :]).astype(jnp.bfloat16)
            y[p] = jnp.zeros_like(y[p])

        for r in range(n_row):
            base = homes[r] * cpairs
            vec = jnp.concatenate([wt[r * rpairs + p] for p in range(rpairs)], axis=1)
            for u in range(0, cpairs, 2):
                cols = slice(u * 128, (u + 2) * 128)
                tail = slice(width + u * 128, width + (u + 2) * 128)
                prod = dot(vec, home[r, :, cols]) + dot(vec, home[r, :, tail])
                y[base + u] = y[base + u] + prod[:, :128]
                y[base + u + 1] = y[base + u + 1] + prod[:, 128:]

        def backward(i, carry):
            prods = [dot(wt[lw[i * UNROLL + u]], emb[i * UNROLL + u]) for u in range(UNROLL)]
            for u in range(UNROLL):
                q = lv[i * UNROLL + u]
                y[q] = y[q] + prods[u]
            return carry

        lax.fori_loop(0, n_group, backward, 0)

        both = jnp.zeros((2 * k, k), jnp.float32)
        for q in range(0, n_dev, 4):
            his, los = [], []
            for d in range(4):
                hi, lo = split2(y[q + d] * ic[q + d, 0:1, :])
                ph[q + d, :k, :] = hi
                ph[q + d, k:, :] = lo
                his.append(hi)
                los.append(lo)
            hi = jnp.concatenate(his, axis=1)
            lo = jnp.concatenate(los, axis=1)
            both = both + dot(jnp.concatenate([hi, lo], axis=0), hi, NT)
        gram = (both[:k] + (both[k:] + both[k:].T)) / total
        linv[...] = inverse_factor(gram)
        return carry

    lax.fori_loop(0, ITERS, iteration, 0)
    lh, ll = split2(linv[...])
    hi, lo = ph[own[0], :k, :], ph[own[0], k:, :]
    out[...] = dot(lh, hi) + dot(ll, hi) + dot(lh, lo)


def split3(x):
    a = lax.reduce_precision(x, 8, 7)
    b = lax.reduce_precision(x - a, 8, 7)
    return [v.astype(jnp.bfloat16) for v in (a, b, x - a - b)]


def whole_on_each(n_row, n_col, blocks, block_row, block_col, counts, vectors, row_mass, col_mass):
    tile = blocks[0, 0]
    n_cap = tile.shape[0]
    own, bsize = row_mass.shape
    k = vectors.shape[1] // bsize
    half = bsize // 2
    part = n_cap // n_col
    n_dev = n_row * n_col
    count = counts[0, 0]
    full = count > OFF_CAP
    bf16 = jnp.bfloat16

    sent = jnp.where(full, tile, jnp.zeros_like(tile)).reshape(n_col, part, bsize * bsize)
    got = lax.all_to_all(sent, "col", split_axis=0, concat_axis=0)
    home = jnp.sum(got.astype(jnp.float32), axis=0).astype(bf16)
    home = home.reshape(part, half, 128).transpose(1, 0, 2).reshape(half * part, 128)
    off = tile[:OFF_CAP].reshape(OFF_CAP * half, 128)

    inv_col = 1.0 / jnp.sqrt(col_mass)
    scaled = (vectors.reshape(own, k, bsize) * inv_col[:, None, :]).astype(bf16)
    scaled = scaled.transpose(1, 0, 2).reshape(k, own * bsize)
    mass = row_mass.reshape(own, half, 2).transpose(0, 2, 1).reshape(own * bsize)
    rows, cols = block_row[0, 0], block_col[0, 0]
    small = jnp.concatenate(
        [rows[:OFF_CAP], cols[:OFF_CAP], count[None], jnp.zeros(128 - 2 * OFF_CAP - 1, jnp.int32)]
    )
    meta = [v.astype(bf16) for v in (rows, cols, small)]
    meta = split3(mass) + split3(inv_col.reshape(own * bsize)) + meta
    meta = jnp.stack(meta + [jnp.zeros(128, bf16)] * (META - len(meta)))
    payload = jnp.concatenate([home, off, scaled, meta], axis=0)
    pay = lax.all_gather(payload, ("col", "row"), axis=0)
    ints = pay[:, payload.shape[0] - META + 8, :32].astype(jnp.int32)
    place = lax.axis_index("col") * n_row + lax.axis_index("row")

    height, width = 2 * n_col * bsize, 2 * n_row * bsize
    slots = n_dev * OFF_CAP + UNROLL
    result = pl.pallas_call(
        functools.partial(kernel, n_row, n_col, n_cap, float(n_dev * own * bsize)),
        out_shape=jax.ShapeDtypeStruct((k, 128), jnp.float32),
        in_specs=[
            pl.BlockSpec(memory_space=pltpu.SMEM),
            pl.BlockSpec(memory_space=pltpu.SMEM),
            pl.BlockSpec(memory_space=pltpu.VMEM),
        ],
        out_specs=pl.BlockSpec(memory_space=pltpu.VMEM),
        scratch_shapes=[
            pltpu.SMEM((slots,), jnp.int32),
            pltpu.SMEM((slots,), jnp.int32),
            pltpu.VMEM((n_row, height, 128), jnp.float32),
            pltpu.VMEM((n_row, height, 2 * width), bf16),
            pltpu.VMEM((slots, 128, 128), bf16),
            pltpu.VMEM((n_dev, k, 128), bf16),
            pltpu.VMEM((n_dev, k, 128), jnp.float32),
            pltpu.VMEM((n_dev, k, 128), bf16),
            pltpu.VMEM((n_dev, k, 128), jnp.float32),
            pltpu.VMEM((n_dev, 2 * k, 128), bf16),
            pltpu.VMEM((n_dev, 8, 128), jnp.float32),
            pltpu.VMEM((n_dev, 8, 128), jnp.float32),
            pltpu.VMEM((k, k), jnp.float32),
        ],
        compiler_params=pltpu.CompilerParams(vmem_limit_bytes=VMEM_LIMIT),
        name="iterate",
    )(ints, place[None].astype(jnp.int32), pay)
    return result.reshape(k, own, bsize).transpose(1, 0, 2).reshape(own, k * bsize)


def rotate(projected, gram):
    lower = jnp.linalg.cholesky(gram)
    inverse = lax.linalg.triangular_solve(
        lower, jnp.eye(gram.shape[0], dtype=jnp.float32), left_side=True, lower=True
    )
    return jnp.einsum(
        "kl,bli->bki",
        inverse,
        projected,
        precision=lax.Precision.HIGHEST,
        preferred_element_type=jnp.float32,
    )


def local_gram(projected):
    return jnp.einsum(
        "bki,bli->kl",
        projected,
        projected,
        precision=lax.Precision.HIGHEST,
        preferred_element_type=jnp.float32,
    )


def split_by_tile(blocks, block_row, block_col, counts, vectors, row_mass, col_mass):
    tile = blocks[0, 0]
    n_cap = tile.shape[0]
    bsize = row_mass.shape[1]
    vecs = vectors.shape[1] // bsize
    own = vectors.shape[0]
    n_row = lax.axis_size("row")
    n_col = lax.axis_size("col")
    row_panel = own * n_col
    col_panel = own * n_row
    total_boxes = float(own * bsize * n_row * n_col)
    rows_idx = block_row[0, 0]
    cols_idx = block_col[0, 0]
    live = jnp.arange(n_cap) < counts[0, 0]
    fwd_ids = jnp.where(live, rows_idx, row_panel)
    bwd_ids = jnp.where(live, cols_idx, col_panel)
    square = tile.reshape(n_cap, bsize, bsize)
    inv_col = 1.0 / jnp.sqrt(col_mass)
    current = vectors.reshape(own, vecs, bsize)
    for step in range(ITERS):
        scaled = (current * inv_col[:, None, :]).astype(jnp.bfloat16).reshape(own, vecs * bsize)
        panel = lax.all_gather(scaled, "row", axis=0, tiled=True)
        forward_taken = jnp.take(panel.reshape(col_panel, vecs, bsize), cols_idx, axis=0)
        forward_product = jnp.einsum(
            "bij,bkj->bki", square, forward_taken, preferred_element_type=jnp.float32
        )
        forward_summed = jax.ops.segment_sum(forward_product, fwd_ids, num_segments=row_panel + 1)
        rows_sum = lax.psum_scatter(
            forward_summed[:row_panel].reshape(row_panel, vecs * bsize),
            "col",
            scatter_dimension=0,
            tiled=True,
        )
        weighted = (rows_sum.reshape(own, vecs, bsize) * row_mass[:, None, :]).astype(jnp.bfloat16)
        whole_rows = lax.all_gather(weighted.reshape(own, vecs * bsize), "col", axis=0, tiled=True)
        taken = jnp.take(whole_rows.reshape(row_panel, vecs, bsize), rows_idx, axis=0)
        product = jnp.einsum("bij,bki->bkj", square, taken, preferred_element_type=jnp.float32)
        summed = jax.ops.segment_sum(product, bwd_ids, num_segments=col_panel + 1)
        cols_sum = lax.psum_scatter(
            summed[:col_panel].reshape(col_panel, vecs * bsize),
            "row",
            scatter_dimension=0,
            tiled=True,
        )
        projected = cols_sum.reshape(own, vecs, bsize) * inv_col[:, None, :]
        gram = lax.psum(local_gram(projected), ("row", "col")) / total_boxes
        current = rotate(projected, gram)
    return current.reshape(own, vecs * bsize)


def per_device(blocks, block_row, block_col, counts, vectors, row_mass, col_mass):
    n_row, n_col = lax.axis_size("row"), lax.axis_size("col")
    own, bsize = row_mass.shape
    n_cap = blocks.shape[2]
    dense = n_row * (own * n_col * bsize) * (own * n_row * bsize) * 4
    fits = dense <= VMEM_LIMIT // 4 and own * bsize == 128 and vectors.shape[1] == bsize * bsize
    fits = fits and n_cap == 128 and n_cap % (16 * n_col) == 0 and n_row % 2 == 0 and n_col % 2 == 0
    args = (blocks, block_row, block_col, counts, vectors, row_mass, col_mass)
    return whole_on_each(n_row, n_col, *args) if fits else split_by_tile(*args)


def solution(mesh):
    in_specs = (
        P("row", "col", None, None),
        P("row", "col", None),
        P("row", "col", None),
        P("row", "col"),
        P(("col", "row"), None),
        P(("row", "col"), None),
        P(("col", "row"), None),
    )
    out_specs = P(("col", "row"), None)
    return jax.shard_map(
        per_device, mesh=mesh, in_specs=in_specs, out_specs=out_specs, check_vma=False
    )
```

```python
import functools

import jax
import jax.numpy as jnp
from jax import lax
from jax.experimental import pallas as pl
from jax.experimental.pallas import tpu as pltpu
from jax.sharding import PartitionSpec as P

ITERS = 4
OFF_CAP = 8
META = 16
UNROLL = 8
VMEM_LIMIT = 56 * 1024 * 1024

NT = (((1,), (1,)), ((), ()))
NN = (((1,), (0,)), ((), ()))


def dot(a, b, dims=NN):
    return lax.dot_general(a, b, dims, preferred_element_type=jnp.float32)


def split2(x):
    hi = x.astype(jnp.bfloat16)
    return hi, (x - hi.astype(jnp.float32)).astype(jnp.bfloat16)


def inverse_factor(gram):
    n = gram.shape[0]
    rows = lax.broadcasted_iota(jnp.int32, (n, n), 0)
    cols = lax.broadcasted_iota(jnp.int32, (n, n), 1)
    eye = (rows == cols).astype(jnp.float32)
    both = jnp.concatenate([gram, eye], axis=1)
    count = n // 8
    tiles = [both[8 * t : 8 * t + 8] for t in range(count)]
    sub = lax.broadcasted_iota(jnp.int32, (8, 2 * n), 0)
    lane = lax.broadcasted_iota(jnp.int32, (8, 2 * n), 1)
    for b in range(count):
        spread = {
            t: [jnp.broadcast_to(tiles[t][:, 8 * b + s : 8 * b + s + 1], (8, 2 * n)) for s in range(8)]
            for t in range(b, count)
        }
        for s in range(8):
            inv = 1.0 / spread[b][s][s : s + 1]
            step = tiles[b][s : s + 1] * inv
            ahead = [spread[b][s2][s : s + 1] * inv for s2 in range(s + 1, 8)]
            for t in range(b, count):
                factor = spread[t][s]
                if t == b:
                    factor = jnp.where(sub > s, factor, 0.0)
                for s2 in range(s + 1, 8):
                    spread[t][s2] = spread[t][s2] - factor * ahead[s2 - s - 1]
                tiles[t] = tiles[t] - factor * step
    out = []
    for t in range(count):
        pivot = jnp.sum(jnp.where(lane == sub + 8 * t, tiles[t], 0.0), axis=1, keepdims=True)
        out.append(tiles[t] * lax.rsqrt(pivot))
    return jnp.concatenate(out, axis=0)[:, n:]


def kernel(
    n_row, n_col, n_cap, total,
    meta, own, mine_small, other_small, mine_home, other_home, out,
    lv, lw, sems, small, full, tmp, home, blk, vs, vb, w, wb, wt, wtb, y, yb, ph, rm, ic, linv,
):
    n_dev = n_row * n_col
    group = n_dev // 2
    k = vs.shape[1]
    half = k // 2
    rpairs, cpairs = n_col, n_row
    rblk, cblk = 2 * rpairs, 2 * cpairs
    part = n_cap // n_col
    vec_at = OFF_CAP * half
    meta_at = vec_at + k
    width = cpairs * 128

    core = own[1]
    copies = [
        pltpu.make_async_copy(src, dst.at[pl.ds(at * group, group)], sems.at[i])
        for i, (src, dst, at) in enumerate(
            [
                (mine_small, small, core),
                (other_small, small, 1 - core),
                (mine_home, full, core),
                (other_home, full, 1 - core),
            ]
        )
    ]
    for copy in copies:
        copy.start()
    copies[0].wait()
    copies[1].wait()

    def at_device(r, c):
        return (c % 2) * group + (c // 2) * n_row + r

    def scatter_pair(pair, blocks, q, x):
        pair[q] = x.astype(pair.dtype)
        blocks[2 * q] = x[:, :k].astype(blocks.dtype)
        blocks[2 * q + 1] = x[:, k:].astype(blocks.dtype)

    for r in range(n_row):
        for c in range(n_col):
            q, p, d = c * n_row + r, r * n_col + c, at_device(r, c)
            rows = small[d, meta_at : meta_at + META, :].astype(jnp.float32)
            rm[p] = jnp.broadcast_to(rows[0:1] + rows[1:2] + rows[2:3], (8, 128))
            ic[q] = jnp.broadcast_to(rows[3:4] + rows[4:5] + rows[5:6], (8, 128))
            scatter_pair(vs, vb, q, small[d, vec_at : vec_at + k, :].astype(jnp.float32))

    def device(d, n):
        count = meta[d, 2 * OFF_CAP]
        count = jnp.where(count > OFF_CAP, 0, count)
        within = lax.rem(d, group)
        chip = within // n_row
        c = 2 * chip + d // group
        r = within - chip * n_row
        for s in range(OFF_CAP):
            lv[n + s] = c * cblk + meta[d, OFF_CAP + s]
            lw[n + s] = r * rblk + meta[d, s]
            x = small[d, s * half : (s + 1) * half, :].astype(jnp.float32)
            blk[n + s] = jnp.concatenate([x[:, :k], x[:, k:]], axis=0).astype(jnp.bfloat16)
        return n + count

    n_live = lax.fori_loop(0, n_dev, device, jnp.int32(0))
    for u in range(UNROLL - 1):
        lv[n_live + u] = 0
        lw[n_live + u] = 0
        blk[n_live + u] = jnp.zeros((k, k), jnp.bfloat16)
    n_group = (n_live + UNROLL - 1) // UNROLL

    copies[2].wait()
    copies[3].wait()
    left = lax.broadcasted_iota(jnp.int32, (rblk, 128), 1) < 64
    homes = []
    for r in range(n_row):
        h = jnp.int32(0)
        for c in range(n_col):
            h = jnp.where(meta[at_device(r, c), 2 * OFF_CAP] > OFF_CAP, c, h)
        homes.append(h)
        index = small[at_device(r, h), meta_at : meta_at + META, :].astype(jnp.float32)
        place = index[7:8] * float(rblk) + index[6:7]
        want = lax.broadcasted_iota(jnp.int32, (cblk * rblk, n_cap), 0).astype(jnp.float32)
        select = jnp.where(want == place, 1.0, 0.0).astype(jnp.bfloat16)

        def build(m, carry, r=r, select=select):
            at = pl.multiple_of(m * part, part)
            slots = jnp.concatenate(
                [full[at_device(r, c), pl.ds(at, part), :] for c in range(n_col)], axis=0
            )
            dense = dot(select, slots)
            for u in range(cpairs):
                a = dense[2 * u * rblk : (2 * u + 1) * rblk]
                b = dense[(2 * u + 1) * rblk : (2 * u + 2) * rblk]
                even = jnp.where(left, a, pltpu.roll(b, 64, 1))
                odd = jnp.where(left, pltpu.roll(a, 64, 1), b)
                tmp[u, pl.ds(m, rblk, stride=k), :] = even
                tmp[u, pl.ds(m + half, rblk, stride=k), :] = odd
            return carry

        lax.fori_loop(0, half, build, 0, unroll=4)

        def cut(i, carry, r=r):
            at = pl.multiple_of(i * k, k)
            for u in range(cpairs):
                hi, lo = split2(tmp[u, pl.ds(at, k), :])
                home[r, pl.ds(at, k), u * 128 : (u + 1) * 128] = hi
                home[r, pl.ds(at, k), width + u * 128 : width + (u + 1) * 128] = lo
            return carry

        lax.fori_loop(0, rblk, cut, 0, unroll=4)

    def iteration(it, carry):
        @pl.when(it > 0)
        def _():
            lh, ll = split2(linv[...])
            turn = jnp.concatenate([lh, lh, ll], axis=1)
            for q in range(0, n_dev, 4):
                hi = jnp.concatenate([ph[q + d, :k, :] for d in range(4)], axis=1)
                lo = jnp.concatenate([ph[q + d, k:, :] for d in range(4)], axis=1)
                current = dot(turn, jnp.concatenate([hi, lo, hi], axis=0))
                for d in range(4):
                    x = current[:, d * 128 : (d + 1) * 128] * ic[q + d, 0:1, :]
                    scatter_pair(vs, vb, q + d, x)

        for b in range(2 * n_dev):
            wb[b] = jnp.zeros_like(wb[b])
        for r in range(n_row):
            base = homes[r] * cpairs
            vec = jnp.concatenate([vs[base + u] for u in range(cpairs)] * 2, axis=1)
            for p in range(0, rpairs, 2):
                prod = dot(vec, home[r, p * 128 : (p + 2) * 128, :], NT)
                w[r * rpairs + p] = prod[:, :128]
                w[r * rpairs + p + 1] = prod[:, 128:]

        def forward(i, carry):
            prods = [dot(vb[lv[i * UNROLL + u]], blk[i * UNROLL + u], NT) for u in range(UNROLL)]
            for u in range(UNROLL):
                b = lw[i * UNROLL + u]
                wb[b] = wb[b] + prods[u]
            return carry

        lax.fori_loop(0, n_group, forward, 0)
        for p in range(n_dev):
            x = w[p] + jnp.concatenate([wb[2 * p], wb[2 * p + 1]], axis=1)
            scatter_pair(wt, wtb, p, x * rm[p, 0:1, :])
            y[p] = jnp.zeros_like(y[p])
            yb[2 * p] = jnp.zeros_like(yb[2 * p])
            yb[2 * p + 1] = jnp.zeros_like(yb[2 * p + 1])

        for r in range(n_row):
            base = homes[r] * cpairs
            vec = jnp.concatenate([wt[r * rpairs + p] for p in range(rpairs)], axis=1)
            for u in range(0, cpairs, 2):
                cols = slice(u * 128, (u + 2) * 128)
                tail = slice(width + u * 128, width + (u + 2) * 128)
                prod = dot(vec, home[r, :, cols]) + dot(vec, home[r, :, tail])
                y[base + u] = y[base + u] + prod[:, :128]
                y[base + u + 1] = y[base + u + 1] + prod[:, 128:]

        def backward(i, carry):
            prods = [dot(wtb[lw[i * UNROLL + u]], blk[i * UNROLL + u]) for u in range(UNROLL)]
            for u in range(UNROLL):
                b = lv[i * UNROLL + u]
                yb[b] = yb[b] + prods[u]
            return carry

        lax.fori_loop(0, n_group, backward, 0)

        both = jnp.zeros((2 * k, k), jnp.float32)
        for q in range(0, n_dev, 4):
            his, los = [], []
            for d in range(q, q + 4):
                x = y[d] + jnp.concatenate([yb[2 * d], yb[2 * d + 1]], axis=1)
                hi, lo = split2(x * ic[d, 0:1, :])
                ph[d, :k, :] = hi
                ph[d, k:, :] = lo
                his.append(hi)
                los.append(lo)
            hi = jnp.concatenate(his, axis=1)
            lo = jnp.concatenate(los, axis=1)
            both = both + dot(jnp.concatenate([hi, lo], axis=0), hi, NT)
        gram = (both[:k] + (both[k:] + both[k:].T)) / total
        linv[...] = inverse_factor(gram)
        return carry

    lax.fori_loop(0, ITERS, iteration, 0)
    lh, ll = split2(linv[...])
    hi, lo = ph[own[0], :k, :], ph[own[0], k:, :]
    x = dot(lh, hi) + dot(ll, hi) + dot(lh, lo)
    out[0] = x[:, :k]
    out[1] = x[:, k:]


def split3(x):
    a = lax.reduce_precision(x, 8, 7)
    b = lax.reduce_precision(x - a, 8, 7)
    return [v.astype(jnp.bfloat16) for v in (a, b, x - a - b)]


def whole_on_each(n_row, n_col, blocks, block_row, block_col, counts, vectors, row_mass, col_mass):
    tile = blocks[0, 0]
    n_cap = tile.shape[0]
    own, bsize = row_mass.shape
    k = vectors.shape[1] // bsize
    half = bsize // 2
    part = n_cap // n_col
    n_dev = n_row * n_col
    count = counts[0, 0]
    has_full = count > OFF_CAP
    bf16 = jnp.bfloat16
    row, chip, core = (lax.axis_index(name) for name in ("row", "chip", "core"))

    off = tile[:OFF_CAP].reshape(OFF_CAP * half, 128)
    inv_col = 1.0 / jnp.sqrt(col_mass)
    scaled = (vectors.reshape(own, k, bsize) * inv_col[:, None, :]).astype(bf16)
    scaled = scaled.transpose(1, 0, 2).reshape(k, own * bsize)
    mass = row_mass.reshape(own, half, 2).transpose(0, 2, 1).reshape(own * bsize)
    rows, cols = block_row[0, 0], block_col[0, 0]
    short = jnp.concatenate(
        [rows[:OFF_CAP], cols[:OFF_CAP], count[None], jnp.zeros(128 - 2 * OFF_CAP - 1, jnp.int32)]
    )
    meta = [v.astype(bf16) for v in (rows, cols, short)]
    meta = split3(mass) + split3(inv_col.reshape(own * bsize)) + meta
    meta = jnp.stack(meta + [jnp.zeros(128, bf16)] * (META - len(meta)))
    small = jnp.concatenate([off, scaled, meta], axis=0)
    mine_small = lax.all_gather(small, ("chip", "row"), axis=0)
    other_small = lax.ppermute(mine_small, "core", [(0, 1), (1, 0)])

    sent = jnp.where(has_full, tile, jnp.zeros_like(tile)).reshape(n_col, part, bsize * bsize)
    got = lax.all_to_all(sent, ("chip", "core"), split_axis=0, concat_axis=0)
    home = jnp.sum(got.astype(jnp.float32), axis=0).astype(bf16)
    home = home.reshape(part, half, 128).transpose(1, 0, 2).reshape(half * part, 128)
    mine_home = lax.all_gather(home, ("chip", "row"), axis=0)
    other_home = lax.ppermute(mine_home, "core", [(0, 1), (1, 0)])

    at = small.shape[0] - META + 8
    mine, other = mine_small[:, at, :32], other_small[:, at, :32]
    first = jnp.where(core == 0, mine, other)
    second = jnp.where(core == 0, other, mine)
    ints = jnp.concatenate([first, second], axis=0).astype(jnp.int32)
    place = jnp.stack([(2 * chip + core) * n_row + row, core]).astype(jnp.int32)

    height, width = 2 * n_col * bsize, 2 * n_row * bsize
    slots = n_dev * OFF_CAP + UNROLL
    pair_f32 = pltpu.VMEM((n_dev, k, 128), jnp.float32)
    pair_bf16 = pltpu.VMEM((n_dev, k, 128), bf16)
    block_f32 = pltpu.VMEM((2 * n_dev, k, bsize), jnp.float32)
    block_bf16 = pltpu.VMEM((2 * n_dev, k, bsize), bf16)
    mass_f32 = pltpu.VMEM((n_dev, 8, 128), jnp.float32)
    result = pl.pallas_call(
        functools.partial(kernel, n_row, n_col, n_cap, float(n_dev * own * bsize)),
        out_shape=jax.ShapeDtypeStruct((own, k, bsize), jnp.float32),
        in_specs=[pl.BlockSpec(memory_space=pltpu.SMEM)] * 2
        + [pl.BlockSpec(memory_space=pl.ANY)] * 4,
        out_specs=pl.BlockSpec(memory_space=pltpu.VMEM),
        scratch_shapes=[
            pltpu.SMEM((slots,), jnp.int32),
            pltpu.SMEM((slots,), jnp.int32),
            pltpu.SemaphoreType.DMA((4,)),
            pltpu.VMEM((n_dev,) + small.shape, bf16),
            pltpu.VMEM((n_dev,) + home.shape, bf16),
            pltpu.VMEM((n_row, height, 128), jnp.float32),
            pltpu.VMEM((n_row, height, 2 * width), bf16),
            pltpu.VMEM((slots, bsize, bsize), bf16),
            pair_bf16, block_bf16, pair_f32, block_f32,
            pair_bf16, block_bf16, pair_f32, block_f32,
            pltpu.VMEM((n_dev, 2 * k, 128), bf16),
            mass_f32, mass_f32,
            pltpu.VMEM((k, k), jnp.float32),
        ],
        compiler_params=pltpu.CompilerParams(vmem_limit_bytes=VMEM_LIMIT),
        name="iterate",
    )(ints, place, mine_small, other_small, mine_home, other_home)
    return result.reshape(own, k * bsize)


def rotate(projected, gram):
    lower = jnp.linalg.cholesky(gram)
    inverse = lax.linalg.triangular_solve(
        lower, jnp.eye(gram.shape[0], dtype=jnp.float32), left_side=True, lower=True
    )
    return jnp.einsum(
        "kl,bli->bki",
        inverse,
        projected,
        precision=lax.Precision.HIGHEST,
        preferred_element_type=jnp.float32,
    )


def local_gram(projected):
    return jnp.einsum(
        "bki,bli->kl",
        projected,
        projected,
        precision=lax.Precision.HIGHEST,
        preferred_element_type=jnp.float32,
    )


def split_by_tile(blocks, block_row, block_col, counts, vectors, row_mass, col_mass):
    tile = blocks[0, 0]
    n_cap = tile.shape[0]
    bsize = row_mass.shape[1]
    vecs = vectors.shape[1] // bsize
    own = vectors.shape[0]
    n_row = lax.axis_size("row")
    n_col = lax.axis_size("col")
    row_panel = own * n_col
    col_panel = own * n_row
    total_boxes = float(own * bsize * n_row * n_col)
    rows_idx = block_row[0, 0]
    cols_idx = block_col[0, 0]
    live = jnp.arange(n_cap) < counts[0, 0]
    fwd_ids = jnp.where(live, rows_idx, row_panel)
    bwd_ids = jnp.where(live, cols_idx, col_panel)
    square = tile.reshape(n_cap, bsize, bsize)
    inv_col = 1.0 / jnp.sqrt(col_mass)
    current = vectors.reshape(own, vecs, bsize)
    for step in range(ITERS):
        scaled = (current * inv_col[:, None, :]).astype(jnp.bfloat16).reshape(own, vecs * bsize)
        panel = lax.all_gather(scaled, "row", axis=0, tiled=True)
        forward_taken = jnp.take(panel.reshape(col_panel, vecs, bsize), cols_idx, axis=0)
        forward_product = jnp.einsum(
            "bij,bkj->bki", square, forward_taken, preferred_element_type=jnp.float32
        )
        forward_summed = jax.ops.segment_sum(forward_product, fwd_ids, num_segments=row_panel + 1)
        rows_sum = lax.psum_scatter(
            forward_summed[:row_panel].reshape(row_panel, vecs * bsize),
            "col",
            scatter_dimension=0,
            tiled=True,
        )
        weighted = (rows_sum.reshape(own, vecs, bsize) * row_mass[:, None, :]).astype(jnp.bfloat16)
        whole_rows = lax.all_gather(weighted.reshape(own, vecs * bsize), "col", axis=0, tiled=True)
        taken = jnp.take(whole_rows.reshape(row_panel, vecs, bsize), rows_idx, axis=0)
        product = jnp.einsum("bij,bki->bkj", square, taken, preferred_element_type=jnp.float32)
        summed = jax.ops.segment_sum(product, bwd_ids, num_segments=col_panel + 1)
        cols_sum = lax.psum_scatter(
            summed[:col_panel].reshape(col_panel, vecs * bsize),
            "row",
            scatter_dimension=0,
            tiled=True,
        )
        projected = cols_sum.reshape(own, vecs, bsize) * inv_col[:, None, :]
        gram = lax.psum(local_gram(projected), ("row", "col")) / total_boxes
        current = rotate(projected, gram)
    return current.reshape(own, vecs * bsize)


def fits(n_row, n_col, blocks, vectors, row_mass):
    own, bsize = row_mass.shape[0] // (n_row * n_col), row_mass.shape[1]
    n_cap = blocks.shape[2]
    dense = n_row * (own * n_col * bsize) * (own * n_row * bsize) * 4
    shapes = own * bsize == 128 and vectors.shape[1] == bsize * bsize and n_cap == 128
    return dense <= VMEM_LIMIT // 4 and shapes and n_cap % (16 * n_col) == 0 and n_row % 4 == 0


def solution(mesh):
    n_row, n_col = mesh.shape["row"], mesh.shape["col"]

    def run(blocks, block_row, block_col, counts, vectors, row_mass, col_mass):
        args = (blocks, block_row, block_col, counts, vectors, row_mass, col_mass)
        if fits(n_row, n_col, blocks, vectors, row_mass):
            devices = mesh.devices.reshape(n_row, n_col // 2, 2)
            grid, col = jax.sharding.Mesh(devices, ("row", "chip", "core")), ("chip", "core")
            body = functools.partial(whole_on_each, n_row, n_col)
        else:
            grid, col, body = mesh, ("col",), split_by_tile
        by_row, by_col = P(("row",) + col, None), P(col + ("row",), None)
        in_specs = (
            P("row", col, None, None), P("row", col, None), P("row", col, None), P("row", col),
            by_col, by_row, by_col,
        )
        return jax.shard_map(
            body, mesh=grid, in_specs=in_specs, out_specs=by_col, check_vma=False
        )(*args)

    return run
```

```python
import functools

import jax
import jax.numpy as jnp
from jax import lax
from jax.experimental import pallas as pl
from jax.experimental.pallas import tpu as pltpu
from jax.sharding import PartitionSpec as P

ITERS = 4
OFF_CAP = 8
META = 16
UNROLL = 8
VMEM_LIMIT = 56 * 1024 * 1024

NT = (((1,), (1,)), ((), ()))
NN = (((1,), (0,)), ((), ()))


def dot(a, b, dims=NN):
    return lax.dot_general(a, b, dims, preferred_element_type=jnp.float32)


def split2(x):
    hi = x.astype(jnp.bfloat16)
    return hi, (x - hi.astype(jnp.float32)).astype(jnp.bfloat16)


def inverse_factor(gram):
    n = gram.shape[0]
    rows = lax.broadcasted_iota(jnp.int32, (n, n), 0)
    cols = lax.broadcasted_iota(jnp.int32, (n, n), 1)
    eye = (rows == cols).astype(jnp.float32)
    both = jnp.concatenate([gram, eye], axis=1)
    count = n // 8
    tiles = [both[8 * t : 8 * t + 8] for t in range(count)]
    sub = lax.broadcasted_iota(jnp.int32, (8, 2 * n), 0)
    lane = lax.broadcasted_iota(jnp.int32, (8, 2 * n), 1)
    for b in range(count):
        spread = {
            t: [jnp.broadcast_to(tiles[t][:, 8 * b + s : 8 * b + s + 1], (8, 2 * n)) for s in range(8)]
            for t in range(b, count)
        }
        for s in range(8):
            inv = 1.0 / spread[b][s][s : s + 1]
            step = tiles[b][s : s + 1] * inv
            ahead = [spread[b][s2][s : s + 1] * inv for s2 in range(s + 1, 8)]
            for t in range(b, count):
                factor = spread[t][s]
                if t == b:
                    factor = jnp.where(sub > s, factor, 0.0)
                for s2 in range(s + 1, 8):
                    spread[t][s2] = spread[t][s2] - factor * ahead[s2 - s - 1]
                tiles[t] = tiles[t] - factor * step
    out = []
    for t in range(count):
        pivot = jnp.sum(jnp.where(lane == sub + 8 * t, tiles[t], 0.0), axis=1, keepdims=True)
        out.append(tiles[t] * lax.rsqrt(pivot))
    return jnp.concatenate(out, axis=0)[:, n:]


def kernel(
    n_row, n_col, n_cap, total,
    meta, own, *rest,
):
    smalls, fulls, out = rest[:8], rest[8:16], rest[16]
    lv, lw, sems, small, full, tmp, home, blk = rest[17:25]
    vs, vb, w, wb, wt, wtb, y, yb, ph, rm, ic, linv = rest[25:]
    n_dev = n_row * n_col
    group = n_dev // 2
    k = vs.shape[1]
    half = k // 2
    rpairs, cpairs = n_col, n_row
    rblk, cblk = 2 * rpairs, 2 * cpairs
    part = n_cap // n_col
    vec_at = OFF_CAP * half
    meta_at = vec_at + k
    width = cpairs * 128

    here, chip, core = own[0], own[1], own[2]
    piece = n_dev // 8
    waits = []
    for i, (srcs, dst) in enumerate([(smalls, small), (fulls, full)]):
        for j, ref in enumerate(srcs):
            copy = pltpu.make_async_copy(ref, dst.at[pl.ds(j * piece, piece)], sems.at[8 * i + j])
            copy.start()
            waits.append(copy)
    for copy in waits[:8]:
        copy.wait()

    def at_device(r, c):
        dr, dc, dk = here ^ r, chip ^ (c // 2), core ^ (c % 2)
        dx, dy = dc & 1, dc >> 1
        order = jnp.where(dr < 2, 4 * dy + 2 * dx, 8 + 4 * dx + 2 * dy)
        return dk * group + order + (dr & 1)

    def scatter_pair(pair, blocks, q, x):
        pair[q] = x.astype(pair.dtype)
        blocks[2 * q] = x[:, :k].astype(blocks.dtype)
        blocks[2 * q + 1] = x[:, k:].astype(blocks.dtype)

    for r in range(n_row):
        for c in range(n_col):
            q, p, d = c * n_row + r, r * n_col + c, at_device(r, c)
            rows = small[d, meta_at : meta_at + META, :].astype(jnp.float32)
            rm[p] = jnp.broadcast_to(rows[0:1] + rows[1:2] + rows[2:3], (8, 128))
            ic[q] = jnp.broadcast_to(rows[3:4] + rows[4:5] + rows[5:6], (8, 128))
            scatter_pair(vs, vb, q, small[d, vec_at : vec_at + k, :].astype(jnp.float32))

    def device(d, n):
        count = meta[d, 2 * OFF_CAP]
        count = jnp.where(count > OFF_CAP, 0, count)
        near = (d & 8) == 0
        one, two = (d >> 1) & 1, (d >> 2) & 1
        dc = jnp.where(near, 2 * two + one, 2 * one + two)
        c = 2 * (chip ^ dc) + (core ^ (d >> 4))
        r = here ^ (jnp.where(near, 0, 2) + (d & 1))
        for s in range(OFF_CAP):
            lv[n + s] = c * cblk + meta[d, OFF_CAP + s]
            lw[n + s] = r * rblk + meta[d, s]
            x = small[d, s * half : (s + 1) * half, :].astype(jnp.float32)
            blk[n + s] = jnp.concatenate([x[:, :k], x[:, k:]], axis=0).astype(jnp.bfloat16)
        return n + count

    n_live = lax.fori_loop(0, n_dev, device, jnp.int32(0))
    for u in range(UNROLL - 1):
        lv[n_live + u] = 0
        lw[n_live + u] = 0
        blk[n_live + u] = jnp.zeros((k, k), jnp.bfloat16)
    n_group = (n_live + UNROLL - 1) // UNROLL

    for copy in waits[8:]:
        copy.wait()
    left = lax.broadcasted_iota(jnp.int32, (rblk, 128), 1) < 64
    homes = []
    for r in range(n_row):
        h = jnp.int32(0)
        for c in range(n_col):
            h = jnp.where(meta[at_device(r, c), 2 * OFF_CAP] > OFF_CAP, c, h)
        homes.append(h)
        index = small[at_device(r, h), meta_at : meta_at + META, :].astype(jnp.float32)
        place = index[7:8] * float(rblk) + index[6:7]
        want = lax.broadcasted_iota(jnp.int32, (cblk * rblk, n_cap), 0).astype(jnp.float32)
        select = jnp.where(want == place, 1.0, 0.0).astype(jnp.bfloat16)

        parts = [at_device(r, 2 * i + j) for j in range(2) for i in range(n_col // 2)]

        def build(m, carry, parts=parts, select=select):
            at = pl.multiple_of(m * part, part)
            slots = jnp.concatenate(
                [full[d, pl.ds(at, part), :] for d in parts], axis=0
            )
            dense = dot(select, slots)
            for u in range(cpairs):
                a = dense[2 * u * rblk : (2 * u + 1) * rblk]
                b = dense[(2 * u + 1) * rblk : (2 * u + 2) * rblk]
                even = jnp.where(left, a, pltpu.roll(b, 64, 1))
                odd = jnp.where(left, pltpu.roll(a, 64, 1), b)
                tmp[u, pl.ds(m, rblk, stride=k), :] = even
                tmp[u, pl.ds(m + half, rblk, stride=k), :] = odd
            return carry

        lax.fori_loop(0, half, build, 0, unroll=4)

        def cut(i, carry, r=r):
            at = pl.multiple_of(i * k, k)
            for u in range(cpairs):
                hi, lo = split2(tmp[u, pl.ds(at, k), :])
                home[r, pl.ds(at, k), u * 128 : (u + 1) * 128] = hi
                home[r, pl.ds(at, k), width + u * 128 : width + (u + 1) * 128] = lo
            return carry

        lax.fori_loop(0, rblk, cut, 0, unroll=4)

    def iteration(it, carry):
        @pl.when(it > 0)
        def _():
            lh, ll = split2(linv[...])
            turn = jnp.concatenate([lh, lh, ll], axis=1)
            for q in range(0, n_dev, 4):
                hi = jnp.concatenate([ph[q + d, :k, :] for d in range(4)], axis=1)
                lo = jnp.concatenate([ph[q + d, k:, :] for d in range(4)], axis=1)
                current = dot(turn, jnp.concatenate([hi, lo, hi], axis=0))
                for d in range(4):
                    x = current[:, d * 128 : (d + 1) * 128] * ic[q + d, 0:1, :]
                    scatter_pair(vs, vb, q + d, x)

        for b in range(2 * n_dev):
            wb[b] = jnp.zeros_like(wb[b])
        for r in range(n_row):
            base = homes[r] * cpairs
            vec = jnp.concatenate([vs[base + u] for u in range(cpairs)] * 2, axis=1)
            for p in range(0, rpairs, 2):
                prod = dot(vec, home[r, p * 128 : (p + 2) * 128, :], NT)
                w[r * rpairs + p] = prod[:, :128]
                w[r * rpairs + p + 1] = prod[:, 128:]

        def forward(i, carry):
            prods = [dot(vb[lv[i * UNROLL + u]], blk[i * UNROLL + u], NT) for u in range(UNROLL)]
            for u in range(UNROLL):
                b = lw[i * UNROLL + u]
                wb[b] = wb[b] + prods[u]
            return carry

        lax.fori_loop(0, n_group, forward, 0)
        for p in range(n_dev):
            x = w[p] + jnp.concatenate([wb[2 * p], wb[2 * p + 1]], axis=1)
            scatter_pair(wt, wtb, p, x * rm[p, 0:1, :])
            y[p] = jnp.zeros_like(y[p])
            yb[2 * p] = jnp.zeros_like(yb[2 * p])
            yb[2 * p + 1] = jnp.zeros_like(yb[2 * p + 1])

        for r in range(n_row):
            base = homes[r] * cpairs
            vec = jnp.concatenate([wt[r * rpairs + p] for p in range(rpairs)], axis=1)
            for u in range(0, cpairs, 2):
                cols = slice(u * 128, (u + 2) * 128)
                tail = slice(width + u * 128, width + (u + 2) * 128)
                prod = dot(vec, home[r, :, cols]) + dot(vec, home[r, :, tail])
                y[base + u] = y[base + u] + prod[:, :128]
                y[base + u + 1] = y[base + u + 1] + prod[:, 128:]

        def backward(i, carry):
            prods = [dot(wtb[lw[i * UNROLL + u]], blk[i * UNROLL + u]) for u in range(UNROLL)]
            for u in range(UNROLL):
                b = lv[i * UNROLL + u]
                yb[b] = yb[b] + prods[u]
            return carry

        lax.fori_loop(0, n_group, backward, 0)

        both = jnp.zeros((2 * k, k), jnp.float32)
        for q in range(0, n_dev, 4):
            his, los = [], []
            for d in range(q, q + 4):
                x = y[d] + jnp.concatenate([yb[2 * d], yb[2 * d + 1]], axis=1)
                hi, lo = split2(x * ic[d, 0:1, :])
                ph[d, :k, :] = hi
                ph[d, k:, :] = lo
                his.append(hi)
                los.append(lo)
            hi = jnp.concatenate(his, axis=1)
            lo = jnp.concatenate(los, axis=1)
            both = both + dot(jnp.concatenate([hi, lo], axis=0), hi, NT)
        gram = (both[:k] + (both[k:] + both[k:].T)) / total
        linv[...] = inverse_factor(gram)
        return carry

    lax.fori_loop(0, ITERS, iteration, 0)
    lh, ll = split2(linv[...])
    place = (2 * chip + core) * n_row + here
    hi, lo = ph[place, :k, :], ph[place, k:, :]
    x = dot(lh, hi) + dot(ll, hi) + dot(lh, lo)
    out[0] = x[:, :k]
    out[1] = x[:, k:]


def split3(x):
    a = lax.reduce_precision(x, 8, 7)
    b = lax.reduce_precision(x - a, 8, 7)
    return [v.astype(jnp.bfloat16) for v in (a, b, x - a - b)]


def swap(x, axis, distance):
    size = lax.axis_size(axis)
    return lax.ppermute(x, axis, [(i, i ^ distance) for i in range(size)])


def spread(x):
    near, far = jnp.stack([x, swap(x, "row", 1)]), jnp.stack([swap(x, "row", 2), swap(x, "row", 3)])
    near = jnp.concatenate([near, swap(near, "chip", 1)])
    far = jnp.concatenate([far, swap(far, "chip", 2)])
    mine = [near, swap(near, "chip", 2), far, swap(far, "chip", 1)]
    return mine + [swap(v, "core", 1) for v in mine]


def full_part(tile, has_full, n_chip, part, chip, core):
    tile = tile.reshape(2, n_chip, part, tile.shape[1])
    none = jnp.zeros(tile.shape[1:], tile.dtype)
    kept, sent = (
        jnp.where(has_full, lax.dynamic_index_in_dim(tile, i, 0, False), none)
        for i in (core, 1 - core)
    )
    both = kept + swap(sent, "core", 1)
    mine = lax.dynamic_index_in_dim(both, chip, 0, False)
    for s in range(1, n_chip):
        mine = mine + swap(lax.dynamic_index_in_dim(both, chip ^ s, 0, False), "chip", s)
    return mine


def whole_on_each(n_row, n_col, blocks, block_row, block_col, counts, vectors, row_mass, col_mass):
    tile = blocks[0, 0]
    n_cap = tile.shape[0]
    own, bsize = row_mass.shape
    k = vectors.shape[1] // bsize
    half = bsize // 2
    part = n_cap // n_col
    n_dev = n_row * n_col
    count = counts[0, 0]
    has_full = count > OFF_CAP
    bf16 = jnp.bfloat16
    row, chip, core = (lax.axis_index(name) for name in ("row", "chip", "core"))

    off = tile[:OFF_CAP].reshape(OFF_CAP * half, 128)
    inv_col = 1.0 / jnp.sqrt(col_mass)
    scaled = (vectors.reshape(own, k, bsize) * inv_col[:, None, :]).astype(bf16)
    scaled = scaled.transpose(1, 0, 2).reshape(k, own * bsize)
    mass = row_mass.reshape(own, half, 2).transpose(0, 2, 1).reshape(own * bsize)
    rows, cols = block_row[0, 0], block_col[0, 0]
    short = jnp.concatenate(
        [rows[:OFF_CAP], cols[:OFF_CAP], count[None], jnp.zeros(128 - 2 * OFF_CAP - 1, jnp.int32)]
    )
    meta = [v.astype(bf16) for v in (rows, cols, short)]
    meta = split3(mass) + split3(inv_col.reshape(own * bsize)) + meta
    meta = jnp.stack(meta + [jnp.zeros(128, bf16)] * (META - len(meta)))
    small = jnp.concatenate([off, scaled, meta], axis=0)
    smalls = spread(small)

    home = full_part(tile, has_full, n_col // 2, part, chip, core)
    home = home.reshape(part, half, 128).transpose(1, 0, 2).reshape(half * part, 128)
    homes = spread(home)

    at = small.shape[0] - META + 8
    ints = jnp.concatenate([v[:, at, :32] for v in smalls], axis=0).astype(jnp.int32)
    place = jnp.stack([row, chip, core]).astype(jnp.int32)

    height, width = 2 * n_col * bsize, 2 * n_row * bsize
    slots = n_dev * OFF_CAP + UNROLL
    pair_f32 = pltpu.VMEM((n_dev, k, 128), jnp.float32)
    pair_bf16 = pltpu.VMEM((n_dev, k, 128), bf16)
    block_f32 = pltpu.VMEM((2 * n_dev, k, bsize), jnp.float32)
    block_bf16 = pltpu.VMEM((2 * n_dev, k, bsize), bf16)
    mass_f32 = pltpu.VMEM((n_dev, 8, 128), jnp.float32)
    result = pl.pallas_call(
        functools.partial(kernel, n_row, n_col, n_cap, float(n_dev * own * bsize)),
        out_shape=jax.ShapeDtypeStruct((own, k, bsize), jnp.float32),
        in_specs=[pl.BlockSpec(memory_space=pltpu.SMEM)] * 2
        + [pl.BlockSpec(memory_space=pl.ANY)] * 16,
        out_specs=pl.BlockSpec(memory_space=pltpu.VMEM),
        scratch_shapes=[
            pltpu.SMEM((slots,), jnp.int32),
            pltpu.SMEM((slots,), jnp.int32),
            pltpu.SemaphoreType.DMA((16,)),
            pltpu.VMEM((n_dev,) + small.shape, bf16),
            pltpu.VMEM((n_dev,) + home.shape, bf16),
            pltpu.VMEM((n_row, height, 128), jnp.float32),
            pltpu.VMEM((n_row, height, 2 * width), bf16),
            pltpu.VMEM((slots, bsize, bsize), bf16),
            pair_bf16, block_bf16, pair_f32, block_f32,
            pair_bf16, block_bf16, pair_f32, block_f32,
            pltpu.VMEM((n_dev, 2 * k, 128), bf16),
            mass_f32, mass_f32,
            pltpu.VMEM((k, k), jnp.float32),
        ],
        compiler_params=pltpu.CompilerParams(vmem_limit_bytes=VMEM_LIMIT),
        name="iterate",
    )(ints, place, *smalls, *homes)
    return result.reshape(own, k * bsize)


def rotate(projected, gram):
    lower = jnp.linalg.cholesky(gram)
    inverse = lax.linalg.triangular_solve(
        lower, jnp.eye(gram.shape[0], dtype=jnp.float32), left_side=True, lower=True
    )
    return jnp.einsum(
        "kl,bli->bki",
        inverse,
        projected,
        precision=lax.Precision.HIGHEST,
        preferred_element_type=jnp.float32,
    )


def local_gram(projected):
    return jnp.einsum(
        "bki,bli->kl",
        projected,
        projected,
        precision=lax.Precision.HIGHEST,
        preferred_element_type=jnp.float32,
    )


def split_by_tile(blocks, block_row, block_col, counts, vectors, row_mass, col_mass):
    tile = blocks[0, 0]
    n_cap = tile.shape[0]
    bsize = row_mass.shape[1]
    vecs = vectors.shape[1] // bsize
    own = vectors.shape[0]
    n_row = lax.axis_size("row")
    n_col = lax.axis_size("col")
    row_panel = own * n_col
    col_panel = own * n_row
    total_boxes = float(own * bsize * n_row * n_col)
    rows_idx = block_row[0, 0]
    cols_idx = block_col[0, 0]
    live = jnp.arange(n_cap) < counts[0, 0]
    fwd_ids = jnp.where(live, rows_idx, row_panel)
    bwd_ids = jnp.where(live, cols_idx, col_panel)
    square = tile.reshape(n_cap, bsize, bsize)
    inv_col = 1.0 / jnp.sqrt(col_mass)
    current = vectors.reshape(own, vecs, bsize)
    for step in range(ITERS):
        scaled = (current * inv_col[:, None, :]).astype(jnp.bfloat16).reshape(own, vecs * bsize)
        panel = lax.all_gather(scaled, "row", axis=0, tiled=True)
        forward_taken = jnp.take(panel.reshape(col_panel, vecs, bsize), cols_idx, axis=0)
        forward_product = jnp.einsum(
            "bij,bkj->bki", square, forward_taken, preferred_element_type=jnp.float32
        )
        forward_summed = jax.ops.segment_sum(forward_product, fwd_ids, num_segments=row_panel + 1)
        rows_sum = lax.psum_scatter(
            forward_summed[:row_panel].reshape(row_panel, vecs * bsize),
            "col",
            scatter_dimension=0,
            tiled=True,
        )
        weighted = (rows_sum.reshape(own, vecs, bsize) * row_mass[:, None, :]).astype(jnp.bfloat16)
        whole_rows = lax.all_gather(weighted.reshape(own, vecs * bsize), "col", axis=0, tiled=True)
        taken = jnp.take(whole_rows.reshape(row_panel, vecs, bsize), rows_idx, axis=0)
        product = jnp.einsum("bij,bki->bkj", square, taken, preferred_element_type=jnp.float32)
        summed = jax.ops.segment_sum(product, bwd_ids, num_segments=col_panel + 1)
        cols_sum = lax.psum_scatter(
            summed[:col_panel].reshape(col_panel, vecs * bsize),
            "row",
            scatter_dimension=0,
            tiled=True,
        )
        projected = cols_sum.reshape(own, vecs, bsize) * inv_col[:, None, :]
        gram = lax.psum(local_gram(projected), ("row", "col")) / total_boxes
        current = rotate(projected, gram)
    return current.reshape(own, vecs * bsize)


def fits(n_row, n_col, blocks, vectors, row_mass):
    own, bsize = row_mass.shape[0] // (n_row * n_col), row_mass.shape[1]
    n_cap = blocks.shape[2]
    dense = n_row * (own * n_col * bsize) * (own * n_row * bsize) * 4
    shapes = own * bsize == 128 and vectors.shape[1] == bsize * bsize and n_cap == 128
    return dense <= VMEM_LIMIT // 4 and shapes and n_cap % (16 * n_col) == 0 and n_row == 4 and n_col == 8


def solution(mesh):
    n_row, n_col = mesh.shape["row"], mesh.shape["col"]

    def run(blocks, block_row, block_col, counts, vectors, row_mass, col_mass):
        args = (blocks, block_row, block_col, counts, vectors, row_mass, col_mass)
        if fits(n_row, n_col, blocks, vectors, row_mass):
            devices = mesh.devices.reshape(n_row, n_col // 2, 2)
            grid, col = jax.sharding.Mesh(devices, ("row", "chip", "core")), ("chip", "core")
            body = functools.partial(whole_on_each, n_row, n_col)
        else:
            grid, col, body = mesh, ("col",), split_by_tile
        by_row, by_col = P(("row",) + col, None), P(col + ("row",), None)
        in_specs = (
            P("row", col, None, None), P("row", col, None), P("row", col, None), P("row", col),
            by_col, by_row, by_col,
        )
        return jax.shard_map(
            body, mesh=grid, in_specs=in_specs, out_specs=by_col, check_vma=False
        )(*args)

    return run
```

```python
import functools

import jax
import jax.numpy as jnp
from jax import lax
from jax.experimental import pallas as pl
from jax.experimental.pallas import tpu as pltpu
from jax.sharding import PartitionSpec as P

ITERS = 4
OFF_CAP = 8
META = 16
UNROLL = 8
VMEM_LIMIT = 40 * 1024 * 1024

NT = (((1,), (1,)), ((), ()))
NN = (((1,), (0,)), ((), ()))


def dot(a, b, dims=NN):
    return lax.dot_general(a, b, dims, preferred_element_type=jnp.float32)


def split2(x):
    hi = x.astype(jnp.bfloat16)
    return hi, (x - hi.astype(jnp.float32)).astype(jnp.bfloat16)


def reciprocal(x):
    y = pl.reciprocal(x, approx=True)
    for _ in range(2):
        y = y * (2.0 - x * y)
    return y


def inverse_factor(gram):
    n = gram.shape[0]
    rows = lax.broadcasted_iota(jnp.int32, (n, n), 0)
    cols = lax.broadcasted_iota(jnp.int32, (n, n), 1)
    eye = (rows == cols).astype(jnp.float32)
    both = jnp.concatenate([gram, eye], axis=1)
    count = n // 8
    tiles = [both[8 * t : 8 * t + 8] for t in range(count)]
    sub = lax.broadcasted_iota(jnp.int32, (8, 2 * n), 0)
    lane = lax.broadcasted_iota(jnp.int32, (8, 2 * n), 1)
    for b in range(count):
        spread = {
            t: [jnp.broadcast_to(tiles[t][:, 8 * b + s : 8 * b + s + 1], (8, 2 * n)) for s in range(8)]
            for t in range(b, count)
        }
        for s in range(8):
            inv = reciprocal(spread[b][s][s : s + 1])
            step = tiles[b][s : s + 1] * inv
            ahead = [spread[b][s2][s : s + 1] * inv for s2 in range(s + 1, 8)]
            for t in range(b, count):
                factor = spread[t][s]
                if t == b:
                    factor = jnp.where(sub > s, factor, 0.0)
                for s2 in range(s + 1, 8):
                    spread[t][s2] = spread[t][s2] - factor * ahead[s2 - s - 1]
                tiles[t] = tiles[t] - factor * step
    out = []
    for t in range(count):
        pivot = jnp.sum(jnp.where(lane == sub + 8 * t, tiles[t], 0.0), axis=1, keepdims=True)
        out.append(tiles[t] * lax.rsqrt(pivot))
    return jnp.concatenate(out, axis=0)[:, n:]


def kernel(
    n_row, n_col, n_cap, total,
    own, *rest,
):
    smalls, fulls, out = rest[:8], rest[8:16], rest[16]
    ints, meta, lv, lw, sems, small, full, tmp, home, blk = rest[17:27]
    vs, vb, w, wb, wt, wtb, y, yb, ph, rm, ic, linv = rest[27:]
    n_dev = n_row * n_col
    group = n_dev // 2
    k = vs.shape[1]
    half = k // 2
    rpairs, cpairs = n_col, n_row
    rblk, cblk = 2 * rpairs, 2 * cpairs
    part = n_cap // n_col
    vec_at = OFF_CAP * half
    meta_at = vec_at + k
    width = cpairs * 128

    here, chip, core = own[0], own[1], own[2]
    piece = n_dev // 8
    waits = []
    for i, (srcs, dst) in enumerate([(smalls, small), (fulls, full)]):
        for j, ref in enumerate(srcs):
            copy = pltpu.make_async_copy(ref, dst.at[pl.ds(j * piece, piece)], sems.at[8 * i + j])
            copy.start()
            waits.append(copy)
    for copy in waits[:8]:
        copy.wait()
    for d in range(n_dev):
        rows = small[d, meta_at : meta_at + META, :].astype(jnp.float32)
        ints[d : d + 1, :] = rows[8:9].astype(jnp.int32)
    to_scalars = pltpu.make_async_copy(ints, meta, sems.at[16])
    to_scalars.start()

    def at_device(r, c):
        dr, dc, dk = here ^ r, chip ^ (c // 2), core ^ (c % 2)
        dx, dy = dc & 1, dc >> 1
        order = jnp.where(dr < 2, 4 * dy + 2 * dx, 8 + 4 * dx + 2 * dy)
        return dk * group + order + (dr & 1)

    def scatter_pair(pair, blocks, q, x):
        pair[q] = x.astype(pair.dtype)
        blocks[2 * q] = x[:, :k].astype(blocks.dtype)
        blocks[2 * q + 1] = x[:, k:].astype(blocks.dtype)

    for r in range(n_row):
        for c in range(n_col):
            q, p, d = c * n_row + r, r * n_col + c, at_device(r, c)
            rows = small[d, meta_at : meta_at + META, :].astype(jnp.float32)
            rm[p] = jnp.broadcast_to(rows[0:1] + rows[1:2] + rows[2:3], (8, 128))
            ic[q] = jnp.broadcast_to(rows[3:4] + rows[4:5] + rows[5:6], (8, 128))
            scatter_pair(vs, vb, q, small[d, vec_at : vec_at + k, :].astype(jnp.float32))

    to_scalars.wait()

    def device(d, n):
        count = meta[d, 2 * OFF_CAP]
        count = jnp.where(count > OFF_CAP, 0, count)
        near = (d & 8) == 0
        one, two = (d >> 1) & 1, (d >> 2) & 1
        dc = jnp.where(near, 2 * two + one, 2 * one + two)
        c = 2 * (chip ^ dc) + (core ^ (d >> 4))
        r = here ^ (jnp.where(near, 0, 2) + (d & 1))
        for s in range(OFF_CAP):
            lv[n + s] = c * cblk + meta[d, OFF_CAP + s]
            lw[n + s] = r * rblk + meta[d, s]
            x = small[d, s * half : (s + 1) * half, :].astype(jnp.float32)
            blk[n + s] = jnp.concatenate([x[:, :k], x[:, k:]], axis=0).astype(jnp.bfloat16)
        return n + count

    n_live = lax.fori_loop(0, n_dev, device, jnp.int32(0))
    for u in range(UNROLL - 1):
        lv[n_live + u] = 0
        lw[n_live + u] = 0
        blk[n_live + u] = jnp.zeros((k, k), jnp.bfloat16)
    n_group = (n_live + UNROLL - 1) // UNROLL

    for copy in waits[8:]:
        copy.wait()
    left = lax.broadcasted_iota(jnp.int32, (rblk, 128), 1) < 64
    homes = []
    for r in range(n_row):
        h = jnp.int32(0)
        for c in range(n_col):
            h = jnp.where(meta[at_device(r, c), 2 * OFF_CAP] > OFF_CAP, c, h)
        homes.append(h)
        index = small[at_device(r, h), meta_at : meta_at + META, :].astype(jnp.float32)
        place = index[7:8] * float(rblk) + index[6:7]
        want = lax.broadcasted_iota(jnp.int32, (cblk * rblk, n_cap), 0).astype(jnp.float32)
        select = jnp.where(want == place, 1.0, 0.0).astype(jnp.bfloat16)

        parts = [at_device(r, 2 * i + j) for j in range(2) for i in range(n_col // 2)]

        def build(m, carry, parts=parts, select=select):
            at = pl.multiple_of(m * part, part)
            slots = jnp.concatenate(
                [full[d, pl.ds(at, part), :] for d in parts], axis=0
            )
            dense = dot(select, slots)
            for u in range(cpairs):
                a = dense[2 * u * rblk : (2 * u + 1) * rblk]
                b = dense[(2 * u + 1) * rblk : (2 * u + 2) * rblk]
                even = jnp.where(left, a, pltpu.roll(b, 64, 1))
                odd = jnp.where(left, pltpu.roll(a, 64, 1), b)
                tmp[u, pl.ds(m, rblk, stride=k), :] = even
                tmp[u, pl.ds(m + half, rblk, stride=k), :] = odd
            return carry

        lax.fori_loop(0, half, build, 0, unroll=4)

        def cut(i, carry, r=r):
            at = pl.multiple_of(i * k, k)
            for u in range(cpairs):
                hi, lo = split2(tmp[u, pl.ds(at, k), :])
                home[r, pl.ds(at, k), u * 128 : (u + 1) * 128] = hi
                home[r, pl.ds(at, k), width + u * 128 : width + (u + 1) * 128] = lo
            return carry

        lax.fori_loop(0, rblk, cut, 0, unroll=4)

    def iteration(it, carry):
        @pl.when(it > 0)
        def _():
            lh, ll = split2(linv[...])
            turn = jnp.concatenate([lh, lh, ll], axis=1)
            for q in range(0, n_dev, 4):
                hi = jnp.concatenate([ph[q + d, :k, :] for d in range(4)], axis=1)
                lo = jnp.concatenate([ph[q + d, k:, :] for d in range(4)], axis=1)
                current = dot(turn, jnp.concatenate([hi, lo, hi], axis=0))
                for d in range(4):
                    x = current[:, d * 128 : (d + 1) * 128] * ic[q + d, 0:1, :]
                    scatter_pair(vs, vb, q + d, x)

        for b in range(2 * n_dev):
            wb[b] = jnp.zeros_like(wb[b])
        for r in range(n_row):
            base = homes[r] * cpairs
            vec = jnp.concatenate([vs[base + u] for u in range(cpairs)] * 2, axis=1)
            for p in range(0, rpairs, 2):
                prod = dot(vec, home[r, p * 128 : (p + 2) * 128, :], NT)
                w[r * rpairs + p] = prod[:, :128]
                w[r * rpairs + p + 1] = prod[:, 128:]

        def forward(i, carry):
            prods = [dot(vb[lv[i * UNROLL + u]], blk[i * UNROLL + u], NT) for u in range(UNROLL)]
            for u in range(UNROLL):
                b = lw[i * UNROLL + u]
                wb[b] = wb[b] + prods[u]
            return carry

        lax.fori_loop(0, n_group, forward, 0)
        for p in range(n_dev):
            x = w[p] + jnp.concatenate([wb[2 * p], wb[2 * p + 1]], axis=1)
            scatter_pair(wt, wtb, p, x * rm[p, 0:1, :])
            y[p] = jnp.zeros_like(y[p])
            yb[2 * p] = jnp.zeros_like(yb[2 * p])
            yb[2 * p + 1] = jnp.zeros_like(yb[2 * p + 1])

        for r in range(n_row):
            base = homes[r] * cpairs
            vec = jnp.concatenate([wt[r * rpairs + p] for p in range(rpairs)], axis=1)
            for u in range(0, cpairs, 2):
                cols = slice(u * 128, (u + 2) * 128)
                tail = slice(width + u * 128, width + (u + 2) * 128)
                prod = dot(vec, home[r, :, cols]) + dot(vec, home[r, :, tail])
                y[base + u] = y[base + u] + prod[:, :128]
                y[base + u + 1] = y[base + u + 1] + prod[:, 128:]

        def backward(i, carry):
            prods = [dot(wtb[lw[i * UNROLL + u]], blk[i * UNROLL + u]) for u in range(UNROLL)]
            for u in range(UNROLL):
                b = lv[i * UNROLL + u]
                yb[b] = yb[b] + prods[u]
            return carry

        lax.fori_loop(0, n_group, backward, 0)

        both = jnp.zeros((2 * k, k), jnp.float32)
        for q in range(0, n_dev, 4):
            his, los = [], []
            for d in range(q, q + 4):
                x = y[d] + jnp.concatenate([yb[2 * d], yb[2 * d + 1]], axis=1)
                hi, lo = split2(x * ic[d, 0:1, :])
                ph[d, :k, :] = hi
                ph[d, k:, :] = lo
                his.append(hi)
                los.append(lo)
            hi = jnp.concatenate(his, axis=1)
            lo = jnp.concatenate(los, axis=1)
            both = both + dot(jnp.concatenate([hi, lo], axis=0), hi, NT)
        gram = (both[:k] + (both[k:] + both[k:].T)) / total
        linv[...] = inverse_factor(gram)
        return carry

    lax.fori_loop(0, ITERS, iteration, 0)
    lh, ll = split2(linv[...])
    place = (2 * chip + core) * n_row + here
    hi, lo = ph[place, :k, :], ph[place, k:, :]
    x = dot(lh, hi) + dot(ll, hi) + dot(lh, lo)
    out[0] = x[:, :k]
    out[1] = x[:, k:]


def split3(x):
    a = lax.reduce_precision(x, 8, 7)
    b = lax.reduce_precision(x - a, 8, 7)
    return [v.astype(jnp.bfloat16) for v in (a, b, x - a - b)]


def swap(x, axis, distance):
    size = lax.axis_size(axis)
    return lax.ppermute(x, axis, [(i, i ^ distance) for i in range(size)])


def along_rows(x):
    return [x] + [swap(x, "row", s) for s in range(1, lax.axis_size("row"))]


def along_chips(x):
    near, far = jnp.stack(x[:2]), jnp.stack(x[2:])
    near = jnp.concatenate([near, swap(near, "chip", 1)])
    far = jnp.concatenate([far, swap(far, "chip", 2)])
    return [near, swap(near, "chip", 2), far, swap(far, "chip", 1)]


def with_other_core(x):
    return x + [swap(v, "core", 1) for v in x]


def full_part(tile, has_full, n_chip, part, chip, core):
    tile = tile.reshape(2, n_chip, part, tile.shape[1])
    none = jnp.zeros(tile.shape[1:], tile.dtype)
    kept, sent = (
        jnp.where(has_full, lax.dynamic_index_in_dim(tile, i, 0, False), none)
        for i in (core, 1 - core)
    )
    both = kept + swap(sent, "core", 1)
    mine = lax.dynamic_index_in_dim(both, chip, 0, False)
    for s in range(1, n_chip):
        mine = mine + swap(lax.dynamic_index_in_dim(both, chip ^ s, 0, False), "chip", s)
    return mine


def whole_on_each(n_row, n_col, blocks, block_row, block_col, counts, vectors, row_mass, col_mass):
    tile = blocks[0, 0]
    n_cap = tile.shape[0]
    own, bsize = row_mass.shape
    k = vectors.shape[1] // bsize
    half = bsize // 2
    part = n_cap // n_col
    n_dev = n_row * n_col
    count = counts[0, 0]
    has_full = count > OFF_CAP
    bf16 = jnp.bfloat16
    row, chip, core = (lax.axis_index(name) for name in ("row", "chip", "core"))

    off = tile[:OFF_CAP].reshape(OFF_CAP * half, 128)
    inv_col = 1.0 / jnp.sqrt(col_mass)
    scaled = (vectors.reshape(own, k, bsize) * inv_col[:, None, :]).astype(bf16)
    scaled = scaled.transpose(1, 0, 2).reshape(k, own * bsize)
    mass = row_mass.reshape(own, half, 2).transpose(0, 2, 1).reshape(own * bsize)
    rows, cols = block_row[0, 0], block_col[0, 0]
    short = jnp.concatenate(
        [rows[:OFF_CAP], cols[:OFF_CAP], count[None], jnp.zeros(128 - 2 * OFF_CAP - 1, jnp.int32)]
    )
    meta = [v.astype(bf16) for v in (rows, cols, short)]
    meta = split3(mass) + split3(inv_col.reshape(own * bsize)) + meta
    meta = jnp.stack(meta + [jnp.zeros(128, bf16)] * (META - len(meta)))
    small = jnp.concatenate([off, scaled, meta], axis=0)
    home = full_part(tile, has_full, n_col // 2, part, chip, core)
    home = home.reshape(part, half, 128).transpose(1, 0, 2).reshape(half * part, 128)

    smalls = along_rows(small)
    home, smalls = lax.optimization_barrier((home, smalls))
    homes, smalls = along_rows(home), along_chips(smalls)
    homes, smalls = lax.optimization_barrier((homes, smalls))
    smalls, homes = with_other_core(smalls), with_other_core(along_chips(homes))

    place = jnp.stack([row, chip, core]).astype(jnp.int32)

    height, width = 2 * n_col * bsize, 2 * n_row * bsize
    slots = n_dev * OFF_CAP + UNROLL
    pair_f32 = pltpu.VMEM((n_dev, k, 128), jnp.float32)
    pair_bf16 = pltpu.VMEM((n_dev, k, 128), bf16)
    block_f32 = pltpu.VMEM((2 * n_dev, k, bsize), jnp.float32)
    block_bf16 = pltpu.VMEM((2 * n_dev, k, bsize), bf16)
    mass_f32 = pltpu.VMEM((n_dev, 8, 128), jnp.float32)
    result = pl.pallas_call(
        functools.partial(kernel, n_row, n_col, n_cap, float(n_dev * own * bsize)),
        out_shape=jax.ShapeDtypeStruct((own, k, bsize), jnp.float32),
        in_specs=[pl.BlockSpec(memory_space=pltpu.SMEM)]
        + [pl.BlockSpec(memory_space=pl.ANY)] * 16,
        out_specs=pl.BlockSpec(memory_space=pltpu.VMEM),
        scratch_shapes=[
            pltpu.VMEM((n_dev, 128), jnp.int32),
            pltpu.SMEM((n_dev, 128), jnp.int32),
            pltpu.SMEM((slots,), jnp.int32),
            pltpu.SMEM((slots,), jnp.int32),
            pltpu.SemaphoreType.DMA((17,)),
            pltpu.VMEM((n_dev,) + small.shape, bf16),
            pltpu.VMEM((n_dev,) + home.shape, bf16),
            pltpu.VMEM((n_row, height, 128), jnp.float32),
            pltpu.VMEM((n_row, height, 2 * width), bf16),
            pltpu.VMEM((slots, bsize, bsize), bf16),
            pair_bf16, block_bf16, pair_f32, block_f32,
            pair_bf16, block_bf16, pair_f32, block_f32,
            pltpu.VMEM((n_dev, 2 * k, 128), bf16),
            mass_f32, mass_f32,
            pltpu.VMEM((k, k), jnp.float32),
        ],
        compiler_params=pltpu.CompilerParams(vmem_limit_bytes=VMEM_LIMIT),
        name="iterate",
    )(place, *smalls, *homes)
    return result.reshape(own, k * bsize)


def rotate(projected, gram):
    lower = jnp.linalg.cholesky(gram)
    inverse = lax.linalg.triangular_solve(
        lower, jnp.eye(gram.shape[0], dtype=jnp.float32), left_side=True, lower=True
    )
    return jnp.einsum(
        "kl,bli->bki",
        inverse,
        projected,
        precision=lax.Precision.HIGHEST,
        preferred_element_type=jnp.float32,
    )


def local_gram(projected):
    return jnp.einsum(
        "bki,bli->kl",
        projected,
        projected,
        precision=lax.Precision.HIGHEST,
        preferred_element_type=jnp.float32,
    )


def split_by_tile(blocks, block_row, block_col, counts, vectors, row_mass, col_mass):
    tile = blocks[0, 0]
    n_cap = tile.shape[0]
    bsize = row_mass.shape[1]
    vecs = vectors.shape[1] // bsize
    own = vectors.shape[0]
    n_row = lax.axis_size("row")
    n_col = lax.axis_size("col")
    row_panel = own * n_col
    col_panel = own * n_row
    total_boxes = float(own * bsize * n_row * n_col)
    rows_idx = block_row[0, 0]
    cols_idx = block_col[0, 0]
    live = jnp.arange(n_cap) < counts[0, 0]
    fwd_ids = jnp.where(live, rows_idx, row_panel)
    bwd_ids = jnp.where(live, cols_idx, col_panel)
    square = tile.reshape(n_cap, bsize, bsize)
    inv_col = 1.0 / jnp.sqrt(col_mass)
    current = vectors.reshape(own, vecs, bsize)
    for step in range(ITERS):
        scaled = (current * inv_col[:, None, :]).astype(jnp.bfloat16).reshape(own, vecs * bsize)
        panel = lax.all_gather(scaled, "row", axis=0, tiled=True)
        forward_taken = jnp.take(panel.reshape(col_panel, vecs, bsize), cols_idx, axis=0)
        forward_product = jnp.einsum(
            "bij,bkj->bki", square, forward_taken, preferred_element_type=jnp.float32
        )
        forward_summed = jax.ops.segment_sum(forward_product, fwd_ids, num_segments=row_panel + 1)
        rows_sum = lax.psum_scatter(
            forward_summed[:row_panel].reshape(row_panel, vecs * bsize),
            "col",
            scatter_dimension=0,
            tiled=True,
        )
        weighted = (rows_sum.reshape(own, vecs, bsize) * row_mass[:, None, :]).astype(jnp.bfloat16)
        whole_rows = lax.all_gather(weighted.reshape(own, vecs * bsize), "col", axis=0, tiled=True)
        taken = jnp.take(whole_rows.reshape(row_panel, vecs, bsize), rows_idx, axis=0)
        product = jnp.einsum("bij,bki->bkj", square, taken, preferred_element_type=jnp.float32)
        summed = jax.ops.segment_sum(product, bwd_ids, num_segments=col_panel + 1)
        cols_sum = lax.psum_scatter(
            summed[:col_panel].reshape(col_panel, vecs * bsize),
            "row",
            scatter_dimension=0,
            tiled=True,
        )
        projected = cols_sum.reshape(own, vecs, bsize) * inv_col[:, None, :]
        gram = lax.psum(local_gram(projected), ("row", "col")) / total_boxes
        current = rotate(projected, gram)
    return current.reshape(own, vecs * bsize)


def fits(n_row, n_col, blocks, vectors, row_mass):
    own, bsize = row_mass.shape[0] // (n_row * n_col), row_mass.shape[1]
    n_cap = blocks.shape[2]
    dense = n_row * (own * n_col * bsize) * (own * n_row * bsize) * 4
    shapes = own * bsize == 128 and vectors.shape[1] == bsize * bsize and n_cap == 128
    return dense <= VMEM_LIMIT // 4 and shapes and n_cap % (16 * n_col) == 0 and n_row == 4 and n_col == 8


def solution(mesh):
    n_row, n_col = mesh.shape["row"], mesh.shape["col"]

    def run(blocks, block_row, block_col, counts, vectors, row_mass, col_mass):
        args = (blocks, block_row, block_col, counts, vectors, row_mass, col_mass)
        if fits(n_row, n_col, blocks, vectors, row_mass):
            devices = mesh.devices.reshape(n_row, n_col // 2, 2)
            grid, col = jax.sharding.Mesh(devices, ("row", "chip", "core")), ("chip", "core")
            body = functools.partial(whole_on_each, n_row, n_col)
        else:
            grid, col, body = mesh, ("col",), split_by_tile
        by_row, by_col = P(("row",) + col, None), P(col + ("row",), None)
        in_specs = (
            P("row", col, None, None), P("row", col, None), P("row", col, None), P("row", col),
            by_col, by_row, by_col,
        )
        return jax.shard_map(
            body, mesh=grid, in_specs=in_specs, out_specs=by_col, check_vma=False
        )(*args)

    return run
```

```python
import functools

import jax
import jax.numpy as jnp
from jax import lax
from jax.experimental import pallas as pl
from jax.experimental.pallas import tpu as pltpu
from jax.sharding import PartitionSpec as P

ITERS = 4
OFF_CAP = 8
META = 16
UNROLL = 16
BATCH = 8
VMEM_LIMIT = 56 * 1024 * 1024

NT = (((1,), (1,)), ((), ()))
NN = (((1,), (0,)), ((), ()))


def dot(a, b, dims=NN):
    return lax.dot_general(a, b, dims, preferred_element_type=jnp.float32)


def split2(x):
    hi = x.astype(jnp.bfloat16)
    return hi, (x - hi.astype(jnp.float32)).astype(jnp.bfloat16)


def reciprocal(x):
    y = pl.reciprocal(x, approx=True)
    for _ in range(2):
        y = y * (2.0 - x * y)
    return y


def inverse_factor(gram):
    n = gram.shape[0]
    rows = lax.broadcasted_iota(jnp.int32, (n, n), 0)
    cols = lax.broadcasted_iota(jnp.int32, (n, n), 1)
    eye = (rows == cols).astype(jnp.float32)
    both = jnp.concatenate([gram, eye], axis=1)
    count = n // 8
    tiles = [both[8 * t : 8 * t + 8] for t in range(count)]
    sub = lax.broadcasted_iota(jnp.int32, (8, 2 * n), 0)
    lane = lax.broadcasted_iota(jnp.int32, (8, 2 * n), 1)
    for b in range(count):
        spread = {
            t: [jnp.broadcast_to(tiles[t][:, 8 * b + s : 8 * b + s + 1], (8, 2 * n)) for s in range(8)]
            for t in range(b, count)
        }
        for s in range(8):
            inv = reciprocal(spread[b][s][s : s + 1])
            step = tiles[b][s : s + 1] * inv
            ahead = [spread[b][s2][s : s + 1] * inv for s2 in range(s + 1, 8)]
            for t in range(b, count):
                factor = spread[t][s]
                if t == b:
                    factor = jnp.where(sub > s, factor, 0.0)
                for s2 in range(s + 1, 8):
                    spread[t][s2] = spread[t][s2] - factor * ahead[s2 - s - 1]
                tiles[t] = tiles[t] - factor * step
    out = []
    for t in range(count):
        pivot = jnp.sum(jnp.where(lane == sub + 8 * t, tiles[t], 0.0), axis=1, keepdims=True)
        out.append(tiles[t] * lax.rsqrt(pivot))
    return jnp.concatenate(out, axis=0)[:, n:]


def kernel(
    n_row, n_col, n_cap, total,
    own, *rest,
):
    smalls, fulls, out = rest[:8], rest[8:16], rest[16]
    ints, meta, lv, lw, sems, small, full, tmp, home, blk = rest[17:27]
    vs, vb, w, wb, wt, wtb, y, yb, ph, rm, ic, linv = rest[27:]
    n_dev = n_row * n_col
    group = n_dev // 2
    k = vs.shape[1]
    half = k // 2
    rpairs, cpairs = n_col, n_row
    rblk, cblk = 2 * rpairs, 2 * cpairs
    part = n_cap // n_col
    vec_at = OFF_CAP * half
    meta_at = vec_at + k
    width = cpairs * 128

    here, chip, core = own[0], own[1], own[2]
    piece = n_dev // 8
    waits = []
    for i, (srcs, dst) in enumerate([(smalls, small), (fulls, full)]):
        for j, ref in enumerate(srcs):
            copy = pltpu.make_async_copy(ref, dst.at[pl.ds(j * piece, piece)], sems.at[8 * i + j])
            copy.start()
            waits.append(copy)
    for copy in waits[:8]:
        copy.wait()
    for d in range(n_dev):
        rows = small[d, meta_at : meta_at + META, :].astype(jnp.float32)
        ints[d : d + 1, :] = rows[8:9].astype(jnp.int32)
    to_scalars = pltpu.make_async_copy(ints, meta, sems.at[16])
    to_scalars.start()

    def at_device(r, c):
        dr, dc, dk = here ^ r, chip ^ (c // 2), core ^ (c % 2)
        dx, dy = dc & 1, dc >> 1
        order = jnp.where(dr < 2, 4 * dy + 2 * dx, 8 + 4 * dx + 2 * dy)
        return dk * group + order + (dr & 1)

    def scatter_pair(pair, blocks, q, x):
        pair[q] = x.astype(pair.dtype)
        blocks[2 * q] = x[:, :k].astype(blocks.dtype)
        blocks[2 * q + 1] = x[:, k:].astype(blocks.dtype)

    for r in range(n_row):
        for c in range(n_col):
            q, p, d = c * n_row + r, r * n_col + c, at_device(r, c)
            rows = small[d, meta_at : meta_at + META, :].astype(jnp.float32)
            rm[p] = jnp.broadcast_to(rows[0:1] + rows[1:2] + rows[2:3], (8, 128))
            ic[q] = jnp.broadcast_to(rows[3:4] + rows[4:5] + rows[5:6], (8, 128))
            scatter_pair(vs, vb, q, small[d, vec_at : vec_at + k, :].astype(jnp.float32))

    to_scalars.wait()

    def device(d, n):
        count = meta[d, 2 * OFF_CAP]
        count = jnp.where(count > OFF_CAP, 0, count)
        near = (d & 8) == 0
        one, two = (d >> 1) & 1, (d >> 2) & 1
        dc = jnp.where(near, 2 * two + one, 2 * one + two)
        c = 2 * (chip ^ dc) + (core ^ (d >> 4))
        r = here ^ (jnp.where(near, 0, 2) + (d & 1))
        for s in range(OFF_CAP):
            lv[n + s] = c * cblk + meta[d, OFF_CAP + s]
            lw[n + s] = r * rblk + meta[d, s]
            x = small[d, s * half : (s + 1) * half, :].astype(jnp.float32)
            blk[n + s] = jnp.concatenate([x[:, :k], x[:, k:]], axis=0).astype(jnp.bfloat16)
        return n + count

    n_live = lax.fori_loop(0, n_dev, device, jnp.int32(0))
    for u in range(UNROLL - 1):
        lv[n_live + u] = 0
        lw[n_live + u] = 0
        blk[n_live + u] = jnp.zeros((k, k), jnp.bfloat16)
    n_group = (n_live + UNROLL - 1) // UNROLL

    for copy in waits[8:]:
        copy.wait()
    left = lax.broadcasted_iota(jnp.int32, (rblk, 128), 1) < 64
    homes = []
    for r in range(n_row):
        h = jnp.int32(0)
        for c in range(n_col):
            h = jnp.where(meta[at_device(r, c), 2 * OFF_CAP] > OFF_CAP, c, h)
        homes.append(h)
        index = small[at_device(r, h), meta_at : meta_at + META, :].astype(jnp.float32)
        place = index[7:8] * float(rblk) + index[6:7]
        want = lax.broadcasted_iota(jnp.int32, (cblk * rblk, n_cap), 0).astype(jnp.float32)
        select = jnp.where(want == place, 1.0, 0.0).astype(jnp.bfloat16)

        parts = [at_device(r, 2 * i + j) for j in range(2) for i in range(n_col // 2)]

        def build(m, carry, parts=parts, select=select):
            at = pl.multiple_of(m * part, part)
            slots = jnp.concatenate(
                [full[d, pl.ds(at, part), :] for d in parts], axis=0
            )
            dense = dot(select, slots)
            for u in range(cpairs):
                a = dense[2 * u * rblk : (2 * u + 1) * rblk]
                b = dense[(2 * u + 1) * rblk : (2 * u + 2) * rblk]
                even = jnp.where(left, a, pltpu.roll(b, 64, 1))
                odd = jnp.where(left, pltpu.roll(a, 64, 1), b)
                tmp[u, pl.ds(m, rblk, stride=k), :] = even
                tmp[u, pl.ds(m + half, rblk, stride=k), :] = odd
            return carry

        lax.fori_loop(0, half, build, 0, unroll=4)

        def cut(i, carry, r=r):
            at = pl.multiple_of(i * k, k)
            for u in range(cpairs):
                hi, lo = split2(tmp[u, pl.ds(at, k), :])
                home[r, pl.ds(at, k), u * 128 : (u + 1) * 128] = hi
                home[r, pl.ds(at, k), width + u * 128 : width + (u + 1) * 128] = lo
            return carry

        lax.fori_loop(0, rblk, cut, 0, unroll=4)

    def clear():
        for q in range(n_dev):
            y[q] = jnp.zeros_like(y[q])
            for ref in (wb, yb):
                ref[2 * q] = jnp.zeros_like(ref[2 * q])
                ref[2 * q + 1] = jnp.zeros_like(ref[2 * q + 1])

    clear()

    def iteration(it, carry):
        @pl.when(it > 0)
        def _():
            lh, ll = split2(linv[...])
            turn = jnp.concatenate([lh, lh, ll], axis=1)
            for q in range(0, n_dev, 4):
                hi = jnp.concatenate([ph[q + d, :k, :] for d in range(4)], axis=1)
                lo = jnp.concatenate([ph[q + d, k:, :] for d in range(4)], axis=1)
                current = dot(turn, jnp.concatenate([hi, lo, hi], axis=0))
                for d in range(4):
                    x = current[:, d * 128 : (d + 1) * 128] * ic[q + d, 0:1, :]
                    scatter_pair(vs, vb, q + d, x)

        for r in range(n_row):
            base = homes[r] * cpairs
            vec = jnp.concatenate([vs[base + u] for u in range(cpairs)] * 2, axis=1)
            for p in range(0, rpairs, 2):
                prod = dot(vec, home[r, p * 128 : (p + 2) * 128, :], NT)
                w[r * rpairs + p] = prod[:, :128]
                w[r * rpairs + p + 1] = prod[:, 128:]

        def forward(i, carry):
            for at in range(0, UNROLL, BATCH):
                slots = [i * UNROLL + at + u for u in range(BATCH)]
                prods = [dot(vb[lv[s]], blk[s], NT) for s in slots]
                for s, prod in zip(slots, prods):
                    wb[lw[s]] = wb[lw[s]] + prod
            return carry

        lax.fori_loop(0, n_group, forward, 0)
        for p in range(n_dev):
            x = w[p] + jnp.concatenate([wb[2 * p], wb[2 * p + 1]], axis=1)
            scatter_pair(wt, wtb, p, x * rm[p, 0:1, :])

        for r in range(n_row):
            base = homes[r] * cpairs
            vec = jnp.concatenate([wt[r * rpairs + p] for p in range(rpairs)], axis=1)
            for u in range(0, cpairs, 2):
                cols = slice(u * 128, (u + 2) * 128)
                tail = slice(width + u * 128, width + (u + 2) * 128)
                prod = dot(vec, home[r, :, cols]) + dot(vec, home[r, :, tail])
                y[base + u] = y[base + u] + prod[:, :128]
                y[base + u + 1] = y[base + u + 1] + prod[:, 128:]

        def backward(i, carry):
            for at in range(0, UNROLL, BATCH):
                slots = [i * UNROLL + at + u for u in range(BATCH)]
                prods = [dot(wtb[lw[s]], blk[s]) for s in slots]
                for s, prod in zip(slots, prods):
                    yb[lv[s]] = yb[lv[s]] + prod
            return carry

        lax.fori_loop(0, n_group, backward, 0)

        both = jnp.zeros((2 * k, k), jnp.float32)
        for q in range(0, n_dev, 4):
            his, los = [], []
            for d in range(q, q + 4):
                x = y[d] + jnp.concatenate([yb[2 * d], yb[2 * d + 1]], axis=1)
                hi, lo = split2(x * ic[d, 0:1, :])
                ph[d, :k, :] = hi
                ph[d, k:, :] = lo
                his.append(hi)
                los.append(lo)
            hi = jnp.concatenate(his, axis=1)
            lo = jnp.concatenate(los, axis=1)
            both = both + dot(jnp.concatenate([hi, lo], axis=0), hi, NT)
        gram = (both[:k] + (both[k:] + both[k:].T)) / total
        clear()
        linv[...] = inverse_factor(gram)
        return carry

    lax.fori_loop(0, ITERS, iteration, 0)
    lh, ll = split2(linv[...])
    place = (2 * chip + core) * n_row + here
    hi, lo = ph[place, :k, :], ph[place, k:, :]
    x = dot(lh, hi) + dot(ll, hi) + dot(lh, lo)
    out[0] = x[:, :k]
    out[1] = x[:, k:]


def split3(x):
    a = lax.reduce_precision(x, 8, 7)
    b = lax.reduce_precision(x - a, 8, 7)
    return [v.astype(jnp.bfloat16) for v in (a, b, x - a - b)]


def swap(x, axis, distance):
    size = lax.axis_size(axis)
    return lax.ppermute(x, axis, [(i, i ^ distance) for i in range(size)])


def along_rows(x):
    return [x] + [swap(x, "row", s) for s in range(1, lax.axis_size("row"))]


def along_one_chip_axis(x):
    near, far = jnp.stack(x[:2]), jnp.stack(x[2:])
    return [
        jnp.concatenate([near, swap(near, "chip", 1)]),
        jnp.concatenate([far, swap(far, "chip", 2)]),
    ]


def along_other_chip_axis(x):
    near, far = x
    return [near, swap(near, "chip", 2), far, swap(far, "chip", 1)]


def with_other_core(x):
    return x + [swap(v, "core", 1) for v in x]


def full_part(tile, has_full, n_chip, part, chip, core):
    tile = tile.reshape(2, n_chip, part, tile.shape[1])
    none = jnp.zeros(tile.shape[1:], tile.dtype)
    kept, sent = (
        jnp.where(has_full, lax.dynamic_index_in_dim(tile, i, 0, False), none)
        for i in (core, 1 - core)
    )
    both = kept + swap(sent, "core", 1)
    mine = lax.dynamic_index_in_dim(both, chip, 0, False)
    for s in range(1, n_chip):
        mine = mine + swap(lax.dynamic_index_in_dim(both, chip ^ s, 0, False), "chip", s)
    return mine


def whole_on_each(n_row, n_col, blocks, block_row, block_col, counts, vectors, row_mass, col_mass):
    tile = blocks[0, 0]
    n_cap = tile.shape[0]
    own, bsize = row_mass.shape
    k = vectors.shape[1] // bsize
    half = bsize // 2
    part = n_cap // n_col
    n_dev = n_row * n_col
    count = counts[0, 0]
    has_full = count > OFF_CAP
    bf16 = jnp.bfloat16
    row, chip, core = (lax.axis_index(name) for name in ("row", "chip", "core"))

    off = tile[:OFF_CAP].reshape(OFF_CAP * half, 128)
    inv_col = 1.0 / jnp.sqrt(col_mass)
    scaled = (vectors.reshape(own, k, bsize) * inv_col[:, None, :]).astype(bf16)
    scaled = scaled.transpose(1, 0, 2).reshape(k, own * bsize)
    mass = row_mass.reshape(own, half, 2).transpose(0, 2, 1).reshape(own * bsize)
    rows, cols = block_row[0, 0], block_col[0, 0]
    short = jnp.concatenate(
        [rows[:OFF_CAP], cols[:OFF_CAP], count[None], jnp.zeros(128 - 2 * OFF_CAP - 1, jnp.int32)]
    )
    meta = [v.astype(bf16) for v in (rows, cols, short)]
    meta = split3(mass) + split3(inv_col.reshape(own * bsize)) + meta
    meta = jnp.stack(meta + [jnp.zeros(128, bf16)] * (META - len(meta)))
    small = jnp.concatenate([off, scaled, meta], axis=0)
    home = full_part(tile, has_full, n_col // 2, part, chip, core)
    home = home.reshape(part, half, 128).transpose(1, 0, 2).reshape(half * part, 128)

    together = lax.optimization_barrier
    smalls = along_rows(small)
    home, smalls[1] = together((home, smalls[1]))
    homes, smalls = along_rows(home), along_one_chip_axis(smalls)
    smalls, homes[1:3] = together((smalls, homes[1:3]))
    homes, smalls = together((homes, along_other_chip_axis(smalls)))
    homes, smalls = together((along_one_chip_axis(homes), with_other_core(smalls)))
    homes = with_other_core(along_other_chip_axis(homes))

    place = jnp.stack([row, chip, core]).astype(jnp.int32)

    height, width = 2 * n_col * bsize, 2 * n_row * bsize
    slots = n_dev * OFF_CAP + UNROLL
    pair_f32 = pltpu.VMEM((n_dev, k, 128), jnp.float32)
    pair_bf16 = pltpu.VMEM((n_dev, k, 128), bf16)
    block_f32 = pltpu.VMEM((2 * n_dev, k, bsize), jnp.float32)
    block_bf16 = pltpu.VMEM((2 * n_dev, k, bsize), bf16)
    mass_f32 = pltpu.VMEM((n_dev, 8, 128), jnp.float32)
    result = pl.pallas_call(
        functools.partial(kernel, n_row, n_col, n_cap, float(n_dev * own * bsize)),
        out_shape=jax.ShapeDtypeStruct((own, k, bsize), jnp.float32),
        in_specs=[pl.BlockSpec(memory_space=pltpu.SMEM)]
        + [pl.BlockSpec(memory_space=pl.ANY)] * 16,
        out_specs=pl.BlockSpec(memory_space=pltpu.VMEM),
        scratch_shapes=[
            pltpu.VMEM((n_dev, 128), jnp.int32),
            pltpu.SMEM((n_dev, 128), jnp.int32),
            pltpu.SMEM((slots,), jnp.int32),
            pltpu.SMEM((slots,), jnp.int32),
            pltpu.SemaphoreType.DMA((17,)),
            pltpu.VMEM((n_dev,) + small.shape, bf16),
            pltpu.VMEM((n_dev,) + home.shape, bf16),
            pltpu.VMEM((n_row, height, 128), jnp.float32),
            pltpu.VMEM((n_row, height, 2 * width), bf16),
            pltpu.VMEM((slots, bsize, bsize), bf16),
            pair_bf16, block_bf16, pair_f32, block_f32,
            pair_bf16, block_bf16, pair_f32, block_f32,
            pltpu.VMEM((n_dev, 2 * k, 128), bf16),
            mass_f32, mass_f32,
            pltpu.VMEM((k, k), jnp.float32),
        ],
        compiler_params=pltpu.CompilerParams(vmem_limit_bytes=VMEM_LIMIT),
        name="iterate",
    )(place, *smalls, *homes)
    return result.reshape(own, k * bsize)


def rotate(projected, gram):
    lower = jnp.linalg.cholesky(gram)
    inverse = lax.linalg.triangular_solve(
        lower, jnp.eye(gram.shape[0], dtype=jnp.float32), left_side=True, lower=True
    )
    return jnp.einsum(
        "kl,bli->bki",
        inverse,
        projected,
        precision=lax.Precision.HIGHEST,
        preferred_element_type=jnp.float32,
    )


def local_gram(projected):
    return jnp.einsum(
        "bki,bli->kl",
        projected,
        projected,
        precision=lax.Precision.HIGHEST,
        preferred_element_type=jnp.float32,
    )


def split_by_tile(blocks, block_row, block_col, counts, vectors, row_mass, col_mass):
    tile = blocks[0, 0]
    n_cap = tile.shape[0]
    bsize = row_mass.shape[1]
    vecs = vectors.shape[1] // bsize
    own = vectors.shape[0]
    n_row = lax.axis_size("row")
    n_col = lax.axis_size("col")
    row_panel = own * n_col
    col_panel = own * n_row
    total_boxes = float(own * bsize * n_row * n_col)
    rows_idx = block_row[0, 0]
    cols_idx = block_col[0, 0]
    live = jnp.arange(n_cap) < counts[0, 0]
    fwd_ids = jnp.where(live, rows_idx, row_panel)
    bwd_ids = jnp.where(live, cols_idx, col_panel)
    square = tile.reshape(n_cap, bsize, bsize)
    inv_col = 1.0 / jnp.sqrt(col_mass)
    current = vectors.reshape(own, vecs, bsize)
    for step in range(ITERS):
        scaled = (current * inv_col[:, None, :]).astype(jnp.bfloat16).reshape(own, vecs * bsize)
        panel = lax.all_gather(scaled, "row", axis=0, tiled=True)
        forward_taken = jnp.take(panel.reshape(col_panel, vecs, bsize), cols_idx, axis=0)
        forward_product = jnp.einsum(
            "bij,bkj->bki", square, forward_taken, preferred_element_type=jnp.float32
        )
        forward_summed = jax.ops.segment_sum(forward_product, fwd_ids, num_segments=row_panel + 1)
        rows_sum = lax.psum_scatter(
            forward_summed[:row_panel].reshape(row_panel, vecs * bsize),
            "col",
            scatter_dimension=0,
            tiled=True,
        )
        weighted = (rows_sum.reshape(own, vecs, bsize) * row_mass[:, None, :]).astype(jnp.bfloat16)
        whole_rows = lax.all_gather(weighted.reshape(own, vecs * bsize), "col", axis=0, tiled=True)
        taken = jnp.take(whole_rows.reshape(row_panel, vecs, bsize), rows_idx, axis=0)
        product = jnp.einsum("bij,bki->bkj", square, taken, preferred_element_type=jnp.float32)
        summed = jax.ops.segment_sum(product, bwd_ids, num_segments=col_panel + 1)
        cols_sum = lax.psum_scatter(
            summed[:col_panel].reshape(col_panel, vecs * bsize),
            "row",
            scatter_dimension=0,
            tiled=True,
        )
        projected = cols_sum.reshape(own, vecs, bsize) * inv_col[:, None, :]
        gram = lax.psum(local_gram(projected), ("row", "col")) / total_boxes
        current = rotate(projected, gram)
    return current.reshape(own, vecs * bsize)


def fits(n_row, n_col, blocks, vectors, row_mass):
    own, bsize = row_mass.shape[0] // (n_row * n_col), row_mass.shape[1]
    n_cap = blocks.shape[2]
    dense = n_row * (own * n_col * bsize) * (own * n_row * bsize) * 4
    shapes = own * bsize == 128 and vectors.shape[1] == bsize * bsize and n_cap == 128
    return dense <= VMEM_LIMIT // 4 and shapes and n_cap % (16 * n_col) == 0 and n_row == 4 and n_col == 8


def solution(mesh):
    n_row, n_col = mesh.shape["row"], mesh.shape["col"]

    def run(blocks, block_row, block_col, counts, vectors, row_mass, col_mass):
        args = (blocks, block_row, block_col, counts, vectors, row_mass, col_mass)
        if fits(n_row, n_col, blocks, vectors, row_mass):
            devices = mesh.devices.reshape(n_row, n_col // 2, 2)
            grid, col = jax.sharding.Mesh(devices, ("row", "chip", "core")), ("chip", "core")
            body = functools.partial(whole_on_each, n_row, n_col)
        else:
            grid, col, body = mesh, ("col",), split_by_tile
        by_row, by_col = P(("row",) + col, None), P(col + ("row",), None)
        in_specs = (
            P("row", col, None, None), P("row", col, None), P("row", col, None), P("row", col),
            by_col, by_row, by_col,
        )
        return jax.shard_map(
            body, mesh=grid, in_specs=in_specs, out_specs=by_col, check_vma=False
        )(*args)

    return run
```

```python
import functools

import jax
import jax.numpy as jnp
from jax import lax
from jax.experimental import pallas as pl
from jax.experimental.pallas import tpu as pltpu
from jax.sharding import PartitionSpec as P

ITERS = 4
OFF_CAP = 8
META = 16
UNROLL = 16
BATCH = 8
VMEM_LIMIT = 56 * 1024 * 1024

NT = (((1,), (1,)), ((), ()))
NN = (((1,), (0,)), ((), ()))


def dot(a, b, dims=NN):
    return lax.dot_general(a, b, dims, preferred_element_type=jnp.float32)


def split2(x):
    hi = x.astype(jnp.bfloat16)
    return hi, (x - hi.astype(jnp.float32)).astype(jnp.bfloat16)


def reciprocal(x):
    y = pl.reciprocal(x, approx=True)
    for _ in range(2):
        y = y * (2.0 - x * y)
    return y


def inverse_factor(gram):
    n = gram.shape[0]
    rows = lax.broadcasted_iota(jnp.int32, (n, n), 0)
    cols = lax.broadcasted_iota(jnp.int32, (n, n), 1)
    eye = (rows == cols).astype(jnp.float32)
    both = jnp.concatenate([gram, eye], axis=1)
    count = n // 8
    tiles = [both[8 * t : 8 * t + 8] for t in range(count)]
    sub = lax.broadcasted_iota(jnp.int32, (8, 2 * n), 0)
    lane = lax.broadcasted_iota(jnp.int32, (8, 2 * n), 1)
    for b in range(count):
        spread = {
            t: [jnp.broadcast_to(tiles[t][:, 8 * b + s : 8 * b + s + 1], (8, 2 * n)) for s in range(8)]
            for t in range(b, count)
        }
        for s in range(8):
            inv = reciprocal(spread[b][s][s : s + 1])
            step = tiles[b][s : s + 1] * inv
            ahead = [spread[b][s2][s : s + 1] * inv for s2 in range(s + 1, 8)]
            for t in range(b, count):
                factor = spread[t][s]
                if t == b:
                    factor = jnp.where(sub > s, factor, 0.0)
                for s2 in range(s + 1, 8):
                    spread[t][s2] = spread[t][s2] - factor * ahead[s2 - s - 1]
                tiles[t] = tiles[t] - factor * step
    out = []
    for t in range(count):
        pivot = jnp.sum(jnp.where(lane == sub + 8 * t, tiles[t], 0.0), axis=1, keepdims=True)
        out.append(tiles[t] * lax.rsqrt(pivot))
    return jnp.concatenate(out, axis=0)[:, n:]


def place_of(own, n_row, n_dev):
    here, chip, core = own[0], own[1], own[2]

    def at_device(r, c):
        dr, dc, dk = here ^ r, chip ^ (c // 2), core ^ (c % 2)
        dx, dy = dc & 1, dc >> 1
        order = jnp.where(dr < 2, 2 * dx, 4 + 2 * dy) + jnp.where(
            jnp.where(dr < 2, dy, dx) > 0, n_dev // 4, 0
        )
        return dk * (n_dev // 2) + order + (dr & 1)

    def device_at(d):
        far, second = (d >> 2) & 1, (d >> 3) & 1
        first = (d >> 1) & 1
        dc = jnp.where(far == 0, 2 * second + first, 2 * first + second)
        return here ^ (2 * far + (d & 1)), 2 * (chip ^ dc) + (core ^ (d >> 4))

    return at_device, device_at


def copy_in(pairs, sems):
    copies = [pltpu.make_async_copy(src, dst, sems.at[i]) for i, (src, dst) in enumerate(pairs)]
    for copy in copies:
        copy.start()
    return copies


def scatter_pair(pair, blocks, q, x):
    k = x.shape[0]
    if pair is not None:
        pair[q] = x.astype(pair.dtype)
    blocks[2 * q] = x[:, :k].astype(blocks.dtype)
    blocks[2 * q + 1] = x[:, k:].astype(blocks.dtype)


def add_products(n_group, blk, dims, from_list, source, to_list, total):
    def group(i, carry):
        for at in range(0, UNROLL, BATCH):
            slots = [i * UNROLL + at + u for u in range(BATCH)]
            prods = [dot(source[from_list[s]], blk[s], dims) for s in slots]
            for s, prod in zip(slots, prods):
                total[to_list[s]] = total[to_list[s]] + prod
        return carry

    lax.fori_loop(0, n_group, group, 0)


def unpack(
    n_row, n_col, own, mine, other,
    lv, lw, nums, place, blk, vs, rm, ic, wb,
    ints, meta, sems, small, vb,
):
    n_dev = n_row * n_col
    k = vs.shape[1]
    half = k // 2
    rblk, cblk = 2 * n_col, 2 * n_row
    vec_at = OFF_CAP * half
    meta_at = vec_at + k
    at_device, device_at = place_of(own, n_row, n_dev)

    first, second = pl.ds(0, n_dev // 2), pl.ds(n_dev // 2, n_dev // 2)
    for copy in copy_in([(mine, small.at[first]), (other, small.at[second])], sems):
        copy.wait()
    for d in range(n_dev):
        rows = small[d, meta_at : meta_at + META, :].astype(jnp.float32)
        ints[d : d + 1, :] = rows[8:9].astype(jnp.int32)
    to_scalars = pltpu.make_async_copy(ints, meta, sems.at[2])
    to_scalars.start()

    for r in range(n_row):
        for c in range(n_col):
            q, p, d = c * n_row + r, r * n_col + c, at_device(r, c)
            rows = small[d, meta_at : meta_at + META, :].astype(jnp.float32)
            rm[p] = jnp.broadcast_to(rows[0:1] + rows[1:2] + rows[2:3], (8, 128))
            ic[q] = jnp.broadcast_to(rows[3:4] + rows[4:5] + rows[5:6], (8, 128))
            scatter_pair(vs, vb, q, small[d, vec_at : vec_at + k, :].astype(jnp.float32))
            wb[2 * p] = jnp.zeros_like(wb[2 * p])
            wb[2 * p + 1] = jnp.zeros_like(wb[2 * p + 1])
    to_scalars.wait()

    def device(d, n):
        count = meta[d, 2 * OFF_CAP]
        count = jnp.where(count > OFF_CAP, 0, count)
        r, c = device_at(d)
        for s in range(OFF_CAP):
            lv[n + s] = c * cblk + meta[d, OFF_CAP + s]
            lw[n + s] = r * rblk + meta[d, s]
            x = small[d, s * half : (s + 1) * half, :].astype(jnp.float32)
            blk[n + s] = jnp.concatenate([x[:, :k], x[:, k:]], axis=0).astype(jnp.bfloat16)
        return n + count

    n_live = lax.fori_loop(0, n_dev, device, jnp.int32(0))
    for u in range(UNROLL - 1):
        lv[n_live + u] = 0
        lw[n_live + u] = 0
        blk[n_live + u] = jnp.zeros((k, k), jnp.bfloat16)
    n_group = (n_live + UNROLL - 1) // UNROLL
    nums[0] = n_group

    for r in range(n_row):
        h = jnp.int32(0)
        for c in range(n_col):
            h = jnp.where(meta[at_device(r, c), 2 * OFF_CAP] > OFF_CAP, c, h)
        nums[1 + r] = h
        index = small[at_device(r, h), meta_at : meta_at + META, :].astype(jnp.float32)
        place[r : r + 1, :] = index[7:8] * float(rblk) + index[6:7]

    add_products(n_group, blk, NT, lv, vb, lw, wb)


def iterate(n_row, n_col, n_cap, total, own, lv, lw, nums, place, *rest):
    sources, fulls, out = rest[:5], rest[5:9], rest[9]
    sems, full, tmp, home, blk, vs, rm, ic, wb = rest[10:19]
    vb, w, wt, wtb, y, yb, ph, linv = rest[19:]
    n_dev = n_row * n_col
    k = vs.shape[1]
    half = k // 2
    rpairs, cpairs = n_col, n_row
    rblk, cblk = 2 * rpairs, 2 * cpairs
    part = n_cap // n_col
    width = cpairs * 128
    at_device, _ = place_of(own, n_row, n_dev)

    at, pairs = 0, []
    for ref in fulls:
        pairs.append((ref, full.at[pl.ds(at, ref.shape[0])]))
        at += ref.shape[0]
    copies = copy_in(pairs + list(zip(sources, (blk, vs, rm, ic, wb))), sems)
    for copy in copies[: len(fulls)]:
        copy.wait()
    n_group = nums[0]

    left = lax.broadcasted_iota(jnp.int32, (rblk, 128), 1) < 64
    homes = []
    for r in range(n_row):
        homes.append(nums[1 + r])
        want = lax.broadcasted_iota(jnp.int32, (cblk * rblk, n_cap), 0).astype(jnp.float32)
        select = jnp.where(want == place[r : r + 1, :], 1.0, 0.0).astype(jnp.bfloat16)

        parts = [at_device(r, 2 * i + j) for j in range(2) for i in range(n_col // 2)]

        def build(m, carry, parts=parts, select=select):
            at = pl.multiple_of(m * part, part)
            slots = jnp.concatenate(
                [full[d, pl.ds(at, part), :] for d in parts], axis=0
            )
            dense = dot(select, slots)
            for u in range(cpairs):
                a = dense[2 * u * rblk : (2 * u + 1) * rblk]
                b = dense[(2 * u + 1) * rblk : (2 * u + 2) * rblk]
                even = jnp.where(left, a, pltpu.roll(b, 64, 1))
                odd = jnp.where(left, pltpu.roll(a, 64, 1), b)
                tmp[u, pl.ds(m, rblk, stride=k), :] = even
                tmp[u, pl.ds(m + half, rblk, stride=k), :] = odd
            return carry

        lax.fori_loop(0, half, build, 0, unroll=4)

        def cut(i, carry, r=r):
            at = pl.multiple_of(i * k, k)
            for u in range(cpairs):
                hi, lo = split2(tmp[u, pl.ds(at, k), :])
                home[r, pl.ds(at, k), u * 128 : (u + 1) * 128] = hi
                home[r, pl.ds(at, k), width + u * 128 : width + (u + 1) * 128] = lo
            return carry

        lax.fori_loop(0, rblk, cut, 0, unroll=4)

    def clear(refs):
        for ref in refs:
            for q in range(ref.shape[0]):
                ref[q] = jnp.zeros_like(ref[q])

    clear([y, yb])
    for copy in copies[len(fulls) :]:
        copy.wait()

    def iteration(it, carry):
        @pl.when(it > 0)
        def _():
            lh, ll = split2(linv[...])
            turn = jnp.concatenate([lh, lh, ll], axis=1)
            for q in range(0, n_dev, 4):
                hi = jnp.concatenate([ph[q + d, :k, :] for d in range(4)], axis=1)
                lo = jnp.concatenate([ph[q + d, k:, :] for d in range(4)], axis=1)
                current = dot(turn, jnp.concatenate([hi, lo, hi], axis=0))
                for d in range(4):
                    x = current[:, d * 128 : (d + 1) * 128] * ic[q + d, 0:1, :]
                    scatter_pair(vs, vb, q + d, x)

        for r in range(n_row):
            base = homes[r] * cpairs
            vec = jnp.concatenate([vs[base + u] for u in range(cpairs)] * 2, axis=1)
            for p in range(0, rpairs, 2):
                prod = dot(vec, home[r, p * 128 : (p + 2) * 128, :], NT)
                w[r * rpairs + p] = prod[:, :128]
                w[r * rpairs + p + 1] = prod[:, 128:]

        @pl.when(it > 0)
        def _():
            add_products(n_group, blk, NT, lv, vb, lw, wb)

        for p in range(n_dev):
            x = w[p] + jnp.concatenate([wb[2 * p], wb[2 * p + 1]], axis=1)
            scatter_pair(wt, wtb, p, x * rm[p, 0:1, :])

        for r in range(n_row):
            base = homes[r] * cpairs
            vec = jnp.concatenate([wt[r * rpairs + p] for p in range(rpairs)], axis=1)
            for u in range(0, cpairs, 2):
                cols = slice(u * 128, (u + 2) * 128)
                tail = slice(width + u * 128, width + (u + 2) * 128)
                prod = dot(vec, home[r, :, cols]) + dot(vec, home[r, :, tail])
                y[base + u] = y[base + u] + prod[:, :128]
                y[base + u + 1] = y[base + u + 1] + prod[:, 128:]

        add_products(n_group, blk, NN, lw, wtb, lv, yb)

        both = jnp.zeros((2 * k, k), jnp.float32)
        for q in range(0, n_dev, 4):
            his, los = [], []
            for d in range(q, q + 4):
                x = y[d] + jnp.concatenate([yb[2 * d], yb[2 * d + 1]], axis=1)
                hi, lo = split2(x * ic[d, 0:1, :])
                ph[d, :k, :] = hi
                ph[d, k:, :] = lo
                his.append(hi)
                los.append(lo)
            hi = jnp.concatenate(his, axis=1)
            lo = jnp.concatenate(los, axis=1)
            both = both + dot(jnp.concatenate([hi, lo], axis=0), hi, NT)
        gram = (both[:k] + (both[k:] + both[k:].T)) / total
        clear([y, yb, wb])
        linv[...] = inverse_factor(gram)
        return carry

    lax.fori_loop(0, ITERS, iteration, 0)
    lh, ll = split2(linv[...])
    q = (2 * own[1] + own[2]) * n_row + own[0]
    hi, lo = ph[q, :k, :], ph[q, k:, :]
    x = dot(lh, hi) + dot(ll, hi) + dot(lh, lo)
    out[0] = x[:, :k]
    out[1] = x[:, k:]


def split3(x):
    a = lax.reduce_precision(x, 8, 7)
    b = lax.reduce_precision(x - a, 8, 7)
    return [v.astype(jnp.bfloat16) for v in (a, b, x - a - b)]


def swap(x, axis, distance):
    size = lax.axis_size(axis)
    return lax.ppermute(x, axis, [(i, i ^ distance) for i in range(size)])


def along_rows(x):
    return [x] + [swap(x, "row", s) for s in range(1, lax.axis_size("row"))]


def along_one_chip_axis(x):
    near, far = jnp.stack(x[:2]), jnp.stack(x[2:])
    return [
        jnp.concatenate([near, swap(near, "chip", 1)]),
        jnp.concatenate([far, swap(far, "chip", 2)]),
    ]


def along_other_chip_axis(x):
    near, far = x
    return [swap(near, "chip", 2), swap(far, "chip", 1)]


def full_part(tile, has_full, n_chip, part, chip, core):
    tile = tile.reshape(2, n_chip, part, tile.shape[1])
    none = jnp.zeros(tile.shape[1:], tile.dtype)
    kept, sent = (
        jnp.where(has_full, lax.dynamic_index_in_dim(tile, i, 0, False), none)
        for i in (core, 1 - core)
    )
    both = kept + swap(sent, "core", 1)
    mine = lax.dynamic_index_in_dim(both, chip, 0, False)
    for s in range(1, n_chip):
        mine = mine + swap(lax.dynamic_index_in_dim(both, chip ^ s, 0, False), "chip", s)
    return mine


def whole_on_each(n_row, n_col, blocks, block_row, block_col, counts, vectors, row_mass, col_mass):
    tile = blocks[0, 0]
    n_cap = tile.shape[0]
    own, bsize = row_mass.shape
    k = vectors.shape[1] // bsize
    half = bsize // 2
    part = n_cap // n_col
    n_dev = n_row * n_col
    count = counts[0, 0]
    has_full = count > OFF_CAP
    bf16 = jnp.bfloat16
    row, chip, core = (lax.axis_index(name) for name in ("row", "chip", "core"))

    off = tile[:OFF_CAP].reshape(OFF_CAP * half, 128)
    inv_col = 1.0 / jnp.sqrt(col_mass)
    scaled = (vectors.reshape(own, k, bsize) * inv_col[:, None, :]).astype(bf16)
    scaled = scaled.transpose(1, 0, 2).reshape(k, own * bsize)
    mass = row_mass.reshape(own, half, 2).transpose(0, 2, 1).reshape(own * bsize)
    rows, cols = block_row[0, 0], block_col[0, 0]
    short = jnp.concatenate(
        [rows[:OFF_CAP], cols[:OFF_CAP], count[None], jnp.zeros(128 - 2 * OFF_CAP - 1, jnp.int32)]
    )
    meta = [v.astype(bf16) for v in (rows, cols, short)]
    meta = split3(mass) + split3(inv_col.reshape(own * bsize)) + meta
    meta = jnp.stack(meta + [jnp.zeros(128, bf16)] * (META - len(meta)))
    small = jnp.concatenate([off, scaled, meta], axis=0)
    home = full_part(tile, has_full, n_col // 2, part, chip, core)
    home = home.reshape(part, half, 128).transpose(1, 0, 2).reshape(half * part, 128)

    together = lax.optimization_barrier
    smalls = along_rows(small)
    home, smalls[1] = together((home, smalls[1]))
    homes, smalls = along_rows(home), along_one_chip_axis(smalls)
    smalls, homes[1:3] = together((smalls, homes[1:3]))
    smalls = jnp.concatenate(smalls + along_other_chip_axis(smalls))
    homes, smalls = together((homes, smalls))
    homes, others = together((along_one_chip_axis(homes), swap(smalls, "core", 1)))
    last = along_other_chip_axis(homes)
    homes = jnp.concatenate(homes)
    other_homes = swap(homes, "core", 1)

    where = jnp.stack([row, chip, core]).astype(jnp.int32)

    height, width = 2 * n_col * bsize, 2 * n_row * bsize
    slots = n_dev * OFF_CAP + UNROLL
    f32, i32 = jnp.float32, jnp.int32
    pair, block, mass = (n_dev, k, 128), (2 * n_dev, k, bsize), (n_dev, 8, 128)
    smem, anywhere = (pl.BlockSpec(memory_space=m) for m in (pltpu.SMEM, pl.ANY))
    vmem = pl.BlockSpec(memory_space=pltpu.VMEM)
    lists = [((slots,), i32), ((slots,), i32), ((1 + n_row,), i32)]
    arrays = [
        ((8, 128), f32), ((slots, bsize, bsize), bf16), (pair, bf16), (mass, f32), (mass, f32), (block, f32),
    ]
    unpacked = pl.pallas_call(
        functools.partial(unpack, n_row, n_col),
        out_shape=[jax.ShapeDtypeStruct(*v) for v in lists + arrays],
        in_specs=[smem, anywhere, anywhere],
        out_specs=[smem] * len(lists) + [vmem] * len(arrays),
        scratch_shapes=[
            pltpu.VMEM((n_dev, 128), i32),
            pltpu.SMEM((n_dev, 128), i32),
            pltpu.SemaphoreType.DMA((3,)),
            pltpu.VMEM((n_dev,) + small.shape, bf16),
            pltpu.VMEM(block, bf16),
        ],
        compiler_params=pltpu.CompilerParams(vmem_limit_bytes=VMEM_LIMIT // 2),
        cost_estimate=pl.CostEstimate(
            flops=2 * slots * bsize**3, bytes_accessed=2 * n_dev * small.size * 2, transcendentals=0
        ),
        name="unpack",
    )(where, smalls, others)
    last, unpacked = together((last, unpacked))
    last = jnp.concatenate(last)
    fulls = [homes, last, other_homes, swap(last, "core", 1)]
    result = pl.pallas_call(
        functools.partial(iterate, n_row, n_col, n_cap, float(n_dev * own * bsize)),
        out_shape=jax.ShapeDtypeStruct((own, k, bsize), f32),
        in_specs=[smem] * 4 + [vmem] + [anywhere] * (5 + len(fulls)),
        out_specs=vmem,
        scratch_shapes=[
            pltpu.SemaphoreType.DMA((5 + len(fulls),)),
            pltpu.VMEM((n_dev,) + home.shape, bf16),
            pltpu.VMEM((n_row, height, 128), f32),
            pltpu.VMEM((n_row, height, 2 * width), bf16),
            *[pltpu.VMEM(*v) for v in arrays[1:]],
            *[
                pltpu.VMEM(*v)
                for v in [
                    (block, bf16), (pair, f32), (pair, bf16), (block, bf16), (pair, f32), (block, f32),
                    ((n_dev, 2 * k, 128), bf16), ((k, k), f32),
                ]
            ],
        ],
        compiler_params=pltpu.CompilerParams(vmem_limit_bytes=VMEM_LIMIT),
        name="iterate",
    )(where, *unpacked, *fulls)
    return result.reshape(own, k * bsize)


def rotate(projected, gram):
    lower = jnp.linalg.cholesky(gram)
    inverse = lax.linalg.triangular_solve(
        lower, jnp.eye(gram.shape[0], dtype=jnp.float32), left_side=True, lower=True
    )
    return jnp.einsum(
        "kl,bli->bki",
        inverse,
        projected,
        precision=lax.Precision.HIGHEST,
        preferred_element_type=jnp.float32,
    )


def local_gram(projected):
    return jnp.einsum(
        "bki,bli->kl",
        projected,
        projected,
        precision=lax.Precision.HIGHEST,
        preferred_element_type=jnp.float32,
    )


def split_by_tile(blocks, block_row, block_col, counts, vectors, row_mass, col_mass):
    tile = blocks[0, 0]
    n_cap = tile.shape[0]
    bsize = row_mass.shape[1]
    vecs = vectors.shape[1] // bsize
    own = vectors.shape[0]
    n_row = lax.axis_size("row")
    n_col = lax.axis_size("col")
    row_panel = own * n_col
    col_panel = own * n_row
    total_boxes = float(own * bsize * n_row * n_col)
    rows_idx = block_row[0, 0]
    cols_idx = block_col[0, 0]
    live = jnp.arange(n_cap) < counts[0, 0]
    fwd_ids = jnp.where(live, rows_idx, row_panel)
    bwd_ids = jnp.where(live, cols_idx, col_panel)
    square = tile.reshape(n_cap, bsize, bsize)
    inv_col = 1.0 / jnp.sqrt(col_mass)
    current = vectors.reshape(own, vecs, bsize)
    for step in range(ITERS):
        scaled = (current * inv_col[:, None, :]).astype(jnp.bfloat16).reshape(own, vecs * bsize)
        panel = lax.all_gather(scaled, "row", axis=0, tiled=True)
        forward_taken = jnp.take(panel.reshape(col_panel, vecs, bsize), cols_idx, axis=0)
        forward_product = jnp.einsum(
            "bij,bkj->bki", square, forward_taken, preferred_element_type=jnp.float32
        )
        forward_summed = jax.ops.segment_sum(forward_product, fwd_ids, num_segments=row_panel + 1)
        rows_sum = lax.psum_scatter(
            forward_summed[:row_panel].reshape(row_panel, vecs * bsize),
            "col",
            scatter_dimension=0,
            tiled=True,
        )
        weighted = (rows_sum.reshape(own, vecs, bsize) * row_mass[:, None, :]).astype(jnp.bfloat16)
        whole_rows = lax.all_gather(weighted.reshape(own, vecs * bsize), "col", axis=0, tiled=True)
        taken = jnp.take(whole_rows.reshape(row_panel, vecs, bsize), rows_idx, axis=0)
        product = jnp.einsum("bij,bki->bkj", square, taken, preferred_element_type=jnp.float32)
        summed = jax.ops.segment_sum(product, bwd_ids, num_segments=col_panel + 1)
        cols_sum = lax.psum_scatter(
            summed[:col_panel].reshape(col_panel, vecs * bsize),
            "row",
            scatter_dimension=0,
            tiled=True,
        )
        projected = cols_sum.reshape(own, vecs, bsize) * inv_col[:, None, :]
        gram = lax.psum(local_gram(projected), ("row", "col")) / total_boxes
        current = rotate(projected, gram)
    return current.reshape(own, vecs * bsize)


def fits(n_row, n_col, blocks, vectors, row_mass):
    own, bsize = row_mass.shape[0] // (n_row * n_col), row_mass.shape[1]
    n_cap = blocks.shape[2]
    dense = n_row * (own * n_col * bsize) * (own * n_row * bsize) * 4
    shapes = own * bsize == 128 and vectors.shape[1] == bsize * bsize and n_cap == 128
    return dense <= VMEM_LIMIT // 4 and shapes and n_cap % (16 * n_col) == 0 and n_row == 4 and n_col == 8


def solution(mesh):
    n_row, n_col = mesh.shape["row"], mesh.shape["col"]

    def run(blocks, block_row, block_col, counts, vectors, row_mass, col_mass):
        args = (blocks, block_row, block_col, counts, vectors, row_mass, col_mass)
        if fits(n_row, n_col, blocks, vectors, row_mass):
            devices = mesh.devices.reshape(n_row, n_col // 2, 2)
            grid, col = jax.sharding.Mesh(devices, ("row", "chip", "core")), ("chip", "core")
            body = functools.partial(whole_on_each, n_row, n_col)
        else:
            grid, col, body = mesh, ("col",), split_by_tile
        by_row, by_col = P(("row",) + col, None), P(col + ("row",), None)
        in_specs = (
            P("row", col, None, None), P("row", col, None), P("row", col, None), P("row", col),
            by_col, by_row, by_col,
        )
        return jax.shard_map(
            body, mesh=grid, in_specs=in_specs, out_specs=by_col, check_vma=False
        )(*args)

    return run
```

```python
import functools

import jax
import jax.numpy as jnp
from jax import lax
from jax.experimental import pallas as pl
from jax.experimental.pallas import tpu as pltpu
from jax.sharding import PartitionSpec as P

ITERS = 4
OFF_CAP = 8
META = 16
UNROLL = 16
BATCH = 4
VMEM_LIMIT = 56 * 1024 * 1024

NT = (((1,), (1,)), ((), ()))
NN = (((1,), (0,)), ((), ()))


def dot(a, b, dims=NN):
    return lax.dot_general(a, b, dims, preferred_element_type=jnp.float32)


def split2(x):
    hi = x.astype(jnp.bfloat16)
    return hi, (x - hi.astype(jnp.float32)).astype(jnp.bfloat16)


def reciprocal(x):
    y = pl.reciprocal(x, approx=True)
    for _ in range(2):
        y = y * (2.0 - x * y)
    return y


def inverse_factor(gram):
    n = gram.shape[0]
    rows = lax.broadcasted_iota(jnp.int32, (n, n), 0)
    cols = lax.broadcasted_iota(jnp.int32, (n, n), 1)
    eye = (rows == cols).astype(jnp.float32)
    both = jnp.concatenate([gram, eye], axis=1)
    count = n // 8
    tiles = [both[8 * t : 8 * t + 8] for t in range(count)]
    sub = lax.broadcasted_iota(jnp.int32, (8, 2 * n), 0)
    lane = lax.broadcasted_iota(jnp.int32, (8, 2 * n), 1)
    for b in range(count):
        spread = {
            t: [jnp.broadcast_to(tiles[t][:, 8 * b + s : 8 * b + s + 1], (8, 2 * n)) for s in range(8)]
            for t in range(b, count)
        }
        for s in range(8):
            inv = reciprocal(spread[b][s][s : s + 1])
            step = tiles[b][s : s + 1] * inv
            ahead = [spread[b][s2][s : s + 1] * inv for s2 in range(s + 1, 8)]
            for t in range(b, count):
                factor = spread[t][s]
                if t == b:
                    factor = jnp.where(sub > s, factor, 0.0)
                for s2 in range(s + 1, 8):
                    spread[t][s2] = spread[t][s2] - factor * ahead[s2 - s - 1]
                tiles[t] = tiles[t] - factor * step
    out = []
    for t in range(count):
        pivot = jnp.sum(jnp.where(lane == sub + 8 * t, tiles[t], 0.0), axis=1, keepdims=True)
        out.append(tiles[t] * lax.rsqrt(pivot))
    return jnp.concatenate(out, axis=0)[:, n:]


def place_of(own, n_row, n_dev):
    here, chip, core = own[0], own[1], own[2]

    def at_device(r, c):
        dr, dc, dk = here ^ r, chip ^ (c // 2), core ^ (c % 2)
        dx, dy = dc & 1, dc >> 1
        order = jnp.where(dr < 2, 2 * dx, 4 + 2 * dy) + jnp.where(
            jnp.where(dr < 2, dy, dx) > 0, n_dev // 4, 0
        )
        return dk * (n_dev // 2) + order + (dr & 1)

    def device_at(d):
        far, second = (d >> 2) & 1, (d >> 3) & 1
        first = (d >> 1) & 1
        dc = jnp.where(far == 0, 2 * second + first, 2 * first + second)
        return here ^ (2 * far + (d & 1)), 2 * (chip ^ dc) + (core ^ (d >> 4))

    return at_device, device_at


def copy_in(pairs, sems):
    copies = [pltpu.make_async_copy(src, dst, sems.at[i]) for i, (src, dst) in enumerate(pairs)]
    for copy in copies:
        copy.start()
    return copies


def left_half(shape):
    return lax.broadcasted_iota(jnp.int32, shape, len(shape) - 1) < 64


def store_twice(pair, twice, q, x):
    pair[q] = x.astype(pair.dtype)
    turned, left = pltpu.roll(x, 64, 1), left_half(x.shape)
    twice[2 * q] = jnp.where(left, x, turned).astype(twice.dtype)
    twice[2 * q + 1] = jnp.where(left, turned, x).astype(twice.dtype)


def gather_pair(q, first, second):
    left = left_half(first.shape[1:])
    apart = jnp.where(left, first[2 * q + 1], second[2 * q])
    return jnp.where(left, first[2 * q], second[2 * q + 1]) + pltpu.roll(apart, 64, 1)


def add_products(n_group, blk, dims, from_list, source, to_list, first, second):
    left = left_half(source.shape[1:])

    def group(i, carry):
        for at in range(0, UNROLL, BATCH):
            pairs = [i * UNROLL + at + u for u in range(BATCH)]
            prods = [
                dot(
                    jnp.where(left, source[from_list[2 * p]], source[from_list[2 * p + 1]]),
                    blk[p],
                    dims,
                )
                for p in pairs
            ]
            for p, prod in zip(pairs, prods):
                a, b = to_list[2 * p], to_list[2 * p + 1]
                first[a] = first[a] + prod
                second[b] = second[b] + prod
        return carry

    lax.fori_loop(0, n_group, group, 0)


def unpack(
    n_row, n_col, own, mine, other,
    lv, lw, nums, place, blk, vs, vd, rm, ic,
    ints, meta, sems, small,
):
    n_dev = n_row * n_col
    k = vs.shape[1]
    half = k // 2
    rblk, cblk = 2 * n_col, 2 * n_row
    vec_at = OFF_CAP * half
    meta_at = vec_at + k
    at_device, device_at = place_of(own, n_row, n_dev)

    first, second = pl.ds(0, n_dev // 2), pl.ds(n_dev // 2, n_dev // 2)
    for copy in copy_in([(mine, small.at[first]), (other, small.at[second])], sems):
        copy.wait()
    for d in range(n_dev):
        rows = small[d, meta_at : meta_at + META, :].astype(jnp.float32)
        ints[d : d + 1, :] = rows[8:9].astype(jnp.int32)
    to_scalars = pltpu.make_async_copy(ints, meta, sems.at[2])
    to_scalars.start()

    for r in range(n_row):
        for c in range(n_col):
            q, p, d = c * n_row + r, r * n_col + c, at_device(r, c)
            rows = small[d, meta_at : meta_at + META, :].astype(jnp.float32)
            rm[p] = jnp.broadcast_to(rows[0:1] + rows[1:2] + rows[2:3], (8, 128))
            ic[q] = jnp.broadcast_to(rows[3:4] + rows[4:5] + rows[5:6], (8, 128))
            store_twice(vs, vd, q, small[d, vec_at : vec_at + k, :].astype(jnp.float32))
    to_scalars.wait()

    lanes = lax.broadcasted_iota(jnp.int32, (half, 128), 1)

    def device(d, n):
        count = meta[d, 2 * OFF_CAP]
        count = jnp.where(count > OFF_CAP, 0, count)
        r, c = device_at(d)
        for s in range(OFF_CAP):
            lv[n + s] = c * cblk + meta[d, OFF_CAP + s]
            lw[n + s] = r * rblk + meta[d, s]
            x = small[d, s * half : (s + 1) * half, :].astype(jnp.float32)
            turned = pltpu.roll(x, 64, 1)
            side = (n + s) % 2
            here = (lanes // 64) == side
            even = jnp.where(here, jnp.where(side == 0, x, turned), 0.0)
            odd = jnp.where(here, jnp.where(side == 0, turned, x), 0.0)
            at = pl.multiple_of(side * k, k)
            both = jnp.concatenate([even, odd], axis=0).astype(jnp.bfloat16)
            blk[(n + s) // 2, pl.ds(at, k), :] = both
        return n + count

    n_live = lax.fori_loop(0, n_dev, device, jnp.int32(0))
    for u in range(2 * UNROLL - 1):
        lv[n_live + u] = 0
        lw[n_live + u] = 0
        at = pl.multiple_of((n_live + u) % 2 * k, k)
        blk[(n_live + u) // 2, pl.ds(at, k), :] = jnp.zeros((k, 128), jnp.bfloat16)
    nums[0] = (n_live + 2 * UNROLL - 1) // (2 * UNROLL)

    for r in range(n_row):
        h = jnp.int32(0)
        for c in range(n_col):
            h = jnp.where(meta[at_device(r, c), 2 * OFF_CAP] > OFF_CAP, c, h)
        nums[1 + r] = h
        index = small[at_device(r, h), meta_at : meta_at + META, :].astype(jnp.float32)
        place[r : r + 1, :] = index[7:8] * float(rblk) + index[6:7]


def iterate(n_row, n_col, n_cap, total, own, lv, lw, nums, place, *rest):
    sources, fulls, out = rest[:5], rest[5:11], rest[11]
    sems, full, tmp, home, blk, vs, vd, rm, ic = rest[12:21]
    w, w1, w2, wt, wd, y, y1, y2, ph, linv = rest[21:]
    n_dev = n_row * n_col
    k = vs.shape[1]
    half = k // 2
    rpairs, cpairs = n_col, n_row
    rblk, cblk = 2 * rpairs, 2 * cpairs
    part = n_cap // n_col
    width = cpairs * 128
    at_device, _ = place_of(own, n_row, n_dev)

    at, pairs = 0, []
    for ref in fulls:
        pairs.append((ref, full.at[pl.ds(at, ref.shape[0])]))
        at += ref.shape[0]
    copies = copy_in(pairs + list(zip(sources, (blk, vs, vd, rm, ic))), sems)
    for copy in copies[: len(fulls)]:
        copy.wait()
    n_group = nums[0]

    left = lax.broadcasted_iota(jnp.int32, (rblk, 128), 1) < 64
    homes = []
    for r in range(n_row):
        homes.append(nums[1 + r])
        want = lax.broadcasted_iota(jnp.int32, (cblk * rblk, n_cap), 0).astype(jnp.float32)
        select = jnp.where(want == place[r : r + 1, :], 1.0, 0.0).astype(jnp.bfloat16)

        parts = [at_device(r, c) for c in range(n_col)]

        def build(m, carry, parts=parts, select=select):
            at = pl.multiple_of(m * part, part)
            slots = jnp.concatenate(
                [full[d, pl.ds(at, part), :] for d in parts], axis=0
            )
            dense = dot(select, slots)
            for u in range(cpairs):
                a = dense[2 * u * rblk : (2 * u + 1) * rblk]
                b = dense[(2 * u + 1) * rblk : (2 * u + 2) * rblk]
                even = jnp.where(left, a, pltpu.roll(b, 64, 1))
                odd = jnp.where(left, pltpu.roll(a, 64, 1), b)
                tmp[u, pl.ds(m, rblk, stride=k), :] = even
                tmp[u, pl.ds(m + half, rblk, stride=k), :] = odd
            return carry

        lax.fori_loop(0, half, build, 0, unroll=4)

        def cut(i, carry, r=r):
            at = pl.multiple_of(i * k, k)
            for u in range(cpairs):
                hi, lo = split2(tmp[u, pl.ds(at, k), :])
                home[r, pl.ds(at, k), u * 128 : (u + 1) * 128] = hi
                home[r, pl.ds(at, k), width + u * 128 : width + (u + 1) * 128] = lo
            return carry

        lax.fori_loop(0, rblk, cut, 0, unroll=4)

    def clear(refs):
        for ref in refs:
            for q in range(ref.shape[0]):
                ref[q] = jnp.zeros_like(ref[q])

    clear([y, y1, y2, w1, w2])
    for copy in copies[len(fulls) :]:
        copy.wait()

    def iteration(it, carry):
        @pl.when(it > 0)
        def _():
            lh, ll = split2(linv[...])
            turn = jnp.concatenate([lh, lh, ll], axis=1)
            for q in range(0, n_dev, 4):
                hi = jnp.concatenate([ph[q + d, :k, :] for d in range(4)], axis=1)
                lo = jnp.concatenate([ph[q + d, k:, :] for d in range(4)], axis=1)
                current = dot(turn, jnp.concatenate([hi, lo, hi], axis=0))
                for d in range(4):
                    x = current[:, d * 128 : (d + 1) * 128] * ic[q + d, 0:1, :]
                    store_twice(vs, vd, q + d, x)

        for r in range(n_row):
            base = homes[r] * cpairs
            vec = jnp.concatenate([vs[base + u] for u in range(cpairs)] * 2, axis=1)
            for p in range(0, rpairs, 2):
                prod = dot(vec, home[r, p * 128 : (p + 2) * 128, :], NT)
                w[r * rpairs + p] = prod[:, :128]
                w[r * rpairs + p + 1] = prod[:, 128:]

        add_products(n_group, blk, NT, lv, vd, lw, w1, w2)
        for p in range(n_dev):
            x = w[p] + gather_pair(p, w1, w2)
            store_twice(wt, wd, p, x * rm[p, 0:1, :])

        for r in range(n_row):
            base = homes[r] * cpairs
            vec = jnp.concatenate([wt[r * rpairs + p] for p in range(rpairs)], axis=1)
            for u in range(0, cpairs, 2):
                cols = slice(u * 128, (u + 2) * 128)
                tail = slice(width + u * 128, width + (u + 2) * 128)
                prod = dot(vec, home[r, :, cols]) + dot(vec, home[r, :, tail])
                y[base + u] = y[base + u] + prod[:, :128]
                y[base + u + 1] = y[base + u + 1] + prod[:, 128:]

        add_products(n_group, blk, NN, lw, wd, lv, y1, y2)

        both = jnp.zeros((2 * k, k), jnp.float32)
        for q in range(0, n_dev, 4):
            his, los = [], []
            for d in range(q, q + 4):
                x = y[d] + gather_pair(d, y1, y2)
                hi, lo = split2(x * ic[d, 0:1, :])
                ph[d, :k, :] = hi
                ph[d, k:, :] = lo
                his.append(hi)
                los.append(lo)
            hi = jnp.concatenate(his, axis=1)
            lo = jnp.concatenate(los, axis=1)
            both = both + dot(jnp.concatenate([hi, lo], axis=0), hi, NT)
        gram = (both[:k] + (both[k:] + both[k:].T)) / total
        clear([y, y1, y2, w1, w2])
        linv[...] = inverse_factor(gram)
        return carry

    lax.fori_loop(0, ITERS, iteration, 0)
    lh, ll = split2(linv[...])
    q = (2 * own[1] + own[2]) * n_row + own[0]
    hi, lo = ph[q, :k, :], ph[q, k:, :]
    x = dot(lh, hi) + dot(ll, hi) + dot(lh, lo)
    out[0] = x[:, :k]
    out[1] = x[:, k:]


def split3(x):
    a = lax.reduce_precision(x, 8, 7)
    b = lax.reduce_precision(x - a, 8, 7)
    return [v.astype(jnp.bfloat16) for v in (a, b, x - a - b)]


def swap(x, axis, distance):
    size = lax.axis_size(axis)
    return lax.ppermute(x, axis, [(i, i ^ distance) for i in range(size)])


def along_rows(x):
    return [x] + [swap(x, "row", s) for s in range(1, lax.axis_size("row"))]


def along_one_chip_axis(x):
    near, far = jnp.stack(x[:2]), jnp.stack(x[2:])
    return [
        jnp.concatenate([near, swap(near, "chip", 1)]),
        jnp.concatenate([far, swap(far, "chip", 2)]),
    ]


def along_other_chip_axis(x):
    near, far = x
    return [swap(near, "chip", 2), swap(far, "chip", 1)]


def whole_on_each(n_row, n_col, blocks, block_row, block_col, counts, vectors, row_mass, col_mass):
    tile = blocks[0, 0]
    n_cap = tile.shape[0]
    own, bsize = row_mass.shape
    k = vectors.shape[1] // bsize
    half = bsize // 2
    part = n_cap // n_col
    n_dev = n_row * n_col
    count = counts[0, 0]
    has_full = count > OFF_CAP
    bf16 = jnp.bfloat16
    row, chip, core = (lax.axis_index(name) for name in ("row", "chip", "core"))

    off = tile[:OFF_CAP].reshape(OFF_CAP * half, 128)
    inv_col = 1.0 / jnp.sqrt(col_mass)
    scaled = (vectors.reshape(own, k, bsize) * inv_col[:, None, :]).astype(bf16)
    scaled = scaled.transpose(1, 0, 2).reshape(k, own * bsize)
    mass = row_mass.reshape(own, half, 2).transpose(0, 2, 1).reshape(own * bsize)
    rows, cols = block_row[0, 0], block_col[0, 0]
    short = jnp.concatenate(
        [rows[:OFF_CAP], cols[:OFF_CAP], count[None], jnp.zeros(128 - 2 * OFF_CAP - 1, jnp.int32)]
    )
    meta = [v.astype(bf16) for v in (rows, cols, short)]
    meta = split3(mass) + split3(inv_col.reshape(own * bsize)) + meta
    meta = jnp.stack(meta + [jnp.zeros(128, bf16)] * (META - len(meta)))
    small = jnp.concatenate([off, scaled, meta], axis=0)
    sent = jnp.where(has_full, tile, jnp.zeros_like(tile)).reshape(n_col, part, bsize * bsize)
    got = lax.all_to_all(sent, ("chip", "core"), split_axis=0, concat_axis=0)
    home = jnp.sum(got.astype(jnp.float32), axis=0).astype(bf16)
    home = home.reshape(part, half, 128).transpose(1, 0, 2).reshape(half * part, 128)

    together = lax.optimization_barrier
    smalls = along_rows(small)
    home, smalls[1] = together((home, smalls[1]))
    homes, smalls = along_rows(home), along_one_chip_axis(smalls)
    smalls, homes[1:3] = together((smalls, homes[1:3]))
    smalls = jnp.concatenate(smalls + along_other_chip_axis(smalls))
    homes, smalls = together((homes, smalls))
    homes, others = together((along_one_chip_axis(homes), swap(smalls, "core", 1)))
    last = along_other_chip_axis(homes)
    homes = jnp.concatenate(homes)
    other_homes = swap(homes, "core", 1)

    where = jnp.stack([row, chip, core]).astype(jnp.int32)

    height, width = 2 * n_col * bsize, 2 * n_row * bsize
    slots = n_dev * OFF_CAP + 2 * UNROLL
    f32, i32 = jnp.float32, jnp.int32
    pair, twice, mass = (n_dev, k, 128), (2 * n_dev, k, 128), (n_dev, 8, 128)
    smem, anywhere = (pl.BlockSpec(memory_space=m) for m in (pltpu.SMEM, pl.ANY))
    vmem = pl.BlockSpec(memory_space=pltpu.VMEM)
    lists = [((slots,), i32), ((slots,), i32), ((1 + n_row,), i32)]
    arrays = [
        ((8, 128), f32), ((slots // 2, 128, 128), bf16), (pair, bf16), (twice, bf16), (mass, f32), (mass, f32),
    ]
    unpacked = pl.pallas_call(
        functools.partial(unpack, n_row, n_col),
        out_shape=[jax.ShapeDtypeStruct(*v) for v in lists + arrays],
        in_specs=[smem, anywhere, anywhere],
        out_specs=[smem] * len(lists) + [vmem] * len(arrays),
        scratch_shapes=[
            pltpu.VMEM((n_dev, 128), i32),
            pltpu.SMEM((n_dev, 128), i32),
            pltpu.SemaphoreType.DMA((3,)),
            pltpu.VMEM((n_dev,) + small.shape, bf16),
        ],
        compiler_params=pltpu.CompilerParams(vmem_limit_bytes=VMEM_LIMIT // 2),
        cost_estimate=pl.CostEstimate(
            flops=2 * slots * bsize**3, bytes_accessed=2 * n_dev * small.size * 2, transcendentals=0
        ),
        name="unpack",
    )(where, smalls, others)
    last, nums = together((last, unpacked[2]))
    unpacked = (*unpacked[:2], nums, *unpacked[3:])
    fulls = [homes, *last, other_homes, *(swap(v, "core", 1) for v in last)]
    result = pl.pallas_call(
        functools.partial(iterate, n_row, n_col, n_cap, float(n_dev * own * bsize)),
        out_shape=jax.ShapeDtypeStruct((own, k, bsize), f32),
        in_specs=[smem] * 4 + [vmem] + [anywhere] * (5 + len(fulls)),
        out_specs=vmem,
        scratch_shapes=[
            pltpu.SemaphoreType.DMA((5 + len(fulls),)),
            pltpu.VMEM((n_dev,) + home.shape, bf16),
            pltpu.VMEM((n_row, height, 128), f32),
            pltpu.VMEM((n_row, height, 2 * width), bf16),
            *[pltpu.VMEM(*v) for v in arrays[1:]],
            *[
                pltpu.VMEM(*v)
                for v in [
                    (pair, f32), (twice, f32), (twice, f32), (pair, bf16), (twice, bf16),
                    (pair, f32), (twice, f32), (twice, f32), ((n_dev, 2 * k, 128), bf16), ((k, k), f32),
                ]
            ],
        ],
        compiler_params=pltpu.CompilerParams(vmem_limit_bytes=VMEM_LIMIT),
        name="iterate",
    )(where, *unpacked, *fulls)
    return result.reshape(own, k * bsize)


def rotate(projected, gram):
    lower = jnp.linalg.cholesky(gram)
    inverse = lax.linalg.triangular_solve(
        lower, jnp.eye(gram.shape[0], dtype=jnp.float32), left_side=True, lower=True
    )
    return jnp.einsum(
        "kl,bli->bki",
        inverse,
        projected,
        precision=lax.Precision.HIGHEST,
        preferred_element_type=jnp.float32,
    )


def local_gram(projected):
    return jnp.einsum(
        "bki,bli->kl",
        projected,
        projected,
        precision=lax.Precision.HIGHEST,
        preferred_element_type=jnp.float32,
    )


def split_by_tile(blocks, block_row, block_col, counts, vectors, row_mass, col_mass):
    tile = blocks[0, 0]
    n_cap = tile.shape[0]
    bsize = row_mass.shape[1]
    vecs = vectors.shape[1] // bsize
    own = vectors.shape[0]
    n_row = lax.axis_size("row")
    n_col = lax.axis_size("col")
    row_panel = own * n_col
    col_panel = own * n_row
    total_boxes = float(own * bsize * n_row * n_col)
    rows_idx = block_row[0, 0]
    cols_idx = block_col[0, 0]
    live = jnp.arange(n_cap) < counts[0, 0]
    fwd_ids = jnp.where(live, rows_idx, row_panel)
    bwd_ids = jnp.where(live, cols_idx, col_panel)
    square = tile.reshape(n_cap, bsize, bsize)
    inv_col = 1.0 / jnp.sqrt(col_mass)
    current = vectors.reshape(own, vecs, bsize)
    for step in range(ITERS):
        scaled = (current * inv_col[:, None, :]).astype(jnp.bfloat16).reshape(own, vecs * bsize)
        panel = lax.all_gather(scaled, "row", axis=0, tiled=True)
        forward_taken = jnp.take(panel.reshape(col_panel, vecs, bsize), cols_idx, axis=0)
        forward_product = jnp.einsum(
            "bij,bkj->bki", square, forward_taken, preferred_element_type=jnp.float32
        )
        forward_summed = jax.ops.segment_sum(forward_product, fwd_ids, num_segments=row_panel + 1)
        rows_sum = lax.psum_scatter(
            forward_summed[:row_panel].reshape(row_panel, vecs * bsize),
            "col",
            scatter_dimension=0,
            tiled=True,
        )
        weighted = (rows_sum.reshape(own, vecs, bsize) * row_mass[:, None, :]).astype(jnp.bfloat16)
        whole_rows = lax.all_gather(weighted.reshape(own, vecs * bsize), "col", axis=0, tiled=True)
        taken = jnp.take(whole_rows.reshape(row_panel, vecs, bsize), rows_idx, axis=0)
        product = jnp.einsum("bij,bki->bkj", square, taken, preferred_element_type=jnp.float32)
        summed = jax.ops.segment_sum(product, bwd_ids, num_segments=col_panel + 1)
        cols_sum = lax.psum_scatter(
            summed[:col_panel].reshape(col_panel, vecs * bsize),
            "row",
            scatter_dimension=0,
            tiled=True,
        )
        projected = cols_sum.reshape(own, vecs, bsize) * inv_col[:, None, :]
        gram = lax.psum(local_gram(projected), ("row", "col")) / total_boxes
        current = rotate(projected, gram)
    return current.reshape(own, vecs * bsize)


def fits(n_row, n_col, blocks, vectors, row_mass):
    own, bsize = row_mass.shape[0] // (n_row * n_col), row_mass.shape[1]
    n_cap = blocks.shape[2]
    dense = n_row * (own * n_col * bsize) * (own * n_row * bsize) * 4
    shapes = own * bsize == 128 and vectors.shape[1] == bsize * bsize and n_cap == 128
    return dense <= VMEM_LIMIT // 4 and shapes and n_cap % (16 * n_col) == 0 and n_row == 4 and n_col == 8


def solution(mesh):
    n_row, n_col = mesh.shape["row"], mesh.shape["col"]

    def run(blocks, block_row, block_col, counts, vectors, row_mass, col_mass):
        args = (blocks, block_row, block_col, counts, vectors, row_mass, col_mass)
        if fits(n_row, n_col, blocks, vectors, row_mass):
            devices = mesh.devices.reshape(n_row, n_col // 2, 2)
            grid, col = jax.sharding.Mesh(devices, ("row", "chip", "core")), ("chip", "core")
            body = functools.partial(whole_on_each, n_row, n_col)
        else:
            grid, col, body = mesh, ("col",), split_by_tile
        by_row, by_col = P(("row",) + col, None), P(col + ("row",), None)
        in_specs = (
            P("row", col, None, None), P("row", col, None), P("row", col, None), P("row", col),
            by_col, by_row, by_col,
        )
        return jax.shard_map(
            body, mesh=grid, in_specs=in_specs, out_specs=by_col, check_vma=False
        )(*args)

    return run
```

```python
import functools

import jax
import jax.numpy as jnp
from jax import lax
from jax.experimental import pallas as pl
from jax.experimental.pallas import tpu as pltpu
from jax.sharding import PartitionSpec as P

ITERS = 4
OFF_CAP = 8
META = 16
UNROLL = 16
BATCH = 4
VMEM_LIMIT = 56 * 1024 * 1024

NT = (((1,), (1,)), ((), ()))
NN = (((1,), (0,)), ((), ()))


def dot(a, b, dims=NN):
    return lax.dot_general(a, b, dims, preferred_element_type=jnp.float32)


def split2(x):
    hi = x.astype(jnp.bfloat16)
    return hi, (x - hi.astype(jnp.float32)).astype(jnp.bfloat16)


def inverse_factor(gram):
    n = gram.shape[0]
    rows = lax.broadcasted_iota(jnp.int32, (n, n), 0)
    cols = lax.broadcasted_iota(jnp.int32, (n, n), 1)
    eye = (rows == cols).astype(jnp.float32)
    both = jnp.concatenate([gram, eye], axis=1)
    count, shape = n // 8, (8, 2 * n)
    tiles = [both[8 * t : 8 * t + 8] for t in range(count)]
    sub = lax.broadcasted_iota(jnp.int32, shape, 0)
    out = []
    for b in range(count):
        column = {
            t: [jnp.broadcast_to(tiles[t][:, 8 * b + s : 8 * b + s + 1], shape) for s in range(8)]
            for t in range(b, count)
        }
        row = [jnp.broadcast_to(tiles[b][s : s + 1], shape) for s in range(8)]
        a = [
            [jnp.broadcast_to(column[b][j][s : s + 1], shape) if j >= s else None for j in range(8)]
            for s in range(8)
        ]
        done = jnp.zeros(shape, jnp.float32)
        for s in range(8):
            root = lax.rsqrt(a[s][s])
            inv = root * root
            inv = inv * (2.0 - a[s][s] * inv)
            step = row[s] * inv
            done = jnp.where(sub == s, row[s] * root, done)
            for i in range(s + 1, 8):
                part = a[s][i] * inv
                for j in range(i, 8):
                    a[i][j] = a[i][j] - part * a[s][j]
                row[i] = row[i] - a[s][i] * step
                for t in range(b + 1, count):
                    column[t][i] = column[t][i] - column[t][s] * part
            for t in range(b + 1, count):
                tiles[t] = tiles[t] - column[t][s] * step
        out.append(done)
    return jnp.concatenate(out, axis=0)[:, n:]


def place_of(own, n_row, n_dev):
    here, chip, core = own[0], own[1], own[2]

    def at_device(r, c):
        dr, dc, dk = here ^ r, chip ^ (c // 2), core ^ (c % 2)
        dx, dy = dc & 1, dc >> 1
        order = jnp.where(dr < 2, 2 * dx, 4 + 2 * dy) + jnp.where(
            jnp.where(dr < 2, dy, dx) > 0, n_dev // 4, 0
        )
        return dk * (n_dev // 2) + order + (dr & 1)

    def device_at(d):
        far, second = (d >> 2) & 1, (d >> 3) & 1
        first = (d >> 1) & 1
        dc = jnp.where(far == 0, 2 * second + first, 2 * first + second)
        return here ^ (2 * far + (d & 1)), 2 * (chip ^ dc) + (core ^ (d >> 4))

    return at_device, device_at


def copy_in(pairs, sems):
    copies = [pltpu.make_async_copy(src, dst, sems.at[i]) for i, (src, dst) in enumerate(pairs)]
    for copy in copies:
        copy.start()
    return copies


def left_half(shape):
    return lax.broadcasted_iota(jnp.int32, shape, len(shape) - 1) < 64


def store_twice(pair, twice, q, x):
    pair[q] = x.astype(pair.dtype)
    turned, left = pltpu.roll(x, 64, 1), left_half(x.shape)
    twice[2 * q] = jnp.where(left, x, turned).astype(twice.dtype)
    twice[2 * q + 1] = jnp.where(left, turned, x).astype(twice.dtype)


def gather_pair(q, first, second):
    left = left_half(first.shape[1:])
    apart = jnp.where(left, first[2 * q + 1], second[2 * q])
    return jnp.where(left, first[2 * q], second[2 * q + 1]) + pltpu.roll(apart, 64, 1)


def add_products(n_group, blk, dims, from_list, source, to_list, first, second):
    left = left_half(source.shape[1:])

    def group(i, carry):
        for at in range(0, UNROLL, BATCH):
            pairs = [i * UNROLL + at + u for u in range(BATCH)]
            prods = [
                dot(
                    jnp.where(left, source[from_list[2 * p]], source[from_list[2 * p + 1]]),
                    blk[p],
                    dims,
                )
                for p in pairs
            ]
            for p, prod in zip(pairs, prods):
                a, b = to_list[2 * p], to_list[2 * p + 1]
                first[a] = first[a] + prod
                second[b] = second[b] + prod
        return carry

    lax.fori_loop(0, n_group, group, 0)


def unpack(n_row, n_col, own, copies, lv, lw, nums, place, blk, vs, vd, rm, ic, ints, meta, sem, small):
    n_dev = n_row * n_col
    k = vs.shape[1]
    half = k // 2
    rblk, cblk = 2 * n_col, 2 * n_row
    vec_at = OFF_CAP * half
    meta_at = vec_at + k
    at_device, device_at = place_of(own, n_row, n_dev)

    for copy in copies:
        copy.wait()
    for d in range(n_dev):
        rows = small[d, meta_at : meta_at + META, :].astype(jnp.float32)
        ints[d : d + 1, :] = rows[8:9].astype(jnp.int32)
    to_scalars = pltpu.make_async_copy(ints, meta, sem)
    to_scalars.start()

    for r in range(n_row):
        for c in range(n_col):
            q, p, d = c * n_row + r, r * n_col + c, at_device(r, c)
            rows = small[d, meta_at : meta_at + META, :].astype(jnp.float32)
            rm[p] = jnp.broadcast_to(rows[0:1] + rows[1:2] + rows[2:3], (8, 128))
            ic[q] = jnp.broadcast_to(rows[3:4] + rows[4:5] + rows[5:6], (8, 128))
            store_twice(vs, vd, q, small[d, vec_at : vec_at + k, :].astype(jnp.float32))
    to_scalars.wait()

    lanes = lax.broadcasted_iota(jnp.int32, (half, 128), 1)

    def device(d, n):
        count = meta[d, 2 * OFF_CAP]
        count = jnp.where(count > OFF_CAP, 0, count)
        r, c = device_at(d)
        for s in range(OFF_CAP):
            lv[n + s] = c * cblk + meta[d, OFF_CAP + s]
            lw[n + s] = r * rblk + meta[d, s]
            x = small[d, s * half : (s + 1) * half, :].astype(jnp.float32)
            turned = pltpu.roll(x, 64, 1)
            side = (n + s) % 2
            here = (lanes // 64) == side
            even = jnp.where(here, jnp.where(side == 0, x, turned), 0.0)
            odd = jnp.where(here, jnp.where(side == 0, turned, x), 0.0)
            at = pl.multiple_of(side * k, k)
            both = jnp.concatenate([even, odd], axis=0).astype(jnp.bfloat16)
            blk[(n + s) // 2, pl.ds(at, k), :] = both
        return n + count

    n_live = lax.fori_loop(0, n_dev, device, jnp.int32(0))
    for u in range(2 * UNROLL - 1):
        lv[n_live + u] = 0
        lw[n_live + u] = 0
        at = pl.multiple_of((n_live + u) % 2 * k, k)
        blk[(n_live + u) // 2, pl.ds(at, k), :] = jnp.zeros((k, 128), jnp.bfloat16)
    nums[0] = (n_live + 2 * UNROLL - 1) // (2 * UNROLL)

    for r in range(n_row):
        h = jnp.int32(0)
        for c in range(n_col):
            h = jnp.where(meta[at_device(r, c), 2 * OFF_CAP] > OFF_CAP, c, h)
        nums[1 + r] = h
        index = small[at_device(r, h), meta_at : meta_at + META, :].astype(jnp.float32)
        place[r : r + 1, :] = index[7:8] * float(rblk) + index[6:7]


def iterate(n_row, n_col, n_cap, total, own, mine, other, *rest):
    fulls, out = rest[:6], rest[6]
    sems, full, tmp, home = rest[7:11]
    unpacked, rest = rest[11:23], rest[23:]
    lv, lw, nums, place, blk, vs, vd, rm, ic, ints, meta, small = unpacked
    w, w1, w2, wt, wd, y, y1, y2, ph, linv = rest
    n_dev = n_row * n_col
    k = vs.shape[1]
    half = k // 2
    rpairs, cpairs = n_col, n_row
    rblk, cblk = 2 * rpairs, 2 * cpairs
    part = n_cap // n_col
    width = cpairs * 128
    at_device, _ = place_of(own, n_row, n_dev)

    def laid_out(refs, whole):
        at, pairs = 0, []
        for ref in refs:
            pairs.append((ref, whole.at[pl.ds(at, ref.shape[0])]))
            at += ref.shape[0]
        return pairs

    copies = copy_in(laid_out([mine, other], small) + laid_out(fulls, full), sems)
    unpack(
        n_row, n_col, own, copies[:2],
        lv, lw, nums, place, blk, vs, vd, rm, ic, ints, meta, sems.at[len(copies)], small,
    )
    n_group = nums[0]
    for copy in copies[2:]:
        copy.wait()

    left = lax.broadcasted_iota(jnp.int32, (rblk, 128), 1) < 64
    homes = []
    for r in range(n_row):
        homes.append(nums[1 + r])
        want = lax.broadcasted_iota(jnp.int32, (cblk * rblk, n_cap), 0).astype(jnp.float32)
        select = jnp.where(want == place[r : r + 1, :], 1.0, 0.0).astype(jnp.bfloat16)

        parts = [at_device(r, c) for c in range(n_col)]

        def build(m, carry, parts=parts, select=select):
            at = pl.multiple_of(m * part, part)
            slots = jnp.concatenate(
                [full[d, pl.ds(at, part), :] for d in parts], axis=0
            )
            dense = dot(select, slots)
            for u in range(cpairs):
                a = dense[2 * u * rblk : (2 * u + 1) * rblk]
                b = dense[(2 * u + 1) * rblk : (2 * u + 2) * rblk]
                even = jnp.where(left, a, pltpu.roll(b, 64, 1))
                odd = jnp.where(left, pltpu.roll(a, 64, 1), b)
                tmp[u, pl.ds(m, rblk, stride=k), :] = even
                tmp[u, pl.ds(m + half, rblk, stride=k), :] = odd
            return carry

        lax.fori_loop(0, half, build, 0, unroll=4)

        def cut(i, carry, r=r):
            at = pl.multiple_of(i * k, k)
            for u in range(cpairs):
                hi, lo = split2(tmp[u, pl.ds(at, k), :])
                home[r, pl.ds(at, k), u * 128 : (u + 1) * 128] = hi
                home[r, pl.ds(at, k), width + u * 128 : width + (u + 1) * 128] = lo
            return carry

        lax.fori_loop(0, rblk, cut, 0, unroll=4)

    def clear(refs):
        for ref in refs:
            for q in range(ref.shape[0]):
                ref[q] = jnp.zeros_like(ref[q])

    clear([y, y1, y2, w1, w2])

    def iteration(it, carry):
        @pl.when(it > 0)
        def _():
            lh, ll = split2(linv[...])
            turn = jnp.concatenate([lh, lh, ll], axis=1)
            for q in range(0, n_dev, 4):
                hi = jnp.concatenate([ph[q + d, :k, :] for d in range(4)], axis=1)
                lo = jnp.concatenate([ph[q + d, k:, :] for d in range(4)], axis=1)
                current = dot(turn, jnp.concatenate([hi, lo, hi], axis=0))
                for d in range(4):
                    x = current[:, d * 128 : (d + 1) * 128] * ic[q + d, 0:1, :]
                    store_twice(vs, vd, q + d, x)

        for r in range(n_row):
            base = homes[r] * cpairs
            vec = jnp.concatenate([vs[base + u] for u in range(cpairs)] * 2, axis=1)
            for p in range(0, rpairs, 2):
                prod = dot(vec, home[r, p * 128 : (p + 2) * 128, :], NT)
                w[r * rpairs + p] = prod[:, :128]
                w[r * rpairs + p + 1] = prod[:, 128:]

        add_products(n_group, blk, NT, lv, vd, lw, w1, w2)
        for p in range(n_dev):
            x = w[p] + gather_pair(p, w1, w2)
            store_twice(wt, wd, p, x * rm[p, 0:1, :])

        for r in range(n_row):
            base = homes[r] * cpairs
            vec = jnp.concatenate([wt[r * rpairs + p] for p in range(rpairs)], axis=1)
            for u in range(0, cpairs, 2):
                cols = slice(u * 128, (u + 2) * 128)
                tail = slice(width + u * 128, width + (u + 2) * 128)
                prod = dot(vec, home[r, :, cols]) + dot(vec, home[r, :, tail])
                y[base + u] = y[base + u] + prod[:, :128]
                y[base + u + 1] = y[base + u + 1] + prod[:, 128:]

        add_products(n_group, blk, NN, lw, wd, lv, y1, y2)

        both = jnp.zeros((2 * k, k), jnp.float32)
        for q in range(0, n_dev, 4):
            his, los = [], []
            for d in range(q, q + 4):
                x = y[d] + gather_pair(d, y1, y2)
                hi, lo = split2(x * ic[d, 0:1, :])
                ph[d, :k, :] = hi
                ph[d, k:, :] = lo
                his.append(hi)
                los.append(lo)
            hi = jnp.concatenate(his, axis=1)
            lo = jnp.concatenate(los, axis=1)
            both = both + dot(jnp.concatenate([hi, lo], axis=0), hi, NT)
        gram = (both[:k] + (both[k:] + both[k:].T)) / total
        clear([y, y1, y2, w1, w2])
        linv[...] = inverse_factor(gram)
        return carry

    lax.fori_loop(0, ITERS, iteration, 0)
    lh, ll = split2(linv[...])
    q = (2 * own[1] + own[2]) * n_row + own[0]
    hi, lo = ph[q, :k, :], ph[q, k:, :]
    x = dot(lh, hi) + dot(ll, hi) + dot(lh, lo)
    out[0] = x[:, :k]
    out[1] = x[:, k:]


def split3(x):
    a = lax.reduce_precision(x, 8, 7)
    b = lax.reduce_precision(x - a, 8, 7)
    return [v.astype(jnp.bfloat16) for v in (a, b, x - a - b)]


def swap(x, axis, distance):
    size = lax.axis_size(axis)
    return lax.ppermute(x, axis, [(i, i ^ distance) for i in range(size)])


def along_rows(x):
    return [x] + [swap(x, "row", s) for s in range(1, lax.axis_size("row"))]


def along_one_chip_axis(x):
    near, far = jnp.stack(x[:2]), jnp.stack(x[2:])
    return [
        jnp.concatenate([near, swap(near, "chip", 1)]),
        jnp.concatenate([far, swap(far, "chip", 2)]),
    ]


def along_other_chip_axis(x):
    near, far = x
    return [swap(near, "chip", 2), swap(far, "chip", 1)]


def whole_on_each(n_row, n_col, blocks, block_row, block_col, counts, vectors, row_mass, col_mass):
    tile = blocks[0, 0]
    n_cap = tile.shape[0]
    own, bsize = row_mass.shape
    k = vectors.shape[1] // bsize
    half = bsize // 2
    part = n_cap // n_col
    n_dev = n_row * n_col
    count = counts[0, 0]
    has_full = count > OFF_CAP
    bf16 = jnp.bfloat16
    row, chip, core = (lax.axis_index(name) for name in ("row", "chip", "core"))

    off = tile[:OFF_CAP].reshape(OFF_CAP * half, 128)
    inv_col = 1.0 / jnp.sqrt(col_mass)
    scaled = (vectors.reshape(own, k, bsize) * inv_col[:, None, :]).astype(bf16)
    scaled = scaled.transpose(1, 0, 2).reshape(k, own * bsize)
    mass = row_mass.reshape(own, half, 2).transpose(0, 2, 1).reshape(own * bsize)
    rows, cols = block_row[0, 0], block_col[0, 0]
    short = jnp.concatenate(
        [rows[:OFF_CAP], cols[:OFF_CAP], count[None], jnp.zeros(128 - 2 * OFF_CAP - 1, jnp.int32)]
    )
    meta = [v.astype(bf16) for v in (rows, cols, short)]
    meta = split3(mass) + split3(inv_col.reshape(own * bsize)) + meta
    meta = jnp.stack(meta + [jnp.zeros(128, bf16)] * (META - len(meta)))
    small = jnp.concatenate([off, scaled, meta], axis=0)
    sent = jnp.where(has_full, tile, jnp.zeros_like(tile)).reshape(n_col, part, bsize * bsize)
    got = lax.all_to_all(sent, ("chip", "core"), split_axis=0, concat_axis=0)
    home = jnp.sum(got.astype(jnp.float32), axis=0).astype(bf16)
    home = home.reshape(part, half, 128).transpose(1, 0, 2).reshape(half * part, 128)

    together = lax.optimization_barrier
    smalls = along_rows(small)
    home, smalls[1] = together((home, smalls[1]))
    homes, smalls = along_rows(home), along_one_chip_axis(smalls)
    smalls, homes[1:3] = together((smalls, homes[1:3]))
    smalls = jnp.concatenate(smalls + along_other_chip_axis(smalls))
    homes, smalls = together((homes, smalls))
    homes, others = together((along_one_chip_axis(homes), swap(smalls, "core", 1)))
    last = along_other_chip_axis(homes)
    homes = jnp.concatenate(homes)
    other_homes = swap(homes, "core", 1)

    fulls = [homes, *last, other_homes, *(swap(v, "core", 1) for v in last)]

    where = jnp.stack([row, chip, core]).astype(jnp.int32)
    height, width = 2 * n_col * bsize, 2 * n_row * bsize
    slots = n_dev * OFF_CAP + 2 * UNROLL
    f32, i32, vmem, smem = jnp.float32, jnp.int32, pltpu.VMEM, pltpu.SMEM
    pair, twice, mass = (n_dev, k, 128), (2 * n_dev, k, 128), (n_dev, 8, 128)
    result = pl.pallas_call(
        functools.partial(iterate, n_row, n_col, n_cap, float(n_dev * own * bsize)),
        out_shape=jax.ShapeDtypeStruct((own, k, bsize), f32),
        in_specs=[pl.BlockSpec(memory_space=smem)]
        + [pl.BlockSpec(memory_space=pl.ANY)] * (2 + len(fulls)),
        out_specs=pl.BlockSpec(memory_space=vmem),
        scratch_shapes=[
            pltpu.SemaphoreType.DMA((3 + len(fulls),)),
            vmem((n_dev,) + home.shape, bf16),
            vmem((n_row, height, 128), f32),
            vmem((n_row, height, 2 * width), bf16),
            smem((slots,), i32),
            smem((slots,), i32),
            smem((1 + n_row,), i32),
            vmem((8, 128), f32),
            vmem((slots // 2, 128, 128), bf16),
            vmem(pair, bf16), vmem(twice, bf16), vmem(mass, f32), vmem(mass, f32),
            vmem((n_dev, 128), i32),
            smem((n_dev, 128), i32),
            vmem((n_dev,) + small.shape, bf16),
            vmem(pair, f32), vmem(twice, f32), vmem(twice, f32), vmem(pair, bf16), vmem(twice, bf16),
            vmem(pair, f32), vmem(twice, f32), vmem(twice, f32),
            vmem((n_dev, 2 * k, 128), bf16),
            vmem((k, k), f32),
        ],
        compiler_params=pltpu.CompilerParams(vmem_limit_bytes=VMEM_LIMIT),
        name="iterate",
    )(where, smalls, others, *fulls)
    return result.reshape(own, k * bsize)


def rotate(projected, gram):
    lower = jnp.linalg.cholesky(gram)
    inverse = lax.linalg.triangular_solve(
        lower, jnp.eye(gram.shape[0], dtype=jnp.float32), left_side=True, lower=True
    )
    return jnp.einsum(
        "kl,bli->bki",
        inverse,
        projected,
        precision=lax.Precision.HIGHEST,
        preferred_element_type=jnp.float32,
    )


def local_gram(projected):
    return jnp.einsum(
        "bki,bli->kl",
        projected,
        projected,
        precision=lax.Precision.HIGHEST,
        preferred_element_type=jnp.float32,
    )


def split_by_tile(blocks, block_row, block_col, counts, vectors, row_mass, col_mass):
    tile = blocks[0, 0]
    n_cap = tile.shape[0]
    bsize = row_mass.shape[1]
    vecs = vectors.shape[1] // bsize
    own = vectors.shape[0]
    n_row = lax.axis_size("row")
    n_col = lax.axis_size("col")
    row_panel = own * n_col
    col_panel = own * n_row
    total_boxes = float(own * bsize * n_row * n_col)
    rows_idx = block_row[0, 0]
    cols_idx = block_col[0, 0]
    live = jnp.arange(n_cap) < counts[0, 0]
    fwd_ids = jnp.where(live, rows_idx, row_panel)
    bwd_ids = jnp.where(live, cols_idx, col_panel)
    square = tile.reshape(n_cap, bsize, bsize)
    inv_col = 1.0 / jnp.sqrt(col_mass)
    current = vectors.reshape(own, vecs, bsize)
    for step in range(ITERS):
        scaled = (current * inv_col[:, None, :]).astype(jnp.bfloat16).reshape(own, vecs * bsize)
        panel = lax.all_gather(scaled, "row", axis=0, tiled=True)
        forward_taken = jnp.take(panel.reshape(col_panel, vecs, bsize), cols_idx, axis=0)
        forward_product = jnp.einsum(
            "bij,bkj->bki", square, forward_taken, preferred_element_type=jnp.float32
        )
        forward_summed = jax.ops.segment_sum(forward_product, fwd_ids, num_segments=row_panel + 1)
        rows_sum = lax.psum_scatter(
            forward_summed[:row_panel].reshape(row_panel, vecs * bsize),
            "col",
            scatter_dimension=0,
            tiled=True,
        )
        weighted = (rows_sum.reshape(own, vecs, bsize) * row_mass[:, None, :]).astype(jnp.bfloat16)
        whole_rows = lax.all_gather(weighted.reshape(own, vecs * bsize), "col", axis=0, tiled=True)
        taken = jnp.take(whole_rows.reshape(row_panel, vecs, bsize), rows_idx, axis=0)
        product = jnp.einsum("bij,bki->bkj", square, taken, preferred_element_type=jnp.float32)
        summed = jax.ops.segment_sum(product, bwd_ids, num_segments=col_panel + 1)
        cols_sum = lax.psum_scatter(
            summed[:col_panel].reshape(col_panel, vecs * bsize),
            "row",
            scatter_dimension=0,
            tiled=True,
        )
        projected = cols_sum.reshape(own, vecs, bsize) * inv_col[:, None, :]
        gram = lax.psum(local_gram(projected), ("row", "col")) / total_boxes
        current = rotate(projected, gram)
    return current.reshape(own, vecs * bsize)


def fits(n_row, n_col, blocks, vectors, row_mass):
    own, bsize = row_mass.shape[0] // (n_row * n_col), row_mass.shape[1]
    n_cap = blocks.shape[2]
    dense = n_row * (own * n_col * bsize) * (own * n_row * bsize) * 4
    shapes = own * bsize == 128 and vectors.shape[1] == bsize * bsize and n_cap == 128
    return dense <= VMEM_LIMIT // 4 and shapes and n_cap % (16 * n_col) == 0 and n_row == 4 and n_col == 8


def solution(mesh):
    n_row, n_col = mesh.shape["row"], mesh.shape["col"]

    def run(blocks, block_row, block_col, counts, vectors, row_mass, col_mass):
        args = (blocks, block_row, block_col, counts, vectors, row_mass, col_mass)
        if fits(n_row, n_col, blocks, vectors, row_mass):
            devices = mesh.devices.reshape(n_row, n_col // 2, 2)
            grid, col = jax.sharding.Mesh(devices, ("row", "chip", "core")), ("chip", "core")
            body = functools.partial(whole_on_each, n_row, n_col)
        else:
            grid, col, body = mesh, ("col",), split_by_tile
        by_row, by_col = P(("row",) + col, None), P(col + ("row",), None)
        in_specs = (
            P("row", col, None, None), P("row", col, None), P("row", col, None), P("row", col),
            by_col, by_row, by_col,
        )
        return jax.shard_map(
            body, mesh=grid, in_specs=in_specs, out_specs=by_col, check_vma=False
        )(*args)

    return run
```

```python
import functools

import jax
import jax.numpy as jnp
from jax import lax
from jax.experimental import pallas as pl
from jax.experimental.pallas import tpu as pltpu
from jax.sharding import PartitionSpec as P

ITERS = 4
OFF_CAP = 8
META = 16
UNROLL = 16
BATCH = 4
VMEM_LIMIT = 56 * 1024 * 1024

NT = (((1,), (1,)), ((), ()))
NN = (((1,), (0,)), ((), ()))


def dot(a, b, dims=NN):
    return lax.dot_general(a, b, dims, preferred_element_type=jnp.float32)


def split2(x):
    hi = x.astype(jnp.bfloat16)
    return hi, (x - hi.astype(jnp.float32)).astype(jnp.bfloat16)


def inverse_factor(gram):
    n = gram.shape[0]
    rows = lax.broadcasted_iota(jnp.int32, (n, n), 0)
    cols = lax.broadcasted_iota(jnp.int32, (n, n), 1)
    eye = (rows == cols).astype(jnp.float32)
    both = jnp.concatenate([gram, eye], axis=1)
    count, shape = n // 8, (8, 2 * n)
    tiles = [both[8 * t : 8 * t + 8] for t in range(count)]
    sub = lax.broadcasted_iota(jnp.int32, shape, 0)
    out = []
    for b in range(count):
        column = {
            t: [jnp.broadcast_to(tiles[t][:, 8 * b + s : 8 * b + s + 1], shape) for s in range(8)]
            for t in range(b, count)
        }
        row = [jnp.broadcast_to(tiles[b][s : s + 1], shape) for s in range(8)]
        a = [
            [jnp.broadcast_to(column[b][j][s : s + 1], shape) if j >= s else None for j in range(8)]
            for s in range(8)
        ]
        done = jnp.zeros(shape, jnp.float32)
        for s in range(8):
            root = lax.rsqrt(a[s][s])
            inv = root * root
            inv = inv * (2.0 - a[s][s] * inv)
            step = row[s] * inv
            done = jnp.where(sub == s, row[s] * root, done)
            for i in range(s + 1, 8):
                part = a[s][i] * inv
                for j in range(i, 8):
                    a[i][j] = a[i][j] - part * a[s][j]
                row[i] = row[i] - a[s][i] * step
                for t in range(b + 1, count):
                    column[t][i] = column[t][i] - column[t][s] * part
            for t in range(b + 1, count):
                tiles[t] = tiles[t] - column[t][s] * step
        out.append(done)
    return jnp.concatenate(out, axis=0)[:, n:]


def place_of(own, n_row, n_dev):
    here, chip, core = own[0], own[1], own[2]

    def at_device(r, c):
        dr, dc, dk = here ^ r, chip ^ (c // 2), core ^ (c % 2)
        dx, dy = dc & 1, dc >> 1
        order = jnp.where(dr < 2, 2 * dx, 4 + 2 * dy) + jnp.where(
            jnp.where(dr < 2, dy, dx) > 0, n_dev // 4, 0
        )
        return dk * (n_dev // 2) + order + (dr & 1)

    def device_at(d):
        far, second = (d >> 2) & 1, (d >> 3) & 1
        first = (d >> 1) & 1
        dc = jnp.where(far == 0, 2 * second + first, 2 * first + second)
        return here ^ (2 * far + (d & 1)), 2 * (chip ^ dc) + (core ^ (d >> 4))

    return at_device, device_at


def copy_in(pairs, sems):
    copies = [pltpu.make_async_copy(src, dst, sems.at[i]) for i, (src, dst) in enumerate(pairs)]
    for copy in copies:
        copy.start()
    return copies


def left_half(shape):
    return lax.broadcasted_iota(jnp.int32, shape, len(shape) - 1) < 64


def store_twice(pair, twice, q, x):
    pair[q] = x.astype(pair.dtype)
    turned, left = pltpu.roll(x, 64, 1), left_half(x.shape)
    twice[2 * q] = jnp.where(left, x, turned).astype(twice.dtype)
    twice[2 * q + 1] = jnp.where(left, turned, x).astype(twice.dtype)


def gather_pair(q, first, second):
    left = left_half(first.shape[1:])
    apart = jnp.where(left, first[2 * q + 1], second[2 * q])
    return jnp.where(left, first[2 * q], second[2 * q + 1]) + pltpu.roll(apart, 64, 1)


def add_products(n_group, blk, dims, from_list, source, to_list, first, second):
    left = left_half(source.shape[1:])

    def group(i, carry):
        for at in range(0, UNROLL, BATCH):
            pairs = [i * UNROLL + at + u for u in range(BATCH)]
            prods = [
                dot(
                    jnp.where(left, source[from_list[2 * p]], source[from_list[2 * p + 1]]),
                    blk[p],
                    dims,
                )
                for p in pairs
            ]
            for p, prod in zip(pairs, prods):
                a, b = to_list[2 * p], to_list[2 * p + 1]
                first[a] = first[a] + prod
                second[b] = second[b] + prod
        return carry

    lax.fori_loop(0, n_group, group, 0)


def unpack(n_row, n_col, own, copies, lv, lw, nums, place, blk, vs, vd, rm, ic, ints, meta, sem, small):
    n_dev = n_row * n_col
    k = vs.shape[1]
    half = k // 2
    rblk, cblk = 2 * n_col, 2 * n_row
    vec_at = OFF_CAP * half
    meta_at = vec_at + k
    at_device, device_at = place_of(own, n_row, n_dev)

    for copy in copies:
        copy.wait()
    for d in range(n_dev):
        rows = small[d, meta_at : meta_at + META, :].astype(jnp.float32)
        ints[d : d + 1, :] = rows[8:9].astype(jnp.int32)
    to_scalars = pltpu.make_async_copy(ints, meta, sem)
    to_scalars.start()

    for r in range(n_row):
        for c in range(n_col):
            q, p, d = c * n_row + r, r * n_col + c, at_device(r, c)
            rows = small[d, meta_at : meta_at + META, :].astype(jnp.float32)
            rm[p] = jnp.broadcast_to(rows[0:1] + rows[1:2] + rows[2:3], (8, 128))
            ic[q] = jnp.broadcast_to(rows[3:4] + rows[4:5] + rows[5:6], (8, 128))
            store_twice(vs, vd, q, small[d, vec_at : vec_at + k, :].astype(jnp.float32))
    to_scalars.wait()

    lanes = lax.broadcasted_iota(jnp.int32, (half, 128), 1)

    def device(d, n):
        count = meta[d, 2 * OFF_CAP]
        count = jnp.where(count > OFF_CAP, 0, count)
        r, c = device_at(d)
        for s in range(OFF_CAP):
            lv[n + s] = c * cblk + meta[d, OFF_CAP + s]
            lw[n + s] = r * rblk + meta[d, s]
            x = small[d, s * half : (s + 1) * half, :].astype(jnp.float32)
            turned = pltpu.roll(x, 64, 1)
            side = (n + s) % 2
            here = (lanes // 64) == side
            even = jnp.where(here, jnp.where(side == 0, x, turned), 0.0)
            odd = jnp.where(here, jnp.where(side == 0, turned, x), 0.0)
            at = pl.multiple_of(side * k, k)
            both = jnp.concatenate([even, odd], axis=0).astype(jnp.bfloat16)
            blk[(n + s) // 2, pl.ds(at, k), :] = both
        return n + count

    n_live = lax.fori_loop(0, n_dev, device, jnp.int32(0))
    for u in range(2 * UNROLL - 1):
        lv[n_live + u] = 0
        lw[n_live + u] = 0
        at = pl.multiple_of((n_live + u) % 2 * k, k)
        blk[(n_live + u) // 2, pl.ds(at, k), :] = jnp.zeros((k, 128), jnp.bfloat16)
    nums[0] = (n_live + 2 * UNROLL - 1) // (2 * UNROLL)

    for r in range(n_row):
        h = jnp.int32(0)
        for c in range(n_col):
            h = jnp.where(meta[at_device(r, c), 2 * OFF_CAP] > OFF_CAP, c, h)
        nums[1 + r] = h
        index = small[at_device(r, h), meta_at : meta_at + META, :].astype(jnp.float32)
        place[r : r + 1, :] = index[7:8] * float(rblk) + index[6:7]


def iterate(n_row, n_col, n_cap, total, own, *rest):
    smalls, fulls, out = rest[:8], rest[8:16], rest[16]
    sems, full, tmp, home = rest[17:21]
    unpacked, rest = rest[21:33], rest[33:]
    lv, lw, nums, place, blk, vs, vd, rm, ic, ints, meta, small = unpacked
    w, w1, w2, wt, wd, y, y1, y2, ph, linv = rest
    n_dev = n_row * n_col
    k = vs.shape[1]
    half = k // 2
    rpairs, cpairs = n_col, n_row
    rblk, cblk = 2 * rpairs, 2 * cpairs
    part = n_cap // n_col
    width = cpairs * 128
    at_device, _ = place_of(own, n_row, n_dev)

    def laid_out(refs, whole):
        at, pairs = 0, []
        for ref in refs:
            pairs.append((ref, whole.at[pl.ds(at, ref.shape[0])]))
            at += ref.shape[0]
        return pairs

    copies = copy_in(laid_out(smalls, small) + laid_out(fulls, full), sems)
    unpack(
        n_row, n_col, own, copies[:8],
        lv, lw, nums, place, blk, vs, vd, rm, ic, ints, meta, sems.at[len(copies)], small,
    )
    n_group = nums[0]
    for copy in copies[8:]:
        copy.wait()

    left = lax.broadcasted_iota(jnp.int32, (rblk, 128), 1) < 64
    homes = []
    for r in range(n_row):
        homes.append(nums[1 + r])
        want = lax.broadcasted_iota(jnp.int32, (cblk * rblk, n_cap), 0).astype(jnp.float32)
        select = jnp.where(want == place[r : r + 1, :], 1.0, 0.0).astype(jnp.bfloat16)

        parts = [at_device(r, 2 * i + j) for j in range(2) for i in range(n_col // 2)]

        def build(m, carry, parts=parts, select=select):
            at = pl.multiple_of(m * part, part)
            slots = jnp.concatenate(
                [full[d, pl.ds(at, part), :] for d in parts], axis=0
            )
            dense = dot(select, slots)
            for u in range(cpairs):
                a = dense[2 * u * rblk : (2 * u + 1) * rblk]
                b = dense[(2 * u + 1) * rblk : (2 * u + 2) * rblk]
                even = jnp.where(left, a, pltpu.roll(b, 64, 1))
                odd = jnp.where(left, pltpu.roll(a, 64, 1), b)
                tmp[u, pl.ds(m, rblk, stride=k), :] = even
                tmp[u, pl.ds(m + half, rblk, stride=k), :] = odd
            return carry

        lax.fori_loop(0, half, build, 0, unroll=4)

        def cut(i, carry, r=r):
            at = pl.multiple_of(i * k, k)
            for u in range(cpairs):
                hi, lo = split2(tmp[u, pl.ds(at, k), :])
                home[r, pl.ds(at, k), u * 128 : (u + 1) * 128] = hi
                home[r, pl.ds(at, k), width + u * 128 : width + (u + 1) * 128] = lo
            return carry

        lax.fori_loop(0, rblk, cut, 0, unroll=4)

    def clear(refs):
        for ref in refs:
            for q in range(ref.shape[0]):
                ref[q] = jnp.zeros_like(ref[q])

    clear([y, y1, y2, w1, w2])

    def iteration(it, carry):
        @pl.when(it > 0)
        def _():
            lh, ll = split2(linv[...])
            turn = jnp.concatenate([lh, lh, ll], axis=1)
            for q in range(0, n_dev, 4):
                hi = jnp.concatenate([ph[q + d, :k, :] for d in range(4)], axis=1)
                lo = jnp.concatenate([ph[q + d, k:, :] for d in range(4)], axis=1)
                current = dot(turn, jnp.concatenate([hi, lo, hi], axis=0))
                for d in range(4):
                    x = current[:, d * 128 : (d + 1) * 128] * ic[q + d, 0:1, :]
                    store_twice(vs, vd, q + d, x)

        for r in range(n_row):
            base = homes[r] * cpairs
            vec = jnp.concatenate([vs[base + u] for u in range(cpairs)] * 2, axis=1)
            for p in range(0, rpairs, 2):
                prod = dot(vec, home[r, p * 128 : (p + 2) * 128, :], NT)
                w[r * rpairs + p] = prod[:, :128]
                w[r * rpairs + p + 1] = prod[:, 128:]

        add_products(n_group, blk, NT, lv, vd, lw, w1, w2)
        for p in range(n_dev):
            x = w[p] + gather_pair(p, w1, w2)
            store_twice(wt, wd, p, x * rm[p, 0:1, :])

        for r in range(n_row):
            base = homes[r] * cpairs
            vec = jnp.concatenate([wt[r * rpairs + p] for p in range(rpairs)], axis=1)
            for u in range(0, cpairs, 2):
                cols = slice(u * 128, (u + 2) * 128)
                tail = slice(width + u * 128, width + (u + 2) * 128)
                prod = dot(vec, home[r, :, cols]) + dot(vec, home[r, :, tail])
                y[base + u] = y[base + u] + prod[:, :128]
                y[base + u + 1] = y[base + u + 1] + prod[:, 128:]

        add_products(n_group, blk, NN, lw, wd, lv, y1, y2)

        both = jnp.zeros((2 * k, k), jnp.float32)
        for q in range(0, n_dev, 4):
            his, los = [], []
            for d in range(q, q + 4):
                x = y[d] + gather_pair(d, y1, y2)
                hi, lo = split2(x * ic[d, 0:1, :])
                ph[d, :k, :] = hi
                ph[d, k:, :] = lo
                his.append(hi)
                los.append(lo)
            hi = jnp.concatenate(his, axis=1)
            lo = jnp.concatenate(los, axis=1)
            both = both + dot(jnp.concatenate([hi, lo], axis=0), hi, NT)
        gram = (both[:k] + (both[k:] + both[k:].T)) / total
        clear([y, y1, y2, w1, w2])
        linv[...] = inverse_factor(gram)
        return carry

    lax.fori_loop(0, ITERS, iteration, 0)
    lh, ll = split2(linv[...])
    q = (2 * own[1] + own[2]) * n_row + own[0]
    hi, lo = ph[q, :k, :], ph[q, k:, :]
    x = dot(lh, hi) + dot(ll, hi) + dot(lh, lo)
    out[0] = x[:, :k]
    out[1] = x[:, k:]


def split3(x):
    a = lax.reduce_precision(x, 8, 7)
    b = lax.reduce_precision(x - a, 8, 7)
    return [v.astype(jnp.bfloat16) for v in (a, b, x - a - b)]


def swap(x, axis, distance):
    size = lax.axis_size(axis)
    return lax.ppermute(x, axis, [(i, i ^ distance) for i in range(size)])


def along_rows(x):
    return [x] + [swap(x, "row", s) for s in range(1, lax.axis_size("row"))]


def along_one_chip_axis(x):
    near, far = jnp.stack(x[:2]), jnp.stack(x[2:])
    return [
        jnp.concatenate([near, swap(near, "chip", 1)]),
        jnp.concatenate([far, swap(far, "chip", 2)]),
    ]


def along_other_chip_axis(x):
    near, far = x
    return [swap(near, "chip", 2), swap(far, "chip", 1)]


def full_part(tile, has_full, n_chip, part, chip, core):
    tile = tile.reshape(2, n_chip, part, tile.shape[1])
    none = jnp.zeros(tile.shape[1:], tile.dtype)
    kept, sent = (
        jnp.where(has_full, lax.dynamic_index_in_dim(tile, i, 0, False), none)
        for i in (core, 1 - core)
    )
    both = kept + swap(sent, "core", 1)
    mine = lax.dynamic_index_in_dim(both, chip, 0, False)
    for s in range(1, n_chip):
        mine = mine + swap(lax.dynamic_index_in_dim(both, chip ^ s, 0, False), "chip", s)
    return mine


def whole_on_each(n_row, n_col, blocks, block_row, block_col, counts, vectors, row_mass, col_mass):
    tile = blocks[0, 0]
    n_cap = tile.shape[0]
    own, bsize = row_mass.shape
    k = vectors.shape[1] // bsize
    half = bsize // 2
    part = n_cap // n_col
    n_dev = n_row * n_col
    count = counts[0, 0]
    has_full = count > OFF_CAP
    bf16 = jnp.bfloat16
    row, chip, core = (lax.axis_index(name) for name in ("row", "chip", "core"))

    off = tile[:OFF_CAP].reshape(OFF_CAP * half, 128)
    inv_col = 1.0 / jnp.sqrt(col_mass)
    scaled = (vectors.reshape(own, k, bsize) * inv_col[:, None, :]).astype(bf16)
    scaled = scaled.transpose(1, 0, 2).reshape(k, own * bsize)
    mass = row_mass.reshape(own, half, 2).transpose(0, 2, 1).reshape(own * bsize)
    rows, cols = block_row[0, 0], block_col[0, 0]
    short = jnp.concatenate(
        [rows[:OFF_CAP], cols[:OFF_CAP], count[None], jnp.zeros(128 - 2 * OFF_CAP - 1, jnp.int32)]
    )
    meta = [v.astype(bf16) for v in (rows, cols, short)]
    meta = split3(mass) + split3(inv_col.reshape(own * bsize)) + meta
    meta = jnp.stack(meta + [jnp.zeros(128, bf16)] * (META - len(meta)))
    small = jnp.concatenate([off, scaled, meta], axis=0)
    home = full_part(tile, has_full, n_col // 2, part, chip, core)
    home = home.reshape(part, half, 128).transpose(1, 0, 2).reshape(half * part, 128)

    together = lax.optimization_barrier
    home, smalls = together((home, along_rows(small)))
    homes, smalls = along_rows(home), along_one_chip_axis(smalls)
    smalls, homes[1] = together((smalls, homes[1]))
    homes, smalls = together((homes, smalls + along_other_chip_axis(smalls)))
    homes = along_one_chip_axis(homes)
    homes = homes + along_other_chip_axis(homes)
    smalls, homes = ([*v, *(swap(x, "core", 1) for x in v)] for v in (smalls, homes))

    where = jnp.stack([row, chip, core]).astype(jnp.int32)
    height, width = 2 * n_col * bsize, 2 * n_row * bsize
    slots = n_dev * OFF_CAP + 2 * UNROLL
    f32, i32, vmem, smem = jnp.float32, jnp.int32, pltpu.VMEM, pltpu.SMEM
    pair, twice, mass = (n_dev, k, 128), (2 * n_dev, k, 128), (n_dev, 8, 128)
    result = pl.pallas_call(
        functools.partial(iterate, n_row, n_col, n_cap, float(n_dev * own * bsize)),
        out_shape=jax.ShapeDtypeStruct((own, k, bsize), f32),
        in_specs=[pl.BlockSpec(memory_space=smem)]
        + [pl.BlockSpec(memory_space=pl.ANY)] * (len(smalls) + len(homes)),
        out_specs=pl.BlockSpec(memory_space=vmem),
        scratch_shapes=[
            pltpu.SemaphoreType.DMA((len(smalls) + len(homes) + 1,)),
            vmem((n_dev,) + home.shape, bf16),
            vmem((n_row, height, 128), f32),
            vmem((n_row, height, 2 * width), bf16),
            smem((slots,), i32),
            smem((slots,), i32),
            smem((1 + n_row,), i32),
            vmem((8, 128), f32),
            vmem((slots // 2, 128, 128), bf16),
            vmem(pair, bf16), vmem(twice, bf16), vmem(mass, f32), vmem(mass, f32),
            vmem((n_dev, 128), i32),
            smem((n_dev, 128), i32),
            vmem((n_dev,) + small.shape, bf16),
            vmem(pair, f32), vmem(twice, f32), vmem(twice, f32), vmem(pair, bf16), vmem(twice, bf16),
            vmem(pair, f32), vmem(twice, f32), vmem(twice, f32),
            vmem((n_dev, 2 * k, 128), bf16),
            vmem((k, k), f32),
        ],
        compiler_params=pltpu.CompilerParams(vmem_limit_bytes=VMEM_LIMIT),
        name="iterate",
    )(where, *smalls, *homes)
    return result.reshape(own, k * bsize)


def rotate(projected, gram):
    lower = jnp.linalg.cholesky(gram)
    inverse = lax.linalg.triangular_solve(
        lower, jnp.eye(gram.shape[0], dtype=jnp.float32), left_side=True, lower=True
    )
    return jnp.einsum(
        "kl,bli->bki",
        inverse,
        projected,
        precision=lax.Precision.HIGHEST,
        preferred_element_type=jnp.float32,
    )


def local_gram(projected):
    return jnp.einsum(
        "bki,bli->kl",
        projected,
        projected,
        precision=lax.Precision.HIGHEST,
        preferred_element_type=jnp.float32,
    )


def split_by_tile(blocks, block_row, block_col, counts, vectors, row_mass, col_mass):
    tile = blocks[0, 0]
    n_cap = tile.shape[0]
    bsize = row_mass.shape[1]
    vecs = vectors.shape[1] // bsize
    own = vectors.shape[0]
    n_row = lax.axis_size("row")
    n_col = lax.axis_size("col")
    row_panel = own * n_col
    col_panel = own * n_row
    total_boxes = float(own * bsize * n_row * n_col)
    rows_idx = block_row[0, 0]
    cols_idx = block_col[0, 0]
    live = jnp.arange(n_cap) < counts[0, 0]
    fwd_ids = jnp.where(live, rows_idx, row_panel)
    bwd_ids = jnp.where(live, cols_idx, col_panel)
    square = tile.reshape(n_cap, bsize, bsize)
    inv_col = 1.0 / jnp.sqrt(col_mass)
    current = vectors.reshape(own, vecs, bsize)
    for step in range(ITERS):
        scaled = (current * inv_col[:, None, :]).astype(jnp.bfloat16).reshape(own, vecs * bsize)
        panel = lax.all_gather(scaled, "row", axis=0, tiled=True)
        forward_taken = jnp.take(panel.reshape(col_panel, vecs, bsize), cols_idx, axis=0)
        forward_product = jnp.einsum(
            "bij,bkj->bki", square, forward_taken, preferred_element_type=jnp.float32
        )
        forward_summed = jax.ops.segment_sum(forward_product, fwd_ids, num_segments=row_panel + 1)
        rows_sum = lax.psum_scatter(
            forward_summed[:row_panel].reshape(row_panel, vecs * bsize),
            "col",
            scatter_dimension=0,
            tiled=True,
        )
        weighted = (rows_sum.reshape(own, vecs, bsize) * row_mass[:, None, :]).astype(jnp.bfloat16)
        whole_rows = lax.all_gather(weighted.reshape(own, vecs * bsize), "col", axis=0, tiled=True)
        taken = jnp.take(whole_rows.reshape(row_panel, vecs, bsize), rows_idx, axis=0)
        product = jnp.einsum("bij,bki->bkj", square, taken, preferred_element_type=jnp.float32)
        summed = jax.ops.segment_sum(product, bwd_ids, num_segments=col_panel + 1)
        cols_sum = lax.psum_scatter(
            summed[:col_panel].reshape(col_panel, vecs * bsize),
            "row",
            scatter_dimension=0,
            tiled=True,
        )
        projected = cols_sum.reshape(own, vecs, bsize) * inv_col[:, None, :]
        gram = lax.psum(local_gram(projected), ("row", "col")) / total_boxes
        current = rotate(projected, gram)
    return current.reshape(own, vecs * bsize)


def fits(n_row, n_col, blocks, vectors, row_mass):
    own, bsize = row_mass.shape[0] // (n_row * n_col), row_mass.shape[1]
    n_cap = blocks.shape[2]
    dense = n_row * (own * n_col * bsize) * (own * n_row * bsize) * 4
    shapes = own * bsize == 128 and vectors.shape[1] == bsize * bsize and n_cap == 128
    return dense <= VMEM_LIMIT // 4 and shapes and n_cap % (16 * n_col) == 0 and n_row == 4 and n_col == 8


def solution(mesh):
    n_row, n_col = mesh.shape["row"], mesh.shape["col"]

    def run(blocks, block_row, block_col, counts, vectors, row_mass, col_mass):
        args = (blocks, block_row, block_col, counts, vectors, row_mass, col_mass)
        if fits(n_row, n_col, blocks, vectors, row_mass):
            devices = mesh.devices.reshape(n_row, n_col // 2, 2)
            grid, col = jax.sharding.Mesh(devices, ("row", "chip", "core")), ("chip", "core")
            body = functools.partial(whole_on_each, n_row, n_col)
        else:
            grid, col, body = mesh, ("col",), split_by_tile
        by_row, by_col = P(("row",) + col, None), P(col + ("row",), None)
        in_specs = (
            P("row", col, None, None), P("row", col, None), P("row", col, None), P("row", col),
            by_col, by_row, by_col,
        )
        return jax.shard_map(
            body, mesh=grid, in_specs=in_specs, out_specs=by_col, check_vma=False
        )(*args)

    return run
```

```python
import functools

import jax
import jax.numpy as jnp
from jax import lax
from jax.experimental import pallas as pl
from jax.experimental.pallas import tpu as pltpu
from jax.sharding import PartitionSpec as P

ITERS = 4
OFF_CAP = 8
META = 16
UNROLL = 16
BATCH = 4
VMEM_LIMIT = 56 * 1024 * 1024

NT = (((1,), (1,)), ((), ()))
NN = (((1,), (0,)), ((), ()))


def dot(a, b, dims=NN):
    return lax.dot_general(a, b, dims, preferred_element_type=jnp.float32)


def split2(x):
    hi = x.astype(jnp.bfloat16)
    return hi, (x - hi.astype(jnp.float32)).astype(jnp.bfloat16)


def inverse_factor(gram):
    n = gram.shape[0]
    rows = lax.broadcasted_iota(jnp.int32, (n, n), 0)
    cols = lax.broadcasted_iota(jnp.int32, (n, n), 1)
    eye = (rows == cols).astype(jnp.float32)
    both = jnp.concatenate([gram, eye], axis=1)
    count, shape = n // 8, (8, 2 * n)
    tiles = [both[8 * t : 8 * t + 8] for t in range(count)]
    sub = lax.broadcasted_iota(jnp.int32, shape, 0)
    out = []
    for b in range(count):
        column = {
            t: [jnp.broadcast_to(tiles[t][:, 8 * b + s : 8 * b + s + 1], shape) for s in range(8)]
            for t in range(b, count)
        }
        row = [jnp.broadcast_to(tiles[b][s : s + 1], shape) for s in range(8)]
        a = [
            [jnp.broadcast_to(column[b][j][s : s + 1], shape) if j >= s else None for j in range(8)]
            for s in range(8)
        ]
        done = jnp.zeros(shape, jnp.float32)
        for s in range(8):
            root = lax.rsqrt(a[s][s])
            inv = root * root
            inv = inv * (2.0 - a[s][s] * inv)
            step = row[s] * inv
            done = jnp.where(sub == s, row[s] * root, done)
            for i in range(s + 1, 8):
                part = a[s][i] * inv
                for j in range(i, 8):
                    a[i][j] = a[i][j] - part * a[s][j]
                row[i] = row[i] - a[s][i] * step
                for t in range(b + 1, count):
                    column[t][i] = column[t][i] - column[t][s] * part
            for t in range(b + 1, count):
                tiles[t] = tiles[t] - column[t][s] * step
        out.append(done)
    return jnp.concatenate(out, axis=0)[:, n:]


def place_of(own, n_row, n_dev):
    here, chip, core = own[0], own[1], own[2]

    def at_device(r, c):
        dr, dc, dk = here ^ r, chip ^ (c // 2), core ^ (c % 2)
        dx, dy = dc & 1, dc >> 1
        order = jnp.where(dr < 2, 2 * dx, 4 + 2 * dy) + jnp.where(
            jnp.where(dr < 2, dy, dx) > 0, n_dev // 4, 0
        )
        return dk * (n_dev // 2) + order + (dr & 1)

    def device_at(d):
        far, second = (d >> 2) & 1, (d >> 3) & 1
        first = (d >> 1) & 1
        dc = jnp.where(far == 0, 2 * second + first, 2 * first + second)
        return here ^ (2 * far + (d & 1)), 2 * (chip ^ dc) + (core ^ (d >> 4))

    return at_device, device_at


def copy_in(pairs, sems):
    copies = [pltpu.make_async_copy(src, dst, sems.at[i]) for i, (src, dst) in enumerate(pairs)]
    for copy in copies:
        copy.start()
    return copies


def left_half(shape):
    return lax.broadcasted_iota(jnp.int32, shape, len(shape) - 1) < 64


def store_twice(pair, twice, q, x):
    pair[q] = x.astype(pair.dtype)
    turned, left = pltpu.roll(x, 64, 1), left_half(x.shape)
    twice[2 * q] = jnp.where(left, x, turned).astype(twice.dtype)
    twice[2 * q + 1] = jnp.where(left, turned, x).astype(twice.dtype)


def gather_pair(q, first, second):
    left = left_half(first.shape[1:])
    apart = jnp.where(left, first[2 * q + 1], second[2 * q])
    return jnp.where(left, first[2 * q], second[2 * q + 1]) + pltpu.roll(apart, 64, 1)


def add_products(n_group, blk, dims, lists, from_at, source, to_at, first, second):
    left = left_half(source.shape[1:])

    def group(i, carry):
        for at in range(0, UNROLL, BATCH):
            pairs = [i * UNROLL + at + u for u in range(BATCH)]
            prods = [
                dot(
                    jnp.where(left, source[lists[from_at + 2 * p]], source[lists[from_at + 2 * p + 1]]),
                    blk[p],
                    dims,
                )
                for p in pairs
            ]
            for p, prod in zip(pairs, prods):
                a, b = lists[to_at + 2 * p], lists[to_at + 2 * p + 1]
                first[a] = first[a] + prod
                second[b] = second[b] + prod
        return carry

    lax.fori_loop(0, n_group, group, 0)


def unpack(
    n_row, n_col, own, mine, other, lists, place, blk, vs, vd, rm, ic, ints, meta, sems, small
):
    n_dev = n_row * n_col
    k = vs.shape[1]
    half = k // 2
    rblk, cblk = 2 * n_col, 2 * n_row
    vec_at = OFF_CAP * half
    meta_at = vec_at + k
    at_device, device_at = place_of(own, n_row, n_dev)
    slots = 2 * blk.shape[0]

    first, second = pl.ds(0, n_dev // 2), pl.ds(n_dev // 2, n_dev // 2)
    for copy in copy_in([(mine, small.at[first]), (other, small.at[second])], sems):
        copy.wait()
    for d in range(n_dev):
        rows = small[d, meta_at : meta_at + META, :].astype(jnp.float32)
        ints[d : d + 1, :] = rows[8:9].astype(jnp.int32)
    to_scalars = pltpu.make_async_copy(ints, meta, sems.at[2])
    to_scalars.start()

    for r in range(n_row):
        for c in range(n_col):
            q, p, d = c * n_row + r, r * n_col + c, at_device(r, c)
            rows = small[d, meta_at : meta_at + META, :].astype(jnp.float32)
            rm[p] = jnp.broadcast_to(rows[0:1] + rows[1:2] + rows[2:3], (8, 128))
            ic[q] = jnp.broadcast_to(rows[3:4] + rows[4:5] + rows[5:6], (8, 128))
            store_twice(vs, vd, q, small[d, vec_at : vec_at + k, :].astype(jnp.float32))
    to_scalars.wait()

    lanes = lax.broadcasted_iota(jnp.int32, (half, 128), 1)

    def device(d, n):
        count = meta[d, 2 * OFF_CAP]
        count = jnp.where(count > OFF_CAP, 0, count)
        r, c = device_at(d)
        for s in range(OFF_CAP):
            lists[n + s] = c * cblk + meta[d, OFF_CAP + s]
            lists[slots + n + s] = r * rblk + meta[d, s]
            x = small[d, s * half : (s + 1) * half, :].astype(jnp.float32)
            turned = pltpu.roll(x, 64, 1)
            side = (n + s) % 2
            here = (lanes // 64) == side
            even = jnp.where(here, jnp.where(side == 0, x, turned), 0.0)
            odd = jnp.where(here, jnp.where(side == 0, turned, x), 0.0)
            at = pl.multiple_of(side * k, k)
            both = jnp.concatenate([even, odd], axis=0).astype(jnp.bfloat16)
            blk[(n + s) // 2, pl.ds(at, k), :] = both
        return n + count

    n_live = lax.fori_loop(0, n_dev, device, jnp.int32(0))
    for u in range(2 * UNROLL - 1):
        lists[n_live + u] = 0
        lists[slots + n_live + u] = 0
        at = pl.multiple_of((n_live + u) % 2 * k, k)
        blk[(n_live + u) // 2, pl.ds(at, k), :] = jnp.zeros((k, 128), jnp.bfloat16)
    lists[2 * slots] = (n_live + 2 * UNROLL - 1) // (2 * UNROLL)

    for r in range(n_row):
        h = jnp.int32(0)
        for c in range(n_col):
            h = jnp.where(meta[at_device(r, c), 2 * OFF_CAP] > OFF_CAP, c, h)
        lists[2 * slots + 1 + r] = h
        index = small[at_device(r, h), meta_at : meta_at + META, :].astype(jnp.float32)
        place[r : r + 1, :] = index[7:8] * float(rblk) + index[6:7]


def iterate(n_row, n_col, n_cap, total, own, lists, place, *rest):
    sources, fulls, out = rest[:5], rest[5:13], rest[13]
    sems, full, tmp, home, blk, vs, vd, rm, ic = rest[14:23]
    w, w1, w2, wt, wd, y, y1, y2, ph, linv = rest[23:]
    slots = 2 * blk.shape[0]
    n_dev = n_row * n_col
    k = vs.shape[1]
    half = k // 2
    rpairs, cpairs = n_col, n_row
    rblk, cblk = 2 * rpairs, 2 * cpairs
    part = n_cap // n_col
    width = cpairs * 128
    at_device, _ = place_of(own, n_row, n_dev)

    def laid_out(refs, whole):
        at, pairs = 0, []
        for ref in refs:
            pairs.append((ref, whole.at[pl.ds(at, ref.shape[0])]))
            at += ref.shape[0]
        return pairs

    copies = copy_in(laid_out(fulls, full) + list(zip(sources, (blk, vs, vd, rm, ic))), sems)
    for copy in copies[: len(fulls)]:
        copy.wait()
    n_group = lists[2 * slots]

    left = lax.broadcasted_iota(jnp.int32, (rblk, 128), 1) < 64
    homes = []
    for r in range(n_row):
        homes.append(lists[2 * slots + 1 + r])
        want = lax.broadcasted_iota(jnp.int32, (cblk * rblk, n_cap), 0).astype(jnp.float32)
        select = jnp.where(want == place[r : r + 1, :], 1.0, 0.0).astype(jnp.bfloat16)

        parts = [at_device(r, 2 * i + j) for j in range(2) for i in range(n_col // 2)]

        def build(m, carry, parts=parts, select=select):
            at = pl.multiple_of(m * part, part)
            slots = jnp.concatenate(
                [full[d, pl.ds(at, part), :] for d in parts], axis=0
            )
            dense = dot(select, slots)
            for u in range(cpairs):
                a = dense[2 * u * rblk : (2 * u + 1) * rblk]
                b = dense[(2 * u + 1) * rblk : (2 * u + 2) * rblk]
                even = jnp.where(left, a, pltpu.roll(b, 64, 1))
                odd = jnp.where(left, pltpu.roll(a, 64, 1), b)
                tmp[u, pl.ds(m, rblk, stride=k), :] = even
                tmp[u, pl.ds(m + half, rblk, stride=k), :] = odd
            return carry

        lax.fori_loop(0, half, build, 0, unroll=8)

        def cut(i, carry, r=r):
            at = pl.multiple_of(i * k, k)
            for u in range(cpairs):
                hi, lo = split2(tmp[u, pl.ds(at, k), :])
                home[r, pl.ds(at, k), u * 128 : (u + 1) * 128] = hi
                home[r, pl.ds(at, k), width + u * 128 : width + (u + 1) * 128] = lo
            return carry

        lax.fori_loop(0, rblk, cut, 0, unroll=8)

    def clear(refs):
        for ref in refs:
            for q in range(ref.shape[0]):
                ref[q] = jnp.zeros_like(ref[q])

    clear([y, y1, y2, w1, w2])
    for copy in copies[len(fulls) :]:
        copy.wait()

    def iteration(it, carry):
        @pl.when(it > 0)
        def _():
            lh, ll = split2(linv[...])
            turn = jnp.concatenate([lh, lh, ll], axis=1)
            for q in range(0, n_dev, 4):
                hi = jnp.concatenate([ph[q + d, :k, :] for d in range(4)], axis=1)
                lo = jnp.concatenate([ph[q + d, k:, :] for d in range(4)], axis=1)
                current = dot(turn, jnp.concatenate([hi, lo, hi], axis=0))
                for d in range(4):
                    x = current[:, d * 128 : (d + 1) * 128] * ic[q + d, 0:1, :]
                    store_twice(vs, vd, q + d, x)

        for r in range(n_row):
            base = homes[r] * cpairs
            vec = jnp.concatenate([vs[base + u] for u in range(cpairs)] * 2, axis=1)
            for p in range(0, rpairs, 2):
                prod = dot(vec, home[r, p * 128 : (p + 2) * 128, :], NT)
                w[r * rpairs + p] = prod[:, :128]
                w[r * rpairs + p + 1] = prod[:, 128:]

        add_products(n_group, blk, NT, lists, 0, vd, slots, w1, w2)
        for p in range(n_dev):
            x = w[p] + gather_pair(p, w1, w2)
            store_twice(wt, wd, p, x * rm[p, 0:1, :])

        for r in range(n_row):
            base = homes[r] * cpairs
            vec = jnp.concatenate([wt[r * rpairs + p] for p in range(rpairs)], axis=1)
            for u in range(0, cpairs, 2):
                cols = slice(u * 128, (u + 2) * 128)
                tail = slice(width + u * 128, width + (u + 2) * 128)
                prod = dot(vec, home[r, :, cols]) + dot(vec, home[r, :, tail])
                y[base + u] = y[base + u] + prod[:, :128]
                y[base + u + 1] = y[base + u + 1] + prod[:, 128:]

        add_products(n_group, blk, NN, lists, slots, wd, 0, y1, y2)

        both = jnp.zeros((2 * k, k), jnp.float32)
        for q in range(0, n_dev, 4):
            his, los = [], []
            for d in range(q, q + 4):
                x = y[d] + gather_pair(d, y1, y2)
                hi, lo = split2(x * ic[d, 0:1, :])
                ph[d, :k, :] = hi
                ph[d, k:, :] = lo
                his.append(hi)
                los.append(lo)
            hi = jnp.concatenate(his, axis=1)
            lo = jnp.concatenate(los, axis=1)
            both = both + dot(jnp.concatenate([hi, lo], axis=0), hi, NT)
        gram = (both[:k] + (both[k:] + both[k:].T)) / total
        clear([y, y1, y2, w1, w2])
        linv[...] = inverse_factor(gram)
        return carry

    lax.fori_loop(0, ITERS, iteration, 0)
    lh, ll = split2(linv[...])
    q = (2 * own[1] + own[2]) * n_row + own[0]
    hi, lo = ph[q, :k, :], ph[q, k:, :]
    w[0] = dot(lh, hi) + dot(ll, hi) + dot(lh, lo)
    even, odd = w[0, pl.ds(0, half, stride=2), :], w[0, pl.ds(1, half, stride=2), :]
    left = left_half(even.shape)
    first = jnp.where(left, even, pltpu.roll(odd, 64, 1))
    second = jnp.where(left, pltpu.roll(even, 64, 1), odd)
    for i in range(half):
        out[0:1, i * 128 : (i + 1) * 128] = first[i : i + 1]
        out[1:2, i * 128 : (i + 1) * 128] = second[i : i + 1]


def split3(x):
    a = lax.reduce_precision(x, 8, 7)
    b = lax.reduce_precision(x - a, 8, 7)
    return [v.astype(jnp.bfloat16) for v in (a, b, x - a - b)]


def swap(x, axis, distance):
    size = lax.axis_size(axis)
    return lax.ppermute(x, axis, [(i, i ^ distance) for i in range(size)])


def along_rows(x):
    return [x] + [swap(x, "row", s) for s in range(1, lax.axis_size("row"))]


def along_one_chip_axis(x):
    near, far = jnp.stack(x[:2]), jnp.stack(x[2:])
    return [
        jnp.concatenate([near, swap(near, "chip", 1)]),
        jnp.concatenate([far, swap(far, "chip", 2)]),
    ]


def along_other_chip_axis(x):
    near, far = x
    return [swap(near, "chip", 2), swap(far, "chip", 1)]


def full_part(tile, has_full, n_chip, part, chip, core):
    tile = tile.reshape(2, n_chip, part, tile.shape[1])
    none = jnp.zeros(tile.shape[1:], tile.dtype)
    kept, sent = (
        jnp.where(has_full, lax.dynamic_index_in_dim(tile, i, 0, False), none)
        for i in (core, 1 - core)
    )
    both = kept + swap(sent, "core", 1)
    mine = lax.dynamic_index_in_dim(both, chip, 0, False)
    for s in range(1, n_chip):
        mine = mine + swap(lax.dynamic_index_in_dim(both, chip ^ s, 0, False), "chip", s)
    return mine


def whole_on_each(n_row, n_col, blocks, block_row, block_col, counts, vectors, row_mass, col_mass):
    tile = blocks[0, 0]
    n_cap = tile.shape[0]
    own, bsize = row_mass.shape
    k = vectors.shape[1] // bsize
    half = bsize // 2
    part = n_cap // n_col
    n_dev = n_row * n_col
    count = counts[0, 0]
    has_full = count > OFF_CAP
    bf16 = jnp.bfloat16
    row, chip, core = (lax.axis_index(name) for name in ("row", "chip", "core"))

    off = tile[:OFF_CAP].reshape(OFF_CAP * half, 128)
    inv_col = 1.0 / jnp.sqrt(col_mass)
    scaled = (vectors.reshape(own, k, bsize) * inv_col[:, None, :]).astype(bf16)
    scaled = scaled.transpose(1, 0, 2).reshape(k, own * bsize)
    mass = row_mass.reshape(own, half, 2).transpose(0, 2, 1).reshape(own * bsize)
    rows, cols = block_row[0, 0], block_col[0, 0]
    short = jnp.concatenate(
        [rows[:OFF_CAP], cols[:OFF_CAP], count[None], jnp.zeros(128 - 2 * OFF_CAP - 1, jnp.int32)]
    )
    meta = [v.astype(bf16) for v in (rows, cols, short)]
    meta = split3(mass) + split3(inv_col.reshape(own * bsize)) + meta
    meta = jnp.stack(meta + [jnp.zeros(128, bf16)] * (META - len(meta)))
    small = jnp.concatenate([off, scaled, meta], axis=0)
    home = full_part(tile, has_full, n_col // 2, part, chip, core)
    home = home.reshape(part, half, 128).transpose(1, 0, 2).reshape(half * part, 128)

    together = lax.optimization_barrier
    home, smalls = together((home, along_rows(small)))
    homes, smalls = along_rows(home), along_one_chip_axis(smalls)
    smalls, homes[1] = together((smalls, homes[1]))
    smalls = jnp.concatenate(smalls + along_other_chip_axis(smalls))
    homes, smalls = together((homes, smalls))
    homes, others = together((along_one_chip_axis(homes), swap(smalls, "core", 1)))
    last = along_other_chip_axis(homes)

    where = jnp.stack([row, chip, core]).astype(jnp.int32)
    height, width = 2 * n_col * bsize, 2 * n_row * bsize
    slots = n_dev * OFF_CAP + 2 * UNROLL
    f32, i32, vmem, smem = jnp.float32, jnp.int32, pltpu.VMEM, pltpu.SMEM
    pair, twice, mass = (n_dev, k, 128), (2 * n_dev, k, 128), (n_dev, 8, 128)
    smem_spec, vmem_spec, any_spec = (pl.BlockSpec(memory_space=m) for m in (smem, vmem, pl.ANY))
    arrays = [
        ((8, 128), f32), ((slots // 2, 128, 128), bf16), (pair, bf16), (twice, bf16), (mass, f32), (mass, f32),
    ]
    lists, *unpacked = pl.pallas_call(
        functools.partial(unpack, n_row, n_col),
        out_shape=[jax.ShapeDtypeStruct((2 * slots + 8,), i32)]
        + [jax.ShapeDtypeStruct(*v) for v in arrays],
        in_specs=[smem_spec, any_spec, any_spec],
        out_specs=[smem_spec] + [vmem_spec] * len(arrays),
        scratch_shapes=[
            vmem((n_dev, 128), i32),
            smem((n_dev, 128), i32),
            pltpu.SemaphoreType.DMA((3,)),
            vmem((n_dev,) + small.shape, bf16),
        ],
        compiler_params=pltpu.CompilerParams(vmem_limit_bytes=VMEM_LIMIT),
        cost_estimate=pl.CostEstimate(
            flops=0, bytes_accessed=4 * n_dev * small.size * 2, transcendentals=0
        ),
        name="unpack",
    )(where, smalls, others)
    last, lists = together((last, lists))
    mine = homes + last
    fulls = mine + [swap(v, "core", 1) for v in mine]
    return pl.pallas_call(
        functools.partial(iterate, n_row, n_col, n_cap, float(n_dev * own * bsize)),
        out_shape=jax.ShapeDtypeStruct((own, k * bsize), f32),
        in_specs=[smem_spec] * 2 + [vmem_spec] + [any_spec] * (5 + len(fulls)),
        out_specs=vmem_spec,
        scratch_shapes=[
            pltpu.SemaphoreType.DMA((5 + len(fulls),)),
            vmem((n_dev,) + home.shape, bf16),
            vmem((n_row, height, 128), f32),
            vmem((n_row, height, 2 * width), bf16),
            *[vmem(*v) for v in arrays[1:]],
            vmem(pair, f32), vmem(twice, f32), vmem(twice, f32), vmem(pair, bf16), vmem(twice, bf16),
            vmem(pair, f32), vmem(twice, f32), vmem(twice, f32),
            vmem((n_dev, 2 * k, 128), bf16),
            vmem((k, k), f32),
        ],
        compiler_params=pltpu.CompilerParams(vmem_limit_bytes=VMEM_LIMIT),
        name="iterate",
    )(where, lists, *unpacked, *fulls)


def rotate(projected, gram):
    lower = jnp.linalg.cholesky(gram)
    inverse = lax.linalg.triangular_solve(
        lower, jnp.eye(gram.shape[0], dtype=jnp.float32), left_side=True, lower=True
    )
    return jnp.einsum(
        "kl,bli->bki",
        inverse,
        projected,
        precision=lax.Precision.HIGHEST,
        preferred_element_type=jnp.float32,
    )


def local_gram(projected):
    return jnp.einsum(
        "bki,bli->kl",
        projected,
        projected,
        precision=lax.Precision.HIGHEST,
        preferred_element_type=jnp.float32,
    )


def split_by_tile(blocks, block_row, block_col, counts, vectors, row_mass, col_mass):
    tile = blocks[0, 0]
    n_cap = tile.shape[0]
    bsize = row_mass.shape[1]
    vecs = vectors.shape[1] // bsize
    own = vectors.shape[0]
    n_row = lax.axis_size("row")
    n_col = lax.axis_size("col")
    row_panel = own * n_col
    col_panel = own * n_row
    total_boxes = float(own * bsize * n_row * n_col)
    rows_idx = block_row[0, 0]
    cols_idx = block_col[0, 0]
    live = jnp.arange(n_cap) < counts[0, 0]
    fwd_ids = jnp.where(live, rows_idx, row_panel)
    bwd_ids = jnp.where(live, cols_idx, col_panel)
    square = tile.reshape(n_cap, bsize, bsize)
    inv_col = 1.0 / jnp.sqrt(col_mass)
    current = vectors.reshape(own, vecs, bsize)
    for step in range(ITERS):
        scaled = (current * inv_col[:, None, :]).astype(jnp.bfloat16).reshape(own, vecs * bsize)
        panel = lax.all_gather(scaled, "row", axis=0, tiled=True)
        forward_taken = jnp.take(panel.reshape(col_panel, vecs, bsize), cols_idx, axis=0)
        forward_product = jnp.einsum(
            "bij,bkj->bki", square, forward_taken, preferred_element_type=jnp.float32
        )
        forward_summed = jax.ops.segment_sum(forward_product, fwd_ids, num_segments=row_panel + 1)
        rows_sum = lax.psum_scatter(
            forward_summed[:row_panel].reshape(row_panel, vecs * bsize),
            "col",
            scatter_dimension=0,
            tiled=True,
        )
        weighted = (rows_sum.reshape(own, vecs, bsize) * row_mass[:, None, :]).astype(jnp.bfloat16)
        whole_rows = lax.all_gather(weighted.reshape(own, vecs * bsize), "col", axis=0, tiled=True)
        taken = jnp.take(whole_rows.reshape(row_panel, vecs, bsize), rows_idx, axis=0)
        product = jnp.einsum("bij,bki->bkj", square, taken, preferred_element_type=jnp.float32)
        summed = jax.ops.segment_sum(product, bwd_ids, num_segments=col_panel + 1)
        cols_sum = lax.psum_scatter(
            summed[:col_panel].reshape(col_panel, vecs * bsize),
            "row",
            scatter_dimension=0,
            tiled=True,
        )
        projected = cols_sum.reshape(own, vecs, bsize) * inv_col[:, None, :]
        gram = lax.psum(local_gram(projected), ("row", "col")) / total_boxes
        current = rotate(projected, gram)
    return current.reshape(own, vecs * bsize)


def fits(n_row, n_col, blocks, vectors, row_mass):
    own, bsize = row_mass.shape[0] // (n_row * n_col), row_mass.shape[1]
    n_cap = blocks.shape[2]
    dense = n_row * (own * n_col * bsize) * (own * n_row * bsize) * 4
    shapes = own * bsize == 128 and vectors.shape[1] == bsize * bsize and n_cap == 128
    return dense <= VMEM_LIMIT // 4 and shapes and n_cap % (16 * n_col) == 0 and n_row == 4 and n_col == 8


def solution(mesh):
    n_row, n_col = mesh.shape["row"], mesh.shape["col"]

    def run(blocks, block_row, block_col, counts, vectors, row_mass, col_mass):
        args = (blocks, block_row, block_col, counts, vectors, row_mass, col_mass)
        if fits(n_row, n_col, blocks, vectors, row_mass):
            devices = mesh.devices.reshape(n_row, n_col // 2, 2)
            grid, col = jax.sharding.Mesh(devices, ("row", "chip", "core")), ("chip", "core")
            body = functools.partial(whole_on_each, n_row, n_col)
        else:
            grid, col, body = mesh, ("col",), split_by_tile
        by_row, by_col = P(("row",) + col, None), P(col + ("row",), None)
        in_specs = (
            P("row", col, None, None), P("row", col, None), P("row", col, None), P("row", col),
            by_col, by_row, by_col,
        )
        return jax.shard_map(
            body, mesh=grid, in_specs=in_specs, out_specs=by_col, check_vma=False
        )(*args)

    return run
```

```python
import functools

import jax
import jax.numpy as jnp
from jax import lax
from jax.experimental import pallas as pl
from jax.experimental.pallas import tpu as pltpu
from jax.sharding import PartitionSpec as P

ITERS = 4
OFF_CAP = 8
META = 16
UNROLL = 16
BATCH = 4
VMEM_LIMIT = 56 * 1024 * 1024

NT = (((1,), (1,)), ((), ()))
NN = (((1,), (0,)), ((), ()))


def dot(a, b, dims=NN):
    return lax.dot_general(a, b, dims, preferred_element_type=jnp.float32)


def split2(x):
    hi = x.astype(jnp.bfloat16)
    return hi, (x - hi.astype(jnp.float32)).astype(jnp.bfloat16)


def inverse_factor(gram):
    n = gram.shape[0]
    rows = lax.broadcasted_iota(jnp.int32, (n, n), 0)
    cols = lax.broadcasted_iota(jnp.int32, (n, n), 1)
    eye = (rows == cols).astype(jnp.float32)
    both = jnp.concatenate([gram, eye], axis=1)
    count, shape = n // 8, (8, 2 * n)
    tiles = [both[8 * t : 8 * t + 8] for t in range(count)]
    sub = lax.broadcasted_iota(jnp.int32, shape, 0)
    out = []
    for b in range(count):
        column = {
            t: [jnp.broadcast_to(tiles[t][:, 8 * b + s : 8 * b + s + 1], shape) for s in range(8)]
            for t in range(b, count)
        }
        row = [jnp.broadcast_to(tiles[b][s : s + 1], shape) for s in range(8)]
        a = [
            [jnp.broadcast_to(column[b][j][s : s + 1], shape) if j >= s else None for j in range(8)]
            for s in range(8)
        ]
        done = jnp.zeros(shape, jnp.float32)
        for s in range(8):
            root = lax.rsqrt(a[s][s])
            inv = root * root
            inv = inv * (2.0 - a[s][s] * inv)
            step = row[s] * inv
            done = jnp.where(sub == s, row[s] * root, done)
            for i in range(s + 1, 8):
                part = a[s][i] * inv
                for j in range(i, 8):
                    a[i][j] = a[i][j] - part * a[s][j]
                row[i] = row[i] - a[s][i] * step
                for t in range(b + 1, count):
                    column[t][i] = column[t][i] - column[t][s] * part
            for t in range(b + 1, count):
                tiles[t] = tiles[t] - column[t][s] * step
        out.append(done)
    return jnp.concatenate(out, axis=0)[:, n:]


def place_of(own, n_row, n_dev):
    chip, core = own[0], own[1]

    def at_device(r, c):
        dc, dk = chip ^ (c // 2), core ^ (c % 2)
        dx, dy = dc & 1, dc >> 1
        first, second = (dx, dy) if r < 2 else (dy, dx)
        return dk * (n_dev // 2) + second * (n_dev // 4) + r // 2 * (n_dev // 8) + first * 2 + r % 2

    def device_at(d):
        far, first, second = (d >> 2) & 1, (d >> 1) & 1, (d >> 3) & 1
        dc = jnp.where(far == 0, 2 * second + first, 2 * first + second)
        return 2 * far + (d & 1), 2 * (chip ^ dc) + (core ^ (d >> 4))

    return at_device, device_at


def copy_in(pairs, sems):
    copies = [pltpu.make_async_copy(src, dst, sems.at[i]) for i, (src, dst) in enumerate(pairs)]
    for copy in copies:
        copy.start()
    return copies


def left_half(shape):
    return lax.broadcasted_iota(jnp.int32, shape, len(shape) - 1) < 64


def store_twice(pair, twice, q, x):
    pair[q] = x.astype(pair.dtype)
    turned, left = pltpu.roll(x, 64, 1), left_half(x.shape)
    twice[2 * q] = jnp.where(left, x, turned).astype(twice.dtype)
    twice[2 * q + 1] = jnp.where(left, turned, x).astype(twice.dtype)


def gather_pair(q, first, second):
    left = left_half(first.shape[1:])
    apart = jnp.where(left, first[2 * q + 1], second[2 * q])
    return jnp.where(left, first[2 * q], second[2 * q + 1]) + pltpu.roll(apart, 64, 1)


def add_products(n_group, blk, dims, lists, from_at, source, to_at, first, second):
    left = left_half(source.shape[1:])

    def group(i, carry):
        for at in range(0, UNROLL, BATCH):
            pairs = [i * UNROLL + at + u for u in range(BATCH)]
            prods = [
                dot(
                    jnp.where(left, source[lists[from_at + 2 * p]], source[lists[from_at + 2 * p + 1]]),
                    blk[p],
                    dims,
                )
                for p in pairs
            ]
            for p, prod in zip(pairs, prods):
                a, b = lists[to_at + 2 * p], lists[to_at + 2 * p + 1]
                first[a] = first[a] + prod
                second[b] = second[b] + prod
        return carry

    lax.fori_loop(0, n_group, group, 0)


def unpack(
    n_row, n_col, own, mine, other, lists, place, blk, vs, vd, rm, ic, ints, meta, sems, small
):
    n_dev = n_row * n_col
    k = vs.shape[1]
    half = k // 2
    rblk, cblk = 2 * n_col, 2 * n_row
    vec_at = OFF_CAP * half
    meta_at = vec_at + k
    at_device, device_at = place_of(own, n_row, n_dev)
    slots = 2 * blk.shape[0]

    first, second = pl.ds(0, n_dev // 2), pl.ds(n_dev // 2, n_dev // 2)
    for copy in copy_in([(mine, small.at[first]), (other, small.at[second])], sems):
        copy.wait()
    for d in range(n_dev):
        rows = small[d, meta_at : meta_at + META, :].astype(jnp.float32)
        ints[d : d + 1, :] = rows[8:9].astype(jnp.int32)
    to_scalars = pltpu.make_async_copy(ints, meta, sems.at[2])
    to_scalars.start()

    for r in range(n_row):
        for c in range(n_col):
            q, p, d = c * n_row + r, r * n_col + c, at_device(r, c)
            rows = small[d, meta_at : meta_at + META, :].astype(jnp.float32)
            rm[p] = jnp.broadcast_to(rows[0:1] + rows[1:2] + rows[2:3], (8, 128))
            ic[q] = jnp.broadcast_to(rows[3:4] + rows[4:5] + rows[5:6], (8, 128))
            store_twice(vs, vd, q, small[d, vec_at : vec_at + k, :].astype(jnp.float32))
    to_scalars.wait()

    lanes = lax.broadcasted_iota(jnp.int32, (half, 128), 1)

    def device(d, n):
        count = meta[d, 2 * OFF_CAP]
        count = jnp.where(count > OFF_CAP, 0, count)
        r, c = device_at(d)
        for s in range(OFF_CAP):
            lists[n + s] = c * cblk + meta[d, OFF_CAP + s]
            lists[slots + n + s] = r * rblk + meta[d, s]
            x = small[d, s * half : (s + 1) * half, :].astype(jnp.float32)
            turned = pltpu.roll(x, 64, 1)
            side = (n + s) % 2
            here = (lanes // 64) == side
            even = jnp.where(here, jnp.where(side == 0, x, turned), 0.0)
            odd = jnp.where(here, jnp.where(side == 0, turned, x), 0.0)
            at = pl.multiple_of(side * k, k)
            both = jnp.concatenate([even, odd], axis=0).astype(jnp.bfloat16)
            blk[(n + s) // 2, pl.ds(at, k), :] = both
        return n + count

    n_live = lax.fori_loop(0, n_dev, device, jnp.int32(0))
    for u in range(2 * UNROLL - 1):
        lists[n_live + u] = 0
        lists[slots + n_live + u] = 0
        at = pl.multiple_of((n_live + u) % 2 * k, k)
        blk[(n_live + u) // 2, pl.ds(at, k), :] = jnp.zeros((k, 128), jnp.bfloat16)
    lists[2 * slots] = (n_live + 2 * UNROLL - 1) // (2 * UNROLL)

    for r in range(n_row):
        h = jnp.int32(0)
        for c in range(n_col):
            h = jnp.where(meta[at_device(r, c), 2 * OFF_CAP] > OFF_CAP, c, h)
        lists[2 * slots + 1 + r] = h
        index = small[at_device(r, h), meta_at : meta_at + META, :].astype(jnp.float32)
        place[r : r + 1, :] = index[7:8] * float(rblk) + index[6:7]


def iterate(n_row, n_col, n_cap, total, own, lists, place, *rest):
    sources, fulls, out = rest[:5], rest[5:13], rest[13]
    sems, full, tmp, home, blk, vs, vd, rm, ic = rest[14:23]
    w, w1, w2, wt, wd, y, y1, y2, ph, linv = rest[23:]
    slots = 2 * blk.shape[0]
    n_dev = n_row * n_col
    k = vs.shape[1]
    half = k // 2
    rpairs, cpairs = n_col, n_row
    rblk, cblk = 2 * rpairs, 2 * cpairs
    part = n_cap // n_col
    width = cpairs * 128
    at_device, _ = place_of(own, n_row, n_dev)

    def laid_out(refs, whole):
        at, pairs = 0, []
        for ref in refs:
            pairs.append((ref, whole.at[pl.ds(at, ref.shape[0])]))
            at += ref.shape[0]
        return pairs

    copies = copy_in(laid_out(fulls, full) + list(zip(sources, (blk, vs, vd, rm, ic))), sems)
    for copy in copies[: len(fulls)]:
        copy.wait()
    n_group = lists[2 * slots]

    left = lax.broadcasted_iota(jnp.int32, (rblk, 128), 1) < 64
    homes = []
    for r in range(n_row):
        homes.append(lists[2 * slots + 1 + r])
        want = lax.broadcasted_iota(jnp.int32, (cblk * rblk, n_cap), 0).astype(jnp.float32)
        select = jnp.where(want == place[r : r + 1, :], 1.0, 0.0).astype(jnp.bfloat16)

        parts = [at_device(r, 2 * i + j) for j in range(2) for i in range(n_col // 2)]

        def build(m, carry, parts=parts, select=select):
            at = pl.multiple_of(m * part, part)
            slots = jnp.concatenate(
                [full[d, pl.ds(at, part), :] for d in parts], axis=0
            )
            dense = dot(select, slots)
            for u in range(cpairs):
                a = dense[2 * u * rblk : (2 * u + 1) * rblk]
                b = dense[(2 * u + 1) * rblk : (2 * u + 2) * rblk]
                even = jnp.where(left, a, pltpu.roll(b, 64, 1))
                odd = jnp.where(left, pltpu.roll(a, 64, 1), b)
                tmp[u, pl.ds(m, rblk, stride=k), :] = even
                tmp[u, pl.ds(m + half, rblk, stride=k), :] = odd
            return carry

        lax.fori_loop(0, half, build, 0, unroll=8)

        def cut(i, carry, r=r):
            at = pl.multiple_of(i * k, k)
            for u in range(cpairs):
                hi, lo = split2(tmp[u, pl.ds(at, k), :])
                home[r, pl.ds(at, k), u * 128 : (u + 1) * 128] = hi
                home[r, pl.ds(at, k), width + u * 128 : width + (u + 1) * 128] = lo
            return carry

        lax.fori_loop(0, rblk, cut, 0, unroll=8)

    def clear(refs):
        for ref in refs:
            for q in range(ref.shape[0]):
                ref[q] = jnp.zeros_like(ref[q])

    clear([y, y1, y2, w1, w2])
    for copy in copies[len(fulls) :]:
        copy.wait()

    def iteration(it, carry):
        @pl.when(it > 0)
        def _():
            lh, ll = split2(linv[...])
            turn = jnp.concatenate([lh, lh, ll], axis=1)
            for q in range(0, n_dev, 4):
                hi = jnp.concatenate([ph[q + d, :k, :] for d in range(4)], axis=1)
                lo = jnp.concatenate([ph[q + d, k:, :] for d in range(4)], axis=1)
                current = dot(turn, jnp.concatenate([hi, lo, hi], axis=0))
                for d in range(4):
                    x = current[:, d * 128 : (d + 1) * 128] * ic[q + d, 0:1, :]
                    store_twice(vs, vd, q + d, x)

        for r in range(n_row):
            base = homes[r] * cpairs
            vec = jnp.concatenate([vs[base + u] for u in range(cpairs)] * 2, axis=1)
            for p in range(0, rpairs, 2):
                prod = dot(vec, home[r, p * 128 : (p + 2) * 128, :], NT)
                w[r * rpairs + p] = prod[:, :128]
                w[r * rpairs + p + 1] = prod[:, 128:]

        add_products(n_group, blk, NT, lists, 0, vd, slots, w1, w2)
        for p in range(n_dev):
            x = w[p] + gather_pair(p, w1, w2)
            store_twice(wt, wd, p, x * rm[p, 0:1, :])

        for r in range(n_row):
            base = homes[r] * cpairs
            vec = jnp.concatenate([wt[r * rpairs + p] for p in range(rpairs)], axis=1)
            for u in range(0, cpairs, 2):
                cols = slice(u * 128, (u + 2) * 128)
                tail = slice(width + u * 128, width + (u + 2) * 128)
                prod = dot(vec, home[r, :, cols]) + dot(vec, home[r, :, tail])
                y[base + u] = y[base + u] + prod[:, :128]
                y[base + u + 1] = y[base + u + 1] + prod[:, 128:]

        add_products(n_group, blk, NN, lists, slots, wd, 0, y1, y2)

        both = jnp.zeros((2 * k, k), jnp.float32)
        for q in range(0, n_dev, 4):
            his, los = [], []
            for d in range(q, q + 4):
                x = y[d] + gather_pair(d, y1, y2)
                hi, lo = split2(x * ic[d, 0:1, :])
                ph[d, :k, :] = hi
                ph[d, k:, :] = lo
                his.append(hi)
                los.append(lo)
            hi = jnp.concatenate(his, axis=1)
            lo = jnp.concatenate(los, axis=1)
            both = both + dot(jnp.concatenate([hi, lo], axis=0), hi, NT)
        gram = (both[:k] + (both[k:] + both[k:].T)) / total
        clear([y, y1, y2, w1, w2])
        linv[...] = inverse_factor(gram)
        return carry

    lax.fori_loop(0, ITERS, iteration, 0)
    lh, ll = split2(linv[...])
    q = (2 * own[0] + own[1]) * n_row + own[2]
    hi, lo = ph[q, :k, :], ph[q, k:, :]
    w[0] = dot(lh, hi) + dot(ll, hi) + dot(lh, lo)
    even, odd = w[0, pl.ds(0, half, stride=2), :], w[0, pl.ds(1, half, stride=2), :]
    left = left_half(even.shape)
    first = jnp.where(left, even, pltpu.roll(odd, 64, 1))
    second = jnp.where(left, pltpu.roll(even, 64, 1), odd)
    for i in range(half):
        out[0:1, i * 128 : (i + 1) * 128] = first[i : i + 1]
        out[1:2, i * 128 : (i + 1) * 128] = second[i : i + 1]


def split3(x):
    a = lax.reduce_precision(x, 8, 7)
    b = lax.reduce_precision(x - a, 8, 7)
    return [v.astype(jnp.bfloat16) for v in (a, b, x - a - b)]


def swap(x, axis, distance):
    size = lax.axis_size(axis)
    return lax.ppermute(x, axis, [(i, i ^ distance) for i in range(size)])


def along_rows(x):
    sent = jnp.broadcast_to(x, (lax.axis_size("row"), *x.shape))
    return lax.all_to_all(sent, "row", split_axis=0, concat_axis=0)


def along_one_chip_axis(x):
    near, far = jnp.split(x, 2)
    return [
        jnp.concatenate([near, swap(near, "chip", 1)]),
        jnp.concatenate([far, swap(far, "chip", 2)]),
    ]


def along_other_chip_axis(x):
    near, far = x
    return [swap(near, "chip", 2), swap(far, "chip", 1)]


def full_part(tile, has_full, n_chip, part, core):
    tile = tile.reshape(2, n_chip, part, tile.shape[1])
    none = jnp.zeros(tile.shape[1:], tile.dtype)
    kept, sent = (
        jnp.where(has_full, lax.dynamic_index_in_dim(tile, i, 0, False), none)
        for i in (core, 1 - core)
    )
    both = kept + swap(sent, "core", 1)
    parts = lax.all_to_all(both, "chip", split_axis=0, concat_axis=0)
    return jnp.sum(parts.astype(jnp.float32), axis=0).astype(tile.dtype)


def whole_on_each(n_row, n_col, blocks, block_row, block_col, counts, vectors, row_mass, col_mass):
    tile = blocks[0, 0]
    n_cap = tile.shape[0]
    own, bsize = row_mass.shape
    k = vectors.shape[1] // bsize
    half = bsize // 2
    part = n_cap // n_col
    n_dev = n_row * n_col
    count = counts[0, 0]
    has_full = count > OFF_CAP
    bf16 = jnp.bfloat16
    row, chip, core = (lax.axis_index(name) for name in ("row", "chip", "core"))

    off = tile[:OFF_CAP].reshape(OFF_CAP * half, 128)
    inv_col = 1.0 / jnp.sqrt(col_mass)
    scaled = (vectors.reshape(own, k, bsize) * inv_col[:, None, :]).astype(bf16)
    scaled = scaled.transpose(1, 0, 2).reshape(k, own * bsize)
    mass = row_mass.reshape(own, half, 2).transpose(0, 2, 1).reshape(own * bsize)
    rows, cols = block_row[0, 0], block_col[0, 0]
    short = jnp.concatenate(
        [rows[:OFF_CAP], cols[:OFF_CAP], count[None], jnp.zeros(128 - 2 * OFF_CAP - 1, jnp.int32)]
    )
    meta = [v.astype(bf16) for v in (rows, cols, short)]
    meta = split3(mass) + split3(inv_col.reshape(own * bsize)) + meta
    meta = jnp.stack(meta + [jnp.zeros(128, bf16)] * (META - len(meta)))
    small = jnp.concatenate([off, scaled, meta], axis=0)
    home = full_part(tile, has_full, n_col // 2, part, core)
    home = home.reshape(part, half, 128).transpose(1, 0, 2).reshape(half * part, 128)

    together = lax.optimization_barrier
    home, smalls = together((home, along_rows(small)))
    homes, smalls = together((along_rows(home), along_one_chip_axis(smalls)))
    smalls = jnp.concatenate(smalls + along_other_chip_axis(smalls))
    homes, others = together((along_one_chip_axis(homes), swap(smalls, "core", 1)))
    last = along_other_chip_axis(homes)

    where = jnp.stack([chip, core, row]).astype(jnp.int32)
    height, width = 2 * n_col * bsize, 2 * n_row * bsize
    slots = n_dev * OFF_CAP + 2 * UNROLL
    f32, i32, vmem, smem = jnp.float32, jnp.int32, pltpu.VMEM, pltpu.SMEM
    pair, twice, mass = (n_dev, k, 128), (2 * n_dev, k, 128), (n_dev, 8, 128)
    smem_spec, vmem_spec, any_spec = (pl.BlockSpec(memory_space=m) for m in (smem, vmem, pl.ANY))
    arrays = [
        ((8, 128), f32), ((slots // 2, 128, 128), bf16), (pair, bf16), (twice, bf16), (mass, f32), (mass, f32),
    ]
    lists, *unpacked = pl.pallas_call(
        functools.partial(unpack, n_row, n_col),
        out_shape=[jax.ShapeDtypeStruct((2 * slots + 8,), i32)]
        + [jax.ShapeDtypeStruct(*v) for v in arrays],
        in_specs=[smem_spec, any_spec, any_spec],
        out_specs=[smem_spec] + [vmem_spec] * len(arrays),
        scratch_shapes=[
            vmem((n_dev, 128), i32),
            smem((n_dev, 128), i32),
            pltpu.SemaphoreType.DMA((3,)),
            vmem((n_dev,) + small.shape, bf16),
        ],
        compiler_params=pltpu.CompilerParams(vmem_limit_bytes=VMEM_LIMIT),
        cost_estimate=pl.CostEstimate(
            flops=0, bytes_accessed=4 * n_dev * small.size * 2, transcendentals=0
        ),
        name="unpack",
    )(where, smalls, others)
    last, lists = together((last, lists))
    mine = homes + last
    fulls = mine + [swap(v, "core", 1) for v in mine]
    return pl.pallas_call(
        functools.partial(iterate, n_row, n_col, n_cap, float(n_dev * own * bsize)),
        out_shape=jax.ShapeDtypeStruct((own, k * bsize), f32),
        in_specs=[smem_spec] * 2 + [vmem_spec] + [any_spec] * (5 + len(fulls)),
        out_specs=vmem_spec,
        scratch_shapes=[
            pltpu.SemaphoreType.DMA((5 + len(fulls),)),
            vmem((n_dev,) + home.shape, bf16),
            vmem((n_row, height, 128), f32),
            vmem((n_row, height, 2 * width), bf16),
            *[vmem(*v) for v in arrays[1:]],
            vmem(pair, f32), vmem(twice, f32), vmem(twice, f32), vmem(pair, bf16), vmem(twice, bf16),
            vmem(pair, f32), vmem(twice, f32), vmem(twice, f32),
            vmem((n_dev, 2 * k, 128), bf16),
            vmem((k, k), f32),
        ],
        compiler_params=pltpu.CompilerParams(vmem_limit_bytes=VMEM_LIMIT),
        name="iterate",
    )(where, lists, *unpacked, *fulls)


def rotate(projected, gram):
    lower = jnp.linalg.cholesky(gram)
    inverse = lax.linalg.triangular_solve(
        lower, jnp.eye(gram.shape[0], dtype=jnp.float32), left_side=True, lower=True
    )
    return jnp.einsum(
        "kl,bli->bki",
        inverse,
        projected,
        precision=lax.Precision.HIGHEST,
        preferred_element_type=jnp.float32,
    )


def local_gram(projected):
    return jnp.einsum(
        "bki,bli->kl",
        projected,
        projected,
        precision=lax.Precision.HIGHEST,
        preferred_element_type=jnp.float32,
    )


def split_by_tile(blocks, block_row, block_col, counts, vectors, row_mass, col_mass):
    tile = blocks[0, 0]
    n_cap = tile.shape[0]
    bsize = row_mass.shape[1]
    vecs = vectors.shape[1] // bsize
    own = vectors.shape[0]
    n_row = lax.axis_size("row")
    n_col = lax.axis_size("col")
    row_panel = own * n_col
    col_panel = own * n_row
    total_boxes = float(own * bsize * n_row * n_col)
    rows_idx = block_row[0, 0]
    cols_idx = block_col[0, 0]
    live = jnp.arange(n_cap) < counts[0, 0]
    fwd_ids = jnp.where(live, rows_idx, row_panel)
    bwd_ids = jnp.where(live, cols_idx, col_panel)
    square = tile.reshape(n_cap, bsize, bsize)
    inv_col = 1.0 / jnp.sqrt(col_mass)
    current = vectors.reshape(own, vecs, bsize)
    for step in range(ITERS):
        scaled = (current * inv_col[:, None, :]).astype(jnp.bfloat16).reshape(own, vecs * bsize)
        panel = lax.all_gather(scaled, "row", axis=0, tiled=True)
        forward_taken = jnp.take(panel.reshape(col_panel, vecs, bsize), cols_idx, axis=0)
        forward_product = jnp.einsum(
            "bij,bkj->bki", square, forward_taken, preferred_element_type=jnp.float32
        )
        forward_summed = jax.ops.segment_sum(forward_product, fwd_ids, num_segments=row_panel + 1)
        rows_sum = lax.psum_scatter(
            forward_summed[:row_panel].reshape(row_panel, vecs * bsize),
            "col",
            scatter_dimension=0,
            tiled=True,
        )
        weighted = (rows_sum.reshape(own, vecs, bsize) * row_mass[:, None, :]).astype(jnp.bfloat16)
        whole_rows = lax.all_gather(weighted.reshape(own, vecs * bsize), "col", axis=0, tiled=True)
        taken = jnp.take(whole_rows.reshape(row_panel, vecs, bsize), rows_idx, axis=0)
        product = jnp.einsum("bij,bki->bkj", square, taken, preferred_element_type=jnp.float32)
        summed = jax.ops.segment_sum(product, bwd_ids, num_segments=col_panel + 1)
        cols_sum = lax.psum_scatter(
            summed[:col_panel].reshape(col_panel, vecs * bsize),
            "row",
            scatter_dimension=0,
            tiled=True,
        )
        projected = cols_sum.reshape(own, vecs, bsize) * inv_col[:, None, :]
        gram = lax.psum(local_gram(projected), ("row", "col")) / total_boxes
        current = rotate(projected, gram)
    return current.reshape(own, vecs * bsize)


def fits(n_row, n_col, blocks, vectors, row_mass):
    own, bsize = row_mass.shape[0] // (n_row * n_col), row_mass.shape[1]
    n_cap = blocks.shape[2]
    dense = n_row * (own * n_col * bsize) * (own * n_row * bsize) * 4
    shapes = own * bsize == 128 and vectors.shape[1] == bsize * bsize and n_cap == 128
    return dense <= VMEM_LIMIT // 4 and shapes and n_cap % (16 * n_col) == 0 and n_row == 4 and n_col == 8


def solution(mesh):
    n_row, n_col = mesh.shape["row"], mesh.shape["col"]

    def run(blocks, block_row, block_col, counts, vectors, row_mass, col_mass):
        args = (blocks, block_row, block_col, counts, vectors, row_mass, col_mass)
        if fits(n_row, n_col, blocks, vectors, row_mass):
            devices = mesh.devices.reshape(n_row, n_col // 2, 2)
            grid, col = jax.sharding.Mesh(devices, ("row", "chip", "core")), ("chip", "core")
            body = functools.partial(whole_on_each, n_row, n_col)
        else:
            grid, col, body = mesh, ("col",), split_by_tile
        by_row, by_col = P(("row",) + col, None), P(col + ("row",), None)
        in_specs = (
            P("row", col, None, None), P("row", col, None), P("row", col, None), P("row", col),
            by_col, by_row, by_col,
        )
        return jax.shard_map(
            body, mesh=grid, in_specs=in_specs, out_specs=by_col, check_vma=False
        )(*args)

    return run
```

```python
import functools

import jax
import jax.numpy as jnp
from jax import lax
from jax.experimental import pallas as pl
from jax.experimental.pallas import tpu as pltpu
from jax.sharding import PartitionSpec as P

ITERS = 4
OFF_CAP = 8
META = 16
UNROLL = 16
BATCH = 4
VMEM_LIMIT = 56 * 1024 * 1024

NT = (((1,), (1,)), ((), ()))
NN = (((1,), (0,)), ((), ()))


def dot(a, b, dims=NN):
    return lax.dot_general(a, b, dims, preferred_element_type=jnp.float32)


def split2(x):
    hi = x.astype(jnp.bfloat16)
    return hi, (x - hi.astype(jnp.float32)).astype(jnp.bfloat16)


def inverse_factor(gram):
    n = gram.shape[0]
    rows = lax.broadcasted_iota(jnp.int32, (n, n), 0)
    cols = lax.broadcasted_iota(jnp.int32, (n, n), 1)
    eye = (rows == cols).astype(jnp.float32)
    both = jnp.concatenate([gram, eye], axis=1)
    count, shape = n // 8, (8, 2 * n)
    tiles = [both[8 * t : 8 * t + 8] for t in range(count)]
    sub = lax.broadcasted_iota(jnp.int32, shape, 0)
    out = []
    for b in range(count):
        column = {
            t: [jnp.broadcast_to(tiles[t][:, 8 * b + s : 8 * b + s + 1], shape) for s in range(8)]
            for t in range(b, count)
        }
        row = [jnp.broadcast_to(tiles[b][s : s + 1], shape) for s in range(8)]
        a = [
            [jnp.broadcast_to(column[b][j][s : s + 1], shape) if j >= s else None for j in range(8)]
            for s in range(8)
        ]
        done = jnp.zeros(shape, jnp.float32)
        for s in range(8):
            root = lax.rsqrt(a[s][s])
            inv = root * root
            inv = inv * (2.0 - a[s][s] * inv)
            step = row[s] * inv
            done = jnp.where(sub == s, row[s] * root, done)
            for i in range(s + 1, 8):
                part = a[s][i] * inv
                for j in range(i, 8):
                    a[i][j] = a[i][j] - part * a[s][j]
                row[i] = row[i] - a[s][i] * step
                for t in range(b + 1, count):
                    column[t][i] = column[t][i] - column[t][s] * part
            for t in range(b + 1, count):
                tiles[t] = tiles[t] - column[t][s] * step
        out.append(done)
    return jnp.concatenate(out, axis=0)[:, n:]


def place_of(own, n_row, n_dev):
    here, chip, core = own[0], own[1], own[2]

    def at_device(r, c):
        dr, dc, dk = here ^ r, chip ^ (c // 2), core ^ (c % 2)
        dx, dy = dc & 1, dc >> 1
        order = jnp.where(dr < 2, 2 * dx, 4 + 2 * dy) + jnp.where(
            jnp.where(dr < 2, dy, dx) > 0, n_dev // 4, 0
        )
        return dk * (n_dev // 2) + order + (dr & 1)

    def device_at(d):
        far, second = (d >> 2) & 1, (d >> 3) & 1
        first = (d >> 1) & 1
        dc = jnp.where(far == 0, 2 * second + first, 2 * first + second)
        return here ^ (2 * far + (d & 1)), 2 * (chip ^ dc) + (core ^ (d >> 4))

    return at_device, device_at


def copy_in(pairs, sems):
    copies = [pltpu.make_async_copy(src, dst, sems.at[i]) for i, (src, dst) in enumerate(pairs)]
    for copy in copies:
        copy.start()
    return copies


def left_half(shape):
    return lax.broadcasted_iota(jnp.int32, shape, len(shape) - 1) < 64


def store_twice(pair, twice, q, x):
    pair[q] = x.astype(pair.dtype)
    turned, left = pltpu.roll(x, 64, 1), left_half(x.shape)
    twice[2 * q] = jnp.where(left, x, turned).astype(twice.dtype)
    twice[2 * q + 1] = jnp.where(left, turned, x).astype(twice.dtype)


def gather_pair(q, first, second):
    left = left_half(first.shape[1:])
    apart = jnp.where(left, first[2 * q + 1], second[2 * q])
    return jnp.where(left, first[2 * q], second[2 * q + 1]) + pltpu.roll(apart, 64, 1)


def add_products(n_group, blk, dims, lists, from_at, source, to_at, first, second):
    left = left_half(source.shape[1:])

    def group(i, carry):
        for at in range(0, UNROLL, BATCH):
            pairs = [i * UNROLL + at + u for u in range(BATCH)]
            prods = [
                dot(
                    jnp.where(left, source[lists[from_at + 2 * p]], source[lists[from_at + 2 * p + 1]]),
                    blk[p],
                    dims,
                )
                for p in pairs
            ]
            for p, prod in zip(pairs, prods):
                a, b = lists[to_at + 2 * p], lists[to_at + 2 * p + 1]
                first[a] = first[a] + prod
                second[b] = second[b] + prod
        return carry

    lax.fori_loop(0, n_group, group, 0)


def unpack(
    n_row, n_col, own, mine, other, lists, place, blk, vs, vd, rm, ic, ints, meta, sems, small
):
    n_dev = n_row * n_col
    k = vs.shape[1]
    half = k // 2
    rblk, cblk = 2 * n_col, 2 * n_row
    vec_at = OFF_CAP * half
    meta_at = vec_at + k
    at_device, device_at = place_of(own, n_row, n_dev)
    slots = 2 * blk.shape[0]

    first, second = pl.ds(0, n_dev // 2), pl.ds(n_dev // 2, n_dev // 2)
    for copy in copy_in([(mine, small.at[first]), (other, small.at[second])], sems):
        copy.wait()
    for d in range(n_dev):
        rows = small[d, meta_at : meta_at + META, :].astype(jnp.float32)
        ints[d : d + 1, :] = rows[8:9].astype(jnp.int32)
    to_scalars = pltpu.make_async_copy(ints, meta, sems.at[2])
    to_scalars.start()

    for r in range(n_row):
        for c in range(n_col):
            q, p, d = c * n_row + r, r * n_col + c, at_device(r, c)
            rows = small[d, meta_at : meta_at + META, :].astype(jnp.float32)
            rm[p] = jnp.broadcast_to(rows[0:1] + rows[1:2] + rows[2:3], (8, 128))
            ic[q] = jnp.broadcast_to(rows[3:4] + rows[4:5] + rows[5:6], (8, 128))
            store_twice(vs, vd, q, small[d, vec_at : vec_at + k, :].astype(jnp.float32))
    to_scalars.wait()

    lanes = lax.broadcasted_iota(jnp.int32, (half, 128), 1)

    def device(d, n):
        count = meta[d, 2 * OFF_CAP]
        count = jnp.where(count > OFF_CAP, 0, count)
        r, c = device_at(d)
        for s in range(OFF_CAP):
            lists[n + s] = c * cblk + meta[d, OFF_CAP + s]
            lists[slots + n + s] = r * rblk + meta[d, s]
            x = small[d, s * half : (s + 1) * half, :].astype(jnp.float32)
            turned = pltpu.roll(x, 64, 1)
            side = (n + s) % 2
            here = (lanes // 64) == side
            even = jnp.where(here, jnp.where(side == 0, x, turned), 0.0)
            odd = jnp.where(here, jnp.where(side == 0, turned, x), 0.0)
            at = pl.multiple_of(side * k, k)
            both = jnp.concatenate([even, odd], axis=0).astype(jnp.bfloat16)
            blk[(n + s) // 2, pl.ds(at, k), :] = both
        return n + count

    n_live = lax.fori_loop(0, n_dev, device, jnp.int32(0))
    for u in range(2 * UNROLL - 1):
        lists[n_live + u] = 0
        lists[slots + n_live + u] = 0
        at = pl.multiple_of((n_live + u) % 2 * k, k)
        blk[(n_live + u) // 2, pl.ds(at, k), :] = jnp.zeros((k, 128), jnp.bfloat16)
    lists[2 * slots] = (n_live + 2 * UNROLL - 1) // (2 * UNROLL)

    for r in range(n_row):
        h = jnp.int32(0)
        for c in range(n_col):
            h = jnp.where(meta[at_device(r, c), 2 * OFF_CAP] > OFF_CAP, c, h)
        lists[2 * slots + 1 + r] = h
        index = small[at_device(r, h), meta_at : meta_at + META, :].astype(jnp.float32)
        place[r : r + 1, :] = index[7:8] * float(rblk) + index[6:7]


def iterate(n_row, n_col, n_cap, total, own, lists, place, *rest):
    sources, fulls, out = rest[:5], rest[5:13], rest[13]
    sems, full, tmp, home, blk, vs, vd, rm, ic = rest[14:23]
    w, w1, w2, wt, wd, y, y1, y2, ph, linv = rest[23:]
    slots = 2 * blk.shape[0]
    n_dev = n_row * n_col
    k = vs.shape[1]
    half = k // 2
    rpairs, cpairs = n_col, n_row
    rblk, cblk = 2 * rpairs, 2 * cpairs
    part = n_cap // n_col
    width = cpairs * 128
    at_device, _ = place_of(own, n_row, n_dev)

    def laid_out(refs, whole):
        at, pairs = 0, []
        for ref in refs:
            pairs.append((ref, whole.at[pl.ds(at, ref.shape[0])]))
            at += ref.shape[0]
        return pairs

    copies = copy_in(laid_out(fulls, full) + list(zip(sources, (blk, vs, vd, rm, ic))), sems)
    for copy in copies[: len(fulls)]:
        copy.wait()
    n_group = lists[2 * slots]

    left = lax.broadcasted_iota(jnp.int32, (rblk, 128), 1) < 64
    homes = []
    for r in range(n_row):
        homes.append(lists[2 * slots + 1 + r])
        want = lax.broadcasted_iota(jnp.int32, (cblk * rblk, n_cap), 0).astype(jnp.float32)
        select = jnp.where(want == place[r : r + 1, :], 1.0, 0.0).astype(jnp.bfloat16)

        parts = [at_device(r, 2 * i + j) for j in range(2) for i in range(n_col // 2)]

        def build(m, carry, parts=parts, select=select):
            at = pl.multiple_of(m * part, part)
            slots = jnp.concatenate(
                [full[d, pl.ds(at, part), :] for d in parts], axis=0
            )
            dense = dot(select, slots)
            for u in range(cpairs):
                a = dense[2 * u * rblk : (2 * u + 1) * rblk]
                b = dense[(2 * u + 1) * rblk : (2 * u + 2) * rblk]
                even = jnp.where(left, a, pltpu.roll(b, 64, 1))
                odd = jnp.where(left, pltpu.roll(a, 64, 1), b)
                tmp[u, pl.ds(m, rblk, stride=k), :] = even
                tmp[u, pl.ds(m + half, rblk, stride=k), :] = odd
            return carry

        lax.fori_loop(0, half, build, 0, unroll=8)

        def cut(i, carry, r=r):
            at = pl.multiple_of(i * k, k)
            for u in range(cpairs):
                hi, lo = split2(tmp[u, pl.ds(at, k), :])
                home[r, pl.ds(at, k), u * 128 : (u + 1) * 128] = hi
                home[r, pl.ds(at, k), width + u * 128 : width + (u + 1) * 128] = lo
            return carry

        lax.fori_loop(0, rblk, cut, 0, unroll=8)

    def clear(refs):
        for ref in refs:
            for q in range(ref.shape[0]):
                ref[q] = jnp.zeros_like(ref[q])

    clear([y, y1, y2, w1, w2])
    for copy in copies[len(fulls) :]:
        copy.wait()

    def iteration(it, carry):
        @pl.when(it > 0)
        def _():
            lh, ll = split2(linv[...])
            turn = jnp.concatenate([lh, lh, ll], axis=1)
            for q in range(0, n_dev, 4):
                hi = jnp.concatenate([ph[q + d, :k, :] for d in range(4)], axis=1)
                lo = jnp.concatenate([ph[q + d, k:, :] for d in range(4)], axis=1)
                current = dot(turn, jnp.concatenate([hi, lo, hi], axis=0))
                for d in range(4):
                    x = current[:, d * 128 : (d + 1) * 128] * ic[q + d, 0:1, :]
                    store_twice(vs, vd, q + d, x)

        for r in range(n_row):
            base = homes[r] * cpairs
            vec = jnp.concatenate([vs[base + u] for u in range(cpairs)] * 2, axis=1)
            for p in range(0, rpairs, 2):
                prod = dot(vec, home[r, p * 128 : (p + 2) * 128, :], NT)
                w[r * rpairs + p] = prod[:, :128]
                w[r * rpairs + p + 1] = prod[:, 128:]

        add_products(n_group, blk, NT, lists, 0, vd, slots, w1, w2)
        for p in range(n_dev):
            x = w[p] + gather_pair(p, w1, w2)
            store_twice(wt, wd, p, x * rm[p, 0:1, :])

        for r in range(n_row):
            base = homes[r] * cpairs
            vec = jnp.concatenate([wt[r * rpairs + p] for p in range(rpairs)], axis=1)
            for u in range(0, cpairs, 2):
                cols = slice(u * 128, (u + 2) * 128)
                tail = slice(width + u * 128, width + (u + 2) * 128)
                prod = dot(vec, home[r, :, cols]) + dot(vec, home[r, :, tail])
                y[base + u] = y[base + u] + prod[:, :128]
                y[base + u + 1] = y[base + u + 1] + prod[:, 128:]

        add_products(n_group, blk, NN, lists, slots, wd, 0, y1, y2)

        both = jnp.zeros((2 * k, k), jnp.float32)
        for q in range(0, n_dev, 4):
            his, los = [], []
            for d in range(q, q + 4):
                x = y[d] + gather_pair(d, y1, y2)
                hi, lo = split2(x * ic[d, 0:1, :])
                ph[d, :k, :] = hi
                ph[d, k:, :] = lo
                his.append(hi)
                los.append(lo)
            hi = jnp.concatenate(his, axis=1)
            lo = jnp.concatenate(los, axis=1)
            both = both + dot(jnp.concatenate([hi, lo], axis=0), hi, NT)
        gram = (both[:k] + (both[k:] + both[k:].T)) / total
        clear([y, y1, y2, w1, w2])
        linv[...] = inverse_factor(gram)
        return carry

    lax.fori_loop(0, ITERS, iteration, 0)
    lh, ll = split2(linv[...])
    q = (2 * own[1] + own[2]) * n_row + own[0]
    hi, lo = ph[q, :k, :], ph[q, k:, :]
    w[0] = dot(lh, hi) + dot(ll, hi) + dot(lh, lo)
    even, odd = w[0, pl.ds(0, half, stride=2), :], w[0, pl.ds(1, half, stride=2), :]
    left = left_half(even.shape)
    first = jnp.where(left, even, pltpu.roll(odd, 64, 1))
    second = jnp.where(left, pltpu.roll(even, 64, 1), odd)
    for i in range(half):
        out[0:1, i * 128 : (i + 1) * 128] = first[i : i + 1]
        out[1:2, i * 128 : (i + 1) * 128] = second[i : i + 1]


def split3(x):
    a = lax.reduce_precision(x, 8, 7)
    b = lax.reduce_precision(x - a, 8, 7)
    return [v.astype(jnp.bfloat16) for v in (a, b, x - a - b)]


def swap(x, axis, distance):
    size = lax.axis_size(axis)
    return lax.ppermute(x, axis, [(i, i ^ distance) for i in range(size)])


def along_rows(x):
    return [x] + [swap(x, "row", s) for s in range(1, lax.axis_size("row"))]


def along_one_chip_axis(x):
    near, far = jnp.stack(x[:2]), jnp.stack(x[2:])
    return [
        jnp.concatenate([near, swap(near, "chip", 1)]),
        jnp.concatenate([far, swap(far, "chip", 2)]),
    ]


def along_other_chip_axis(x):
    near, far = x
    return [swap(near, "chip", 2), swap(far, "chip", 1)]


def full_part(tile, has_full, n_chip, part, chip, core):
    tile = tile.reshape(2, n_chip, part, tile.shape[1])
    none = jnp.zeros(tile.shape[1:], tile.dtype)
    kept, sent = (
        jnp.where(has_full, lax.dynamic_index_in_dim(tile, i, 0, False), none)
        for i in (core, 1 - core)
    )
    both = kept + swap(sent, "core", 1)
    mine = lax.dynamic_index_in_dim(both, chip, 0, False)
    for s in range(1, n_chip):
        mine = mine + swap(lax.dynamic_index_in_dim(both, chip ^ s, 0, False), "chip", s)
    return mine


def whole_on_each(n_row, n_col, blocks, block_row, block_col, counts, vectors, row_mass, col_mass):
    tile = blocks[0, 0]
    n_cap = tile.shape[0]
    own, bsize = row_mass.shape
    k = vectors.shape[1] // bsize
    half = bsize // 2
    part = n_cap // n_col
    n_dev = n_row * n_col
    count = counts[0, 0]
    has_full = count > OFF_CAP
    bf16 = jnp.bfloat16
    row, chip, core = (lax.axis_index(name) for name in ("row", "chip", "core"))

    off = tile[:OFF_CAP].reshape(OFF_CAP * half, 128)
    inv_col = 1.0 / jnp.sqrt(col_mass)
    scaled = (vectors.reshape(own, k, bsize) * inv_col[:, None, :]).astype(bf16)
    scaled = scaled.transpose(1, 0, 2).reshape(k, own * bsize)
    mass = row_mass.reshape(own, half, 2).transpose(0, 2, 1).reshape(own * bsize)
    rows, cols = block_row[0, 0], block_col[0, 0]
    short = jnp.concatenate(
        [rows[:OFF_CAP], cols[:OFF_CAP], count[None], jnp.zeros(128 - 2 * OFF_CAP - 1, jnp.int32)]
    )
    meta = [v.astype(bf16) for v in (rows, cols, short)]
    meta = split3(mass) + split3(inv_col.reshape(own * bsize)) + meta
    meta = jnp.stack(meta + [jnp.zeros(128, bf16)] * (META - len(meta)))
    small = jnp.concatenate([off, scaled, meta], axis=0)
    home = full_part(tile, has_full, n_col // 2, part, chip, core)
    home = home.reshape(part, half, 128).transpose(1, 0, 2).reshape(half * part, 128)

    together = lax.optimization_barrier
    home, smalls = together((home, along_rows(small)))
    homes, smalls = along_rows(home), along_one_chip_axis(smalls)
    smalls, homes[1] = together((smalls, homes[1]))
    smalls = jnp.concatenate(smalls + along_other_chip_axis(smalls))
    homes, smalls = together((homes, smalls))
    others = swap(smalls, "core", 1)
    homes = along_one_chip_axis(homes)
    last = along_other_chip_axis(homes)

    where = jnp.stack([row, chip, core]).astype(jnp.int32)
    height, width = 2 * n_col * bsize, 2 * n_row * bsize
    slots = n_dev * OFF_CAP + 2 * UNROLL
    f32, i32, vmem, smem = jnp.float32, jnp.int32, pltpu.VMEM, pltpu.SMEM
    pair, twice, mass = (n_dev, k, 128), (2 * n_dev, k, 128), (n_dev, 8, 128)
    smem_spec, vmem_spec, any_spec = (pl.BlockSpec(memory_space=m) for m in (smem, vmem, pl.ANY))
    arrays = [
        ((8, 128), f32), ((slots // 2, 128, 128), bf16), (pair, bf16), (twice, bf16), (mass, f32), (mass, f32),
    ]
    lists, *unpacked = pl.pallas_call(
        functools.partial(unpack, n_row, n_col),
        out_shape=[jax.ShapeDtypeStruct((2 * slots + 8,), i32)]
        + [jax.ShapeDtypeStruct(*v) for v in arrays],
        in_specs=[smem_spec, any_spec, any_spec],
        out_specs=[smem_spec] + [vmem_spec] * len(arrays),
        scratch_shapes=[
            vmem((n_dev, 128), i32),
            smem((n_dev, 128), i32),
            pltpu.SemaphoreType.DMA((3,)),
            vmem((n_dev,) + small.shape, bf16),
        ],
        compiler_params=pltpu.CompilerParams(vmem_limit_bytes=VMEM_LIMIT),
        cost_estimate=pl.CostEstimate(
            flops=0, bytes_accessed=4 * n_dev * small.size * 2, transcendentals=0
        ),
        name="unpack",
    )(where, smalls, others)
    last, lists = together((last, lists))
    mine = homes + last
    fulls = mine + [swap(v, "core", 1) for v in mine]
    return pl.pallas_call(
        functools.partial(iterate, n_row, n_col, n_cap, float(n_dev * own * bsize)),
        out_shape=jax.ShapeDtypeStruct((own, k * bsize), f32),
        in_specs=[smem_spec] * 2 + [vmem_spec] + [any_spec] * (5 + len(fulls)),
        out_specs=vmem_spec,
        scratch_shapes=[
            pltpu.SemaphoreType.DMA((5 + len(fulls),)),
            vmem((n_dev,) + home.shape, bf16),
            vmem((n_row, height, 128), f32),
            vmem((n_row, height, 2 * width), bf16),
            *[vmem(*v) for v in arrays[1:]],
            vmem(pair, f32), vmem(twice, f32), vmem(twice, f32), vmem(pair, bf16), vmem(twice, bf16),
            vmem(pair, f32), vmem(twice, f32), vmem(twice, f32),
            vmem((n_dev, 2 * k, 128), bf16),
            vmem((k, k), f32),
        ],
        compiler_params=pltpu.CompilerParams(vmem_limit_bytes=VMEM_LIMIT),
        name="iterate",
    )(where, lists, *unpacked, *fulls)


def rotate(projected, gram):
    lower = jnp.linalg.cholesky(gram)
    inverse = lax.linalg.triangular_solve(
        lower, jnp.eye(gram.shape[0], dtype=jnp.float32), left_side=True, lower=True
    )
    return jnp.einsum(
        "kl,bli->bki",
        inverse,
        projected,
        precision=lax.Precision.HIGHEST,
        preferred_element_type=jnp.float32,
    )


def local_gram(projected):
    return jnp.einsum(
        "bki,bli->kl",
        projected,
        projected,
        precision=lax.Precision.HIGHEST,
        preferred_element_type=jnp.float32,
    )


def split_by_tile(blocks, block_row, block_col, counts, vectors, row_mass, col_mass):
    tile = blocks[0, 0]
    n_cap = tile.shape[0]
    bsize = row_mass.shape[1]
    vecs = vectors.shape[1] // bsize
    own = vectors.shape[0]
    n_row = lax.axis_size("row")
    n_col = lax.axis_size("col")
    row_panel = own * n_col
    col_panel = own * n_row
    total_boxes = float(own * bsize * n_row * n_col)
    rows_idx = block_row[0, 0]
    cols_idx = block_col[0, 0]
    live = jnp.arange(n_cap) < counts[0, 0]
    fwd_ids = jnp.where(live, rows_idx, row_panel)
    bwd_ids = jnp.where(live, cols_idx, col_panel)
    square = tile.reshape(n_cap, bsize, bsize)
    inv_col = 1.0 / jnp.sqrt(col_mass)
    current = vectors.reshape(own, vecs, bsize)
    for step in range(ITERS):
        scaled = (current * inv_col[:, None, :]).astype(jnp.bfloat16).reshape(own, vecs * bsize)
        panel = lax.all_gather(scaled, "row", axis=0, tiled=True)
        forward_taken = jnp.take(panel.reshape(col_panel, vecs, bsize), cols_idx, axis=0)
        forward_product = jnp.einsum(
            "bij,bkj->bki", square, forward_taken, preferred_element_type=jnp.float32
        )
        forward_summed = jax.ops.segment_sum(forward_product, fwd_ids, num_segments=row_panel + 1)
        rows_sum = lax.psum_scatter(
            forward_summed[:row_panel].reshape(row_panel, vecs * bsize),
            "col",
            scatter_dimension=0,
            tiled=True,
        )
        weighted = (rows_sum.reshape(own, vecs, bsize) * row_mass[:, None, :]).astype(jnp.bfloat16)
        whole_rows = lax.all_gather(weighted.reshape(own, vecs * bsize), "col", axis=0, tiled=True)
        taken = jnp.take(whole_rows.reshape(row_panel, vecs, bsize), rows_idx, axis=0)
        product = jnp.einsum("bij,bki->bkj", square, taken, preferred_element_type=jnp.float32)
        summed = jax.ops.segment_sum(product, bwd_ids, num_segments=col_panel + 1)
        cols_sum = lax.psum_scatter(
            summed[:col_panel].reshape(col_panel, vecs * bsize),
            "row",
            scatter_dimension=0,
            tiled=True,
        )
        projected = cols_sum.reshape(own, vecs, bsize) * inv_col[:, None, :]
        gram = lax.psum(local_gram(projected), ("row", "col")) / total_boxes
        current = rotate(projected, gram)
    return current.reshape(own, vecs * bsize)


def fits(n_row, n_col, blocks, vectors, row_mass):
    own, bsize = row_mass.shape[0] // (n_row * n_col), row_mass.shape[1]
    n_cap = blocks.shape[2]
    dense = n_row * (own * n_col * bsize) * (own * n_row * bsize) * 4
    shapes = own * bsize == 128 and vectors.shape[1] == bsize * bsize and n_cap == 128
    return dense <= VMEM_LIMIT // 4 and shapes and n_cap % (16 * n_col) == 0 and n_row == 4 and n_col == 8


def solution(mesh):
    n_row, n_col = mesh.shape["row"], mesh.shape["col"]

    def run(blocks, block_row, block_col, counts, vectors, row_mass, col_mass):
        args = (blocks, block_row, block_col, counts, vectors, row_mass, col_mass)
        if fits(n_row, n_col, blocks, vectors, row_mass):
            devices = mesh.devices.reshape(n_row, n_col // 2, 2)
            grid, col = jax.sharding.Mesh(devices, ("row", "chip", "core")), ("chip", "core")
            body = functools.partial(whole_on_each, n_row, n_col)
        else:
            grid, col, body = mesh, ("col",), split_by_tile
        by_row, by_col = P(("row",) + col, None), P(col + ("row",), None)
        in_specs = (
            P("row", col, None, None), P("row", col, None), P("row", col, None), P("row", col),
            by_col, by_row, by_col,
        )
        return jax.shard_map(
            body, mesh=grid, in_specs=in_specs, out_specs=by_col, check_vma=False
        )(*args)

    return run
```

```python
import functools

import jax
import jax.numpy as jnp
from jax import lax
from jax.experimental import pallas as pl
from jax.experimental.pallas import tpu as pltpu
from jax.sharding import PartitionSpec as P

ITERS = 4
OFF_CAP = 8
META = 16
UNROLL = 16
BATCH = 4
VMEM_LIMIT = 40 * 1024 * 1024

NT = (((1,), (1,)), ((), ()))
NN = (((1,), (0,)), ((), ()))


def dot(a, b, dims=NN):
    return lax.dot_general(a, b, dims, preferred_element_type=jnp.float32)


def split2(x):
    hi = x.astype(jnp.bfloat16)
    return hi, (x - hi.astype(jnp.float32)).astype(jnp.bfloat16)


def inverse_factor(gram):
    n = gram.shape[0]
    rows = lax.broadcasted_iota(jnp.int32, (n, n), 0)
    cols = lax.broadcasted_iota(jnp.int32, (n, n), 1)
    eye = (rows == cols).astype(jnp.float32)
    both = jnp.concatenate([gram, eye], axis=1)
    count, shape = n // 8, (8, 2 * n)
    tiles = [both[8 * t : 8 * t + 8] for t in range(count)]
    sub = lax.broadcasted_iota(jnp.int32, shape, 0)
    out = []
    for b in range(count):
        column = {
            t: [jnp.broadcast_to(tiles[t][:, 8 * b + s : 8 * b + s + 1], shape) for s in range(8)]
            for t in range(b, count)
        }
        row = [jnp.broadcast_to(tiles[b][s : s + 1], shape) for s in range(8)]
        a = [
            [jnp.broadcast_to(column[b][j][s : s + 1], shape) if j >= s else None for j in range(8)]
            for s in range(8)
        ]
        done = jnp.zeros(shape, jnp.float32)
        for s in range(8):
            root = lax.rsqrt(a[s][s])
            inv = root * root
            inv = inv * (2.0 - a[s][s] * inv)
            step = row[s] * inv
            done = jnp.where(sub == s, row[s] * root, done)
            for i in range(s + 1, 8):
                part = a[s][i] * inv
                for j in range(i, 8):
                    a[i][j] = a[i][j] - part * a[s][j]
                row[i] = row[i] - a[s][i] * step
                for t in range(b + 1, count):
                    column[t][i] = column[t][i] - column[t][s] * part
            for t in range(b + 1, count):
                tiles[t] = tiles[t] - column[t][s] * step
        out.append(done)
    return jnp.concatenate(out, axis=0)[:, n:]


def place_of(own, n_row, n_dev):
    here, chip, core = own[0], own[1], own[2]

    def at_device(r, c):
        dr, dc, dk = here ^ r, chip ^ (c // 2), core ^ (c % 2)
        dx, dy = dc & 1, dc >> 1
        order = jnp.where(dr < 2, 2 * dx, 4 + 2 * dy) + jnp.where(
            jnp.where(dr < 2, dy, dx) > 0, n_dev // 4, 0
        )
        return dk * (n_dev // 2) + order + (dr & 1)

    def device_at(d):
        far, second = (d >> 2) & 1, (d >> 3) & 1
        first = (d >> 1) & 1
        dc = jnp.where(far == 0, 2 * second + first, 2 * first + second)
        return here ^ (2 * far + (d & 1)), 2 * (chip ^ dc) + (core ^ (d >> 4))

    return at_device, device_at


def copy_in(pairs, sems):
    copies = [pltpu.make_async_copy(src, dst, sems.at[i]) for i, (src, dst) in enumerate(pairs)]
    for copy in copies:
        copy.start()
    return copies


def left_half(shape):
    return lax.broadcasted_iota(jnp.int32, shape, len(shape) - 1) < 64


def store_twice(pair, twice, q, x):
    pair[q] = x.astype(pair.dtype)
    turned, left = pltpu.roll(x, 64, 1), left_half(x.shape)
    twice[2 * q] = jnp.where(left, x, turned).astype(twice.dtype)
    twice[2 * q + 1] = jnp.where(left, turned, x).astype(twice.dtype)


def gather_pair(q, first, second):
    left = left_half(first.shape[1:])
    apart = jnp.where(left, first[2 * q + 1], second[2 * q])
    return jnp.where(left, first[2 * q], second[2 * q + 1]) + pltpu.roll(apart, 64, 1)


def add_products(n_group, blk, dims, lists, from_at, source, to_at, first, second):
    left = left_half(source.shape[1:])

    def group(i, carry):
        for at in range(0, UNROLL, BATCH):
            pairs = [i * UNROLL + at + u for u in range(BATCH)]
            prods = [
                dot(
                    jnp.where(left, source[lists[from_at + 2 * p]], source[lists[from_at + 2 * p + 1]]),
                    blk[p],
                    dims,
                )
                for p in pairs
            ]
            for p, prod in zip(pairs, prods):
                a, b = lists[to_at + 2 * p], lists[to_at + 2 * p + 1]
                first[a] = first[a] + prod
                second[b] = second[b] + prod
        return carry

    lax.fori_loop(0, n_group, group, 0)


def unpack(
    n_row, n_col, own, mine, other, lists, place, blk, vs, vd, rm, ic, ints, meta, sems, small
):
    n_dev = n_row * n_col
    k = vs.shape[1]
    half = k // 2
    rblk, cblk = 2 * n_col, 2 * n_row
    vec_at = OFF_CAP * half
    meta_at = vec_at + k
    at_device, device_at = place_of(own, n_row, n_dev)
    slots = 2 * blk.shape[0]

    first, second = pl.ds(0, n_dev // 2), pl.ds(n_dev // 2, n_dev // 2)
    for copy in copy_in([(mine, small.at[first]), (other, small.at[second])], sems):
        copy.wait()
    for d in range(n_dev):
        rows = small[d, meta_at : meta_at + META, :].astype(jnp.float32)
        ints[d : d + 1, :] = rows[8:9].astype(jnp.int32)
    to_scalars = pltpu.make_async_copy(ints, meta, sems.at[2])
    to_scalars.start()

    for r in range(n_row):
        for c in range(n_col):
            q, p, d = c * n_row + r, r * n_col + c, at_device(r, c)
            rows = small[d, meta_at : meta_at + META, :].astype(jnp.float32)
            rm[p] = jnp.broadcast_to(rows[0:1] + rows[1:2] + rows[2:3], (8, 128))
            ic[q] = jnp.broadcast_to(rows[3:4] + rows[4:5] + rows[5:6], (8, 128))
            store_twice(vs, vd, q, small[d, vec_at : vec_at + k, :].astype(jnp.float32))
    to_scalars.wait()

    lanes = lax.broadcasted_iota(jnp.int32, (half, 128), 1)

    def device(d, n):
        count = meta[d, 2 * OFF_CAP]
        count = jnp.where(count > OFF_CAP, 0, count)
        r, c = device_at(d)
        for s in range(OFF_CAP):
            lists[n + s] = c * cblk + meta[d, OFF_CAP + s]
            lists[slots + n + s] = r * rblk + meta[d, s]
            x = small[d, s * half : (s + 1) * half, :].astype(jnp.float32)
            turned = pltpu.roll(x, 64, 1)
            side = (n + s) % 2
            here = (lanes // 64) == side
            even = jnp.where(here, jnp.where(side == 0, x, turned), 0.0)
            odd = jnp.where(here, jnp.where(side == 0, turned, x), 0.0)
            at = pl.multiple_of(side * k, k)
            both = jnp.concatenate([even, odd], axis=0).astype(jnp.bfloat16)
            blk[(n + s) // 2, pl.ds(at, k), :] = both
        return n + count

    n_live = lax.fori_loop(0, n_dev, device, jnp.int32(0))
    for u in range(2 * UNROLL - 1):
        lists[n_live + u] = 0
        lists[slots + n_live + u] = 0
        at = pl.multiple_of((n_live + u) % 2 * k, k)
        blk[(n_live + u) // 2, pl.ds(at, k), :] = jnp.zeros((k, 128), jnp.bfloat16)
    lists[2 * slots] = (n_live + 2 * UNROLL - 1) // (2 * UNROLL)

    for r in range(n_row):
        h = jnp.int32(0)
        for c in range(n_col):
            h = jnp.where(meta[at_device(r, c), 2 * OFF_CAP] > OFF_CAP, c, h)
        lists[2 * slots + 1 + r] = h
        index = small[at_device(r, h), meta_at : meta_at + META, :].astype(jnp.float32)
        place[r : r + 1, :] = index[7:8] * float(rblk) + index[6:7]


def iterate(n_row, n_col, n_cap, total, own, lists, place, *rest):
    sources, fulls, out = rest[:5], rest[5:13], rest[13]
    sems, full, tmp, home, blk, vs, vd, rm, ic = rest[14:23]
    w, w1, w2, wt, wd, y, y1, y2, ph, linv = rest[23:]
    slots = 2 * blk.shape[0]
    n_dev = n_row * n_col
    k = vs.shape[1]
    half = k // 2
    rpairs, cpairs = n_col, n_row
    rblk, cblk = 2 * rpairs, 2 * cpairs
    part = n_cap // n_col
    width = cpairs * 128
    at_device, _ = place_of(own, n_row, n_dev)

    def laid_out(refs, whole):
        at, pairs = 0, []
        for ref in refs:
            pairs.append((ref, whole.at[pl.ds(at, ref.shape[0])]))
            at += ref.shape[0]
        return pairs

    copies = copy_in(laid_out(fulls, full) + list(zip(sources, (blk, vs, vd, rm, ic))), sems)
    for copy in copies[: len(fulls)]:
        copy.wait()
    n_group = lists[2 * slots]

    left = lax.broadcasted_iota(jnp.int32, (rblk, 128), 1) < 64
    homes = []
    for r in range(n_row):
        homes.append(lists[2 * slots + 1 + r])
        want = lax.broadcasted_iota(jnp.int32, (cblk * rblk, n_cap), 0).astype(jnp.float32)
        select = jnp.where(want == place[r : r + 1, :], 1.0, 0.0).astype(jnp.bfloat16)

        parts = [at_device(r, 2 * i + j) for j in range(2) for i in range(n_col // 2)]

        def build(m, carry, parts=parts, select=select):
            at = pl.multiple_of(m * part, part)
            slots = jnp.concatenate(
                [full[d, pl.ds(at, part), :] for d in parts], axis=0
            )
            dense = dot(select, slots)
            for u in range(cpairs):
                a = dense[2 * u * rblk : (2 * u + 1) * rblk]
                b = dense[(2 * u + 1) * rblk : (2 * u + 2) * rblk]
                even = jnp.where(left, a, pltpu.roll(b, 64, 1))
                odd = jnp.where(left, pltpu.roll(a, 64, 1), b)
                tmp[u, pl.ds(m, rblk, stride=k), :] = even
                tmp[u, pl.ds(m + half, rblk, stride=k), :] = odd
            return carry

        lax.fori_loop(0, half, build, 0, unroll=8)

        def cut(i, carry, r=r):
            at = pl.multiple_of(i * k, k)
            for u in range(cpairs):
                hi, lo = split2(tmp[u, pl.ds(at, k), :])
                home[r, pl.ds(at, k), u * 128 : (u + 1) * 128] = hi
                home[r, pl.ds(at, k), width + u * 128 : width + (u + 1) * 128] = lo
            return carry

        lax.fori_loop(0, rblk, cut, 0, unroll=8)

    def clear(refs):
        for ref in refs:
            for q in range(ref.shape[0]):
                ref[q] = jnp.zeros_like(ref[q])

    clear([y, y1, y2, w1, w2])
    for copy in copies[len(fulls) :]:
        copy.wait()

    def iteration(it, carry):
        @pl.when(it > 0)
        def _():
            lh, ll = split2(linv[...])
            turn = jnp.concatenate([lh, lh, ll], axis=1)
            for q in range(0, n_dev, 4):
                hi = jnp.concatenate([ph[q + d, :k, :] for d in range(4)], axis=1)
                lo = jnp.concatenate([ph[q + d, k:, :] for d in range(4)], axis=1)
                current = dot(turn, jnp.concatenate([hi, lo, hi], axis=0))
                for d in range(4):
                    x = current[:, d * 128 : (d + 1) * 128] * ic[q + d, 0:1, :]
                    store_twice(vs, vd, q + d, x)

        for r in range(n_row):
            base = homes[r] * cpairs
            vec = jnp.concatenate([vs[base + u] for u in range(cpairs)] * 2, axis=1)
            for p in range(0, rpairs, 2):
                prod = dot(vec, home[r, p * 128 : (p + 2) * 128, :], NT)
                w[r * rpairs + p] = prod[:, :128]
                w[r * rpairs + p + 1] = prod[:, 128:]

        add_products(n_group, blk, NT, lists, 0, vd, slots, w1, w2)
        for p in range(n_dev):
            x = w[p] + gather_pair(p, w1, w2)
            store_twice(wt, wd, p, x * rm[p, 0:1, :])

        for r in range(n_row):
            base = homes[r] * cpairs
            vec = jnp.concatenate([wt[r * rpairs + p] for p in range(rpairs)], axis=1)
            for u in range(0, cpairs, 2):
                cols = slice(u * 128, (u + 2) * 128)
                tail = slice(width + u * 128, width + (u + 2) * 128)
                prod = dot(vec, home[r, :, cols]) + dot(vec, home[r, :, tail])
                y[base + u] = y[base + u] + prod[:, :128]
                y[base + u + 1] = y[base + u + 1] + prod[:, 128:]

        add_products(n_group, blk, NN, lists, slots, wd, 0, y1, y2)

        both = jnp.zeros((2 * k, k), jnp.float32)
        for q in range(0, n_dev, 4):
            his, los = [], []
            for d in range(q, q + 4):
                x = y[d] + gather_pair(d, y1, y2)
                hi, lo = split2(x * ic[d, 0:1, :])
                ph[d, :k, :] = hi
                ph[d, k:, :] = lo
                his.append(hi)
                los.append(lo)
            hi = jnp.concatenate(his, axis=1)
            lo = jnp.concatenate(los, axis=1)
            both = both + dot(jnp.concatenate([hi, lo], axis=0), hi, NT)
        gram = (both[:k] + (both[k:] + both[k:].T)) / total
        clear([y, y1, y2, w1, w2])
        linv[...] = inverse_factor(gram)
        return carry

    lax.fori_loop(0, ITERS, iteration, 0)
    lh, ll = split2(linv[...])
    q = (2 * own[1] + own[2]) * n_row + own[0]
    hi, lo = ph[q, :k, :], ph[q, k:, :]
    w[0] = dot(lh, hi) + dot(ll, hi) + dot(lh, lo)
    even, odd = w[0, pl.ds(0, half, stride=2), :], w[0, pl.ds(1, half, stride=2), :]
    left = left_half(even.shape)
    first = jnp.where(left, even, pltpu.roll(odd, 64, 1))
    second = jnp.where(left, pltpu.roll(even, 64, 1), odd)
    for i in range(half):
        out[0:1, i * 128 : (i + 1) * 128] = first[i : i + 1]
        out[1:2, i * 128 : (i + 1) * 128] = second[i : i + 1]


def split3(x):
    a = lax.reduce_precision(x, 8, 7)
    b = lax.reduce_precision(x - a, 8, 7)
    return [v.astype(jnp.bfloat16) for v in (a, b, x - a - b)]


def swap(x, axis, distance):
    size = lax.axis_size(axis)
    return lax.ppermute(x, axis, [(i, i ^ distance) for i in range(size)])


def along_rows(x):
    return [x] + [swap(x, "row", s) for s in range(1, lax.axis_size("row"))]


def along_one_chip_axis(x):
    near, far = jnp.stack(x[:2]), jnp.stack(x[2:])
    return [
        jnp.concatenate([near, swap(near, "chip", 1)]),
        jnp.concatenate([far, swap(far, "chip", 2)]),
    ]


def along_other_chip_axis(x):
    near, far = x
    return [swap(near, "chip", 2), swap(far, "chip", 1)]


def full_part(tile, has_full, n_chip, part, chip, core):
    tile = tile.reshape(2, n_chip, part, tile.shape[1])
    none = jnp.zeros(tile.shape[1:], tile.dtype)
    kept, sent = (
        jnp.where(has_full, lax.dynamic_index_in_dim(tile, i, 0, False), none)
        for i in (core, 1 - core)
    )
    both = kept + swap(sent, "core", 1)
    mine = lax.dynamic_index_in_dim(both, chip, 0, False)
    for s in range(1, n_chip):
        mine = mine + swap(lax.dynamic_index_in_dim(both, chip ^ s, 0, False), "chip", s)
    return mine


def whole_on_each(n_row, n_col, blocks, block_row, block_col, counts, vectors, row_mass, col_mass):
    tile = blocks[0, 0]
    n_cap = tile.shape[0]
    own, bsize = row_mass.shape
    k = vectors.shape[1] // bsize
    half = bsize // 2
    part = n_cap // n_col
    n_dev = n_row * n_col
    count = counts[0, 0]
    has_full = count > OFF_CAP
    bf16 = jnp.bfloat16
    row, chip, core = (lax.axis_index(name) for name in ("row", "chip", "core"))

    off = tile[:OFF_CAP].reshape(OFF_CAP * half, 128)
    inv_col = 1.0 / jnp.sqrt(col_mass)
    scaled = (vectors.reshape(own, k, bsize) * inv_col[:, None, :]).astype(bf16)
    scaled = scaled.transpose(1, 0, 2).reshape(k, own * bsize)
    mass = row_mass.reshape(own, half, 2).transpose(0, 2, 1).reshape(own * bsize)
    rows, cols = block_row[0, 0], block_col[0, 0]
    short = jnp.concatenate(
        [rows[:OFF_CAP], cols[:OFF_CAP], count[None], jnp.zeros(128 - 2 * OFF_CAP - 1, jnp.int32)]
    )
    meta = [v.astype(bf16) for v in (rows, cols, short)]
    meta = split3(mass) + split3(inv_col.reshape(own * bsize)) + meta
    meta = jnp.stack(meta + [jnp.zeros(128, bf16)] * (META - len(meta)))
    small = jnp.concatenate([off, scaled, meta], axis=0)
    home = full_part(tile, has_full, n_col // 2, part, chip, core)
    home = home.reshape(part, half, 128).transpose(1, 0, 2).reshape(half * part, 128)

    together = lax.optimization_barrier
    where = jnp.stack([row, chip, core]).astype(jnp.int32)
    home, smalls, where = together((home, along_rows(small), where))
    homes, smalls = along_rows(home), along_one_chip_axis(smalls)
    smalls, homes[1] = together((smalls, homes[1]))
    smalls = jnp.concatenate(smalls + along_other_chip_axis(smalls))
    homes, smalls = together((homes, smalls))
    others = swap(smalls, "core", 1)
    homes = along_one_chip_axis(homes)
    last = along_other_chip_axis(homes)

    height, width = 2 * n_col * bsize, 2 * n_row * bsize
    slots = n_dev * OFF_CAP + 2 * UNROLL
    f32, i32, vmem, smem = jnp.float32, jnp.int32, pltpu.VMEM, pltpu.SMEM
    pair, twice, mass = (n_dev, k, 128), (2 * n_dev, k, 128), (n_dev, 8, 128)
    smem_spec, vmem_spec, any_spec = (pl.BlockSpec(memory_space=m) for m in (smem, vmem, pl.ANY))
    arrays = [
        ((8, 128), f32), ((slots // 2, 128, 128), bf16), (pair, bf16), (twice, bf16), (mass, f32), (mass, f32),
    ]
    lists, *unpacked = pl.pallas_call(
        functools.partial(unpack, n_row, n_col),
        out_shape=[jax.ShapeDtypeStruct((2 * slots + 8,), i32)]
        + [jax.ShapeDtypeStruct(*v) for v in arrays],
        in_specs=[smem_spec, any_spec, any_spec],
        out_specs=[smem_spec] + [vmem_spec] * len(arrays),
        scratch_shapes=[
            vmem((n_dev, 128), i32),
            smem((n_dev, 128), i32),
            pltpu.SemaphoreType.DMA((3,)),
            vmem((n_dev,) + small.shape, bf16),
        ],
        compiler_params=pltpu.CompilerParams(vmem_limit_bytes=VMEM_LIMIT),
        cost_estimate=pl.CostEstimate(
            flops=0, bytes_accessed=4 * n_dev * small.size * 2, transcendentals=0
        ),
        name="unpack",
    )(where, smalls, others)
    last, lists = together((last, lists))
    mine = homes + last
    fulls = mine + [swap(v, "core", 1) for v in mine]
    return pl.pallas_call(
        functools.partial(iterate, n_row, n_col, n_cap, float(n_dev * own * bsize)),
        out_shape=jax.ShapeDtypeStruct((own, k * bsize), f32),
        in_specs=[smem_spec] * 2 + [vmem_spec] + [any_spec] * (5 + len(fulls)),
        out_specs=vmem_spec,
        scratch_shapes=[
            pltpu.SemaphoreType.DMA((5 + len(fulls),)),
            vmem((n_dev,) + home.shape, bf16),
            vmem((n_row, height, 128), f32),
            vmem((n_row, height, 2 * width), bf16),
            *[vmem(*v) for v in arrays[1:]],
            vmem(pair, f32), vmem(twice, f32), vmem(twice, f32), vmem(pair, bf16), vmem(twice, bf16),
            vmem(pair, f32), vmem(twice, f32), vmem(twice, f32),
            vmem((n_dev, 2 * k, 128), bf16),
            vmem((k, k), f32),
        ],
        compiler_params=pltpu.CompilerParams(vmem_limit_bytes=VMEM_LIMIT),
        name="iterate",
    )(where, lists, *unpacked, *fulls)


def rotate(projected, gram):
    lower = jnp.linalg.cholesky(gram)
    inverse = lax.linalg.triangular_solve(
        lower, jnp.eye(gram.shape[0], dtype=jnp.float32), left_side=True, lower=True
    )
    return jnp.einsum(
        "kl,bli->bki",
        inverse,
        projected,
        precision=lax.Precision.HIGHEST,
        preferred_element_type=jnp.float32,
    )


def local_gram(projected):
    return jnp.einsum(
        "bki,bli->kl",
        projected,
        projected,
        precision=lax.Precision.HIGHEST,
        preferred_element_type=jnp.float32,
    )


def split_by_tile(blocks, block_row, block_col, counts, vectors, row_mass, col_mass):
    tile = blocks[0, 0]
    n_cap = tile.shape[0]
    bsize = row_mass.shape[1]
    vecs = vectors.shape[1] // bsize
    own = vectors.shape[0]
    n_row = lax.axis_size("row")
    n_col = lax.axis_size("col")
    row_panel = own * n_col
    col_panel = own * n_row
    total_boxes = float(own * bsize * n_row * n_col)
    rows_idx = block_row[0, 0]
    cols_idx = block_col[0, 0]
    live = jnp.arange(n_cap) < counts[0, 0]
    fwd_ids = jnp.where(live, rows_idx, row_panel)
    bwd_ids = jnp.where(live, cols_idx, col_panel)
    square = tile.reshape(n_cap, bsize, bsize)
    inv_col = 1.0 / jnp.sqrt(col_mass)
    current = vectors.reshape(own, vecs, bsize)
    for step in range(ITERS):
        scaled = (current * inv_col[:, None, :]).astype(jnp.bfloat16).reshape(own, vecs * bsize)
        panel = lax.all_gather(scaled, "row", axis=0, tiled=True)
        forward_taken = jnp.take(panel.reshape(col_panel, vecs, bsize), cols_idx, axis=0)
        forward_product = jnp.einsum(
            "bij,bkj->bki", square, forward_taken, preferred_element_type=jnp.float32
        )
        forward_summed = jax.ops.segment_sum(forward_product, fwd_ids, num_segments=row_panel + 1)
        rows_sum = lax.psum_scatter(
            forward_summed[:row_panel].reshape(row_panel, vecs * bsize),
            "col",
            scatter_dimension=0,
            tiled=True,
        )
        weighted = (rows_sum.reshape(own, vecs, bsize) * row_mass[:, None, :]).astype(jnp.bfloat16)
        whole_rows = lax.all_gather(weighted.reshape(own, vecs * bsize), "col", axis=0, tiled=True)
        taken = jnp.take(whole_rows.reshape(row_panel, vecs, bsize), rows_idx, axis=0)
        product = jnp.einsum("bij,bki->bkj", square, taken, preferred_element_type=jnp.float32)
        summed = jax.ops.segment_sum(product, bwd_ids, num_segments=col_panel + 1)
        cols_sum = lax.psum_scatter(
            summed[:col_panel].reshape(col_panel, vecs * bsize),
            "row",
            scatter_dimension=0,
            tiled=True,
        )
        projected = cols_sum.reshape(own, vecs, bsize) * inv_col[:, None, :]
        gram = lax.psum(local_gram(projected), ("row", "col")) / total_boxes
        current = rotate(projected, gram)
    return current.reshape(own, vecs * bsize)


def fits(n_row, n_col, blocks, vectors, row_mass):
    own, bsize = row_mass.shape[0] // (n_row * n_col), row_mass.shape[1]
    n_cap = blocks.shape[2]
    dense = n_row * (own * n_col * bsize) * (own * n_row * bsize) * 4
    shapes = own * bsize == 128 and vectors.shape[1] == bsize * bsize and n_cap == 128
    return dense <= VMEM_LIMIT // 4 and shapes and n_cap % (16 * n_col) == 0 and n_row == 4 and n_col == 8


def solution(mesh):
    n_row, n_col = mesh.shape["row"], mesh.shape["col"]

    def run(blocks, block_row, block_col, counts, vectors, row_mass, col_mass):
        args = (blocks, block_row, block_col, counts, vectors, row_mass, col_mass)
        if fits(n_row, n_col, blocks, vectors, row_mass):
            devices = mesh.devices.reshape(n_row, n_col // 2, 2)
            grid, col = jax.sharding.Mesh(devices, ("row", "chip", "core")), ("chip", "core")
            body = functools.partial(whole_on_each, n_row, n_col)
        else:
            grid, col, body = mesh, ("col",), split_by_tile
        by_row, by_col = P(("row",) + col, None), P(col + ("row",), None)
        in_specs = (
            P("row", col, None, None), P("row", col, None), P("row", col, None), P("row", col),
            by_col, by_row, by_col,
        )
        return jax.shard_map(
            body, mesh=grid, in_specs=in_specs, out_specs=by_col, check_vma=False
        )(*args)

    return run
```

```python
import functools

import jax
import jax.numpy as jnp
from jax import lax
from jax.experimental import pallas as pl
from jax.experimental.pallas import tpu as pltpu
from jax.sharding import PartitionSpec as P

ITERS = 4
OFF_CAP = 8
META = 16
UNROLL = 16
BATCH = 4
VMEM_LIMIT = 40 * 1024 * 1024

NT = (((1,), (1,)), ((), ()))
NN = (((1,), (0,)), ((), ()))


def dot(a, b, dims=NN):
    return lax.dot_general(a, b, dims, preferred_element_type=jnp.float32)


def split2(x):
    hi = x.astype(jnp.bfloat16)
    return hi, (x - hi.astype(jnp.float32)).astype(jnp.bfloat16)


def inverse_factor(gram):
    n = gram.shape[0]
    rows = lax.broadcasted_iota(jnp.int32, (n, n), 0)
    cols = lax.broadcasted_iota(jnp.int32, (n, n), 1)
    eye = (rows == cols).astype(jnp.float32)
    both = jnp.concatenate([gram, eye], axis=1)
    count, shape = n // 8, (8, 2 * n)
    tiles = [both[8 * t : 8 * t + 8] for t in range(count)]
    sub = lax.broadcasted_iota(jnp.int32, shape, 0)
    out = []
    for b in range(count):
        column = {
            t: [jnp.broadcast_to(tiles[t][:, 8 * b + s : 8 * b + s + 1], shape) for s in range(8)]
            for t in range(b, count)
        }
        row = [jnp.broadcast_to(tiles[b][s : s + 1], shape) for s in range(8)]
        a = [
            [jnp.broadcast_to(column[b][j][s : s + 1], shape) if j >= s else None for j in range(8)]
            for s in range(8)
        ]
        done = jnp.zeros(shape, jnp.float32)
        for s in range(8):
            root = lax.rsqrt(a[s][s])
            inv = root * root
            inv = inv * (2.0 - a[s][s] * inv)
            step = row[s] * inv
            done = jnp.where(sub == s, row[s] * root, done)
            for i in range(s + 1, 8):
                part = a[s][i] * inv
                for j in range(i, 8):
                    a[i][j] = a[i][j] - part * a[s][j]
                row[i] = row[i] - a[s][i] * step
                for t in range(b + 1, count):
                    column[t][i] = column[t][i] - column[t][s] * part
            for t in range(b + 1, count):
                tiles[t] = tiles[t] - column[t][s] * step
        out.append(done)
    return jnp.concatenate(out, axis=0)[:, n:]


def place_of(own, n_row, n_dev):
    here, chip, core = own[0], own[1], own[2]

    def at_device(r, c):
        dr, dc, dk = here ^ r, chip ^ (c // 2), core ^ (c % 2)
        dx, dy = dc & 1, dc >> 1
        order = jnp.where(dr < 2, 2 * dx, 4 + 2 * dy) + jnp.where(
            jnp.where(dr < 2, dy, dx) > 0, n_dev // 4, 0
        )
        return dk * (n_dev // 2) + order + (dr & 1)

    def device_at(d):
        far, second = (d >> 2) & 1, (d >> 3) & 1
        first = (d >> 1) & 1
        dc = jnp.where(far == 0, 2 * second + first, 2 * first + second)
        return here ^ (2 * far + (d & 1)), 2 * (chip ^ dc) + (core ^ (d >> 4))

    return at_device, device_at


def copy_in(pairs, sems):
    copies = [pltpu.make_async_copy(src, dst, sems.at[i]) for i, (src, dst) in enumerate(pairs)]
    for copy in copies:
        copy.start()
    return copies


def left_half(shape):
    return lax.broadcasted_iota(jnp.int32, shape, len(shape) - 1) < 64


def store_twice(pair, twice, q, x):
    pair[q] = x.astype(pair.dtype)
    turned, left = pltpu.roll(x, 64, 1), left_half(x.shape)
    twice[2 * q] = jnp.where(left, x, turned).astype(twice.dtype)
    twice[2 * q + 1] = jnp.where(left, turned, x).astype(twice.dtype)


def gather_pair(q, first, second):
    left = left_half(first.shape[1:])
    apart = jnp.where(left, first[2 * q + 1], second[2 * q])
    return jnp.where(left, first[2 * q], second[2 * q + 1]) + pltpu.roll(apart, 64, 1)


def add_products(n_group, blk, dims, lists, from_at, source, to_at, first, second):
    left = left_half(source.shape[1:])

    def multiply(pairs):
        return [
            dot(
                jnp.where(left, source[lists[from_at + 2 * p]], source[lists[from_at + 2 * p + 1]]),
                blk[p],
                dims,
            )
            for p in pairs
        ]

    def add(pairs, prods):
        for p, prod in zip(pairs, prods):
            a, b = lists[to_at + 2 * p], lists[to_at + 2 * p + 1]
            first[a] = first[a] + prod
            second[b] = second[b] + prod

    def group(i, carry):
        batches = [
            [i * UNROLL + at + u for u in range(BATCH)] for at in range(0, UNROLL, BATCH)
        ]
        prods = multiply(batches[0])
        for now, later in zip(batches, batches[1:]):
            ahead = multiply(later)
            add(now, prods)
            prods = ahead
        add(batches[-1], prods)
        return carry

    lax.fori_loop(0, n_group, group, 0)


def unpack(
    n_row, n_col, own, mine, other, lists, place, blk, vs, vd, rm, ic, ints, meta, sems, small
):
    n_dev = n_row * n_col
    k = vs.shape[1]
    half = k // 2
    rblk, cblk = 2 * n_col, 2 * n_row
    vec_at = OFF_CAP * half
    meta_at = vec_at + k
    at_device, device_at = place_of(own, n_row, n_dev)
    slots = 2 * blk.shape[0]

    first, second = pl.ds(0, n_dev // 2), pl.ds(n_dev // 2, n_dev // 2)
    for copy in copy_in([(mine, small.at[first]), (other, small.at[second])], sems):
        copy.wait()
    for d in range(n_dev):
        rows = small[d, meta_at : meta_at + META, :].astype(jnp.float32)
        ints[d : d + 1, :] = rows[8:9].astype(jnp.int32)
    to_scalars = pltpu.make_async_copy(ints, meta, sems.at[2])
    to_scalars.start()

    for r in range(n_row):
        for c in range(n_col):
            q, p, d = c * n_row + r, r * n_col + c, at_device(r, c)
            rows = small[d, meta_at : meta_at + META, :].astype(jnp.float32)
            rm[p] = jnp.broadcast_to(rows[0:1] + rows[1:2] + rows[2:3], (8, 128))
            ic[q] = jnp.broadcast_to(rows[3:4] + rows[4:5] + rows[5:6], (8, 128))
            store_twice(vs, vd, q, small[d, vec_at : vec_at + k, :].astype(jnp.float32))
    to_scalars.wait()

    lanes = lax.broadcasted_iota(jnp.int32, (half, 128), 1)

    def device(d, n):
        count = meta[d, 2 * OFF_CAP]
        count = jnp.where(count > OFF_CAP, 0, count)
        r, c = device_at(d)
        for s in range(OFF_CAP):
            lists[n + s] = c * cblk + meta[d, OFF_CAP + s]
            lists[slots + n + s] = r * rblk + meta[d, s]
            x = small[d, s * half : (s + 1) * half, :].astype(jnp.float32)
            turned = pltpu.roll(x, 64, 1)
            side = (n + s) % 2
            here = (lanes // 64) == side
            even = jnp.where(here, jnp.where(side == 0, x, turned), 0.0)
            odd = jnp.where(here, jnp.where(side == 0, turned, x), 0.0)
            at = pl.multiple_of(side * k, k)
            both = jnp.concatenate([even, odd], axis=0).astype(jnp.bfloat16)
            blk[(n + s) // 2, pl.ds(at, k), :] = both
        return n + count

    n_live = lax.fori_loop(0, n_dev, device, jnp.int32(0))
    for u in range(2 * UNROLL - 1):
        lists[n_live + u] = 0
        lists[slots + n_live + u] = 0
        at = pl.multiple_of((n_live + u) % 2 * k, k)
        blk[(n_live + u) // 2, pl.ds(at, k), :] = jnp.zeros((k, 128), jnp.bfloat16)
    lists[2 * slots] = (n_live + 2 * UNROLL - 1) // (2 * UNROLL)

    for r in range(n_row):
        h = jnp.int32(0)
        for c in range(n_col):
            h = jnp.where(meta[at_device(r, c), 2 * OFF_CAP] > OFF_CAP, c, h)
        lists[2 * slots + 1 + r] = h
        index = small[at_device(r, h), meta_at : meta_at + META, :].astype(jnp.float32)
        place[r : r + 1, :] = index[7:8] * float(rblk) + index[6:7]


def iterate(n_row, n_col, n_cap, total, own, lists, place, *rest):
    sources, fulls, out = rest[:5], rest[5:13], rest[13]
    sems, full, tmp, home, blk, vs, vd, rm, ic = rest[14:23]
    w, w1, w2, wt, wd, y, y1, y2, ph, linv = rest[23:]
    slots = 2 * blk.shape[0]
    n_dev = n_row * n_col
    k = vs.shape[1]
    half = k // 2
    rpairs, cpairs = n_col, n_row
    rblk, cblk = 2 * rpairs, 2 * cpairs
    part = n_cap // n_col
    width = cpairs * 128
    at_device, _ = place_of(own, n_row, n_dev)

    def laid_out(refs, whole):
        at, pairs = 0, []
        for ref in refs:
            pairs.append((ref, whole.at[pl.ds(at, ref.shape[0])]))
            at += ref.shape[0]
        return pairs

    copies = copy_in(laid_out(fulls, full) + list(zip(sources, (blk, vs, vd, rm, ic))), sems)
    for copy in copies[: len(fulls)]:
        copy.wait()
    n_group = lists[2 * slots]

    left = lax.broadcasted_iota(jnp.int32, (rblk, 128), 1) < 64
    homes = []
    for r in range(n_row):
        homes.append(lists[2 * slots + 1 + r])
        want = lax.broadcasted_iota(jnp.int32, (cblk * rblk, n_cap), 0).astype(jnp.float32)
        select = jnp.where(want == place[r : r + 1, :], 1.0, 0.0).astype(jnp.bfloat16)

        parts = [at_device(r, 2 * i + j) for j in range(2) for i in range(n_col // 2)]

        def build(i, carry, parts=parts, select=select):
            ms = [4 * i + d for d in range(4)]
            denses = []
            for m in ms:
                at = pl.multiple_of(m * part, part)
                slots = jnp.concatenate([full[d, pl.ds(at, part), :] for d in parts], axis=0)
                denses.append(dot(select, slots))
            for m, dense in zip(ms, denses):
                for u in range(cpairs):
                    a = dense[2 * u * rblk : (2 * u + 1) * rblk]
                    b = dense[(2 * u + 1) * rblk : (2 * u + 2) * rblk]
                    even = jnp.where(left, a, pltpu.roll(b, 64, 1))
                    odd = jnp.where(left, pltpu.roll(a, 64, 1), b)
                    tmp[u, pl.ds(m, rblk, stride=k), :] = even
                    tmp[u, pl.ds(m + half, rblk, stride=k), :] = odd
            return carry

        lax.fori_loop(0, half // 4, build, 0, unroll=2)

        def cut(i, carry, r=r):
            at = pl.multiple_of(i * k, k)
            for u in range(cpairs):
                hi, lo = split2(tmp[u, pl.ds(at, k), :])
                home[r, pl.ds(at, k), u * 128 : (u + 1) * 128] = hi
                home[r, pl.ds(at, k), width + u * 128 : width + (u + 1) * 128] = lo
            return carry

        lax.fori_loop(0, rblk, cut, 0, unroll=8)

    def clear(refs):
        for ref in refs:
            for q in range(ref.shape[0]):
                ref[q] = jnp.zeros_like(ref[q])

    clear([y, y1, y2, w1, w2])
    for copy in copies[len(fulls) :]:
        copy.wait()

    def iteration(it, carry):
        @pl.when(it > 0)
        def _():
            lh, ll = split2(linv[...])
            turn = jnp.concatenate([lh, lh, ll], axis=1)
            for q in range(0, n_dev, 4):
                hi = jnp.concatenate([ph[q + d, :k, :] for d in range(4)], axis=1)
                lo = jnp.concatenate([ph[q + d, k:, :] for d in range(4)], axis=1)
                current = dot(turn, jnp.concatenate([hi, lo, hi], axis=0))
                for d in range(4):
                    x = current[:, d * 128 : (d + 1) * 128] * ic[q + d, 0:1, :]
                    store_twice(vs, vd, q + d, x)

        for r in range(n_row):
            base = homes[r] * cpairs
            vec = jnp.concatenate([vs[base + u] for u in range(cpairs)] * 2, axis=1)
            for p in range(0, rpairs, 2):
                prod = dot(vec, home[r, p * 128 : (p + 2) * 128, :], NT)
                w[r * rpairs + p] = prod[:, :128]
                w[r * rpairs + p + 1] = prod[:, 128:]

        add_products(n_group, blk, NT, lists, 0, vd, slots, w1, w2)
        for p in range(n_dev):
            x = w[p] + gather_pair(p, w1, w2)
            store_twice(wt, wd, p, x * rm[p, 0:1, :])

        def back(r, u):
            vec = jnp.concatenate([wt[r * rpairs + p] for p in range(rpairs)], axis=1)
            cols = slice(u * 128, (u + 2) * 128)
            tail = slice(width + u * 128, width + (u + 2) * 128)
            return dot(vec, home[r, :, cols]) + dot(vec, home[r, :, tail])

        steps = [(r, u) for r in range(n_row) for u in range(0, cpairs, 2)]
        prod = back(*steps[0])
        for i, (r, u) in enumerate(steps):
            ahead = back(*steps[i + 1]) if i + 1 < len(steps) else None
            q = homes[r] * cpairs + u
            y[q] = y[q] + prod[:, :128]
            y[q + 1] = y[q + 1] + prod[:, 128:]
            prod = ahead

        add_products(n_group, blk, NN, lists, slots, wd, 0, y1, y2)

        both = jnp.zeros((2 * k, k), jnp.float32)
        for q in range(0, n_dev, 4):
            his, los = [], []
            for d in range(q, q + 4):
                x = y[d] + gather_pair(d, y1, y2)
                hi, lo = split2(x * ic[d, 0:1, :])
                ph[d, :k, :] = hi
                ph[d, k:, :] = lo
                his.append(hi)
                los.append(lo)
            hi = jnp.concatenate(his, axis=1)
            lo = jnp.concatenate(los, axis=1)
            both = both + dot(jnp.concatenate([hi, lo], axis=0), hi, NT)
        gram = (both[:k] + (both[k:] + both[k:].T)) / total
        clear([y, y1, y2, w1, w2])
        linv[...] = inverse_factor(gram)
        return carry

    lax.fori_loop(0, ITERS, iteration, 0)
    lh, ll = split2(linv[...])
    q = (2 * own[1] + own[2]) * n_row + own[0]
    hi, lo = ph[q, :k, :], ph[q, k:, :]
    w[0] = dot(lh, hi) + dot(ll, hi) + dot(lh, lo)
    even, odd = w[0, pl.ds(0, half, stride=2), :], w[0, pl.ds(1, half, stride=2), :]
    left = left_half(even.shape)
    first = jnp.where(left, even, pltpu.roll(odd, 64, 1))
    second = jnp.where(left, pltpu.roll(even, 64, 1), odd)
    for i in range(half):
        out[0:1, i * 128 : (i + 1) * 128] = first[i : i + 1]
        out[1:2, i * 128 : (i + 1) * 128] = second[i : i + 1]


def split3(x):
    a = lax.reduce_precision(x, 8, 7)
    b = lax.reduce_precision(x - a, 8, 7)
    return [v.astype(jnp.bfloat16) for v in (a, b, x - a - b)]


def swap(x, axis, distance):
    size = lax.axis_size(axis)
    return lax.ppermute(x, axis, [(i, i ^ distance) for i in range(size)])


def along_rows(x):
    return [x] + [swap(x, "row", s) for s in range(1, lax.axis_size("row"))]


def along_one_chip_axis(x):
    near, far = jnp.stack(x[:2]), jnp.stack(x[2:])
    return [
        jnp.concatenate([near, swap(near, "chip", 1)]),
        jnp.concatenate([far, swap(far, "chip", 2)]),
    ]


def along_other_chip_axis(x):
    near, far = x
    return [swap(near, "chip", 2), swap(far, "chip", 1)]


def full_part(tile, has_full, n_chip, part, chip, core):
    tile = tile.reshape(2, n_chip, part, tile.shape[1])
    none = jnp.zeros(tile.shape[1:], tile.dtype)
    kept, sent = (
        jnp.where(has_full, lax.dynamic_index_in_dim(tile, i, 0, False), none)
        for i in (core, 1 - core)
    )
    both = kept + swap(sent, "core", 1)
    mine = lax.dynamic_index_in_dim(both, chip, 0, False)
    for s in range(1, n_chip):
        mine = mine + swap(lax.dynamic_index_in_dim(both, chip ^ s, 0, False), "chip", s)
    return mine


def whole_on_each(n_row, n_col, blocks, block_row, block_col, counts, vectors, row_mass, col_mass):
    tile = blocks[0, 0]
    n_cap = tile.shape[0]
    own, bsize = row_mass.shape
    k = vectors.shape[1] // bsize
    half = bsize // 2
    part = n_cap // n_col
    n_dev = n_row * n_col
    count = counts[0, 0]
    has_full = count > OFF_CAP
    bf16 = jnp.bfloat16
    row, chip, core = (lax.axis_index(name) for name in ("row", "chip", "core"))

    off = tile[:OFF_CAP].reshape(OFF_CAP * half, 128)
    inv_col = 1.0 / jnp.sqrt(col_mass)
    scaled = (vectors.reshape(own, k, bsize) * inv_col[:, None, :]).astype(bf16)
    scaled = scaled.transpose(1, 0, 2).reshape(k, own * bsize)
    mass = row_mass.reshape(own, half, 2).transpose(0, 2, 1).reshape(own * bsize)
    rows, cols = block_row[0, 0], block_col[0, 0]
    short = jnp.concatenate(
        [rows[:OFF_CAP], cols[:OFF_CAP], count[None], jnp.zeros(128 - 2 * OFF_CAP - 1, jnp.int32)]
    )
    meta = [v.astype(bf16) for v in (rows, cols, short)]
    meta = split3(mass) + split3(inv_col.reshape(own * bsize)) + meta
    meta = jnp.stack(meta + [jnp.zeros(128, bf16)] * (META - len(meta)))
    small = jnp.concatenate([off, scaled, meta], axis=0)
    home = full_part(tile, has_full, n_col // 2, part, chip, core)
    home = home.reshape(part, half, 128).transpose(1, 0, 2).reshape(half * part, 128)

    together = lax.optimization_barrier
    where = jnp.stack([row, chip, core]).astype(jnp.int32)
    home, smalls, where = together((home, along_rows(small), where))
    homes, smalls = along_rows(home), along_one_chip_axis(smalls)
    smalls, homes[1] = together((smalls, homes[1]))
    smalls = jnp.concatenate(smalls + along_other_chip_axis(smalls))
    homes, smalls = together((homes, smalls))
    others = swap(smalls, "core", 1)
    homes = along_one_chip_axis(homes)
    last = along_other_chip_axis(homes)

    height, width = 2 * n_col * bsize, 2 * n_row * bsize
    slots = n_dev * OFF_CAP + 2 * UNROLL
    f32, i32, vmem, smem = jnp.float32, jnp.int32, pltpu.VMEM, pltpu.SMEM
    pair, twice, mass = (n_dev, k, 128), (2 * n_dev, k, 128), (n_dev, 8, 128)
    smem_spec, vmem_spec, any_spec = (pl.BlockSpec(memory_space=m) for m in (smem, vmem, pl.ANY))
    arrays = [
        ((8, 128), f32), ((slots // 2, 128, 128), bf16), (pair, bf16), (twice, bf16), (mass, f32), (mass, f32),
    ]
    lists, *unpacked = pl.pallas_call(
        functools.partial(unpack, n_row, n_col),
        out_shape=[jax.ShapeDtypeStruct((2 * slots + 8,), i32)]
        + [jax.ShapeDtypeStruct(*v) for v in arrays],
        in_specs=[smem_spec, any_spec, any_spec],
        out_specs=[smem_spec] + [vmem_spec] * len(arrays),
        scratch_shapes=[
            vmem((n_dev, 128), i32),
            smem((n_dev, 128), i32),
            pltpu.SemaphoreType.DMA((3,)),
            vmem((n_dev,) + small.shape, bf16),
        ],
        compiler_params=pltpu.CompilerParams(vmem_limit_bytes=VMEM_LIMIT),
        cost_estimate=pl.CostEstimate(
            flops=0, bytes_accessed=4 * n_dev * small.size * 2, transcendentals=0
        ),
        name="unpack",
    )(where, smalls, others)
    last, lists = together((last, lists))
    mine = homes + last
    fulls = mine + [swap(v, "core", 1) for v in mine]
    return pl.pallas_call(
        functools.partial(iterate, n_row, n_col, n_cap, float(n_dev * own * bsize)),
        out_shape=jax.ShapeDtypeStruct((own, k * bsize), f32),
        in_specs=[smem_spec] * 2 + [vmem_spec] + [any_spec] * (5 + len(fulls)),
        out_specs=vmem_spec,
        scratch_shapes=[
            pltpu.SemaphoreType.DMA((5 + len(fulls),)),
            vmem((n_dev,) + home.shape, bf16),
            vmem((n_row, height, 128), f32),
            vmem((n_row, height, 2 * width), bf16),
            *[vmem(*v) for v in arrays[1:]],
            vmem(pair, f32), vmem(twice, f32), vmem(twice, f32), vmem(pair, bf16), vmem(twice, bf16),
            vmem(pair, f32), vmem(twice, f32), vmem(twice, f32),
            vmem((n_dev, 2 * k, 128), bf16),
            vmem((k, k), f32),
        ],
        compiler_params=pltpu.CompilerParams(vmem_limit_bytes=VMEM_LIMIT),
        name="iterate",
    )(where, lists, *unpacked, *fulls)


def rotate(projected, gram):
    lower = jnp.linalg.cholesky(gram)
    inverse = lax.linalg.triangular_solve(
        lower, jnp.eye(gram.shape[0], dtype=jnp.float32), left_side=True, lower=True
    )
    return jnp.einsum(
        "kl,bli->bki",
        inverse,
        projected,
        precision=lax.Precision.HIGHEST,
        preferred_element_type=jnp.float32,
    )


def local_gram(projected):
    return jnp.einsum(
        "bki,bli->kl",
        projected,
        projected,
        precision=lax.Precision.HIGHEST,
        preferred_element_type=jnp.float32,
    )


def split_by_tile(blocks, block_row, block_col, counts, vectors, row_mass, col_mass):
    tile = blocks[0, 0]
    n_cap = tile.shape[0]
    bsize = row_mass.shape[1]
    vecs = vectors.shape[1] // bsize
    own = vectors.shape[0]
    n_row = lax.axis_size("row")
    n_col = lax.axis_size("col")
    row_panel = own * n_col
    col_panel = own * n_row
    total_boxes = float(own * bsize * n_row * n_col)
    rows_idx = block_row[0, 0]
    cols_idx = block_col[0, 0]
    live = jnp.arange(n_cap) < counts[0, 0]
    fwd_ids = jnp.where(live, rows_idx, row_panel)
    bwd_ids = jnp.where(live, cols_idx, col_panel)
    square = tile.reshape(n_cap, bsize, bsize)
    inv_col = 1.0 / jnp.sqrt(col_mass)
    current = vectors.reshape(own, vecs, bsize)
    for step in range(ITERS):
        scaled = (current * inv_col[:, None, :]).astype(jnp.bfloat16).reshape(own, vecs * bsize)
        panel = lax.all_gather(scaled, "row", axis=0, tiled=True)
        forward_taken = jnp.take(panel.reshape(col_panel, vecs, bsize), cols_idx, axis=0)
        forward_product = jnp.einsum(
            "bij,bkj->bki", square, forward_taken, preferred_element_type=jnp.float32
        )
        forward_summed = jax.ops.segment_sum(forward_product, fwd_ids, num_segments=row_panel + 1)
        rows_sum = lax.psum_scatter(
            forward_summed[:row_panel].reshape(row_panel, vecs * bsize),
            "col",
            scatter_dimension=0,
            tiled=True,
        )
        weighted = (rows_sum.reshape(own, vecs, bsize) * row_mass[:, None, :]).astype(jnp.bfloat16)
        whole_rows = lax.all_gather(weighted.reshape(own, vecs * bsize), "col", axis=0, tiled=True)
        taken = jnp.take(whole_rows.reshape(row_panel, vecs, bsize), rows_idx, axis=0)
        product = jnp.einsum("bij,bki->bkj", square, taken, preferred_element_type=jnp.float32)
        summed = jax.ops.segment_sum(product, bwd_ids, num_segments=col_panel + 1)
        cols_sum = lax.psum_scatter(
            summed[:col_panel].reshape(col_panel, vecs * bsize),
            "row",
            scatter_dimension=0,
            tiled=True,
        )
        projected = cols_sum.reshape(own, vecs, bsize) * inv_col[:, None, :]
        gram = lax.psum(local_gram(projected), ("row", "col")) / total_boxes
        current = rotate(projected, gram)
    return current.reshape(own, vecs * bsize)


def fits(n_row, n_col, blocks, vectors, row_mass):
    own, bsize = row_mass.shape[0] // (n_row * n_col), row_mass.shape[1]
    n_cap = blocks.shape[2]
    dense = n_row * (own * n_col * bsize) * (own * n_row * bsize) * 4
    shapes = own * bsize == 128 and vectors.shape[1] == bsize * bsize and n_cap == 128
    return dense <= VMEM_LIMIT // 4 and shapes and n_cap % (16 * n_col) == 0 and n_row == 4 and n_col == 8


def solution(mesh):
    n_row, n_col = mesh.shape["row"], mesh.shape["col"]

    def run(blocks, block_row, block_col, counts, vectors, row_mass, col_mass):
        args = (blocks, block_row, block_col, counts, vectors, row_mass, col_mass)
        if fits(n_row, n_col, blocks, vectors, row_mass):
            devices = mesh.devices.reshape(n_row, n_col // 2, 2)
            grid, col = jax.sharding.Mesh(devices, ("row", "chip", "core")), ("chip", "core")
            body = functools.partial(whole_on_each, n_row, n_col)
        else:
            grid, col, body = mesh, ("col",), split_by_tile
        by_row, by_col = P(("row",) + col, None), P(col + ("row",), None)
        in_specs = (
            P("row", col, None, None), P("row", col, None), P("row", col, None), P("row", col),
            by_col, by_row, by_col,
        )
        return jax.shard_map(
            body, mesh=grid, in_specs=in_specs, out_specs=by_col, check_vma=False
        )(*args)

    return run
```

```python
import functools

import jax
import jax.numpy as jnp
from jax import lax
from jax.experimental import pallas as pl
from jax.experimental.pallas import tpu as pltpu
from jax.sharding import PartitionSpec as P

ITERS = 4
OFF_CAP = 8
META = 16
UNROLL = 16
BATCH = 4
VMEM_LIMIT = 40 * 1024 * 1024

NT = (((1,), (1,)), ((), ()))
NN = (((1,), (0,)), ((), ()))


def dot(a, b, dims=NN):
    return lax.dot_general(a, b, dims, preferred_element_type=jnp.float32)


def split2(x):
    hi = x.astype(jnp.bfloat16)
    return hi, (x - hi.astype(jnp.float32)).astype(jnp.bfloat16)


def inverse_factor(gram):
    n = gram.shape[0]
    rows = lax.broadcasted_iota(jnp.int32, (n, n), 0)
    cols = lax.broadcasted_iota(jnp.int32, (n, n), 1)
    eye = (rows == cols).astype(jnp.float32)
    both = jnp.concatenate([gram, eye], axis=1)
    count, shape = n // 8, (8, 2 * n)
    tiles = [both[8 * t : 8 * t + 8] for t in range(count)]
    sub = lax.broadcasted_iota(jnp.int32, shape, 0)
    out = []
    for b in range(count):
        column = {
            t: [jnp.broadcast_to(tiles[t][:, 8 * b + s : 8 * b + s + 1], shape) for s in range(8)]
            for t in range(b, count)
        }
        row = [jnp.broadcast_to(tiles[b][s : s + 1], shape) for s in range(8)]
        a = [
            [jnp.broadcast_to(column[b][j][s : s + 1], shape) if j >= s else None for j in range(8)]
            for s in range(8)
        ]
        done = jnp.zeros(shape, jnp.float32)
        for s in range(8):
            root = lax.rsqrt(a[s][s])
            inv = root * root
            inv = inv * (2.0 - a[s][s] * inv)
            step = row[s] * inv
            done = jnp.where(sub == s, row[s] * root, done)
            for i in range(s + 1, 8):
                part = a[s][i] * inv
                for j in range(i, 8):
                    a[i][j] = a[i][j] - part * a[s][j]
                row[i] = row[i] - a[s][i] * step
                for t in range(b + 1, count):
                    column[t][i] = column[t][i] - column[t][s] * part
            for t in range(b + 1, count):
                tiles[t] = tiles[t] - column[t][s] * step
        out.append(done)
    return jnp.concatenate(out, axis=0)[:, n:]


def place_of(own, n_row, n_dev):
    here, chip, core = own[0], own[1], own[2]

    def at_device(r, c):
        dr, dc, dk = here ^ r, chip ^ (c // 2), core ^ (c % 2)
        dx, dy = dc & 1, dc >> 1
        order = jnp.where(dr < 2, 2 * dx, 4 + 2 * dy) + jnp.where(
            jnp.where(dr < 2, dy, dx) > 0, n_dev // 4, 0
        )
        return dk * (n_dev // 2) + order + (dr & 1)

    def device_at(d):
        far, second = (d >> 2) & 1, (d >> 3) & 1
        first = (d >> 1) & 1
        dc = jnp.where(far == 0, 2 * second + first, 2 * first + second)
        return here ^ (2 * far + (d & 1)), 2 * (chip ^ dc) + (core ^ (d >> 4))

    return at_device, device_at


def copy_in(pairs, sems):
    copies = [pltpu.make_async_copy(src, dst, sems.at[i]) for i, (src, dst) in enumerate(pairs)]
    for copy in copies:
        copy.start()
    return copies


def clear(refs):
    for ref in refs:
        for q in range(ref.shape[0]):
            ref[q] = jnp.zeros_like(ref[q])


def left_half(shape):
    return lax.broadcasted_iota(jnp.int32, shape, len(shape) - 1) < 64


def store_twice(pair, twice, q, x):
    pair[q] = x.astype(pair.dtype)
    turned, left = pltpu.roll(x, 64, 1), left_half(x.shape)
    twice[2 * q] = jnp.where(left, x, turned).astype(twice.dtype)
    twice[2 * q + 1] = jnp.where(left, turned, x).astype(twice.dtype)


def gather_pair(q, first, second):
    left = left_half(first.shape[1:])
    apart = jnp.where(left, first[2 * q + 1], second[2 * q])
    return jnp.where(left, first[2 * q], second[2 * q + 1]) + pltpu.roll(apart, 64, 1)


def add_products(n_group, blk, dims, lists, from_at, source, to_at, first, second):
    left = left_half(source.shape[1:])

    def multiply(pairs):
        return [
            dot(
                jnp.where(left, source[lists[from_at + 2 * p]], source[lists[from_at + 2 * p + 1]]),
                blk[p],
                dims,
            )
            for p in pairs
        ]

    def add(pairs, prods):
        for p, prod in zip(pairs, prods):
            a, b = lists[to_at + 2 * p], lists[to_at + 2 * p + 1]
            first[a] = first[a] + prod
            second[b] = second[b] + prod

    def group(i, carry):
        batches = [
            [i * UNROLL + at + u for u in range(BATCH)] for at in range(0, UNROLL, BATCH)
        ]
        prods = multiply(batches[0])
        for now, later in zip(batches, batches[1:]):
            ahead = multiply(later)
            add(now, prods)
            prods = ahead
        add(batches[-1], prods)
        return carry

    lax.fori_loop(0, n_group, group, 0)


def unpack(
    n_row, n_col, own, mine, other,
    lists, place, blk, vs, vd, rm, ic, w1, w2, ints, meta, sems, small,
):
    n_dev = n_row * n_col
    k = vs.shape[1]
    half = k // 2
    rblk, cblk = 2 * n_col, 2 * n_row
    vec_at = OFF_CAP * half
    meta_at = vec_at + k
    at_device, device_at = place_of(own, n_row, n_dev)
    slots = 2 * blk.shape[0]

    first, second = pl.ds(0, n_dev // 2), pl.ds(n_dev // 2, n_dev // 2)
    for copy in copy_in([(mine, small.at[first]), (other, small.at[second])], sems):
        copy.wait()
    for d in range(n_dev):
        rows = small[d, meta_at : meta_at + META, :].astype(jnp.float32)
        ints[d : d + 1, :] = rows[8:9].astype(jnp.int32)
    to_scalars = pltpu.make_async_copy(ints, meta, sems.at[2])
    to_scalars.start()

    for r in range(n_row):
        for c in range(n_col):
            q, p, d = c * n_row + r, r * n_col + c, at_device(r, c)
            rows = small[d, meta_at : meta_at + META, :].astype(jnp.float32)
            rm[p] = jnp.broadcast_to(rows[0:1] + rows[1:2] + rows[2:3], (8, 128))
            ic[q] = jnp.broadcast_to(rows[3:4] + rows[4:5] + rows[5:6], (8, 128))
            store_twice(vs, vd, q, small[d, vec_at : vec_at + k, :].astype(jnp.float32))
    to_scalars.wait()

    lanes = lax.broadcasted_iota(jnp.int32, (half, 128), 1)

    def device(d, n):
        count = meta[d, 2 * OFF_CAP]
        count = jnp.where(count > OFF_CAP, 0, count)
        r, c = device_at(d)
        for s in range(OFF_CAP):
            lists[n + s] = c * cblk + meta[d, OFF_CAP + s]
            lists[slots + n + s] = r * rblk + meta[d, s]
            x = small[d, s * half : (s + 1) * half, :].astype(jnp.float32)
            turned = pltpu.roll(x, 64, 1)
            side = (n + s) % 2
            here = (lanes // 64) == side
            even = jnp.where(here, jnp.where(side == 0, x, turned), 0.0)
            odd = jnp.where(here, jnp.where(side == 0, turned, x), 0.0)
            at = pl.multiple_of(side * k, k)
            both = jnp.concatenate([even, odd], axis=0).astype(jnp.bfloat16)
            blk[(n + s) // 2, pl.ds(at, k), :] = both
        return n + count

    n_live = lax.fori_loop(0, n_dev, device, jnp.int32(0))
    for u in range(2 * UNROLL - 1):
        lists[n_live + u] = 0
        lists[slots + n_live + u] = 0
        at = pl.multiple_of((n_live + u) % 2 * k, k)
        blk[(n_live + u) // 2, pl.ds(at, k), :] = jnp.zeros((k, 128), jnp.bfloat16)
    lists[2 * slots] = (n_live + 2 * UNROLL - 1) // (2 * UNROLL)

    for r in range(n_row):
        h = jnp.int32(0)
        for c in range(n_col):
            h = jnp.where(meta[at_device(r, c), 2 * OFF_CAP] > OFF_CAP, c, h)
        lists[2 * slots + 1 + r] = h
        index = small[at_device(r, h), meta_at : meta_at + META, :].astype(jnp.float32)
        place[r : r + 1, :] = index[7:8] * float(rblk) + index[6:7]

    clear([w1, w2])
    add_products(lists[2 * slots], blk, NT, lists, 0, vd, slots, w1, w2)


def iterate(n_row, n_col, n_cap, total, own, lists, place, *rest):
    sources, fulls, out = rest[:7], rest[7:15], rest[15]
    sems, full, tmp, home, blk, vs, vd, rm, ic, w1, w2 = rest[16:27]
    w, wt, wd, y, y1, y2, ph, linv = rest[27:]
    slots = 2 * blk.shape[0]
    n_dev = n_row * n_col
    k = vs.shape[1]
    half = k // 2
    rpairs, cpairs = n_col, n_row
    rblk, cblk = 2 * rpairs, 2 * cpairs
    part = n_cap // n_col
    width = cpairs * 128
    at_device, _ = place_of(own, n_row, n_dev)

    def laid_out(refs, whole):
        at, pairs = 0, []
        for ref in refs:
            pairs.append((ref, whole.at[pl.ds(at, ref.shape[0])]))
            at += ref.shape[0]
        return pairs

    copies = copy_in(laid_out(fulls, full) + list(zip(sources, (blk, vs, vd, rm, ic, w1, w2))), sems)
    for copy in copies[: len(fulls)]:
        copy.wait()
    n_group = lists[2 * slots]

    left = lax.broadcasted_iota(jnp.int32, (rblk, 128), 1) < 64
    homes = []
    for r in range(n_row):
        homes.append(lists[2 * slots + 1 + r])
        want = lax.broadcasted_iota(jnp.int32, (cblk * rblk, n_cap), 0).astype(jnp.float32)
        select = jnp.where(want == place[r : r + 1, :], 1.0, 0.0).astype(jnp.bfloat16)

        parts = [at_device(r, 2 * i + j) for j in range(2) for i in range(n_col // 2)]

        def build(i, carry, parts=parts, select=select):
            ms = [4 * i + d for d in range(4)]
            denses = []
            for m in ms:
                at = pl.multiple_of(m * part, part)
                slots = jnp.concatenate([full[d, pl.ds(at, part), :] for d in parts], axis=0)
                denses.append(dot(select, slots))
            for m, dense in zip(ms, denses):
                for u in range(cpairs):
                    a = dense[2 * u * rblk : (2 * u + 1) * rblk]
                    b = dense[(2 * u + 1) * rblk : (2 * u + 2) * rblk]
                    even = jnp.where(left, a, pltpu.roll(b, 64, 1))
                    odd = jnp.where(left, pltpu.roll(a, 64, 1), b)
                    tmp[u, pl.ds(m, rblk, stride=k), :] = even
                    tmp[u, pl.ds(m + half, rblk, stride=k), :] = odd
            return carry

        lax.fori_loop(0, half // 4, build, 0, unroll=2)

        def cut(i, carry, r=r):
            at = pl.multiple_of(i * k, k)
            for u in range(cpairs):
                hi, lo = split2(tmp[u, pl.ds(at, k), :])
                home[r, pl.ds(at, k), u * 128 : (u + 1) * 128] = hi
                home[r, pl.ds(at, k), width + u * 128 : width + (u + 1) * 128] = lo
            return carry

        lax.fori_loop(0, rblk, cut, 0, unroll=8)

    clear([y, y1, y2])
    for copy in copies[len(fulls) :]:
        copy.wait()

    def iteration(it, carry):
        @pl.when(it > 0)
        def _():
            lh, ll = split2(linv[...])
            turn = jnp.concatenate([lh, lh, ll], axis=1)
            for q in range(0, n_dev, 4):
                hi = jnp.concatenate([ph[q + d, :k, :] for d in range(4)], axis=1)
                lo = jnp.concatenate([ph[q + d, k:, :] for d in range(4)], axis=1)
                current = dot(turn, jnp.concatenate([hi, lo, hi], axis=0))
                for d in range(4):
                    x = current[:, d * 128 : (d + 1) * 128] * ic[q + d, 0:1, :]
                    store_twice(vs, vd, q + d, x)

        for r in range(n_row):
            base = homes[r] * cpairs
            vec = jnp.concatenate([vs[base + u] for u in range(cpairs)] * 2, axis=1)
            for p in range(0, rpairs, 2):
                prod = dot(vec, home[r, p * 128 : (p + 2) * 128, :], NT)
                w[r * rpairs + p] = prod[:, :128]
                w[r * rpairs + p + 1] = prod[:, 128:]

        @pl.when(it > 0)
        def _():
            add_products(n_group, blk, NT, lists, 0, vd, slots, w1, w2)

        for p in range(n_dev):
            x = w[p] + gather_pair(p, w1, w2)
            store_twice(wt, wd, p, x * rm[p, 0:1, :])

        def back(r, u):
            vec = jnp.concatenate([wt[r * rpairs + p] for p in range(rpairs)], axis=1)
            cols = slice(u * 128, (u + 2) * 128)
            tail = slice(width + u * 128, width + (u + 2) * 128)
            return dot(vec, home[r, :, cols]) + dot(vec, home[r, :, tail])

        steps = [(r, u) for r in range(n_row) for u in range(0, cpairs, 2)]
        prod = back(*steps[0])
        for i, (r, u) in enumerate(steps):
            ahead = back(*steps[i + 1]) if i + 1 < len(steps) else None
            q = homes[r] * cpairs + u
            y[q] = y[q] + prod[:, :128]
            y[q + 1] = y[q + 1] + prod[:, 128:]
            prod = ahead

        add_products(n_group, blk, NN, lists, slots, wd, 0, y1, y2)

        both = jnp.zeros((2 * k, k), jnp.float32)
        for q in range(0, n_dev, 4):
            his, los = [], []
            for d in range(q, q + 4):
                x = y[d] + gather_pair(d, y1, y2)
                hi, lo = split2(x * ic[d, 0:1, :])
                ph[d, :k, :] = hi
                ph[d, k:, :] = lo
                his.append(hi)
                los.append(lo)
            hi = jnp.concatenate(his, axis=1)
            lo = jnp.concatenate(los, axis=1)
            both = both + dot(jnp.concatenate([hi, lo], axis=0), hi, NT)
        gram = (both[:k] + (both[k:] + both[k:].T)) / total
        clear([y, y1, y2, w1, w2])
        linv[...] = inverse_factor(gram)
        return carry

    lax.fori_loop(0, ITERS, iteration, 0)
    lh, ll = split2(linv[...])
    q = (2 * own[1] + own[2]) * n_row + own[0]
    hi, lo = ph[q, :k, :], ph[q, k:, :]
    w[0] = dot(lh, hi) + dot(ll, hi) + dot(lh, lo)
    even, odd = w[0, pl.ds(0, half, stride=2), :], w[0, pl.ds(1, half, stride=2), :]
    left = left_half(even.shape)
    first = jnp.where(left, even, pltpu.roll(odd, 64, 1))
    second = jnp.where(left, pltpu.roll(even, 64, 1), odd)
    for i in range(half):
        out[0:1, i * 128 : (i + 1) * 128] = first[i : i + 1]
        out[1:2, i * 128 : (i + 1) * 128] = second[i : i + 1]


def split3(x):
    a = lax.reduce_precision(x, 8, 7)
    b = lax.reduce_precision(x - a, 8, 7)
    return [v.astype(jnp.bfloat16) for v in (a, b, x - a - b)]


def swap(x, axis, distance):
    size = lax.axis_size(axis)
    return lax.ppermute(x, axis, [(i, i ^ distance) for i in range(size)])


def along_rows(x):
    return [x] + [swap(x, "row", s) for s in range(1, lax.axis_size("row"))]


def along_one_chip_axis(x):
    near, far = jnp.stack(x[:2]), jnp.stack(x[2:])
    return [
        jnp.concatenate([near, swap(near, "chip", 1)]),
        jnp.concatenate([far, swap(far, "chip", 2)]),
    ]


def along_other_chip_axis(x):
    near, far = x
    return [swap(near, "chip", 2), swap(far, "chip", 1)]


def full_part(tile, has_full, n_chip, part, chip, core):
    tile = tile.reshape(2, n_chip, part, tile.shape[1])
    none = jnp.zeros(tile.shape[1:], tile.dtype)
    kept, sent = (
        jnp.where(has_full, lax.dynamic_index_in_dim(tile, i, 0, False), none)
        for i in (core, 1 - core)
    )
    both = kept + swap(sent, "core", 1)
    mine = lax.dynamic_index_in_dim(both, chip, 0, False)
    for s in range(1, n_chip):
        mine = mine + swap(lax.dynamic_index_in_dim(both, chip ^ s, 0, False), "chip", s)
    return mine


def whole_on_each(n_row, n_col, blocks, block_row, block_col, counts, vectors, row_mass, col_mass):
    tile = blocks[0, 0]
    n_cap = tile.shape[0]
    own, bsize = row_mass.shape
    k = vectors.shape[1] // bsize
    half = bsize // 2
    part = n_cap // n_col
    n_dev = n_row * n_col
    count = counts[0, 0]
    has_full = count > OFF_CAP
    bf16 = jnp.bfloat16
    row, chip, core = (lax.axis_index(name) for name in ("row", "chip", "core"))

    off = tile[:OFF_CAP].reshape(OFF_CAP * half, 128)
    inv_col = 1.0 / jnp.sqrt(col_mass)
    scaled = (vectors.reshape(own, k, bsize) * inv_col[:, None, :]).astype(bf16)
    scaled = scaled.transpose(1, 0, 2).reshape(k, own * bsize)
    mass = row_mass.reshape(own, half, 2).transpose(0, 2, 1).reshape(own * bsize)
    rows, cols = block_row[0, 0], block_col[0, 0]
    short = jnp.concatenate(
        [rows[:OFF_CAP], cols[:OFF_CAP], count[None], jnp.zeros(128 - 2 * OFF_CAP - 1, jnp.int32)]
    )
    meta = [v.astype(bf16) for v in (rows, cols, short)]
    meta = split3(mass) + split3(inv_col.reshape(own * bsize)) + meta
    meta = jnp.stack(meta + [jnp.zeros(128, bf16)] * (META - len(meta)))
    small = jnp.concatenate([off, scaled, meta], axis=0)
    home = full_part(tile, has_full, n_col // 2, part, chip, core)
    home = home.reshape(part, half, 128).transpose(1, 0, 2).reshape(half * part, 128)

    together = lax.optimization_barrier
    where = jnp.stack([row, chip, core]).astype(jnp.int32)
    home, smalls, where = together((home, along_rows(small), where))
    homes, smalls = along_rows(home), along_one_chip_axis(smalls)
    smalls, homes[1] = together((smalls, homes[1]))
    smalls = jnp.concatenate(smalls + along_other_chip_axis(smalls))
    homes, smalls = together((homes, smalls))
    others = swap(smalls, "core", 1)
    homes = along_one_chip_axis(homes)
    last = along_other_chip_axis(homes)

    height, width = 2 * n_col * bsize, 2 * n_row * bsize
    slots = n_dev * OFF_CAP + 2 * UNROLL
    f32, i32, vmem, smem = jnp.float32, jnp.int32, pltpu.VMEM, pltpu.SMEM
    pair, twice, mass = (n_dev, k, 128), (2 * n_dev, k, 128), (n_dev, 8, 128)
    smem_spec, vmem_spec, any_spec = (pl.BlockSpec(memory_space=m) for m in (smem, vmem, pl.ANY))
    arrays = [
        ((8, 128), f32), ((slots // 2, 128, 128), bf16), (pair, bf16), (twice, bf16), (mass, f32), (mass, f32),
        (twice, f32), (twice, f32),
    ]
    lists, *unpacked = pl.pallas_call(
        functools.partial(unpack, n_row, n_col),
        out_shape=[jax.ShapeDtypeStruct((2 * slots + 8,), i32)]
        + [jax.ShapeDtypeStruct(*v) for v in arrays],
        in_specs=[smem_spec, any_spec, any_spec],
        out_specs=[smem_spec] + [vmem_spec] * len(arrays),
        scratch_shapes=[
            vmem((n_dev, 128), i32),
            smem((n_dev, 128), i32),
            pltpu.SemaphoreType.DMA((3,)),
            vmem((n_dev,) + small.shape, bf16),
        ],
        compiler_params=pltpu.CompilerParams(vmem_limit_bytes=VMEM_LIMIT),
        cost_estimate=pl.CostEstimate(
            flops=0, bytes_accessed=4 * n_dev * small.size * 2, transcendentals=0
        ),
        name="unpack",
    )(where, smalls, others)
    last, lists = together((last, lists))
    mine = homes + last
    fulls = mine + [swap(v, "core", 1) for v in mine]
    return pl.pallas_call(
        functools.partial(iterate, n_row, n_col, n_cap, float(n_dev * own * bsize)),
        out_shape=jax.ShapeDtypeStruct((own, k * bsize), f32),
        in_specs=[smem_spec] * 2 + [vmem_spec] + [any_spec] * (len(arrays) - 1 + len(fulls)),
        out_specs=vmem_spec,
        scratch_shapes=[
            pltpu.SemaphoreType.DMA((len(arrays) - 1 + len(fulls),)),
            vmem((n_dev,) + home.shape, bf16),
            vmem((n_row, height, 128), f32),
            vmem((n_row, height, 2 * width), bf16),
            *[vmem(*v) for v in arrays[1:]],
            vmem(pair, f32), vmem(pair, bf16), vmem(twice, bf16),
            vmem(pair, f32), vmem(twice, f32), vmem(twice, f32),
            vmem((n_dev, 2 * k, 128), bf16),
            vmem((k, k), f32),
        ],
        compiler_params=pltpu.CompilerParams(vmem_limit_bytes=VMEM_LIMIT),
        name="iterate",
    )(where, lists, *unpacked, *fulls)


def rotate(projected, gram):
    lower = jnp.linalg.cholesky(gram)
    inverse = lax.linalg.triangular_solve(
        lower, jnp.eye(gram.shape[0], dtype=jnp.float32), left_side=True, lower=True
    )
    return jnp.einsum(
        "kl,bli->bki",
        inverse,
        projected,
        precision=lax.Precision.HIGHEST,
        preferred_element_type=jnp.float32,
    )


def local_gram(projected):
    return jnp.einsum(
        "bki,bli->kl",
        projected,
        projected,
        precision=lax.Precision.HIGHEST,
        preferred_element_type=jnp.float32,
    )


def split_by_tile(blocks, block_row, block_col, counts, vectors, row_mass, col_mass):
    tile = blocks[0, 0]
    n_cap = tile.shape[0]
    bsize = row_mass.shape[1]
    vecs = vectors.shape[1] // bsize
    own = vectors.shape[0]
    n_row = lax.axis_size("row")
    n_col = lax.axis_size("col")
    row_panel = own * n_col
    col_panel = own * n_row
    total_boxes = float(own * bsize * n_row * n_col)
    rows_idx = block_row[0, 0]
    cols_idx = block_col[0, 0]
    live = jnp.arange(n_cap) < counts[0, 0]
    fwd_ids = jnp.where(live, rows_idx, row_panel)
    bwd_ids = jnp.where(live, cols_idx, col_panel)
    square = tile.reshape(n_cap, bsize, bsize)
    inv_col = 1.0 / jnp.sqrt(col_mass)
    current = vectors.reshape(own, vecs, bsize)
    for step in range(ITERS):
        scaled = (current * inv_col[:, None, :]).astype(jnp.bfloat16).reshape(own, vecs * bsize)
        panel = lax.all_gather(scaled, "row", axis=0, tiled=True)
        forward_taken = jnp.take(panel.reshape(col_panel, vecs, bsize), cols_idx, axis=0)
        forward_product = jnp.einsum(
            "bij,bkj->bki", square, forward_taken, preferred_element_type=jnp.float32
        )
        forward_summed = jax.ops.segment_sum(forward_product, fwd_ids, num_segments=row_panel + 1)
        rows_sum = lax.psum_scatter(
            forward_summed[:row_panel].reshape(row_panel, vecs * bsize),
            "col",
            scatter_dimension=0,
            tiled=True,
        )
        weighted = (rows_sum.reshape(own, vecs, bsize) * row_mass[:, None, :]).astype(jnp.bfloat16)
        whole_rows = lax.all_gather(weighted.reshape(own, vecs * bsize), "col", axis=0, tiled=True)
        taken = jnp.take(whole_rows.reshape(row_panel, vecs, bsize), rows_idx, axis=0)
        product = jnp.einsum("bij,bki->bkj", square, taken, preferred_element_type=jnp.float32)
        summed = jax.ops.segment_sum(product, bwd_ids, num_segments=col_panel + 1)
        cols_sum = lax.psum_scatter(
            summed[:col_panel].reshape(col_panel, vecs * bsize),
            "row",
            scatter_dimension=0,
            tiled=True,
        )
        projected = cols_sum.reshape(own, vecs, bsize) * inv_col[:, None, :]
        gram = lax.psum(local_gram(projected), ("row", "col")) / total_boxes
        current = rotate(projected, gram)
    return current.reshape(own, vecs * bsize)


def fits(n_row, n_col, blocks, vectors, row_mass):
    own, bsize = row_mass.shape[0] // (n_row * n_col), row_mass.shape[1]
    n_cap = blocks.shape[2]
    dense = n_row * (own * n_col * bsize) * (own * n_row * bsize) * 4
    shapes = own * bsize == 128 and vectors.shape[1] == bsize * bsize and n_cap == 128
    return dense <= VMEM_LIMIT // 4 and shapes and n_cap % (16 * n_col) == 0 and n_row == 4 and n_col == 8


def solution(mesh):
    n_row, n_col = mesh.shape["row"], mesh.shape["col"]

    def run(blocks, block_row, block_col, counts, vectors, row_mass, col_mass):
        args = (blocks, block_row, block_col, counts, vectors, row_mass, col_mass)
        if fits(n_row, n_col, blocks, vectors, row_mass):
            devices = mesh.devices.reshape(n_row, n_col // 2, 2)
            grid, col = jax.sharding.Mesh(devices, ("row", "chip", "core")), ("chip", "core")
            body = functools.partial(whole_on_each, n_row, n_col)
        else:
            grid, col, body = mesh, ("col",), split_by_tile
        by_row, by_col = P(("row",) + col, None), P(col + ("row",), None)
        in_specs = (
            P("row", col, None, None), P("row", col, None), P("row", col, None), P("row", col),
            by_col, by_row, by_col,
        )
        return jax.shard_map(
            body, mesh=grid, in_specs=in_specs, out_specs=by_col, check_vma=False
        )(*args)

    return run
```

```python
import functools

import jax
import jax.numpy as jnp
from jax import lax
from jax.experimental import pallas as pl
from jax.experimental.pallas import tpu as pltpu
from jax.sharding import PartitionSpec as P

ITERS = 4
OFF_CAP = 8
META = 16
UNROLL = 16
BATCH = 4
VMEM_LIMIT = 36 * 1024 * 1024

NT = (((1,), (1,)), ((), ()))
NN = (((1,), (0,)), ((), ()))


def dot(a, b, dims=NN):
    return lax.dot_general(a, b, dims, preferred_element_type=jnp.float32)


def split2(x):
    hi = x.astype(jnp.bfloat16)
    return hi, (x - hi.astype(jnp.float32)).astype(jnp.bfloat16)


def inverse_factor(gram):
    n = gram.shape[0]
    rows = lax.broadcasted_iota(jnp.int32, (n, n), 0)
    cols = lax.broadcasted_iota(jnp.int32, (n, n), 1)
    eye = (rows == cols).astype(jnp.float32)
    both = jnp.concatenate([gram, eye], axis=1)
    count, shape = n // 8, (8, 2 * n)
    tiles = [both[8 * t : 8 * t + 8] for t in range(count)]
    sub = lax.broadcasted_iota(jnp.int32, shape, 0)
    out = []
    for b in range(count):
        column = {
            t: [jnp.broadcast_to(tiles[t][:, 8 * b + s : 8 * b + s + 1], shape) for s in range(8)]
            for t in range(b, count)
        }
        row = [jnp.broadcast_to(tiles[b][s : s + 1], shape) for s in range(8)]
        a = [
            [jnp.broadcast_to(column[b][j][s : s + 1], shape) if j >= s else None for j in range(8)]
            for s in range(8)
        ]
        done = jnp.zeros(shape, jnp.float32)
        for s in range(8):
            root = lax.rsqrt(a[s][s])
            inv = root * root
            inv = inv * (2.0 - a[s][s] * inv)
            step = row[s] * inv
            done = jnp.where(sub == s, row[s] * root, done)
            for i in range(s + 1, 8):
                part = a[s][i] * inv
                for j in range(i, 8):
                    a[i][j] = a[i][j] - part * a[s][j]
                row[i] = row[i] - a[s][i] * step
                for t in range(b + 1, count):
                    column[t][i] = column[t][i] - column[t][s] * part
            for t in range(b + 1, count):
                tiles[t] = tiles[t] - column[t][s] * step
        out.append(done)
    return jnp.concatenate(out, axis=0)[:, n:]


def place_of(own, n_row, n_dev):
    here, chip, core = own[0], own[1], own[2]

    def at_device(r, c):
        dr, dc, dk = here ^ r, chip ^ (c // 2), core ^ (c % 2)
        dx, dy = dc & 1, dc >> 1
        order = jnp.where(dr < 2, 2 * dx, 4 + 2 * dy) + jnp.where(
            jnp.where(dr < 2, dy, dx) > 0, n_dev // 4, 0
        )
        return dk * (n_dev // 2) + order + (dr & 1)

    def device_at(d):
        far, second = (d >> 2) & 1, (d >> 3) & 1
        first = (d >> 1) & 1
        dc = jnp.where(far == 0, 2 * second + first, 2 * first + second)
        return here ^ (2 * far + (d & 1)), 2 * (chip ^ dc) + (core ^ (d >> 4))

    return at_device, device_at


def copy_in(pairs, sems):
    copies = [pltpu.make_async_copy(src, dst, sems.at[i]) for i, (src, dst) in enumerate(pairs)]
    for copy in copies:
        copy.start()
    return copies


def clear(refs):
    for ref in refs:
        for q in range(ref.shape[0]):
            ref[q] = jnp.zeros_like(ref[q])


def left_half(shape):
    return lax.broadcasted_iota(jnp.int32, shape, len(shape) - 1) < 64


def store_twice(pair, twice, q, x):
    pair[q] = x.astype(pair.dtype)
    turned, left = pltpu.roll(x, 64, 1), left_half(x.shape)
    twice[2 * q] = jnp.where(left, x, turned).astype(twice.dtype)
    twice[2 * q + 1] = jnp.where(left, turned, x).astype(twice.dtype)


def gather_pair(q, first, second):
    left = left_half(first.shape[1:])
    apart = jnp.where(left, first[2 * q + 1], second[2 * q])
    return jnp.where(left, first[2 * q], second[2 * q + 1]) + pltpu.roll(apart, 64, 1)


def add_products(n_group, blk, dims, lists, from_at, source, to_at, first, second):
    left = left_half(source.shape[1:])

    def multiply(pairs):
        return [
            dot(
                jnp.where(left, source[lists[from_at + 2 * p]], source[lists[from_at + 2 * p + 1]]),
                blk[p],
                dims,
            )
            for p in pairs
        ]

    def add(pairs, prods):
        for p, prod in zip(pairs, prods):
            a, b = lists[to_at + 2 * p], lists[to_at + 2 * p + 1]
            first[a] = first[a] + prod
            second[b] = second[b] + prod

    def group(i, carry):
        batches = [
            [i * UNROLL + at + u for u in range(BATCH)] for at in range(0, UNROLL, BATCH)
        ]
        prods = multiply(batches[0])
        for now, later in zip(batches, batches[1:]):
            ahead = multiply(later)
            add(now, prods)
            prods = ahead
        add(batches[-1], prods)
        return carry

    lax.fori_loop(0, n_group, group, 0)


def unpack(
    n_row, n_col, own, mine, other,
    lists, place, blk, rm, ic, vs, vd, w1, w2, ints, meta, sems, small,
):
    n_dev = n_row * n_col
    k = vs.shape[1]
    half = k // 2
    rblk, cblk = 2 * n_col, 2 * n_row
    vec_at = OFF_CAP * half
    meta_at = vec_at + k
    at_device, device_at = place_of(own, n_row, n_dev)
    slots = 2 * blk.shape[0]

    first, second = pl.ds(0, n_dev // 2), pl.ds(n_dev // 2, n_dev // 2)
    for copy in copy_in([(mine, small.at[first]), (other, small.at[second])], sems):
        copy.wait()
    for d in range(n_dev):
        rows = small[d, meta_at : meta_at + META, :].astype(jnp.float32)
        ints[d : d + 1, :] = rows[8:9].astype(jnp.int32)
    to_scalars = pltpu.make_async_copy(ints, meta, sems.at[2])
    to_scalars.start()

    for r in range(n_row):
        for c in range(n_col):
            q, p, d = c * n_row + r, r * n_col + c, at_device(r, c)
            rows = small[d, meta_at : meta_at + META, :].astype(jnp.float32)
            rm[p] = jnp.broadcast_to(rows[0:1] + rows[1:2] + rows[2:3], (8, 128))
            ic[q] = jnp.broadcast_to(rows[3:4] + rows[4:5] + rows[5:6], (8, 128))
            store_twice(vs, vd, q, small[d, vec_at : vec_at + k, :].astype(jnp.float32))
    to_scalars.wait()

    lanes = lax.broadcasted_iota(jnp.int32, (half, 128), 1)

    def device(d, n):
        count = meta[d, 2 * OFF_CAP]
        count = jnp.where(count > OFF_CAP, 0, count)
        r, c = device_at(d)
        for s in range(OFF_CAP):
            lists[n + s] = c * cblk + meta[d, OFF_CAP + s]
            lists[slots + n + s] = r * rblk + meta[d, s]
            x = small[d, s * half : (s + 1) * half, :].astype(jnp.float32)
            turned = pltpu.roll(x, 64, 1)
            side = (n + s) % 2
            here = (lanes // 64) == side
            even = jnp.where(here, jnp.where(side == 0, x, turned), 0.0)
            odd = jnp.where(here, jnp.where(side == 0, turned, x), 0.0)
            at = pl.multiple_of(side * k, k)
            both = jnp.concatenate([even, odd], axis=0).astype(jnp.bfloat16)
            blk[(n + s) // 2, pl.ds(at, k), :] = both
        return n + count

    n_live = lax.fori_loop(0, n_dev, device, jnp.int32(0))
    for u in range(2 * UNROLL - 1):
        lists[n_live + u] = 0
        lists[slots + n_live + u] = 0
        at = pl.multiple_of((n_live + u) % 2 * k, k)
        blk[(n_live + u) // 2, pl.ds(at, k), :] = jnp.zeros((k, 128), jnp.bfloat16)
    lists[2 * slots] = (n_live + 2 * UNROLL - 1) // (2 * UNROLL)

    for r in range(n_row):
        h = jnp.int32(0)
        for c in range(n_col):
            h = jnp.where(meta[at_device(r, c), 2 * OFF_CAP] > OFF_CAP, c, h)
        lists[2 * slots + 1 + r] = h
        index = small[at_device(r, h), meta_at : meta_at + META, :].astype(jnp.float32)
        place[r : r + 1, :] = index[7:8] * float(rblk) + index[6:7]

    clear([w1, w2])
    add_products(lists[2 * slots], blk, NT, lists, 0, vd, slots, w1, w2)


def iterate(n_row, n_col, n_cap, total, own, lists, place, *rest):
    blk, rm, ic, *starts = rest[:7]
    fulls, out = rest[7:15], rest[15]
    sems, full, tmp, home, vs, vd, w1, w2 = rest[16:24]
    w, wt, wd, y, y1, y2, ph, linv = rest[24:]
    slots = 2 * blk.shape[0]
    n_dev = n_row * n_col
    k = vs.shape[1]
    half = k // 2
    rpairs, cpairs = n_col, n_row
    rblk, cblk = 2 * rpairs, 2 * cpairs
    part = n_cap // n_col
    width = cpairs * 128
    at_device, _ = place_of(own, n_row, n_dev)

    def laid_out(refs, whole):
        at, pairs = 0, []
        for ref in refs:
            pairs.append((ref, whole.at[pl.ds(at, ref.shape[0])]))
            at += ref.shape[0]
        return pairs

    copies = copy_in(laid_out(fulls, full), sems)
    for start, ref in zip(starts, (vs, vd, w1, w2)):
        for q in range(ref.shape[0]):
            ref[q] = start[q]
    clear([y, y1, y2])
    for copy in copies:
        copy.wait()
    n_group = lists[2 * slots]

    left = lax.broadcasted_iota(jnp.int32, (rblk, 128), 1) < 64
    homes = []
    for r in range(n_row):
        homes.append(lists[2 * slots + 1 + r])
        want = lax.broadcasted_iota(jnp.int32, (cblk * rblk, n_cap), 0).astype(jnp.float32)
        select = jnp.where(want == place[r : r + 1, :], 1.0, 0.0).astype(jnp.bfloat16)

        parts = [at_device(r, 2 * i + j) for j in range(2) for i in range(n_col // 2)]

        def build(i, carry, parts=parts, select=select):
            ms = [4 * i + d for d in range(4)]
            denses = []
            for m in ms:
                at = pl.multiple_of(m * part, part)
                slots = jnp.concatenate([full[d, pl.ds(at, part), :] for d in parts], axis=0)
                denses.append(dot(select, slots))
            for m, dense in zip(ms, denses):
                for u in range(cpairs):
                    a = dense[2 * u * rblk : (2 * u + 1) * rblk]
                    b = dense[(2 * u + 1) * rblk : (2 * u + 2) * rblk]
                    even = jnp.where(left, a, pltpu.roll(b, 64, 1))
                    odd = jnp.where(left, pltpu.roll(a, 64, 1), b)
                    tmp[u, pl.ds(m, rblk, stride=k), :] = even
                    tmp[u, pl.ds(m + half, rblk, stride=k), :] = odd
            return carry

        lax.fori_loop(0, half // 4, build, 0, unroll=2)

        def cut(i, carry, r=r):
            at = pl.multiple_of(i * k, k)
            for u in range(cpairs):
                hi, lo = split2(tmp[u, pl.ds(at, k), :])
                home[r, pl.ds(at, k), u * 128 : (u + 1) * 128] = hi
                home[r, pl.ds(at, k), width + u * 128 : width + (u + 1) * 128] = lo
            return carry

        lax.fori_loop(0, rblk, cut, 0, unroll=8)


    def iteration(it, carry):
        @pl.when(it > 0)
        def _():
            lh, ll = split2(linv[...])
            turn = jnp.concatenate([lh, lh, ll], axis=1)
            for q in range(0, n_dev, 4):
                hi = jnp.concatenate([ph[q + d, :k, :] for d in range(4)], axis=1)
                lo = jnp.concatenate([ph[q + d, k:, :] for d in range(4)], axis=1)
                current = dot(turn, jnp.concatenate([hi, lo, hi], axis=0))
                for d in range(4):
                    x = current[:, d * 128 : (d + 1) * 128] * ic[q + d, 0:1, :]
                    store_twice(vs, vd, q + d, x)

        for r in range(n_row):
            base = homes[r] * cpairs
            vec = jnp.concatenate([vs[base + u] for u in range(cpairs)] * 2, axis=1)
            for p in range(0, rpairs, 2):
                prod = dot(vec, home[r, p * 128 : (p + 2) * 128, :], NT)
                w[r * rpairs + p] = prod[:, :128]
                w[r * rpairs + p + 1] = prod[:, 128:]

        @pl.when(it > 0)
        def _():
            add_products(n_group, blk, NT, lists, 0, vd, slots, w1, w2)

        for p in range(n_dev):
            x = w[p] + gather_pair(p, w1, w2)
            store_twice(wt, wd, p, x * rm[p, 0:1, :])

        def back(r, u):
            vec = jnp.concatenate([wt[r * rpairs + p] for p in range(rpairs)], axis=1)
            cols = slice(u * 128, (u + 2) * 128)
            tail = slice(width + u * 128, width + (u + 2) * 128)
            return dot(vec, home[r, :, cols]) + dot(vec, home[r, :, tail])

        steps = [(r, u) for r in range(n_row) for u in range(0, cpairs, 2)]
        prod = back(*steps[0])
        for i, (r, u) in enumerate(steps):
            ahead = back(*steps[i + 1]) if i + 1 < len(steps) else None
            q = homes[r] * cpairs + u
            y[q] = y[q] + prod[:, :128]
            y[q + 1] = y[q + 1] + prod[:, 128:]
            prod = ahead

        add_products(n_group, blk, NN, lists, slots, wd, 0, y1, y2)

        both = jnp.zeros((2 * k, k), jnp.float32)
        for q in range(0, n_dev, 4):
            his, los = [], []
            for d in range(q, q + 4):
                x = y[d] + gather_pair(d, y1, y2)
                hi, lo = split2(x * ic[d, 0:1, :])
                ph[d, :k, :] = hi
                ph[d, k:, :] = lo
                his.append(hi)
                los.append(lo)
            hi = jnp.concatenate(his, axis=1)
            lo = jnp.concatenate(los, axis=1)
            both = both + dot(jnp.concatenate([hi, lo], axis=0), hi, NT)
        gram = (both[:k] + (both[k:] + both[k:].T)) / total
        clear([y, y1, y2, w1, w2])
        linv[...] = inverse_factor(gram)
        return carry

    lax.fori_loop(0, ITERS, iteration, 0)
    lh, ll = split2(linv[...])
    q = (2 * own[1] + own[2]) * n_row + own[0]
    hi, lo = ph[q, :k, :], ph[q, k:, :]
    w[0] = dot(lh, hi) + dot(ll, hi) + dot(lh, lo)
    even, odd = w[0, pl.ds(0, half, stride=2), :], w[0, pl.ds(1, half, stride=2), :]
    left = left_half(even.shape)
    first = jnp.where(left, even, pltpu.roll(odd, 64, 1))
    second = jnp.where(left, pltpu.roll(even, 64, 1), odd)
    for i in range(half):
        out[0:1, i * 128 : (i + 1) * 128] = first[i : i + 1]
        out[1:2, i * 128 : (i + 1) * 128] = second[i : i + 1]


def split3(x):
    a = lax.reduce_precision(x, 8, 7)
    b = lax.reduce_precision(x - a, 8, 7)
    return [v.astype(jnp.bfloat16) for v in (a, b, x - a - b)]


def swap(x, axis, distance):
    size = lax.axis_size(axis)
    return lax.ppermute(x, axis, [(i, i ^ distance) for i in range(size)])


def along_rows(x):
    return [x] + [swap(x, "row", s) for s in range(1, lax.axis_size("row"))]


def along_one_chip_axis(x):
    near, far = jnp.stack(x[:2]), jnp.stack(x[2:])
    return [
        jnp.concatenate([near, swap(near, "chip", 1)]),
        jnp.concatenate([far, swap(far, "chip", 2)]),
    ]


def along_other_chip_axis(x):
    near, far = x
    return [swap(near, "chip", 2), swap(far, "chip", 1)]


def full_part(tile, has_full, n_chip, part, chip, core):
    tile = tile.reshape(2, n_chip, part, tile.shape[1])
    none = jnp.zeros(tile.shape[1:], tile.dtype)
    kept, sent = (
        jnp.where(has_full, lax.dynamic_index_in_dim(tile, i, 0, False), none)
        for i in (core, 1 - core)
    )
    both = kept + swap(sent, "core", 1)
    mine = lax.dynamic_index_in_dim(both, chip, 0, False)
    for s in range(1, n_chip):
        mine = mine + swap(lax.dynamic_index_in_dim(both, chip ^ s, 0, False), "chip", s)
    return mine


def whole_on_each(n_row, n_col, blocks, block_row, block_col, counts, vectors, row_mass, col_mass):
    tile = blocks[0, 0]
    n_cap = tile.shape[0]
    own, bsize = row_mass.shape
    k = vectors.shape[1] // bsize
    half = bsize // 2
    part = n_cap // n_col
    n_dev = n_row * n_col
    count = counts[0, 0]
    has_full = count > OFF_CAP
    bf16 = jnp.bfloat16
    row, chip, core = (lax.axis_index(name) for name in ("row", "chip", "core"))

    off = tile[:OFF_CAP].reshape(OFF_CAP * half, 128)
    inv_col = 1.0 / jnp.sqrt(col_mass)
    scaled = (vectors.reshape(own, k, bsize) * inv_col[:, None, :]).astype(bf16)
    scaled = scaled.transpose(1, 0, 2).reshape(k, own * bsize)
    mass = row_mass.reshape(own, half, 2).transpose(0, 2, 1).reshape(own * bsize)
    rows, cols = block_row[0, 0], block_col[0, 0]
    short = jnp.concatenate(
        [rows[:OFF_CAP], cols[:OFF_CAP], count[None], jnp.zeros(128 - 2 * OFF_CAP - 1, jnp.int32)]
    )
    meta = [v.astype(bf16) for v in (rows, cols, short)]
    meta = split3(mass) + split3(inv_col.reshape(own * bsize)) + meta
    meta = jnp.stack(meta + [jnp.zeros(128, bf16)] * (META - len(meta)))
    small = jnp.concatenate([off, scaled, meta], axis=0)
    home = full_part(tile, has_full, n_col // 2, part, chip, core)
    home = home.reshape(part, half, 128).transpose(1, 0, 2).reshape(half * part, 128)

    together = lax.optimization_barrier
    where = jnp.stack([row, chip, core]).astype(jnp.int32)
    home, smalls, where = together((home, along_rows(small), where))
    homes, smalls = along_rows(home), along_one_chip_axis(smalls)
    smalls, homes[1] = together((smalls, homes[1]))
    smalls = jnp.concatenate(smalls + along_other_chip_axis(smalls))
    homes, smalls = together((homes, smalls))
    others = swap(smalls, "core", 1)
    homes = along_one_chip_axis(homes)
    last = along_other_chip_axis(homes)

    height, width = 2 * n_col * bsize, 2 * n_row * bsize
    slots = n_dev * OFF_CAP + 2 * UNROLL
    f32, i32, vmem, smem = jnp.float32, jnp.int32, pltpu.VMEM, pltpu.SMEM
    pair, twice, mass = (n_dev, k, 128), (2 * n_dev, k, 128), (n_dev, 8, 128)
    smem_spec, vmem_spec, any_spec = (pl.BlockSpec(memory_space=m) for m in (smem, vmem, pl.ANY))
    arrays = [
        ((8, 128), f32), ((slots // 2, 128, 128), bf16), (mass, f32), (mass, f32),
        (pair, bf16), (twice, bf16), (twice, f32), (twice, f32),
    ]
    lists, *unpacked = pl.pallas_call(
        functools.partial(unpack, n_row, n_col),
        out_shape=[jax.ShapeDtypeStruct((2 * slots + 8,), i32)]
        + [vmem(*v) for v in arrays],
        in_specs=[smem_spec, any_spec, any_spec],
        out_specs=[smem_spec] + [vmem_spec] * len(arrays),
        scratch_shapes=[
            vmem((n_dev, 128), i32),
            smem((n_dev, 128), i32),
            pltpu.SemaphoreType.DMA((3,)),
            vmem((n_dev,) + small.shape, bf16),
        ],
        compiler_params=pltpu.CompilerParams(vmem_limit_bytes=VMEM_LIMIT // 2),
        cost_estimate=pl.CostEstimate(
            flops=0, bytes_accessed=4 * n_dev * small.size * 2, transcendentals=0
        ),
        name="unpack",
    )(where, smalls, others)
    last, lists = together((last, lists))
    mine = homes + last
    fulls = mine + [swap(v, "core", 1) for v in mine]
    return pl.pallas_call(
        functools.partial(iterate, n_row, n_col, n_cap, float(n_dev * own * bsize)),
        out_shape=jax.ShapeDtypeStruct((own, k * bsize), f32),
        in_specs=[smem_spec] * 2 + [vmem_spec] * len(arrays) + [any_spec] * len(fulls),
        out_specs=vmem_spec,
        scratch_shapes=[
            pltpu.SemaphoreType.DMA((len(fulls),)),
            vmem((n_dev,) + home.shape, bf16),
            vmem((n_row, height, 128), f32),
            vmem((n_row, height, 2 * width), bf16),
            *[vmem(*v) for v in arrays[4:]],
            vmem(pair, f32), vmem(pair, bf16), vmem(twice, bf16),
            vmem(pair, f32), vmem(twice, f32), vmem(twice, f32),
            vmem((n_dev, 2 * k, 128), bf16),
            vmem((k, k), f32),
        ],
        compiler_params=pltpu.CompilerParams(vmem_limit_bytes=VMEM_LIMIT),
        name="iterate",
    )(where, lists, *(pltpu.with_memory_space_constraint(v, vmem) for v in unpacked), *fulls)


def rotate(projected, gram):
    lower = jnp.linalg.cholesky(gram)
    inverse = lax.linalg.triangular_solve(
        lower, jnp.eye(gram.shape[0], dtype=jnp.float32), left_side=True, lower=True
    )
    return jnp.einsum(
        "kl,bli->bki",
        inverse,
        projected,
        precision=lax.Precision.HIGHEST,
        preferred_element_type=jnp.float32,
    )


def local_gram(projected):
    return jnp.einsum(
        "bki,bli->kl",
        projected,
        projected,
        precision=lax.Precision.HIGHEST,
        preferred_element_type=jnp.float32,
    )


def split_by_tile(blocks, block_row, block_col, counts, vectors, row_mass, col_mass):
    tile = blocks[0, 0]
    n_cap = tile.shape[0]
    bsize = row_mass.shape[1]
    vecs = vectors.shape[1] // bsize
    own = vectors.shape[0]
    n_row = lax.axis_size("row")
    n_col = lax.axis_size("col")
    row_panel = own * n_col
    col_panel = own * n_row
    total_boxes = float(own * bsize * n_row * n_col)
    rows_idx = block_row[0, 0]
    cols_idx = block_col[0, 0]
    live = jnp.arange(n_cap) < counts[0, 0]
    fwd_ids = jnp.where(live, rows_idx, row_panel)
    bwd_ids = jnp.where(live, cols_idx, col_panel)
    square = tile.reshape(n_cap, bsize, bsize)
    inv_col = 1.0 / jnp.sqrt(col_mass)
    current = vectors.reshape(own, vecs, bsize)
    for step in range(ITERS):
        scaled = (current * inv_col[:, None, :]).astype(jnp.bfloat16).reshape(own, vecs * bsize)
        panel = lax.all_gather(scaled, "row", axis=0, tiled=True)
        forward_taken = jnp.take(panel.reshape(col_panel, vecs, bsize), cols_idx, axis=0)
        forward_product = jnp.einsum(
            "bij,bkj->bki", square, forward_taken, preferred_element_type=jnp.float32
        )
        forward_summed = jax.ops.segment_sum(forward_product, fwd_ids, num_segments=row_panel + 1)
        rows_sum = lax.psum_scatter(
            forward_summed[:row_panel].reshape(row_panel, vecs * bsize),
            "col",
            scatter_dimension=0,
            tiled=True,
        )
        weighted = (rows_sum.reshape(own, vecs, bsize) * row_mass[:, None, :]).astype(jnp.bfloat16)
        whole_rows = lax.all_gather(weighted.reshape(own, vecs * bsize), "col", axis=0, tiled=True)
        taken = jnp.take(whole_rows.reshape(row_panel, vecs, bsize), rows_idx, axis=0)
        product = jnp.einsum("bij,bki->bkj", square, taken, preferred_element_type=jnp.float32)
        summed = jax.ops.segment_sum(product, bwd_ids, num_segments=col_panel + 1)
        cols_sum = lax.psum_scatter(
            summed[:col_panel].reshape(col_panel, vecs * bsize),
            "row",
            scatter_dimension=0,
            tiled=True,
        )
        projected = cols_sum.reshape(own, vecs, bsize) * inv_col[:, None, :]
        gram = lax.psum(local_gram(projected), ("row", "col")) / total_boxes
        current = rotate(projected, gram)
    return current.reshape(own, vecs * bsize)


def fits(n_row, n_col, blocks, vectors, row_mass):
    own, bsize = row_mass.shape[0] // (n_row * n_col), row_mass.shape[1]
    n_cap = blocks.shape[2]
    dense = n_row * (own * n_col * bsize) * (own * n_row * bsize) * 4
    shapes = own * bsize == 128 and vectors.shape[1] == bsize * bsize and n_cap == 128
    return dense <= VMEM_LIMIT // 4 and shapes and n_cap % (16 * n_col) == 0 and n_row == 4 and n_col == 8


def solution(mesh):
    n_row, n_col = mesh.shape["row"], mesh.shape["col"]

    def run(blocks, block_row, block_col, counts, vectors, row_mass, col_mass):
        args = (blocks, block_row, block_col, counts, vectors, row_mass, col_mass)
        if fits(n_row, n_col, blocks, vectors, row_mass):
            devices = mesh.devices.reshape(n_row, n_col // 2, 2)
            grid, col = jax.sharding.Mesh(devices, ("row", "chip", "core")), ("chip", "core")
            body = functools.partial(whole_on_each, n_row, n_col)
        else:
            grid, col, body = mesh, ("col",), split_by_tile
        by_row, by_col = P(("row",) + col, None), P(col + ("row",), None)
        in_specs = (
            P("row", col, None, None), P("row", col, None), P("row", col, None), P("row", col),
            by_col, by_row, by_col,
        )
        return jax.shard_map(
            body, mesh=grid, in_specs=in_specs, out_specs=by_col, check_vma=False
        )(*args)

    return run
```

```python
import functools

import jax
import jax.numpy as jnp
from jax import lax
from jax.experimental import pallas as pl
from jax.experimental.pallas import tpu as pltpu
from jax.sharding import PartitionSpec as P

ITERS = 4
OFF_CAP = 8
META = 16
UNROLL = 16
BATCH = 4
VMEM_LIMIT = 36 * 1024 * 1024

NT = (((1,), (1,)), ((), ()))
NN = (((1,), (0,)), ((), ()))


def dot(a, b, dims=NN):
    return lax.dot_general(a, b, dims, preferred_element_type=jnp.float32)


def split2(x):
    hi = x.astype(jnp.bfloat16)
    return hi, (x - hi.astype(jnp.float32)).astype(jnp.bfloat16)


def inverse_factor(gram):
    n = gram.shape[0]
    rows = lax.broadcasted_iota(jnp.int32, (n, n), 0)
    cols = lax.broadcasted_iota(jnp.int32, (n, n), 1)
    eye = (rows == cols).astype(jnp.float32)
    both = jnp.concatenate([gram, eye], axis=1)
    count, shape = n // 8, (8, 2 * n)
    tiles = [both[8 * t : 8 * t + 8] for t in range(count)]
    sub = lax.broadcasted_iota(jnp.int32, shape, 0)
    out = []
    for b in range(count):
        column = {
            t: [jnp.broadcast_to(tiles[t][:, 8 * b + s : 8 * b + s + 1], shape) for s in range(8)]
            for t in range(b, count)
        }
        row = [jnp.broadcast_to(tiles[b][s : s + 1], shape) for s in range(8)]
        a = [
            [jnp.broadcast_to(column[b][j][s : s + 1], shape) if j >= s else None for j in range(8)]
            for s in range(8)
        ]
        done = jnp.zeros(shape, jnp.float32)
        for s in range(8):
            root = lax.rsqrt(a[s][s])
            inv = root * root
            inv = inv * (2.0 - a[s][s] * inv)
            step = row[s] * inv
            done = jnp.where(sub == s, row[s] * root, done)
            for i in range(s + 1, 8):
                part = a[s][i] * inv
                for j in range(i, 8):
                    a[i][j] = a[i][j] - part * a[s][j]
                row[i] = row[i] - a[s][i] * step
                for t in range(b + 1, count):
                    column[t][i] = column[t][i] - column[t][s] * part
            for t in range(b + 1, count):
                tiles[t] = tiles[t] - column[t][s] * step
        out.append(done)
    return jnp.concatenate(out, axis=0)[:, n:]


def place_of(own, n_row, n_dev):
    here, chip, core = own[0], own[1], own[2]

    def at_device(r, c):
        dr, dc, dk = here ^ r, chip ^ (c // 2), core ^ (c % 2)
        dx, dy = dc & 1, dc >> 1
        order = jnp.where(dr < 2, 2 * dx, 4 + 2 * dy) + jnp.where(
            jnp.where(dr < 2, dy, dx) > 0, n_dev // 4, 0
        )
        return dk * (n_dev // 2) + order + (dr & 1)

    def device_at(d):
        far, second = (d >> 2) & 1, (d >> 3) & 1
        first = (d >> 1) & 1
        dc = jnp.where(far == 0, 2 * second + first, 2 * first + second)
        return here ^ (2 * far + (d & 1)), 2 * (chip ^ dc) + (core ^ (d >> 4))

    return at_device, device_at


def copy_in(pairs, sems):
    copies = [pltpu.make_async_copy(src, dst, sems.at[i]) for i, (src, dst) in enumerate(pairs)]
    for copy in copies:
        copy.start()
    return copies


def clear(refs):
    for ref in refs:
        for q in range(ref.shape[0]):
            ref[q] = jnp.zeros_like(ref[q])


def left_half(shape):
    return lax.broadcasted_iota(jnp.int32, shape, len(shape) - 1) < 64


def store_twice(pair, twice, q, x):
    pair[q] = x.astype(pair.dtype)
    turned, left = pltpu.roll(x, 64, 1), left_half(x.shape)
    twice[2 * q] = jnp.where(left, x, turned).astype(twice.dtype)
    twice[2 * q + 1] = jnp.where(left, turned, x).astype(twice.dtype)


def gather_pair(q, first, second):
    left = left_half(first.shape[1:])
    apart = jnp.where(left, first[2 * q + 1], second[2 * q])
    return jnp.where(left, first[2 * q], second[2 * q + 1]) + pltpu.roll(apart, 64, 1)


def add_products(n_group, blk, dims, lists, from_at, source, to_at, first, second):
    left = left_half(source.shape[1:])

    def multiply(pairs):
        return [
            dot(
                jnp.where(left, source[lists[from_at + 2 * p]], source[lists[from_at + 2 * p + 1]]),
                blk[p],
                dims,
            )
            for p in pairs
        ]

    def add(pairs, prods):
        for p, prod in zip(pairs, prods):
            a, b = lists[to_at + 2 * p], lists[to_at + 2 * p + 1]
            first[a] = first[a] + prod
            second[b] = second[b] + prod

    def group(i, carry):
        batches = [
            [i * UNROLL + at + u for u in range(BATCH)] for at in range(0, UNROLL, BATCH)
        ]
        prods = multiply(batches[0])
        for now, later in zip(batches, batches[1:]):
            ahead = multiply(later)
            add(now, prods)
            prods = ahead
        add(batches[-1], prods)
        return carry

    lax.fori_loop(0, n_group, group, 0)


def unpack(
    n_row, n_col, own, mine, other,
    lists, place, blk, rm, ic, vs, vd, w1, w2, ints, meta, sems, small,
):
    n_dev = n_row * n_col
    k = vs.shape[1]
    half = k // 2
    rblk, cblk = 2 * n_col, 2 * n_row
    vec_at = OFF_CAP * half
    meta_at = vec_at + k
    at_device, device_at = place_of(own, n_row, n_dev)
    slots = 2 * blk.shape[0]

    first, second = pl.ds(0, n_dev // 2), pl.ds(n_dev // 2, n_dev // 2)
    for copy in copy_in([(mine, small.at[first]), (other, small.at[second])], sems):
        copy.wait()
    for d in range(n_dev):
        rows = small[d, meta_at : meta_at + META, :].astype(jnp.float32)
        ints[d : d + 1, :] = rows[8:9].astype(jnp.int32)
    to_scalars = pltpu.make_async_copy(ints, meta, sems.at[2])
    to_scalars.start()

    for r in range(n_row):
        for c in range(n_col):
            q, p, d = c * n_row + r, r * n_col + c, at_device(r, c)
            rows = small[d, meta_at : meta_at + META, :].astype(jnp.float32)
            rm[p] = jnp.broadcast_to(rows[0:1] + rows[1:2] + rows[2:3], (8, 128))
            ic[q] = jnp.broadcast_to(rows[3:4] + rows[4:5] + rows[5:6], (8, 128))
            store_twice(vs, vd, q, small[d, vec_at : vec_at + k, :].astype(jnp.float32))
    to_scalars.wait()

    lanes = lax.broadcasted_iota(jnp.int32, (half, 128), 1)

    def device(d, n):
        count = meta[d, 2 * OFF_CAP]
        count = jnp.where(count > OFF_CAP, 0, count)
        r, c = device_at(d)
        for s in range(OFF_CAP):
            lists[n + s] = c * cblk + meta[d, OFF_CAP + s]
            lists[slots + n + s] = r * rblk + meta[d, s]
            x = small[d, s * half : (s + 1) * half, :].astype(jnp.float32)
            turned = pltpu.roll(x, 64, 1)
            side = (n + s) % 2
            here = (lanes // 64) == side
            even = jnp.where(here, jnp.where(side == 0, x, turned), 0.0)
            odd = jnp.where(here, jnp.where(side == 0, turned, x), 0.0)
            at = pl.multiple_of(side * k, k)
            both = jnp.concatenate([even, odd], axis=0).astype(jnp.bfloat16)
            blk[(n + s) // 2, pl.ds(at, k), :] = both
        return n + count

    n_live = lax.fori_loop(0, n_dev, device, jnp.int32(0))
    for u in range(2 * UNROLL - 1):
        lists[n_live + u] = 0
        lists[slots + n_live + u] = 0
        at = pl.multiple_of((n_live + u) % 2 * k, k)
        blk[(n_live + u) // 2, pl.ds(at, k), :] = jnp.zeros((k, 128), jnp.bfloat16)
    lists[2 * slots] = (n_live + 2 * UNROLL - 1) // (2 * UNROLL)

    for r in range(n_row):
        h = jnp.int32(0)
        for c in range(n_col):
            h = jnp.where(meta[at_device(r, c), 2 * OFF_CAP] > OFF_CAP, c, h)
        lists[2 * slots + 1 + r] = h
        index = small[at_device(r, h), meta_at : meta_at + META, :].astype(jnp.float32)
        place[r : r + 1, :] = index[7:8] * float(rblk) + index[6:7]

    clear([w1, w2])
    add_products(lists[2 * slots], blk, NT, lists, 0, vd, slots, w1, w2)


def iterate(n_row, n_col, n_cap, total, own, lists, place, *rest):
    blk, rm, ic, *starts = rest[:7]
    fulls, out = rest[7:15], rest[15]
    sems, full, tmp, home, vs, vd, w1, w2 = rest[16:24]
    w, wt, wd, y, y1, y2, ph, linv = rest[24:]
    slots = 2 * blk.shape[0]
    n_dev = n_row * n_col
    k = vs.shape[1]
    half = k // 2
    rpairs, cpairs = n_col, n_row
    rblk, cblk = 2 * rpairs, 2 * cpairs
    part = n_cap // n_col
    width = cpairs * 128
    at_device, _ = place_of(own, n_row, n_dev)

    def laid_out(refs, whole):
        at, pairs = 0, []
        for ref in refs:
            pairs.append((ref, whole.at[pl.ds(at, ref.shape[0])]))
            at += ref.shape[0]
        return pairs

    copies = copy_in(laid_out(fulls, full), sems)
    for start, ref in zip(starts, (vs, vd, w1, w2)):
        for q in range(ref.shape[0]):
            ref[q] = start[q]
    clear([y, y1, y2])
    for copy in copies:
        copy.wait()
    n_group = lists[2 * slots]

    left = lax.broadcasted_iota(jnp.int32, (rblk, 128), 1) < 64
    homes = []
    for r in range(n_row):
        homes.append(lists[2 * slots + 1 + r])
        want = lax.broadcasted_iota(jnp.int32, (cblk * rblk, n_cap), 0).astype(jnp.float32)
        select = jnp.where(want == place[r : r + 1, :], 1.0, 0.0).astype(jnp.bfloat16)

        parts = [at_device(r, 2 * i + j) for j in range(2) for i in range(n_col // 2)]

        def build(i, carry, parts=parts, select=select):
            ms = [4 * i + d for d in range(4)]
            denses = []
            for m in ms:
                at = pl.multiple_of(m * part, part)
                slots = jnp.concatenate([full[d, pl.ds(at, part), :] for d in parts], axis=0)
                denses.append(dot(select, slots))
            for m, dense in zip(ms, denses):
                for u in range(cpairs):
                    a = dense[2 * u * rblk : (2 * u + 1) * rblk]
                    b = dense[(2 * u + 1) * rblk : (2 * u + 2) * rblk]
                    even = jnp.where(left, a, pltpu.roll(b, 64, 1))
                    odd = jnp.where(left, pltpu.roll(a, 64, 1), b)
                    tmp[u, pl.ds(m, rblk, stride=k), :] = even
                    tmp[u, pl.ds(m + half, rblk, stride=k), :] = odd
            return carry

        lax.fori_loop(0, half // 4, build, 0, unroll=2)

        def cut(i, carry, r=r):
            at = pl.multiple_of(i * k, k)
            for u in range(cpairs):
                hi, lo = split2(tmp[u, pl.ds(at, k), :])
                home[r, pl.ds(at, k), u * 128 : (u + 1) * 128] = hi
                home[r, pl.ds(at, k), width + u * 128 : width + (u + 1) * 128] = lo
            return carry

        lax.fori_loop(0, rblk, cut, 0, unroll=8)


    def iteration(it, carry):
        @pl.when(it > 0)
        def _():
            lh, ll = split2(linv[...])
            turn = jnp.concatenate([lh, lh, ll], axis=1)
            for q in range(0, n_dev, 4):
                hi = jnp.concatenate([ph[q + d, :k, :] for d in range(4)], axis=1)
                lo = jnp.concatenate([ph[q + d, k:, :] for d in range(4)], axis=1)
                current = dot(turn, jnp.concatenate([hi, lo, hi], axis=0))
                for d in range(4):
                    x = current[:, d * 128 : (d + 1) * 128] * ic[q + d, 0:1, :]
                    store_twice(vs, vd, q + d, x)

        for r in range(n_row):
            base = homes[r] * cpairs
            vec = jnp.concatenate([vs[base + u] for u in range(cpairs)] * 2, axis=1)
            for p in range(0, rpairs, 2):
                prod = dot(vec, home[r, p * 128 : (p + 2) * 128, :], NT)
                w[r * rpairs + p] = prod[:, :128]
                w[r * rpairs + p + 1] = prod[:, 128:]

        @pl.when(it > 0)
        def _():
            add_products(n_group, blk, NT, lists, 0, vd, slots, w1, w2)

        for p in range(n_dev):
            x = w[p] + gather_pair(p, w1, w2)
            store_twice(wt, wd, p, x * rm[p, 0:1, :])

        def back(r, u):
            vec = jnp.concatenate([wt[r * rpairs + p] for p in range(rpairs)], axis=1)
            cols = slice(u * 128, (u + 2) * 128)
            tail = slice(width + u * 128, width + (u + 2) * 128)
            return dot(vec, home[r, :, cols]) + dot(vec, home[r, :, tail])

        steps = [(r, u) for r in range(n_row) for u in range(0, cpairs, 2)]
        prod = back(*steps[0])
        for i, (r, u) in enumerate(steps):
            ahead = back(*steps[i + 1]) if i + 1 < len(steps) else None
            q = homes[r] * cpairs + u
            y[q] = y[q] + prod[:, :128]
            y[q + 1] = y[q + 1] + prod[:, 128:]
            prod = ahead

        add_products(n_group, blk, NN, lists, slots, wd, 0, y1, y2)

        both = jnp.zeros((2 * k, k), jnp.float32)
        for q in range(0, n_dev, 4):
            his, los = [], []
            for d in range(q, q + 4):
                x = y[d] + gather_pair(d, y1, y2)
                hi, lo = split2(x * ic[d, 0:1, :])
                ph[d, :k, :] = hi
                ph[d, k:, :] = lo
                his.append(hi)
                los.append(lo)
            hi = jnp.concatenate(his, axis=1)
            lo = jnp.concatenate(los, axis=1)
            both = both + dot(jnp.concatenate([hi, lo], axis=0), hi, NT)
        gram = (both[:k] + (both[k:] + both[k:].T)) / total
        clear([y, y1, y2, w1, w2])
        linv[...] = inverse_factor(gram)
        return carry

    lax.fori_loop(0, ITERS, iteration, 0)
    lh, ll = split2(linv[...])
    q = (2 * own[1] + own[2]) * n_row + own[0]
    hi, lo = ph[q, :k, :], ph[q, k:, :]
    w[0] = dot(lh, hi) + dot(ll, hi) + dot(lh, lo)
    even, odd = w[0, pl.ds(0, half, stride=2), :], w[0, pl.ds(1, half, stride=2), :]
    left = left_half(even.shape)
    first = jnp.where(left, even, pltpu.roll(odd, 64, 1))
    second = jnp.where(left, pltpu.roll(even, 64, 1), odd)
    for i in range(half):
        out[0:1, i * 128 : (i + 1) * 128] = first[i : i + 1]
        out[1:2, i * 128 : (i + 1) * 128] = second[i : i + 1]


def split3(x):
    parts = []
    for _ in range(3):
        parts.append(x.astype(jnp.bfloat16).astype(jnp.float32))
        x = x - parts[-1]
    return parts


def prepare(count, *rest):
    sources, out, sems, first, second, both = rest[:5], *rest[5:10]
    for copy in copy_in(list(zip(sources, rest[10:])), sems):
        copy.wait()
    rows, cols, vectors, row_mass, col_mass = rest[10:]
    f32, bf16 = jnp.float32, jnp.bfloat16
    half = first.shape[0]
    for i in range(half):
        first[i : i + 1, :] = vectors[0:1, i * 128 : (i + 1) * 128]
        second[i : i + 1, :] = vectors[1:2, i * 128 : (i + 1) * 128]
    x, z = first[...], second[...]
    left = left_half(x.shape)
    both[pl.ds(0, half, stride=2), :] = jnp.where(left, x, pltpu.roll(z, 64, 1))
    both[pl.ds(1, half, stride=2), :] = jnp.where(left, pltpu.roll(x, 64, 1), z)
    inv = 1.0 / jnp.sqrt(jnp.concatenate([col_mass[0:1, :], col_mass[1:2, :]], axis=1))
    out[: 2 * half, :] = (both[...] * inv).astype(bf16)

    sub = lax.broadcasted_iota(jnp.int32, (META, 128), 0)

    def stacked(at, values):
        result = jnp.zeros((META, 128), f32)
        for i, value in enumerate(values):
            result = jnp.where(sub == at + i, value, result)
        return result

    mass = jnp.concatenate([row_mass[0:1, :], row_mass[1:2, :]], axis=1)
    source = lax.broadcasted_iota(jnp.int32, (128, 128), 0)
    lane = lax.broadcasted_iota(jnp.int32, (128, 128), 1)
    chosen = source == (lane // 64) * 64 + 2 * (lane % half) + (lane % 64) // half
    masses = dot(stacked(0, split3(mass)).astype(bf16), jnp.where(chosen, 1.0, 0.0).astype(bf16))
    r, c = rows[...].astype(f32), cols[...].astype(f32)
    lane = lane[:8]
    moved = pltpu.roll(jnp.broadcast_to(c, (8, 128)), OFF_CAP, 1)
    short = jnp.where(lane == 2 * OFF_CAP, count[0, 0].astype(f32), 0.0)
    short = jnp.where(lane < OFF_CAP, r, jnp.where(lane < 2 * OFF_CAP, moved, short))
    packed = masses + stacked(3, split3(inv) + [r, c, short[0:1]])
    out[2 * half :, :] = packed.astype(bf16)


def swap(x, axis, distance):
    size = lax.axis_size(axis)
    return lax.ppermute(x, axis, [(i, i ^ distance) for i in range(size)])


def along_rows(x):
    return [x] + [swap(x, "row", s) for s in range(1, lax.axis_size("row"))]


def along_one_chip_axis(x):
    near, far = jnp.stack(x[:2]), jnp.stack(x[2:])
    return [
        jnp.concatenate([near, swap(near, "chip", 1)]),
        jnp.concatenate([far, swap(far, "chip", 2)]),
    ]


def along_other_chip_axis(x):
    near, far = x
    return [swap(near, "chip", 2), swap(far, "chip", 1)]


def full_part(tile, has_full, n_chip, part, chip, core):
    tile = tile.reshape(2, n_chip, part, tile.shape[1])
    none = jnp.zeros(tile.shape[1:], tile.dtype)
    kept, sent = (
        jnp.where(has_full, lax.dynamic_index_in_dim(tile, i, 0, False), none)
        for i in (core, 1 - core)
    )
    both = kept + swap(sent, "core", 1)
    mine = lax.dynamic_index_in_dim(both, chip, 0, False)
    for s in range(1, n_chip):
        mine = mine + swap(lax.dynamic_index_in_dim(both, chip ^ s, 0, False), "chip", s)
    return mine


def whole_on_each(n_row, n_col, blocks, block_row, block_col, counts, vectors, row_mass, col_mass):
    tile = blocks[0, 0]
    n_cap = tile.shape[0]
    own, bsize = row_mass.shape
    k = vectors.shape[1] // bsize
    half = bsize // 2
    part = n_cap // n_col
    n_dev = n_row * n_col
    count = counts[0, 0]
    has_full = count > OFF_CAP
    bf16 = jnp.bfloat16
    row, chip, core = (lax.axis_index(name) for name in ("row", "chip", "core"))

    off = tile[:OFF_CAP].reshape(OFF_CAP * half, 128)
    sources = (block_row[0], block_col[0], vectors, row_mass, col_mass)
    laid_out = pl.pallas_call(
        prepare,
        out_shape=jax.ShapeDtypeStruct((k + META, own * bsize), bf16),
        in_specs=[pl.BlockSpec(memory_space=pltpu.SMEM)]
        + [pl.BlockSpec(memory_space=pltpu.HBM)] * len(sources),
        out_specs=pl.BlockSpec(memory_space=pltpu.VMEM),
        scratch_shapes=[pltpu.SemaphoreType.DMA((len(sources),))]
        + [pltpu.VMEM((rows, own * bsize), jnp.float32) for rows in (half, half, k)]
        + [pltpu.VMEM(v.shape, v.dtype) for v in sources],
        name="prepare",
    )(counts, *(pltpu.with_memory_space_constraint(v, pltpu.HBM) for v in sources))
    small = jnp.concatenate([off, laid_out], axis=0)

    home = full_part(tile, has_full, n_col // 2, part, chip, core)
    home = home.reshape(part, half, 128).transpose(1, 0, 2).reshape(half * part, 128)

    together = lax.optimization_barrier
    where = jnp.stack([row, chip, core]).astype(jnp.int32)
    home, smalls, where = together((home, along_rows(small), where))
    homes, smalls = along_rows(home), along_one_chip_axis(smalls)
    smalls, homes[1] = together((smalls, homes[1]))
    smalls = jnp.concatenate(smalls + along_other_chip_axis(smalls))
    homes, smalls = together((homes, smalls))
    others = swap(smalls, "core", 1)
    homes = along_one_chip_axis(homes)
    last = along_other_chip_axis(homes)

    height, width = 2 * n_col * bsize, 2 * n_row * bsize
    slots = n_dev * OFF_CAP + 2 * UNROLL
    f32, i32, vmem, smem = jnp.float32, jnp.int32, pltpu.VMEM, pltpu.SMEM
    pair, twice, mass = (n_dev, k, 128), (2 * n_dev, k, 128), (n_dev, 8, 128)
    smem_spec, vmem_spec, any_spec = (pl.BlockSpec(memory_space=m) for m in (smem, vmem, pl.ANY))
    arrays = [
        ((8, 128), f32), ((slots // 2, 128, 128), bf16), (mass, f32), (mass, f32),
        (pair, bf16), (twice, bf16), (twice, f32), (twice, f32),
    ]
    lists, *unpacked = pl.pallas_call(
        functools.partial(unpack, n_row, n_col),
        out_shape=[jax.ShapeDtypeStruct((2 * slots + 8,), i32)]
        + [vmem(*v) for v in arrays],
        in_specs=[smem_spec, any_spec, any_spec],
        out_specs=[smem_spec] + [vmem_spec] * len(arrays),
        scratch_shapes=[
            vmem((n_dev, 128), i32),
            smem((n_dev, 128), i32),
            pltpu.SemaphoreType.DMA((3,)),
            vmem((n_dev,) + small.shape, bf16),
        ],
        compiler_params=pltpu.CompilerParams(vmem_limit_bytes=VMEM_LIMIT // 2),
        cost_estimate=pl.CostEstimate(
            flops=0, bytes_accessed=4 * n_dev * small.size * 2, transcendentals=0
        ),
        name="unpack",
    )(where, smalls, others)
    last, lists = together((last, lists))
    mine = homes + last
    fulls = mine + [swap(v, "core", 1) for v in mine]
    return pl.pallas_call(
        functools.partial(iterate, n_row, n_col, n_cap, float(n_dev * own * bsize)),
        out_shape=jax.ShapeDtypeStruct((own, k * bsize), f32),
        in_specs=[smem_spec] * 2 + [vmem_spec] * len(arrays) + [any_spec] * len(fulls),
        out_specs=vmem_spec,
        scratch_shapes=[
            pltpu.SemaphoreType.DMA((len(fulls),)),
            vmem((n_dev,) + home.shape, bf16),
            vmem((n_row, height, 128), f32),
            vmem((n_row, height, 2 * width), bf16),
            *[vmem(*v) for v in arrays[4:]],
            vmem(pair, f32), vmem(pair, bf16), vmem(twice, bf16),
            vmem(pair, f32), vmem(twice, f32), vmem(twice, f32),
            vmem((n_dev, 2 * k, 128), bf16),
            vmem((k, k), f32),
        ],
        compiler_params=pltpu.CompilerParams(vmem_limit_bytes=VMEM_LIMIT),
        name="iterate",
    )(where, lists, *(pltpu.with_memory_space_constraint(v, vmem) for v in unpacked), *fulls)


def rotate(projected, gram):
    lower = jnp.linalg.cholesky(gram)
    inverse = lax.linalg.triangular_solve(
        lower, jnp.eye(gram.shape[0], dtype=jnp.float32), left_side=True, lower=True
    )
    return jnp.einsum(
        "kl,bli->bki",
        inverse,
        projected,
        precision=lax.Precision.HIGHEST,
        preferred_element_type=jnp.float32,
    )


def local_gram(projected):
    return jnp.einsum(
        "bki,bli->kl",
        projected,
        projected,
        precision=lax.Precision.HIGHEST,
        preferred_element_type=jnp.float32,
    )


def split_by_tile(blocks, block_row, block_col, counts, vectors, row_mass, col_mass):
    tile = blocks[0, 0]
    n_cap = tile.shape[0]
    bsize = row_mass.shape[1]
    vecs = vectors.shape[1] // bsize
    own = vectors.shape[0]
    n_row = lax.axis_size("row")
    n_col = lax.axis_size("col")
    row_panel = own * n_col
    col_panel = own * n_row
    total_boxes = float(own * bsize * n_row * n_col)
    rows_idx = block_row[0, 0]
    cols_idx = block_col[0, 0]
    live = jnp.arange(n_cap) < counts[0, 0]
    fwd_ids = jnp.where(live, rows_idx, row_panel)
    bwd_ids = jnp.where(live, cols_idx, col_panel)
    square = tile.reshape(n_cap, bsize, bsize)
    inv_col = 1.0 / jnp.sqrt(col_mass)
    current = vectors.reshape(own, vecs, bsize)
    for step in range(ITERS):
        scaled = (current * inv_col[:, None, :]).astype(jnp.bfloat16).reshape(own, vecs * bsize)
        panel = lax.all_gather(scaled, "row", axis=0, tiled=True)
        forward_taken = jnp.take(panel.reshape(col_panel, vecs, bsize), cols_idx, axis=0)
        forward_product = jnp.einsum(
            "bij,bkj->bki", square, forward_taken, preferred_element_type=jnp.float32
        )
        forward_summed = jax.ops.segment_sum(forward_product, fwd_ids, num_segments=row_panel + 1)
        rows_sum = lax.psum_scatter(
            forward_summed[:row_panel].reshape(row_panel, vecs * bsize),
            "col",
            scatter_dimension=0,
            tiled=True,
        )
        weighted = (rows_sum.reshape(own, vecs, bsize) * row_mass[:, None, :]).astype(jnp.bfloat16)
        whole_rows = lax.all_gather(weighted.reshape(own, vecs * bsize), "col", axis=0, tiled=True)
        taken = jnp.take(whole_rows.reshape(row_panel, vecs, bsize), rows_idx, axis=0)
        product = jnp.einsum("bij,bki->bkj", square, taken, preferred_element_type=jnp.float32)
        summed = jax.ops.segment_sum(product, bwd_ids, num_segments=col_panel + 1)
        cols_sum = lax.psum_scatter(
            summed[:col_panel].reshape(col_panel, vecs * bsize),
            "row",
            scatter_dimension=0,
            tiled=True,
        )
        projected = cols_sum.reshape(own, vecs, bsize) * inv_col[:, None, :]
        gram = lax.psum(local_gram(projected), ("row", "col")) / total_boxes
        current = rotate(projected, gram)
    return current.reshape(own, vecs * bsize)


def fits(n_row, n_col, blocks, vectors, row_mass):
    own, bsize = row_mass.shape[0] // (n_row * n_col), row_mass.shape[1]
    n_cap = blocks.shape[2]
    dense = n_row * (own * n_col * bsize) * (own * n_row * bsize) * 4
    shapes = own * bsize == 128 and vectors.shape[1] == bsize * bsize and n_cap == 128
    return dense <= VMEM_LIMIT // 4 and shapes and n_cap % (16 * n_col) == 0 and n_row == 4 and n_col == 8


def solution(mesh):
    n_row, n_col = mesh.shape["row"], mesh.shape["col"]

    def run(blocks, block_row, block_col, counts, vectors, row_mass, col_mass):
        args = (blocks, block_row, block_col, counts, vectors, row_mass, col_mass)
        if fits(n_row, n_col, blocks, vectors, row_mass):
            devices = mesh.devices.reshape(n_row, n_col // 2, 2)
            grid, col = jax.sharding.Mesh(devices, ("row", "chip", "core")), ("chip", "core")
            body = functools.partial(whole_on_each, n_row, n_col)
        else:
            grid, col, body = mesh, ("col",), split_by_tile
        by_row, by_col = P(("row",) + col, None), P(col + ("row",), None)
        in_specs = (
            P("row", col, None, None), P("row", col, None), P("row", col, None), P("row", col),
            by_col, by_row, by_col,
        )
        return jax.shard_map(
            body, mesh=grid, in_specs=in_specs, out_specs=by_col, check_vma=False
        )(*args)

    return run
```

```python
import functools

import jax
import jax.numpy as jnp
from jax import lax
from jax.experimental import pallas as pl
from jax.experimental.pallas import tpu as pltpu
from jax.sharding import PartitionSpec as P

ITERS = 4
OFF_CAP = 8
META = 16
UNROLL = 16
BATCH = 4
VMEM_LIMIT = 36 * 1024 * 1024

NT = (((1,), (1,)), ((), ()))
NN = (((1,), (0,)), ((), ()))


def dot(a, b, dims=NN):
    return lax.dot_general(a, b, dims, preferred_element_type=jnp.float32)


def split2(x):
    hi = x.astype(jnp.bfloat16)
    return hi, (x - hi.astype(jnp.float32)).astype(jnp.bfloat16)


def inverse_factor(gram):
    n = gram.shape[0]
    rows = lax.broadcasted_iota(jnp.int32, (n, n), 0)
    cols = lax.broadcasted_iota(jnp.int32, (n, n), 1)
    eye = (rows == cols).astype(jnp.float32)
    both = jnp.concatenate([gram, eye], axis=1)
    count, shape = n // 8, (8, 2 * n)
    tiles = [both[8 * t : 8 * t + 8] for t in range(count)]
    sub = lax.broadcasted_iota(jnp.int32, shape, 0)
    out = []
    for b in range(count):
        column = {
            t: [jnp.broadcast_to(tiles[t][:, 8 * b + s : 8 * b + s + 1], shape) for s in range(8)]
            for t in range(b, count)
        }
        row = [jnp.broadcast_to(tiles[b][s : s + 1], shape) for s in range(8)]
        a = [
            [jnp.broadcast_to(column[b][j][s : s + 1], shape) if j >= s else None for j in range(8)]
            for s in range(8)
        ]
        done = jnp.zeros(shape, jnp.float32)
        for s in range(8):
            root = lax.rsqrt(a[s][s])
            inv = root * root
            inv = inv * (2.0 - a[s][s] * inv)
            step = row[s] * inv
            done = jnp.where(sub == s, row[s] * root, done)
            for i in range(s + 1, 8):
                part = a[s][i] * inv
                for j in range(i, 8):
                    a[i][j] = a[i][j] - part * a[s][j]
                row[i] = row[i] - a[s][i] * step
                for t in range(b + 1, count):
                    column[t][i] = column[t][i] - column[t][s] * part
            for t in range(b + 1, count):
                tiles[t] = tiles[t] - column[t][s] * step
        out.append(done)
    return jnp.concatenate(out, axis=0)[:, n:]


def place_of(own, n_row, n_dev):
    here, chip, core = own[0], own[1], own[2]

    def at_device(r, c):
        dr, dc, dk = here ^ r, chip ^ (c // 2), core ^ (c % 2)
        dx, dy = dc & 1, dc >> 1
        order = jnp.where(dr < 2, 2 * dx, 4 + 2 * dy) + jnp.where(
            jnp.where(dr < 2, dy, dx) > 0, n_dev // 4, 0
        )
        return dk * (n_dev // 2) + order + (dr & 1)

    def device_at(d):
        far, second = (d >> 2) & 1, (d >> 3) & 1
        first = (d >> 1) & 1
        dc = jnp.where(far == 0, 2 * second + first, 2 * first + second)
        return here ^ (2 * far + (d & 1)), 2 * (chip ^ dc) + (core ^ (d >> 4))

    return at_device, device_at


def copy_in(pairs, sems):
    copies = [pltpu.make_async_copy(src, dst, sems.at[i]) for i, (src, dst) in enumerate(pairs)]
    for copy in copies:
        copy.start()
    return copies


def clear(refs):
    for ref in refs:
        for q in range(ref.shape[0]):
            ref[q] = jnp.zeros_like(ref[q])


def left_half(shape):
    return lax.broadcasted_iota(jnp.int32, shape, len(shape) - 1) < 64


def store_twice(pair, twice, q, x):
    pair[q] = x.astype(pair.dtype)
    turned, left = pltpu.roll(x, 64, 1), left_half(x.shape)
    twice[2 * q] = jnp.where(left, x, turned).astype(twice.dtype)
    twice[2 * q + 1] = jnp.where(left, turned, x).astype(twice.dtype)


def gather_pair(q, first, second):
    left = left_half(first.shape[1:])
    apart = jnp.where(left, first[2 * q + 1], second[2 * q])
    return jnp.where(left, first[2 * q], second[2 * q + 1]) + pltpu.roll(apart, 64, 1)


def add_products(n_group, blk, dims, lists, from_at, source, to_at, first, second):
    left = left_half(source.shape[1:])

    def multiply(pairs):
        return [
            dot(
                jnp.where(left, source[lists[from_at + 2 * p]], source[lists[from_at + 2 * p + 1]]),
                blk[p],
                dims,
            )
            for p in pairs
        ]

    def add(pairs, prods):
        for p, prod in zip(pairs, prods):
            a, b = lists[to_at + 2 * p], lists[to_at + 2 * p + 1]
            first[a] = first[a] + prod
            second[b] = second[b] + prod

    def group(i, carry):
        batches = [
            [i * UNROLL + at + u for u in range(BATCH)] for at in range(0, UNROLL, BATCH)
        ]
        prods = multiply(batches[0])
        for now, later in zip(batches, batches[1:]):
            ahead = multiply(later)
            add(now, prods)
            prods = ahead
        add(batches[-1], prods)
        return carry

    lax.fori_loop(0, n_group, group, 0)


def unpack(
    n_row, n_col, own, mine, other,
    lists, place, blk, rm, ic, vs, vd, w1, w2, ints, meta, sems, small,
):
    n_dev = n_row * n_col
    k = vs.shape[1]
    half = k // 2
    rblk, cblk = 2 * n_col, 2 * n_row
    vec_at = OFF_CAP * half
    meta_at = vec_at + k
    at_device, device_at = place_of(own, n_row, n_dev)
    slots = 2 * blk.shape[0]

    first, second = pl.ds(0, n_dev // 2), pl.ds(n_dev // 2, n_dev // 2)
    for copy in copy_in([(mine, small.at[first]), (other, small.at[second])], sems):
        copy.wait()
    for d in range(n_dev):
        rows = small[d, meta_at : meta_at + META, :].astype(jnp.float32)
        ints[d : d + 1, :] = rows[8:9].astype(jnp.int32)
    to_scalars = pltpu.make_async_copy(ints, meta, sems.at[2])
    to_scalars.start()

    for r in range(n_row):
        for c in range(n_col):
            q, p, d = c * n_row + r, r * n_col + c, at_device(r, c)
            rows = small[d, meta_at : meta_at + META, :].astype(jnp.float32)
            rm[p] = jnp.broadcast_to(rows[0:1] + rows[1:2] + rows[2:3], (8, 128))
            ic[q] = jnp.broadcast_to(rows[3:4] + rows[4:5] + rows[5:6], (8, 128))
            store_twice(vs, vd, q, small[d, vec_at : vec_at + k, :].astype(jnp.float32))
    to_scalars.wait()

    lanes = lax.broadcasted_iota(jnp.int32, (half, 128), 1)

    def device(d, n):
        count = meta[d, 2 * OFF_CAP]
        count = jnp.where(count > OFF_CAP, 0, count)
        r, c = device_at(d)
        for s in range(OFF_CAP):
            lists[n + s] = c * cblk + meta[d, OFF_CAP + s]
            lists[slots + n + s] = r * rblk + meta[d, s]
            x = small[d, s * half : (s + 1) * half, :].astype(jnp.float32)
            turned = pltpu.roll(x, 64, 1)
            side = (n + s) % 2
            here = (lanes // 64) == side
            even = jnp.where(here, jnp.where(side == 0, x, turned), 0.0)
            odd = jnp.where(here, jnp.where(side == 0, turned, x), 0.0)
            at = pl.multiple_of(side * k, k)
            both = jnp.concatenate([even, odd], axis=0).astype(jnp.bfloat16)
            blk[(n + s) // 2, pl.ds(at, k), :] = both
        return n + count

    n_live = lax.fori_loop(0, n_dev, device, jnp.int32(0))
    for u in range(2 * UNROLL - 1):
        lists[n_live + u] = 0
        lists[slots + n_live + u] = 0
        at = pl.multiple_of((n_live + u) % 2 * k, k)
        blk[(n_live + u) // 2, pl.ds(at, k), :] = jnp.zeros((k, 128), jnp.bfloat16)
    lists[2 * slots] = (n_live + 2 * UNROLL - 1) // (2 * UNROLL)

    for r in range(n_row):
        h = jnp.int32(0)
        for c in range(n_col):
            h = jnp.where(meta[at_device(r, c), 2 * OFF_CAP] > OFF_CAP, c, h)
        lists[2 * slots + 1 + r] = h
        index = small[at_device(r, h), meta_at : meta_at + META, :].astype(jnp.float32)
        place[r : r + 1, :] = index[7:8] * float(rblk) + index[6:7]

    clear([w1, w2])
    add_products(lists[2 * slots], blk, NT, lists, 0, vd, slots, w1, w2)


def iterate(n_row, n_col, n_cap, total, own, lists, place, *rest):
    blk, rm, ic, *starts = rest[:7]
    fulls, out = rest[7:15], rest[15]
    sems, full, tmp, home, vs, vd, w1, w2 = rest[16:24]
    w, wt, wd, y, y1, y2, ph, linv = rest[24:]
    slots = 2 * blk.shape[0]
    n_dev = n_row * n_col
    k = vs.shape[1]
    half = k // 2
    rpairs, cpairs = n_col, n_row
    rblk, cblk = 2 * rpairs, 2 * cpairs
    part = n_cap // n_col
    width = cpairs * 128
    at_device, _ = place_of(own, n_row, n_dev)

    def laid_out(refs, whole):
        at, pairs = 0, []
        for ref in refs:
            pairs.append((ref, whole.at[pl.ds(at, ref.shape[0])]))
            at += ref.shape[0]
        return pairs

    copies = copy_in(laid_out(fulls, full), sems)
    for start, ref in zip(starts, (vs, vd, w1, w2)):
        for q in range(ref.shape[0]):
            ref[q] = start[q]
    clear([y, y1, y2])
    for copy in copies:
        copy.wait()
    n_group = lists[2 * slots]

    left = lax.broadcasted_iota(jnp.int32, (rblk, 128), 1) < 64
    homes = []
    for r in range(n_row):
        homes.append(lists[2 * slots + 1 + r])
        want = lax.broadcasted_iota(jnp.int32, (cblk * rblk, n_cap), 0).astype(jnp.float32)
        select = jnp.where(want == place[r : r + 1, :], 1.0, 0.0).astype(jnp.bfloat16)

        parts = [at_device(r, 2 * i + j) for j in range(2) for i in range(n_col // 2)]

        def build(i, carry, parts=parts, select=select):
            ms = [4 * i + d for d in range(4)]
            denses = []
            for m in ms:
                at = pl.multiple_of(m * part, part)
                slots = jnp.concatenate([full[d, pl.ds(at, part), :] for d in parts], axis=0)
                denses.append(dot(select, slots))
            for m, dense in zip(ms, denses):
                for u in range(cpairs):
                    a = dense[2 * u * rblk : (2 * u + 1) * rblk]
                    b = dense[(2 * u + 1) * rblk : (2 * u + 2) * rblk]
                    even = jnp.where(left, a, pltpu.roll(b, 64, 1))
                    odd = jnp.where(left, pltpu.roll(a, 64, 1), b)
                    tmp[u, pl.ds(m, rblk, stride=k), :] = even
                    tmp[u, pl.ds(m + half, rblk, stride=k), :] = odd
            return carry

        lax.fori_loop(0, half // 4, build, 0, unroll=2)

        def cut(i, carry, r=r):
            at = pl.multiple_of(i * k, k)
            for u in range(cpairs):
                hi, lo = split2(tmp[u, pl.ds(at, k), :])
                home[r, pl.ds(at, k), u * 128 : (u + 1) * 128] = hi
                home[r, pl.ds(at, k), width + u * 128 : width + (u + 1) * 128] = lo
            return carry

        lax.fori_loop(0, rblk, cut, 0, unroll=8)


    def iteration(it, carry):
        @pl.when(it > 0)
        def _():
            lh, ll = split2(linv[...])
            turn = jnp.concatenate([lh, lh, ll], axis=1)
            for q in range(0, n_dev, 4):
                hi = jnp.concatenate([ph[q + d, :k, :] for d in range(4)], axis=1)
                lo = jnp.concatenate([ph[q + d, k:, :] for d in range(4)], axis=1)
                current = dot(turn, jnp.concatenate([hi, lo, hi], axis=0))
                for d in range(4):
                    x = current[:, d * 128 : (d + 1) * 128] * ic[q + d, 0:1, :]
                    store_twice(vs, vd, q + d, x)

        for r in range(n_row):
            base = homes[r] * cpairs
            vec = jnp.concatenate([vs[base + u] for u in range(cpairs)] * 2, axis=1)
            for p in range(0, rpairs, 2):
                prod = dot(vec, home[r, p * 128 : (p + 2) * 128, :], NT)
                w[r * rpairs + p] = prod[:, :128]
                w[r * rpairs + p + 1] = prod[:, 128:]

        @pl.when(it > 0)
        def _():
            add_products(n_group, blk, NT, lists, 0, vd, slots, w1, w2)

        for p in range(n_dev):
            x = w[p] + gather_pair(p, w1, w2)
            store_twice(wt, wd, p, x * rm[p, 0:1, :])

        def back(r, u):
            vec = jnp.concatenate([wt[r * rpairs + p] for p in range(rpairs)], axis=1)
            cols = slice(u * 128, (u + 2) * 128)
            tail = slice(width + u * 128, width + (u + 2) * 128)
            return dot(vec, home[r, :, cols]) + dot(vec, home[r, :, tail])

        steps = [(r, u) for r in range(n_row) for u in range(0, cpairs, 2)]
        prod = back(*steps[0])
        for i, (r, u) in enumerate(steps):
            ahead = back(*steps[i + 1]) if i + 1 < len(steps) else None
            q = homes[r] * cpairs + u
            y[q] = y[q] + prod[:, :128]
            y[q + 1] = y[q + 1] + prod[:, 128:]
            prod = ahead

        add_products(n_group, blk, NN, lists, slots, wd, 0, y1, y2)

        both = jnp.zeros((2 * k, k), jnp.float32)
        for q in range(0, n_dev, 4):
            his, los = [], []
            for d in range(q, q + 4):
                x = y[d] + gather_pair(d, y1, y2)
                hi, lo = split2(x * ic[d, 0:1, :])
                ph[d, :k, :] = hi
                ph[d, k:, :] = lo
                his.append(hi)
                los.append(lo)
            hi = jnp.concatenate(his, axis=1)
            lo = jnp.concatenate(los, axis=1)
            both = both + dot(jnp.concatenate([hi, lo], axis=0), hi, NT)
        gram = (both[:k] + (both[k:] + both[k:].T)) / total
        clear([y, y1, y2, w1, w2])
        linv[...] = inverse_factor(gram)
        return carry

    lax.fori_loop(0, ITERS, iteration, 0)
    lh, ll = split2(linv[...])
    q = (2 * own[1] + own[2]) * n_row + own[0]
    hi, lo = ph[q, :k, :], ph[q, k:, :]
    w[0] = dot(lh, hi) + dot(ll, hi) + dot(lh, lo)
    even, odd = w[0, pl.ds(0, half, stride=2), :], w[0, pl.ds(1, half, stride=2), :]
    left = left_half(even.shape)
    first = jnp.where(left, even, pltpu.roll(odd, 64, 1))
    second = jnp.where(left, pltpu.roll(even, 64, 1), odd)
    for i in range(half):
        out[0:1, i * 128 : (i + 1) * 128] = first[i : i + 1]
        out[1:2, i * 128 : (i + 1) * 128] = second[i : i + 1]


def split3(x):
    parts = []
    for _ in range(3):
        parts.append(x.astype(jnp.bfloat16).astype(jnp.float32))
        x = x - parts[-1]
    return parts


def prepare(count, *rest):
    sources, out, sems, spread, first, second, both = rest[:6], *rest[6:12]
    sources = (sources[0].at[pl.ds(0, 16)], *sources[1:])
    for copy in copy_in(list(zip(sources, rest[12:])), sems):
        copy.wait()
    tile, rows, cols, vectors, row_mass, col_mass = rest[12:]
    f32, bf16 = jnp.float32, jnp.bfloat16
    half = first.shape[0]
    vec_at = OFF_CAP * half
    slots = tile[...].astype(f32)[:OFF_CAP]
    for i in range(half):
        spread[pl.ds(i, OFF_CAP, stride=half), :] = slots[:, i * 128 : (i + 1) * 128]
        first[i : i + 1, :] = vectors[0:1, i * 128 : (i + 1) * 128]
        second[i : i + 1, :] = vectors[1:2, i * 128 : (i + 1) * 128]
    x, z = first[...], second[...]
    left = left_half(x.shape)
    both[pl.ds(0, half, stride=2), :] = jnp.where(left, x, pltpu.roll(z, 64, 1))
    both[pl.ds(1, half, stride=2), :] = jnp.where(left, pltpu.roll(x, 64, 1), z)
    inv = 1.0 / jnp.sqrt(jnp.concatenate([col_mass[0:1, :], col_mass[1:2, :]], axis=1))
    out[:vec_at, :] = spread[...].astype(bf16)
    out[vec_at : vec_at + 2 * half, :] = (both[...] * inv).astype(bf16)

    sub = lax.broadcasted_iota(jnp.int32, (META, 128), 0)

    def stacked(at, values):
        result = jnp.zeros((META, 128), f32)
        for i, value in enumerate(values):
            result = jnp.where(sub == at + i, value, result)
        return result

    mass = jnp.concatenate([row_mass[0:1, :], row_mass[1:2, :]], axis=1)
    source = lax.broadcasted_iota(jnp.int32, (128, 128), 0)
    lane = lax.broadcasted_iota(jnp.int32, (128, 128), 1)
    chosen = source == (lane // 64) * 64 + 2 * (lane % half) + (lane % 64) // half
    masses = dot(stacked(0, split3(mass)).astype(bf16), jnp.where(chosen, 1.0, 0.0).astype(bf16))
    r, c = rows[...].astype(f32), cols[...].astype(f32)
    lane = lane[:8]
    moved = pltpu.roll(jnp.broadcast_to(c, (8, 128)), OFF_CAP, 1)
    short = jnp.where(lane == 2 * OFF_CAP, count[0, 0].astype(f32), 0.0)
    short = jnp.where(lane < OFF_CAP, r, jnp.where(lane < 2 * OFF_CAP, moved, short))
    packed = masses + stacked(3, split3(inv) + [r, c, short[0:1]])
    out[vec_at + 2 * half :, :] = packed.astype(bf16)


def swap(x, axis, distance):
    size = lax.axis_size(axis)
    return lax.ppermute(x, axis, [(i, i ^ distance) for i in range(size)])


def along_rows(x):
    return [x] + [swap(x, "row", s) for s in range(1, lax.axis_size("row"))]


def along_one_chip_axis(x):
    near, far = jnp.stack(x[:2]), jnp.stack(x[2:])
    return [
        jnp.concatenate([near, swap(near, "chip", 1)]),
        jnp.concatenate([far, swap(far, "chip", 2)]),
    ]


def along_other_chip_axis(x):
    near, far = x
    return [swap(near, "chip", 2), swap(far, "chip", 1)]


def full_part(tile, has_full, n_chip, part, chip, core):
    tile = tile.reshape(2, n_chip, part, tile.shape[1])
    none = jnp.zeros(tile.shape[1:], tile.dtype)
    kept, sent = (
        jnp.where(has_full, lax.dynamic_index_in_dim(tile, i, 0, False), none)
        for i in (core, 1 - core)
    )
    both = kept + swap(sent, "core", 1)
    mine = lax.dynamic_index_in_dim(both, chip, 0, False)
    for s in range(1, n_chip):
        mine = mine + swap(lax.dynamic_index_in_dim(both, chip ^ s, 0, False), "chip", s)
    return mine


def whole_on_each(n_row, n_col, blocks, block_row, block_col, counts, vectors, row_mass, col_mass):
    tile = blocks[0, 0]
    n_cap = tile.shape[0]
    own, bsize = row_mass.shape
    k = vectors.shape[1] // bsize
    half = bsize // 2
    part = n_cap // n_col
    n_dev = n_row * n_col
    count = counts[0, 0]
    has_full = count > OFF_CAP
    bf16 = jnp.bfloat16
    row, chip, core = (lax.axis_index(name) for name in ("row", "chip", "core"))

    sources = (tile, block_row[0], block_col[0], vectors, row_mass, col_mass)
    small = pl.pallas_call(
        prepare,
        out_shape=jax.ShapeDtypeStruct((OFF_CAP * half + k + META, own * bsize), bf16),
        in_specs=[pl.BlockSpec(memory_space=pltpu.SMEM)]
        + [pl.BlockSpec(memory_space=pltpu.HBM)] * len(sources),
        out_specs=pl.BlockSpec(memory_space=pltpu.VMEM),
        scratch_shapes=[pltpu.SemaphoreType.DMA((len(sources),))]
        + [pltpu.VMEM((rows, own * bsize), jnp.float32) for rows in (OFF_CAP * half, half, half, k)]
        + [pltpu.VMEM((16, bsize * bsize), bf16)]
        + [pltpu.VMEM(v.shape, v.dtype) for v in sources[1:]],
        name="prepare",
    )(counts, *(pltpu.with_memory_space_constraint(v, pltpu.HBM) for v in sources))

    home = full_part(tile, has_full, n_col // 2, part, chip, core)
    home = home.reshape(part, half, 128).transpose(1, 0, 2).reshape(half * part, 128)

    together = lax.optimization_barrier
    where = jnp.stack([row, chip, core]).astype(jnp.int32)
    home, smalls, where = together((home, along_rows(small), where))
    homes, smalls = along_rows(home), along_one_chip_axis(smalls)
    smalls, homes[1] = together((smalls, homes[1]))
    smalls = jnp.concatenate(smalls + along_other_chip_axis(smalls))
    homes, smalls = together((homes, smalls))
    others = swap(smalls, "core", 1)
    homes = along_one_chip_axis(homes)
    last = along_other_chip_axis(homes)

    height, width = 2 * n_col * bsize, 2 * n_row * bsize
    slots = n_dev * OFF_CAP + 2 * UNROLL
    f32, i32, vmem, smem = jnp.float32, jnp.int32, pltpu.VMEM, pltpu.SMEM
    pair, twice, mass = (n_dev, k, 128), (2 * n_dev, k, 128), (n_dev, 8, 128)
    smem_spec, vmem_spec, any_spec = (pl.BlockSpec(memory_space=m) for m in (smem, vmem, pl.ANY))
    arrays = [
        ((8, 128), f32), ((slots // 2, 128, 128), bf16), (mass, f32), (mass, f32),
        (pair, bf16), (twice, bf16), (twice, f32), (twice, f32),
    ]
    lists, *unpacked = pl.pallas_call(
        functools.partial(unpack, n_row, n_col),
        out_shape=[jax.ShapeDtypeStruct((2 * slots + 8,), i32)]
        + [vmem(*v) for v in arrays],
        in_specs=[smem_spec, any_spec, any_spec],
        out_specs=[smem_spec] + [vmem_spec] * len(arrays),
        scratch_shapes=[
            vmem((n_dev, 128), i32),
            smem((n_dev, 128), i32),
            pltpu.SemaphoreType.DMA((3,)),
            vmem((n_dev,) + small.shape, bf16),
        ],
        compiler_params=pltpu.CompilerParams(vmem_limit_bytes=VMEM_LIMIT // 2),
        cost_estimate=pl.CostEstimate(
            flops=0, bytes_accessed=4 * n_dev * small.size * 2, transcendentals=0
        ),
        name="unpack",
    )(where, smalls, others)
    last, lists = together((last, lists))
    mine = homes + last
    fulls = mine + [swap(v, "core", 1) for v in mine]
    return pl.pallas_call(
        functools.partial(iterate, n_row, n_col, n_cap, float(n_dev * own * bsize)),
        out_shape=jax.ShapeDtypeStruct((own, k * bsize), f32),
        in_specs=[smem_spec] * 2 + [vmem_spec] * len(arrays) + [any_spec] * len(fulls),
        out_specs=vmem_spec,
        scratch_shapes=[
            pltpu.SemaphoreType.DMA((len(fulls),)),
            vmem((n_dev,) + home.shape, bf16),
            vmem((n_row, height, 128), f32),
            vmem((n_row, height, 2 * width), bf16),
            *[vmem(*v) for v in arrays[4:]],
            vmem(pair, f32), vmem(pair, bf16), vmem(twice, bf16),
            vmem(pair, f32), vmem(twice, f32), vmem(twice, f32),
            vmem((n_dev, 2 * k, 128), bf16),
            vmem((k, k), f32),
        ],
        compiler_params=pltpu.CompilerParams(vmem_limit_bytes=VMEM_LIMIT),
        name="iterate",
    )(where, lists, *(pltpu.with_memory_space_constraint(v, vmem) for v in unpacked), *fulls)


def rotate(projected, gram):
    lower = jnp.linalg.cholesky(gram)
    inverse = lax.linalg.triangular_solve(
        lower, jnp.eye(gram.shape[0], dtype=jnp.float32), left_side=True, lower=True
    )
    return jnp.einsum(
        "kl,bli->bki",
        inverse,
        projected,
        precision=lax.Precision.HIGHEST,
        preferred_element_type=jnp.float32,
    )


def local_gram(projected):
    return jnp.einsum(
        "bki,bli->kl",
        projected,
        projected,
        precision=lax.Precision.HIGHEST,
        preferred_element_type=jnp.float32,
    )


def split_by_tile(blocks, block_row, block_col, counts, vectors, row_mass, col_mass):
    tile = blocks[0, 0]
    n_cap = tile.shape[0]
    bsize = row_mass.shape[1]
    vecs = vectors.shape[1] // bsize
    own = vectors.shape[0]
    n_row = lax.axis_size("row")
    n_col = lax.axis_size("col")
    row_panel = own * n_col
    col_panel = own * n_row
    total_boxes = float(own * bsize * n_row * n_col)
    rows_idx = block_row[0, 0]
    cols_idx = block_col[0, 0]
    live = jnp.arange(n_cap) < counts[0, 0]
    fwd_ids = jnp.where(live, rows_idx, row_panel)
    bwd_ids = jnp.where(live, cols_idx, col_panel)
    square = tile.reshape(n_cap, bsize, bsize)
    inv_col = 1.0 / jnp.sqrt(col_mass)
    current = vectors.reshape(own, vecs, bsize)
    for step in range(ITERS):
        scaled = (current * inv_col[:, None, :]).astype(jnp.bfloat16).reshape(own, vecs * bsize)
        panel = lax.all_gather(scaled, "row", axis=0, tiled=True)
        forward_taken = jnp.take(panel.reshape(col_panel, vecs, bsize), cols_idx, axis=0)
        forward_product = jnp.einsum(
            "bij,bkj->bki", square, forward_taken, preferred_element_type=jnp.float32
        )
        forward_summed = jax.ops.segment_sum(forward_product, fwd_ids, num_segments=row_panel + 1)
        rows_sum = lax.psum_scatter(
            forward_summed[:row_panel].reshape(row_panel, vecs * bsize),
            "col",
            scatter_dimension=0,
            tiled=True,
        )
        weighted = (rows_sum.reshape(own, vecs, bsize) * row_mass[:, None, :]).astype(jnp.bfloat16)
        whole_rows = lax.all_gather(weighted.reshape(own, vecs * bsize), "col", axis=0, tiled=True)
        taken = jnp.take(whole_rows.reshape(row_panel, vecs, bsize), rows_idx, axis=0)
        product = jnp.einsum("bij,bki->bkj", square, taken, preferred_element_type=jnp.float32)
        summed = jax.ops.segment_sum(product, bwd_ids, num_segments=col_panel + 1)
        cols_sum = lax.psum_scatter(
            summed[:col_panel].reshape(col_panel, vecs * bsize),
            "row",
            scatter_dimension=0,
            tiled=True,
        )
        projected = cols_sum.reshape(own, vecs, bsize) * inv_col[:, None, :]
        gram = lax.psum(local_gram(projected), ("row", "col")) / total_boxes
        current = rotate(projected, gram)
    return current.reshape(own, vecs * bsize)


def fits(n_row, n_col, blocks, vectors, row_mass):
    own, bsize = row_mass.shape[0] // (n_row * n_col), row_mass.shape[1]
    n_cap = blocks.shape[2]
    dense = n_row * (own * n_col * bsize) * (own * n_row * bsize) * 4
    shapes = own * bsize == 128 and vectors.shape[1] == bsize * bsize and n_cap == 128
    return dense <= VMEM_LIMIT // 4 and shapes and n_cap % (16 * n_col) == 0 and n_row == 4 and n_col == 8


def solution(mesh):
    n_row, n_col = mesh.shape["row"], mesh.shape["col"]

    def run(blocks, block_row, block_col, counts, vectors, row_mass, col_mass):
        args = (blocks, block_row, block_col, counts, vectors, row_mass, col_mass)
        if fits(n_row, n_col, blocks, vectors, row_mass):
            devices = mesh.devices.reshape(n_row, n_col // 2, 2)
            grid, col = jax.sharding.Mesh(devices, ("row", "chip", "core")), ("chip", "core")
            body = functools.partial(whole_on_each, n_row, n_col)
        else:
            grid, col, body = mesh, ("col",), split_by_tile
        by_row, by_col = P(("row",) + col, None), P(col + ("row",), None)
        in_specs = (
            P("row", col, None, None), P("row", col, None), P("row", col, None), P("row", col),
            by_col, by_row, by_col,
        )
        return jax.shard_map(
            body, mesh=grid, in_specs=in_specs, out_specs=by_col, check_vma=False
        )(*args)

    return run
```

```python
import functools

import jax
import jax.numpy as jnp
from jax import lax
from jax.experimental import pallas as pl
from jax.experimental.pallas import tpu as pltpu
from jax.sharding import PartitionSpec as P

ITERS = 4
OFF_CAP = 8
META = 16
UNROLL = 16
BATCH = 4
VMEM_LIMIT = 36 * 1024 * 1024

NT = (((1,), (1,)), ((), ()))
NN = (((1,), (0,)), ((), ()))


def dot(a, b, dims=NN):
    return lax.dot_general(a, b, dims, preferred_element_type=jnp.float32)


def split2(x):
    hi = x.astype(jnp.bfloat16)
    return hi, (x - hi.astype(jnp.float32)).astype(jnp.bfloat16)


def inverse_factor(gram):
    n = gram.shape[0]
    rows = lax.broadcasted_iota(jnp.int32, (n, n), 0)
    cols = lax.broadcasted_iota(jnp.int32, (n, n), 1)
    eye = (rows == cols).astype(jnp.float32)
    both = jnp.concatenate([gram, eye], axis=1)
    count, shape = n // 8, (8, 2 * n)
    tiles = [both[8 * t : 8 * t + 8] for t in range(count)]
    sub = lax.broadcasted_iota(jnp.int32, shape, 0)
    out = []
    for b in range(count):
        column = {
            t: [jnp.broadcast_to(tiles[t][:, 8 * b + s : 8 * b + s + 1], shape) for s in range(8)]
            for t in range(b, count)
        }
        row = [jnp.broadcast_to(tiles[b][s : s + 1], shape) for s in range(8)]
        a = [
            [jnp.broadcast_to(column[b][j][s : s + 1], shape) if j >= s else None for j in range(8)]
            for s in range(8)
        ]
        done = jnp.zeros(shape, jnp.float32)
        for s in range(8):
            root = lax.rsqrt(a[s][s])
            inv = root * root
            inv = inv * (2.0 - a[s][s] * inv)
            step = row[s] * inv
            done = jnp.where(sub == s, row[s] * root, done)
            for i in range(s + 1, 8):
                part = a[s][i] * inv
                for j in range(i, 8):
                    a[i][j] = a[i][j] - part * a[s][j]
                row[i] = row[i] - a[s][i] * step
                for t in range(b + 1, count):
                    column[t][i] = column[t][i] - column[t][s] * part
            for t in range(b + 1, count):
                tiles[t] = tiles[t] - column[t][s] * step
        out.append(done)
    return jnp.concatenate(out, axis=0)[:, n:]


def place_of(own, n_row, n_dev):
    here, chip, core = own[0], own[1], own[2]

    def at_device(r, c):
        dr, dc, dk = here ^ r, chip ^ (c // 2), core ^ (c % 2)
        dx, dy = dc & 1, dc >> 1
        order = jnp.where(dr < 2, 2 * dx, 4 + 2 * dy) + jnp.where(
            jnp.where(dr < 2, dy, dx) > 0, n_dev // 4, 0
        )
        return dk * (n_dev // 2) + order + (dr & 1)

    def device_at(d):
        far, second = (d >> 2) & 1, (d >> 3) & 1
        first = (d >> 1) & 1
        dc = jnp.where(far == 0, 2 * second + first, 2 * first + second)
        return here ^ (2 * far + (d & 1)), 2 * (chip ^ dc) + (core ^ (d >> 4))

    return at_device, device_at


def copy_in(pairs, sems):
    copies = [pltpu.make_async_copy(src, dst, sems.at[i]) for i, (src, dst) in enumerate(pairs)]
    for copy in copies:
        copy.start()
    return copies


def clear(refs):
    for ref in refs:
        for q in range(ref.shape[0]):
            ref[q] = jnp.zeros_like(ref[q])


def left_half(shape):
    return lax.broadcasted_iota(jnp.int32, shape, len(shape) - 1) < 64


def store_twice(pair, twice, q, x):
    pair[q] = x.astype(pair.dtype)
    turned, left = pltpu.roll(x, 64, 1), left_half(x.shape)
    twice[2 * q] = jnp.where(left, x, turned).astype(twice.dtype)
    twice[2 * q + 1] = jnp.where(left, turned, x).astype(twice.dtype)


def gather_pair(q, first, second):
    left = left_half(first.shape[1:])
    apart = jnp.where(left, first[2 * q + 1], second[2 * q])
    return jnp.where(left, first[2 * q], second[2 * q + 1]) + pltpu.roll(apart, 64, 1)


def add_products(n_group, blk, dims, lists, from_at, source, to_at, first, second):
    left = left_half(source.shape[1:])

    def multiply(pairs):
        return [
            dot(
                jnp.where(left, source[lists[from_at + 2 * p]], source[lists[from_at + 2 * p + 1]]),
                blk[p],
                dims,
            )
            for p in pairs
        ]

    def add(pairs, prods):
        for p, prod in zip(pairs, prods):
            a, b = lists[to_at + 2 * p], lists[to_at + 2 * p + 1]
            first[a] = first[a] + prod
            second[b] = second[b] + prod

    def group(i, carry):
        batches = [
            [i * UNROLL + at + u for u in range(BATCH)] for at in range(0, UNROLL, BATCH)
        ]
        prods = multiply(batches[0])
        for now, later in zip(batches, batches[1:]):
            ahead = multiply(later)
            add(now, prods)
            prods = ahead
        add(batches[-1], prods)
        return carry

    lax.fori_loop(0, n_group, group, 0)


def unpack(
    n_row, n_col, own, mine, other,
    lists, place, blk, rm, ic, vs, vd, w1, w2, ints, meta, sems, small,
):
    n_dev = n_row * n_col
    k = vs.shape[1]
    half = k // 2
    rblk, cblk = 2 * n_col, 2 * n_row
    vec_at = OFF_CAP * half
    meta_at = vec_at + k
    at_device, device_at = place_of(own, n_row, n_dev)
    slots = 2 * blk.shape[0]

    first, second = pl.ds(0, n_dev // 2), pl.ds(n_dev // 2, n_dev // 2)
    for copy in copy_in([(mine, small.at[first]), (other, small.at[second])], sems):
        copy.wait()
    for d in range(n_dev):
        rows = small[d, meta_at : meta_at + META, :].astype(jnp.float32)
        ints[d : d + 1, :] = rows[8:9].astype(jnp.int32)
    to_scalars = pltpu.make_async_copy(ints, meta, sems.at[2])
    to_scalars.start()

    for r in range(n_row):
        for c in range(n_col):
            q, p, d = c * n_row + r, r * n_col + c, at_device(r, c)
            rows = small[d, meta_at : meta_at + META, :].astype(jnp.float32)
            rm[p] = jnp.broadcast_to(rows[0:1] + rows[1:2] + rows[2:3], (8, 128))
            ic[q] = jnp.broadcast_to(rows[3:4] + rows[4:5] + rows[5:6], (8, 128))
            store_twice(vs, vd, q, small[d, vec_at : vec_at + k, :].astype(jnp.float32))
    to_scalars.wait()

    lanes = lax.broadcasted_iota(jnp.int32, (half, 128), 1)

    def device(d, n):
        count = meta[d, 2 * OFF_CAP]
        count = jnp.where(count > OFF_CAP, 0, count)
        r, c = device_at(d)
        for s in range(OFF_CAP):
            lists[n + s] = c * cblk + meta[d, OFF_CAP + s]
            lists[slots + n + s] = r * rblk + meta[d, s]
            x = small[d, s * half : (s + 1) * half, :].astype(jnp.float32)
            turned = pltpu.roll(x, 64, 1)
            side = (n + s) % 2
            here = (lanes // 64) == side
            even = jnp.where(here, jnp.where(side == 0, x, turned), 0.0)
            odd = jnp.where(here, jnp.where(side == 0, turned, x), 0.0)
            at = pl.multiple_of(side * k, k)
            both = jnp.concatenate([even, odd], axis=0).astype(jnp.bfloat16)
            blk[(n + s) // 2, pl.ds(at, k), :] = both
        return n + count

    n_live = lax.fori_loop(0, n_dev, device, jnp.int32(0))
    for u in range(2 * UNROLL - 1):
        lists[n_live + u] = 0
        lists[slots + n_live + u] = 0
        at = pl.multiple_of((n_live + u) % 2 * k, k)
        blk[(n_live + u) // 2, pl.ds(at, k), :] = jnp.zeros((k, 128), jnp.bfloat16)
    lists[2 * slots] = (n_live + 2 * UNROLL - 1) // (2 * UNROLL)

    for r in range(n_row):
        h = jnp.int32(0)
        for c in range(n_col):
            h = jnp.where(meta[at_device(r, c), 2 * OFF_CAP] > OFF_CAP, c, h)
        lists[2 * slots + 1 + r] = h
        index = small[at_device(r, h), meta_at : meta_at + META, :].astype(jnp.float32)
        place[r : r + 1, :] = index[7:8] * float(rblk) + index[6:7]

    clear([w1, w2])
    add_products(lists[2 * slots], blk, NT, lists, 0, vd, slots, w1, w2)


def iterate(n_row, n_col, n_cap, total, own, lists, place, *rest):
    blk, rm, ic, *starts = rest[:7]
    fulls, out = rest[7:15], rest[15]
    sems, full, tmp, home, vs, vd, w1, w2 = rest[16:24]
    w, wt, wd, y, y1, y2, ph, linv = rest[24:]
    slots = 2 * blk.shape[0]
    n_dev = n_row * n_col
    k = vs.shape[1]
    half = k // 2
    rpairs, cpairs = n_col, n_row
    rblk, cblk = 2 * rpairs, 2 * cpairs
    part = n_cap // n_col
    width = cpairs * 128
    at_device, _ = place_of(own, n_row, n_dev)

    def laid_out(refs, whole):
        at, pairs = 0, []
        for ref in refs:
            pairs.append((ref, whole.at[pl.ds(at, ref.shape[0])]))
            at += ref.shape[0]
        return pairs

    copies = copy_in(laid_out(fulls, full), sems)
    for start, ref in zip(starts, (vs, vd, w1, w2)):
        for q in range(ref.shape[0]):
            ref[q] = start[q]
    clear([y, y1, y2])
    for copy in copies:
        copy.wait()
    n_group = lists[2 * slots]

    left = lax.broadcasted_iota(jnp.int32, (rblk, 128), 1) < 64
    homes = []
    for r in range(n_row):
        homes.append(lists[2 * slots + 1 + r])
        want = lax.broadcasted_iota(jnp.int32, (cblk * rblk, n_cap), 0).astype(jnp.float32)
        select = jnp.where(want == place[r : r + 1, :], 1.0, 0.0).astype(jnp.bfloat16)

        parts = [at_device(r, 2 * i + j) for j in range(2) for i in range(n_col // 2)]

        def build(i, carry, parts=parts, select=select):
            ms = [4 * i + d for d in range(4)]
            denses = []
            for m in ms:
                at = pl.multiple_of(m * part, part)
                slots = jnp.concatenate([full[d, pl.ds(at, part), :] for d in parts], axis=0)
                denses.append(dot(select, slots))
            for m, dense in zip(ms, denses):
                for u in range(cpairs):
                    a = dense[2 * u * rblk : (2 * u + 1) * rblk]
                    b = dense[(2 * u + 1) * rblk : (2 * u + 2) * rblk]
                    even = jnp.where(left, a, pltpu.roll(b, 64, 1))
                    odd = jnp.where(left, pltpu.roll(a, 64, 1), b)
                    tmp[u, pl.ds(m, rblk, stride=k), :] = even
                    tmp[u, pl.ds(m + half, rblk, stride=k), :] = odd
            return carry

        lax.fori_loop(0, half // 4, build, 0, unroll=2)

        def cut(i, carry, r=r):
            at = pl.multiple_of(i * k, k)
            for u in range(cpairs):
                hi, lo = split2(tmp[u, pl.ds(at, k), :])
                home[r, pl.ds(at, k), u * 128 : (u + 1) * 128] = hi
                home[r, pl.ds(at, k), width + u * 128 : width + (u + 1) * 128] = lo
            return carry

        lax.fori_loop(0, rblk, cut, 0, unroll=8)


    def iteration(it, carry):
        @pl.when(it > 0)
        def _():
            lh, ll = split2(linv[...])
            turn = jnp.concatenate([lh, lh, ll], axis=1)
            for q in range(0, n_dev, 4):
                hi = jnp.concatenate([ph[q + d, :k, :] for d in range(4)], axis=1)
                lo = jnp.concatenate([ph[q + d, k:, :] for d in range(4)], axis=1)
                current = dot(turn, jnp.concatenate([hi, lo, hi], axis=0))
                for d in range(4):
                    x = current[:, d * 128 : (d + 1) * 128] * ic[q + d, 0:1, :]
                    store_twice(vs, vd, q + d, x)

        for r in range(n_row):
            base = homes[r] * cpairs
            vec = jnp.concatenate([vs[base + u] for u in range(cpairs)] * 2, axis=1)
            for p in range(0, rpairs, 2):
                prod = dot(vec, home[r, p * 128 : (p + 2) * 128, :], NT)
                w[r * rpairs + p] = prod[:, :128]
                w[r * rpairs + p + 1] = prod[:, 128:]

        @pl.when(it > 0)
        def _():
            add_products(n_group, blk, NT, lists, 0, vd, slots, w1, w2)

        for p in range(n_dev):
            x = w[p] + gather_pair(p, w1, w2)
            store_twice(wt, wd, p, x * rm[p, 0:1, :])

        def back(r, u):
            vec = jnp.concatenate([wt[r * rpairs + p] for p in range(rpairs)], axis=1)
            cols = slice(u * 128, (u + 2) * 128)
            tail = slice(width + u * 128, width + (u + 2) * 128)
            return dot(vec, home[r, :, cols]) + dot(vec, home[r, :, tail])

        steps = [(r, u) for r in range(n_row) for u in range(0, cpairs, 2)]
        prod = back(*steps[0])
        for i, (r, u) in enumerate(steps):
            ahead = back(*steps[i + 1]) if i + 1 < len(steps) else None
            q = homes[r] * cpairs + u
            y[q] = y[q] + prod[:, :128]
            y[q + 1] = y[q + 1] + prod[:, 128:]
            prod = ahead

        add_products(n_group, blk, NN, lists, slots, wd, 0, y1, y2)

        both = jnp.zeros((2 * k, k), jnp.float32)
        for q in range(0, n_dev, 4):
            his, los = [], []
            for d in range(q, q + 4):
                x = y[d] + gather_pair(d, y1, y2)
                hi, lo = split2(x * ic[d, 0:1, :])
                ph[d, :k, :] = hi
                ph[d, k:, :] = lo
                his.append(hi)
                los.append(lo)
            hi = jnp.concatenate(his, axis=1)
            lo = jnp.concatenate(los, axis=1)
            both = both + dot(jnp.concatenate([hi, lo], axis=0), hi, NT)
        gram = (both[:k] + (both[k:] + both[k:].T)) / total
        clear([y, y1, y2, w1, w2])
        linv[...] = inverse_factor(gram)
        return carry

    lax.fori_loop(0, ITERS, iteration, 0)
    lh, ll = split2(linv[...])
    q = (2 * own[1] + own[2]) * n_row + own[0]
    hi, lo = ph[q, :k, :], ph[q, k:, :]
    w[0] = dot(lh, hi) + dot(ll, hi) + dot(lh, lo)
    even, odd = w[0, pl.ds(0, half, stride=2), :], w[0, pl.ds(1, half, stride=2), :]
    left = left_half(even.shape)
    first = jnp.where(left, even, pltpu.roll(odd, 64, 1))
    second = jnp.where(left, pltpu.roll(even, 64, 1), odd)
    for i in range(half):
        out[0:1, i * 128 : (i + 1) * 128] = first[i : i + 1]
        out[1:2, i * 128 : (i + 1) * 128] = second[i : i + 1]


def split3(x):
    parts = []
    for _ in range(3):
        parts.append(x.astype(jnp.bfloat16).astype(jnp.float32))
        x = x - parts[-1]
    return parts


def prepare(count, *rest):
    sources, out, sems, spread, first, second, both = rest[:6], *rest[6:12]
    sources = (sources[0].at[pl.ds(0, 16)], *sources[1:])
    for copy in copy_in(list(zip(sources, rest[12:])), sems):
        copy.wait()
    tile, rows, cols, vectors, row_mass, col_mass = rest[12:]
    f32, bf16 = jnp.float32, jnp.bfloat16
    half = first.shape[0]
    vec_at = OFF_CAP * half
    slots = tile[...].astype(f32)[:OFF_CAP]
    for i in range(half):
        spread[pl.ds(i, OFF_CAP, stride=half), :] = slots[:, i * 128 : (i + 1) * 128]
        first[i : i + 1, :] = vectors[0:1, i * 128 : (i + 1) * 128]
        second[i : i + 1, :] = vectors[1:2, i * 128 : (i + 1) * 128]
    x, z = first[...], second[...]
    left = left_half(x.shape)
    both[pl.ds(0, half, stride=2), :] = jnp.where(left, x, pltpu.roll(z, 64, 1))
    both[pl.ds(1, half, stride=2), :] = jnp.where(left, pltpu.roll(x, 64, 1), z)
    inv = 1.0 / jnp.sqrt(jnp.concatenate([col_mass[0:1, :], col_mass[1:2, :]], axis=1))
    out[:vec_at, :] = spread[...].astype(bf16)
    out[vec_at : vec_at + 2 * half, :] = (both[...] * inv).astype(bf16)

    sub = lax.broadcasted_iota(jnp.int32, (META, 128), 0)

    def stacked(at, values):
        result = jnp.zeros((META, 128), f32)
        for i, value in enumerate(values):
            result = jnp.where(sub == at + i, value, result)
        return result

    mass = jnp.concatenate([row_mass[0:1, :], row_mass[1:2, :]], axis=1)
    source = lax.broadcasted_iota(jnp.int32, (128, 128), 0)
    lane = lax.broadcasted_iota(jnp.int32, (128, 128), 1)
    chosen = source == (lane // 64) * 64 + 2 * (lane % half) + (lane % 64) // half
    masses = dot(stacked(0, split3(mass)).astype(bf16), jnp.where(chosen, 1.0, 0.0).astype(bf16))
    r, c = rows[...].astype(f32), cols[...].astype(f32)
    lane = lane[:8]
    moved = pltpu.roll(jnp.broadcast_to(c, (8, 128)), OFF_CAP, 1)
    short = jnp.where(lane == 2 * OFF_CAP, count[0, 0].astype(f32), 0.0)
    short = jnp.where(lane < OFF_CAP, r, jnp.where(lane < 2 * OFF_CAP, moved, short))
    packed = masses + stacked(3, split3(inv) + [r, c, short[0:1]])
    out[vec_at + 2 * half :, :] = packed.astype(bf16)


def swap(x, axis, distance):
    size = lax.axis_size(axis)
    return lax.ppermute(x, axis, [(i, i ^ distance) for i in range(size)])


def along_rows(x):
    return [x] + [swap(x, "row", s) for s in range(1, lax.axis_size("row"))]


def along_one_chip_axis(x):
    near, far = jnp.stack(x[:2]), jnp.stack(x[2:])
    return [
        jnp.concatenate([near, swap(near, "chip", 1)]),
        jnp.concatenate([far, swap(far, "chip", 2)]),
    ]


def along_other_chip_axis(x):
    near, far = x
    return [swap(near, "chip", 2), swap(far, "chip", 1)]


def full_part(tile, has_full, n_chip, part, chip, core):
    tile = tile.reshape(2, n_chip, part, tile.shape[1])
    none = jnp.zeros(tile.shape[1:], tile.dtype)
    kept, sent = (
        jnp.where(has_full, lax.dynamic_index_in_dim(tile, i, 0, False), none)
        for i in (core, 1 - core)
    )
    both = kept + swap(sent, "core", 1)
    mine = lax.dynamic_index_in_dim(both, chip, 0, False)
    for s in range(1, n_chip):
        mine = mine + swap(lax.dynamic_index_in_dim(both, chip ^ s, 0, False), "chip", s)
    return mine


def whole_on_each(n_row, n_col, blocks, block_row, block_col, counts, vectors, row_mass, col_mass):
    tile = blocks[0, 0]
    n_cap = tile.shape[0]
    own, bsize = row_mass.shape
    k = vectors.shape[1] // bsize
    half = bsize // 2
    part = n_cap // n_col
    n_dev = n_row * n_col
    count = counts[0, 0]
    has_full = count > OFF_CAP
    bf16 = jnp.bfloat16
    row, chip, core = (lax.axis_index(name) for name in ("row", "chip", "core"))

    sources = (tile, block_row[0], block_col[0], vectors, row_mass, col_mass)
    small = pl.pallas_call(
        prepare,
        out_shape=jax.ShapeDtypeStruct((OFF_CAP * half + k + META, own * bsize), bf16),
        in_specs=[pl.BlockSpec(memory_space=pltpu.SMEM)]
        + [pl.BlockSpec(memory_space=pltpu.HBM)] * len(sources),
        out_specs=pl.BlockSpec(memory_space=pltpu.VMEM),
        scratch_shapes=[pltpu.SemaphoreType.DMA((len(sources),))]
        + [pltpu.VMEM((rows, own * bsize), jnp.float32) for rows in (OFF_CAP * half, half, half, k)]
        + [pltpu.VMEM((16, bsize * bsize), bf16)]
        + [pltpu.VMEM(v.shape, v.dtype) for v in sources[1:]],
        name="prepare",
    )(counts, *(pltpu.with_memory_space_constraint(v, pltpu.HBM) for v in sources))

    home = full_part(tile, has_full, n_col // 2, part, chip, core)
    home = home.reshape(part, half, 128).transpose(1, 0, 2).reshape(half * part, 128)

    together = lax.optimization_barrier
    where = jnp.stack([row, chip, core]).astype(jnp.int32)
    smalls = along_rows(small)
    homes, smalls = along_rows(home), along_one_chip_axis(smalls)
    smalls, homes[1], where = together((smalls, homes[1], where))
    smalls = jnp.concatenate(smalls + along_other_chip_axis(smalls))
    homes, smalls = together((homes, smalls))
    others = swap(smalls, "core", 1)
    homes = along_one_chip_axis(homes)
    last = along_other_chip_axis(homes)

    height, width = 2 * n_col * bsize, 2 * n_row * bsize
    slots = n_dev * OFF_CAP + 2 * UNROLL
    f32, i32, vmem, smem = jnp.float32, jnp.int32, pltpu.VMEM, pltpu.SMEM
    pair, twice, mass = (n_dev, k, 128), (2 * n_dev, k, 128), (n_dev, 8, 128)
    smem_spec, vmem_spec, any_spec = (pl.BlockSpec(memory_space=m) for m in (smem, vmem, pl.ANY))
    arrays = [
        ((8, 128), f32), ((slots // 2, 128, 128), bf16), (mass, f32), (mass, f32),
        (pair, bf16), (twice, bf16), (twice, f32), (twice, f32),
    ]
    lists, *unpacked = pl.pallas_call(
        functools.partial(unpack, n_row, n_col),
        out_shape=[jax.ShapeDtypeStruct((2 * slots + 8,), i32)]
        + [vmem(*v) for v in arrays],
        in_specs=[smem_spec, any_spec, any_spec],
        out_specs=[smem_spec] + [vmem_spec] * len(arrays),
        scratch_shapes=[
            vmem((n_dev, 128), i32),
            smem((n_dev, 128), i32),
            pltpu.SemaphoreType.DMA((3,)),
            vmem((n_dev,) + small.shape, bf16),
        ],
        compiler_params=pltpu.CompilerParams(vmem_limit_bytes=VMEM_LIMIT // 2),
        cost_estimate=pl.CostEstimate(
            flops=0, bytes_accessed=4 * n_dev * small.size * 2, transcendentals=0
        ),
        name="unpack",
    )(where, smalls, others)
    last, lists = together((last, lists))
    mine = homes + last
    fulls = mine + [swap(v, "core", 1) for v in mine]
    return pl.pallas_call(
        functools.partial(iterate, n_row, n_col, n_cap, float(n_dev * own * bsize)),
        out_shape=jax.ShapeDtypeStruct((own, k * bsize), f32),
        in_specs=[smem_spec] * 2 + [vmem_spec] * len(arrays) + [any_spec] * len(fulls),
        out_specs=vmem_spec,
        scratch_shapes=[
            pltpu.SemaphoreType.DMA((len(fulls),)),
            vmem((n_dev,) + home.shape, bf16),
            vmem((n_row, height, 128), f32),
            vmem((n_row, height, 2 * width), bf16),
            *[vmem(*v) for v in arrays[4:]],
            vmem(pair, f32), vmem(pair, bf16), vmem(twice, bf16),
            vmem(pair, f32), vmem(twice, f32), vmem(twice, f32),
            vmem((n_dev, 2 * k, 128), bf16),
            vmem((k, k), f32),
        ],
        compiler_params=pltpu.CompilerParams(vmem_limit_bytes=VMEM_LIMIT),
        name="iterate",
    )(where, lists, *(pltpu.with_memory_space_constraint(v, vmem) for v in unpacked), *fulls)


def rotate(projected, gram):
    lower = jnp.linalg.cholesky(gram)
    inverse = lax.linalg.triangular_solve(
        lower, jnp.eye(gram.shape[0], dtype=jnp.float32), left_side=True, lower=True
    )
    return jnp.einsum(
        "kl,bli->bki",
        inverse,
        projected,
        precision=lax.Precision.HIGHEST,
        preferred_element_type=jnp.float32,
    )


def local_gram(projected):
    return jnp.einsum(
        "bki,bli->kl",
        projected,
        projected,
        precision=lax.Precision.HIGHEST,
        preferred_element_type=jnp.float32,
    )


def split_by_tile(blocks, block_row, block_col, counts, vectors, row_mass, col_mass):
    tile = blocks[0, 0]
    n_cap = tile.shape[0]
    bsize = row_mass.shape[1]
    vecs = vectors.shape[1] // bsize
    own = vectors.shape[0]
    n_row = lax.axis_size("row")
    n_col = lax.axis_size("col")
    row_panel = own * n_col
    col_panel = own * n_row
    total_boxes = float(own * bsize * n_row * n_col)
    rows_idx = block_row[0, 0]
    cols_idx = block_col[0, 0]
    live = jnp.arange(n_cap) < counts[0, 0]
    fwd_ids = jnp.where(live, rows_idx, row_panel)
    bwd_ids = jnp.where(live, cols_idx, col_panel)
    square = tile.reshape(n_cap, bsize, bsize)
    inv_col = 1.0 / jnp.sqrt(col_mass)
    current = vectors.reshape(own, vecs, bsize)
    for step in range(ITERS):
        scaled = (current * inv_col[:, None, :]).astype(jnp.bfloat16).reshape(own, vecs * bsize)
        panel = lax.all_gather(scaled, "row", axis=0, tiled=True)
        forward_taken = jnp.take(panel.reshape(col_panel, vecs, bsize), cols_idx, axis=0)
        forward_product = jnp.einsum(
            "bij,bkj->bki", square, forward_taken, preferred_element_type=jnp.float32
        )
        forward_summed = jax.ops.segment_sum(forward_product, fwd_ids, num_segments=row_panel + 1)
        rows_sum = lax.psum_scatter(
            forward_summed[:row_panel].reshape(row_panel, vecs * bsize),
            "col",
            scatter_dimension=0,
            tiled=True,
        )
        weighted = (rows_sum.reshape(own, vecs, bsize) * row_mass[:, None, :]).astype(jnp.bfloat16)
        whole_rows = lax.all_gather(weighted.reshape(own, vecs * bsize), "col", axis=0, tiled=True)
        taken = jnp.take(whole_rows.reshape(row_panel, vecs, bsize), rows_idx, axis=0)
        product = jnp.einsum("bij,bki->bkj", square, taken, preferred_element_type=jnp.float32)
        summed = jax.ops.segment_sum(product, bwd_ids, num_segments=col_panel + 1)
        cols_sum = lax.psum_scatter(
            summed[:col_panel].reshape(col_panel, vecs * bsize),
            "row",
            scatter_dimension=0,
            tiled=True,
        )
        projected = cols_sum.reshape(own, vecs, bsize) * inv_col[:, None, :]
        gram = lax.psum(local_gram(projected), ("row", "col")) / total_boxes
        current = rotate(projected, gram)
    return current.reshape(own, vecs * bsize)


def fits(n_row, n_col, blocks, vectors, row_mass):
    own, bsize = row_mass.shape[0] // (n_row * n_col), row_mass.shape[1]
    n_cap = blocks.shape[2]
    dense = n_row * (own * n_col * bsize) * (own * n_row * bsize) * 4
    shapes = own * bsize == 128 and vectors.shape[1] == bsize * bsize and n_cap == 128
    return dense <= VMEM_LIMIT // 4 and shapes and n_cap % (16 * n_col) == 0 and n_row == 4 and n_col == 8


def solution(mesh):
    n_row, n_col = mesh.shape["row"], mesh.shape["col"]

    def run(blocks, block_row, block_col, counts, vectors, row_mass, col_mass):
        args = (blocks, block_row, block_col, counts, vectors, row_mass, col_mass)
        if fits(n_row, n_col, blocks, vectors, row_mass):
            devices = mesh.devices.reshape(n_row, n_col // 2, 2)
            grid, col = jax.sharding.Mesh(devices, ("row", "chip", "core")), ("chip", "core")
            body = functools.partial(whole_on_each, n_row, n_col)
        else:
            grid, col, body = mesh, ("col",), split_by_tile
        by_row, by_col = P(("row",) + col, None), P(col + ("row",), None)
        in_specs = (
            P("row", col, None, None), P("row", col, None), P("row", col, None), P("row", col),
            by_col, by_row, by_col,
        )
        return jax.shard_map(
            body, mesh=grid, in_specs=in_specs, out_specs=by_col, check_vma=False
        )(*args)

    return run
```

```python
import functools

import jax
import jax.numpy as jnp
from jax import lax
from jax.experimental import pallas as pl
from jax.experimental.pallas import tpu as pltpu
from jax.sharding import PartitionSpec as P

ITERS = 4
OFF_CAP = 8
META = 16
UNROLL = 16
BATCH = 4
VMEM_LIMIT = 36 * 1024 * 1024

NT = (((1,), (1,)), ((), ()))
NN = (((1,), (0,)), ((), ()))


def dot(a, b, dims=NN):
    return lax.dot_general(a, b, dims, preferred_element_type=jnp.float32)


def split2(x):
    hi = x.astype(jnp.bfloat16)
    return hi, (x - hi.astype(jnp.float32)).astype(jnp.bfloat16)


def inverse_factor(gram):
    n = gram.shape[0]
    rows = lax.broadcasted_iota(jnp.int32, (n, n), 0)
    cols = lax.broadcasted_iota(jnp.int32, (n, n), 1)
    eye = (rows == cols).astype(jnp.float32)
    both = jnp.concatenate([gram, eye], axis=1)
    count, shape = n // 8, (8, 2 * n)
    tiles = [both[8 * t : 8 * t + 8] for t in range(count)]
    sub = lax.broadcasted_iota(jnp.int32, shape, 0)
    out = []
    for b in range(count):
        column = {
            t: [jnp.broadcast_to(tiles[t][:, 8 * b + s : 8 * b + s + 1], shape) for s in range(8)]
            for t in range(b, count)
        }
        row = [jnp.broadcast_to(tiles[b][s : s + 1], shape) for s in range(8)]
        a = [
            [jnp.broadcast_to(column[b][j][s : s + 1], shape) if j >= s else None for j in range(8)]
            for s in range(8)
        ]
        done = jnp.zeros(shape, jnp.float32)
        for s in range(8):
            root = lax.rsqrt(a[s][s])
            inv = root * root
            inv = inv * (2.0 - a[s][s] * inv)
            step = row[s] * inv
            done = jnp.where(sub == s, row[s] * root, done)
            for i in range(s + 1, 8):
                part = a[s][i] * inv
                for j in range(i, 8):
                    a[i][j] = a[i][j] - part * a[s][j]
                row[i] = row[i] - a[s][i] * step
                for t in range(b + 1, count):
                    column[t][i] = column[t][i] - column[t][s] * part
            for t in range(b + 1, count):
                tiles[t] = tiles[t] - column[t][s] * step
        out.append(done)
    return jnp.concatenate(out, axis=0)[:, n:]


def place_of(own, n_row, n_dev):
    here, chip, core = own[0], own[1], own[2]

    def at_device(r, c):
        dr, dc, dk = here ^ r, chip ^ (c // 2), core ^ (c % 2)
        dx, dy = dc & 1, dc >> 1
        order = jnp.where(dr < 2, 2 * dx, 4 + 2 * dy) + jnp.where(
            jnp.where(dr < 2, dy, dx) > 0, n_dev // 4, 0
        )
        return dk * (n_dev // 2) + order + (dr & 1)

    def device_at(d):
        far, second = (d >> 2) & 1, (d >> 3) & 1
        first = (d >> 1) & 1
        dc = jnp.where(far == 0, 2 * second + first, 2 * first + second)
        return here ^ (2 * far + (d & 1)), 2 * (chip ^ dc) + (core ^ (d >> 4))

    return at_device, device_at


def copy_in(pairs, sems):
    copies = [pltpu.make_async_copy(src, dst, sems.at[i]) for i, (src, dst) in enumerate(pairs)]
    for copy in copies:
        copy.start()
    return copies


def clear(refs):
    for ref in refs:
        for q in range(ref.shape[0]):
            ref[q] = jnp.zeros_like(ref[q])


def left_half(shape):
    return lax.broadcasted_iota(jnp.int32, shape, len(shape) - 1) < 64


def store_twice(pair, twice, q, x):
    pair[q] = x.astype(pair.dtype)
    turned, left = pltpu.roll(x, 64, 1), left_half(x.shape)
    twice[2 * q] = jnp.where(left, x, turned).astype(twice.dtype)
    twice[2 * q + 1] = jnp.where(left, turned, x).astype(twice.dtype)


def gather_pair(q, first, second):
    left = left_half(first.shape[1:])
    apart = jnp.where(left, first[2 * q + 1], second[2 * q])
    return jnp.where(left, first[2 * q], second[2 * q + 1]) + pltpu.roll(apart, 64, 1)


def add_products(n_group, blk, dims, lists, from_at, source, to_at, first, second):
    left = left_half(source.shape[1:])

    def multiply(pairs):
        return [
            dot(
                jnp.where(left, source[lists[from_at + 2 * p]], source[lists[from_at + 2 * p + 1]]),
                blk[p],
                dims,
            )
            for p in pairs
        ]

    def add(pairs, prods):
        for p, prod in zip(pairs, prods):
            a, b = lists[to_at + 2 * p], lists[to_at + 2 * p + 1]
            first[a] = first[a] + prod
            second[b] = second[b] + prod

    def group(i, carry):
        batches = [
            [i * UNROLL + at + u for u in range(BATCH)] for at in range(0, UNROLL, BATCH)
        ]
        prods = multiply(batches[0])
        for now, later in zip(batches, batches[1:]):
            ahead = multiply(later)
            add(now, prods)
            prods = ahead
        add(batches[-1], prods)
        return carry

    lax.fori_loop(0, n_group, group, 0)


def unpack(
    n_row, n_col, own, mine, other,
    lists, place, blk, rm, ic, vs, vd, w1, w2, ints, meta, sems, small,
):
    n_dev = n_row * n_col
    k = vs.shape[1]
    half = k // 2
    rblk, cblk = 2 * n_col, 2 * n_row
    vec_at = OFF_CAP * half
    meta_at = vec_at + k
    at_device, device_at = place_of(own, n_row, n_dev)
    slots = 2 * blk.shape[0]

    first, second = pl.ds(0, n_dev // 2), pl.ds(n_dev // 2, n_dev // 2)
    for copy in copy_in([(mine, small.at[first]), (other, small.at[second])], sems):
        copy.wait()
    for d in range(n_dev):
        rows = small[d, meta_at : meta_at + META, :].astype(jnp.float32)
        ints[d : d + 1, :] = rows[8:9].astype(jnp.int32)
    to_scalars = pltpu.make_async_copy(ints, meta, sems.at[2])
    to_scalars.start()

    for r in range(n_row):
        for c in range(n_col):
            q, p, d = c * n_row + r, r * n_col + c, at_device(r, c)
            rows = small[d, meta_at : meta_at + META, :].astype(jnp.float32)
            rm[p] = jnp.broadcast_to(rows[0:1] + rows[1:2] + rows[2:3], (8, 128))
            ic[q] = jnp.broadcast_to(rows[3:4] + rows[4:5] + rows[5:6], (8, 128))
            store_twice(vs, vd, q, small[d, vec_at : vec_at + k, :].astype(jnp.float32))
    to_scalars.wait()

    lanes = lax.broadcasted_iota(jnp.int32, (half, 128), 1)

    def device(d, n):
        count = meta[d, 2 * OFF_CAP]
        count = jnp.where(count > OFF_CAP, 0, count)
        r, c = device_at(d)
        for s in range(OFF_CAP):
            lists[n + s] = c * cblk + meta[d, OFF_CAP + s]
            lists[slots + n + s] = r * rblk + meta[d, s]
            x = small[d, s * half : (s + 1) * half, :].astype(jnp.float32)
            turned = pltpu.roll(x, 64, 1)
            side = (n + s) % 2
            here = (lanes // 64) == side
            even = jnp.where(here, jnp.where(side == 0, x, turned), 0.0)
            odd = jnp.where(here, jnp.where(side == 0, turned, x), 0.0)
            at = pl.multiple_of(side * k, k)
            both = jnp.concatenate([even, odd], axis=0).astype(jnp.bfloat16)
            blk[(n + s) // 2, pl.ds(at, k), :] = both
        return n + count

    n_live = lax.fori_loop(0, n_dev, device, jnp.int32(0))
    for u in range(2 * UNROLL - 1):
        lists[n_live + u] = 0
        lists[slots + n_live + u] = 0
        at = pl.multiple_of((n_live + u) % 2 * k, k)
        blk[(n_live + u) // 2, pl.ds(at, k), :] = jnp.zeros((k, 128), jnp.bfloat16)
    lists[2 * slots] = (n_live + 2 * UNROLL - 1) // (2 * UNROLL)

    for r in range(n_row):
        h = jnp.int32(0)
        for c in range(n_col):
            h = jnp.where(meta[at_device(r, c), 2 * OFF_CAP] > OFF_CAP, c, h)
        lists[2 * slots + 1 + r] = h
        index = small[at_device(r, h), meta_at : meta_at + META, :].astype(jnp.float32)
        place[r : r + 1, :] = index[7:8] * float(rblk) + index[6:7]

    clear([w1, w2])
    add_products(lists[2 * slots], blk, NT, lists, 0, vd, slots, w1, w2)


def iterate(n_row, n_col, n_cap, total, own, lists, place, *rest):
    blk, rm, ic, *starts = rest[:7]
    fulls, out = rest[7:15], rest[15]
    sems, full, tmp, home, vs, vd, w1, w2 = rest[16:24]
    w, wt, wd, y, y1, y2, ph, linv = rest[24:]
    slots = 2 * blk.shape[0]
    n_dev = n_row * n_col
    k = vs.shape[1]
    half = k // 2
    rpairs, cpairs = n_col, n_row
    rblk, cblk = 2 * rpairs, 2 * cpairs
    part = n_cap // n_col
    width = cpairs * 128
    at_device, _ = place_of(own, n_row, n_dev)

    def laid_out(refs, whole):
        at, pairs = 0, []
        for ref in refs:
            pairs.append((ref, whole.at[pl.ds(at, ref.shape[0])]))
            at += ref.shape[0]
        return pairs

    pairs = laid_out(fulls, full)
    copies = copy_in(pairs[0::2] + pairs[1::2], sems)
    for start, ref in zip(starts, (vs, vd, w1, w2)):
        for q in range(ref.shape[0]):
            ref[q] = start[q]
    clear([y, y1, y2])
    n_group = lists[2 * slots]

    left = lax.broadcasted_iota(jnp.int32, (rblk, 128), 1) < 64
    homes = [lists[2 * slots + 1 + r] for r in range(n_row)]
    for distance in range(n_row):
        if distance % 2 == 0:
            for copy in copies[2 * distance : 2 * distance + 4]:
                copy.wait()
        r = own[0] ^ distance
        want = lax.broadcasted_iota(jnp.int32, (cblk * rblk, n_cap), 0).astype(jnp.float32)
        select = jnp.where(want == place[pl.ds(r, 1), :], 1.0, 0.0).astype(jnp.bfloat16)

        parts = [at_device(r, 2 * i + j) for j in range(2) for i in range(n_col // 2)]

        def build(i, carry, parts=parts, select=select):
            ms = [4 * i + d for d in range(4)]
            denses = []
            for m in ms:
                at = pl.multiple_of(m * part, part)
                slots = jnp.concatenate([full[d, pl.ds(at, part), :] for d in parts], axis=0)
                denses.append(dot(select, slots))
            for m, dense in zip(ms, denses):
                for u in range(cpairs):
                    a = dense[2 * u * rblk : (2 * u + 1) * rblk]
                    b = dense[(2 * u + 1) * rblk : (2 * u + 2) * rblk]
                    even = jnp.where(left, a, pltpu.roll(b, 64, 1))
                    odd = jnp.where(left, pltpu.roll(a, 64, 1), b)
                    tmp[u, pl.ds(m, rblk, stride=k), :] = even
                    tmp[u, pl.ds(m + half, rblk, stride=k), :] = odd
            return carry

        lax.fori_loop(0, half // 4, build, 0, unroll=2)

        def cut(i, carry, r=r):
            at = pl.multiple_of(i * k, k)
            for u in range(cpairs):
                hi, lo = split2(tmp[u, pl.ds(at, k), :])
                home[r, pl.ds(at, k), u * 128 : (u + 1) * 128] = hi
                home[r, pl.ds(at, k), width + u * 128 : width + (u + 1) * 128] = lo
            return carry

        lax.fori_loop(0, rblk, cut, 0, unroll=8)


    def iteration(it, carry):
        @pl.when(it > 0)
        def _():
            lh, ll = split2(linv[...])
            turn = jnp.concatenate([lh, lh, ll], axis=1)
            for q in range(0, n_dev, 4):
                hi = jnp.concatenate([ph[q + d, :k, :] for d in range(4)], axis=1)
                lo = jnp.concatenate([ph[q + d, k:, :] for d in range(4)], axis=1)
                current = dot(turn, jnp.concatenate([hi, lo, hi], axis=0))
                for d in range(4):
                    x = current[:, d * 128 : (d + 1) * 128] * ic[q + d, 0:1, :]
                    store_twice(vs, vd, q + d, x)

        for r in range(n_row):
            base = homes[r] * cpairs
            vec = jnp.concatenate([vs[base + u] for u in range(cpairs)] * 2, axis=1)
            for p in range(0, rpairs, 2):
                prod = dot(vec, home[r, p * 128 : (p + 2) * 128, :], NT)
                w[r * rpairs + p] = prod[:, :128]
                w[r * rpairs + p + 1] = prod[:, 128:]

        @pl.when(it > 0)
        def _():
            add_products(n_group, blk, NT, lists, 0, vd, slots, w1, w2)

        for p in range(n_dev):
            x = w[p] + gather_pair(p, w1, w2)
            store_twice(wt, wd, p, x * rm[p, 0:1, :])

        def back(r, u):
            vec = jnp.concatenate([wt[r * rpairs + p] for p in range(rpairs)], axis=1)
            cols = slice(u * 128, (u + 2) * 128)
            tail = slice(width + u * 128, width + (u + 2) * 128)
            return dot(vec, home[r, :, cols]) + dot(vec, home[r, :, tail])

        steps = [(r, u) for r in range(n_row) for u in range(0, cpairs, 2)]
        prod = back(*steps[0])
        for i, (r, u) in enumerate(steps):
            ahead = back(*steps[i + 1]) if i + 1 < len(steps) else None
            q = homes[r] * cpairs + u
            y[q] = y[q] + prod[:, :128]
            y[q + 1] = y[q + 1] + prod[:, 128:]
            prod = ahead

        add_products(n_group, blk, NN, lists, slots, wd, 0, y1, y2)

        both = jnp.zeros((2 * k, k), jnp.float32)
        for q in range(0, n_dev, 4):
            his, los = [], []
            for d in range(q, q + 4):
                x = y[d] + gather_pair(d, y1, y2)
                hi, lo = split2(x * ic[d, 0:1, :])
                ph[d, :k, :] = hi
                ph[d, k:, :] = lo
                his.append(hi)
                los.append(lo)
            hi = jnp.concatenate(his, axis=1)
            lo = jnp.concatenate(los, axis=1)
            both = both + dot(jnp.concatenate([hi, lo], axis=0), hi, NT)
        gram = (both[:k] + (both[k:] + both[k:].T)) / total
        clear([y, y1, y2, w1, w2])
        linv[...] = inverse_factor(gram)
        return carry

    lax.fori_loop(0, ITERS, iteration, 0)
    lh, ll = split2(linv[...])
    q = (2 * own[1] + own[2]) * n_row + own[0]
    hi, lo = ph[q, :k, :], ph[q, k:, :]
    w[0] = dot(lh, hi) + dot(ll, hi) + dot(lh, lo)
    even, odd = w[0, pl.ds(0, half, stride=2), :], w[0, pl.ds(1, half, stride=2), :]
    left = left_half(even.shape)
    first = jnp.where(left, even, pltpu.roll(odd, 64, 1))
    second = jnp.where(left, pltpu.roll(even, 64, 1), odd)
    for i in range(half):
        out[0:1, i * 128 : (i + 1) * 128] = first[i : i + 1]
        out[1:2, i * 128 : (i + 1) * 128] = second[i : i + 1]


def split3(x):
    parts = []
    for _ in range(3):
        parts.append(x.astype(jnp.bfloat16).astype(jnp.float32))
        x = x - parts[-1]
    return parts


def prepare(count, *rest):
    sources, out, sems, spread, first, second, both = rest[:6], *rest[6:12]
    sources = (sources[0].at[pl.ds(0, 16)], *sources[1:])
    for copy in copy_in(list(zip(sources, rest[12:])), sems):
        copy.wait()
    tile, rows, cols, vectors, row_mass, col_mass = rest[12:]
    f32, bf16 = jnp.float32, jnp.bfloat16
    half = first.shape[0]
    vec_at = OFF_CAP * half
    slots = tile[...].astype(f32)[:OFF_CAP]
    for i in range(half):
        spread[pl.ds(i, OFF_CAP, stride=half), :] = slots[:, i * 128 : (i + 1) * 128]
        first[i : i + 1, :] = vectors[0:1, i * 128 : (i + 1) * 128]
        second[i : i + 1, :] = vectors[1:2, i * 128 : (i + 1) * 128]
    x, z = first[...], second[...]
    left = left_half(x.shape)
    both[pl.ds(0, half, stride=2), :] = jnp.where(left, x, pltpu.roll(z, 64, 1))
    both[pl.ds(1, half, stride=2), :] = jnp.where(left, pltpu.roll(x, 64, 1), z)
    inv = 1.0 / jnp.sqrt(jnp.concatenate([col_mass[0:1, :], col_mass[1:2, :]], axis=1))
    out[:vec_at, :] = spread[...].astype(bf16)
    out[vec_at : vec_at + 2 * half, :] = (both[...] * inv).astype(bf16)

    sub = lax.broadcasted_iota(jnp.int32, (META, 128), 0)

    def stacked(at, values):
        result = jnp.zeros((META, 128), f32)
        for i, value in enumerate(values):
            result = jnp.where(sub == at + i, value, result)
        return result

    mass = jnp.concatenate([row_mass[0:1, :], row_mass[1:2, :]], axis=1)
    source = lax.broadcasted_iota(jnp.int32, (128, 128), 0)
    lane = lax.broadcasted_iota(jnp.int32, (128, 128), 1)
    chosen = source == (lane // 64) * 64 + 2 * (lane % half) + (lane % 64) // half
    masses = dot(stacked(0, split3(mass)).astype(bf16), jnp.where(chosen, 1.0, 0.0).astype(bf16))
    r, c = rows[...].astype(f32), cols[...].astype(f32)
    lane = lane[:8]
    moved = pltpu.roll(jnp.broadcast_to(c, (8, 128)), OFF_CAP, 1)
    short = jnp.where(lane == 2 * OFF_CAP, count[0, 0].astype(f32), 0.0)
    short = jnp.where(lane < OFF_CAP, r, jnp.where(lane < 2 * OFF_CAP, moved, short))
    packed = masses + stacked(3, split3(inv) + [r, c, short[0:1]])
    out[vec_at + 2 * half :, :] = packed.astype(bf16)


def swap(x, axis, distance):
    size = lax.axis_size(axis)
    return lax.ppermute(x, axis, [(i, i ^ distance) for i in range(size)])


def along_rows(x):
    return [x] + [swap(x, "row", s) for s in range(1, lax.axis_size("row"))]


def along_one_chip_axis(x):
    near, far = jnp.stack(x[:2]), jnp.stack(x[2:])
    return [
        jnp.concatenate([near, swap(near, "chip", 1)]),
        jnp.concatenate([far, swap(far, "chip", 2)]),
    ]


def along_other_chip_axis(x):
    near, far = x
    return [swap(near, "chip", 2), swap(far, "chip", 1)]


def full_part(tile, has_full, n_chip, part, chip, core):
    tile = tile.reshape(2, n_chip, part, tile.shape[1])
    none = jnp.zeros(tile.shape[1:], tile.dtype)
    kept, sent = (
        jnp.where(has_full, lax.dynamic_index_in_dim(tile, i, 0, False), none)
        for i in (core, 1 - core)
    )
    both = kept + swap(sent, "core", 1)
    mine = lax.dynamic_index_in_dim(both, chip, 0, False)
    for s in range(1, n_chip):
        mine = mine + swap(lax.dynamic_index_in_dim(both, chip ^ s, 0, False), "chip", s)
    return mine


def whole_on_each(n_row, n_col, blocks, block_row, block_col, counts, vectors, row_mass, col_mass):
    tile = blocks[0, 0]
    n_cap = tile.shape[0]
    own, bsize = row_mass.shape
    k = vectors.shape[1] // bsize
    half = bsize // 2
    part = n_cap // n_col
    n_dev = n_row * n_col
    count = counts[0, 0]
    has_full = count > OFF_CAP
    bf16 = jnp.bfloat16
    row, chip, core = (lax.axis_index(name) for name in ("row", "chip", "core"))

    sources = (tile, block_row[0], block_col[0], vectors, row_mass, col_mass)
    small = pl.pallas_call(
        prepare,
        out_shape=jax.ShapeDtypeStruct((OFF_CAP * half + k + META, own * bsize), bf16),
        in_specs=[pl.BlockSpec(memory_space=pltpu.SMEM)]
        + [pl.BlockSpec(memory_space=pltpu.HBM)] * len(sources),
        out_specs=pl.BlockSpec(memory_space=pltpu.VMEM),
        scratch_shapes=[pltpu.SemaphoreType.DMA((len(sources),))]
        + [pltpu.VMEM((rows, own * bsize), jnp.float32) for rows in (OFF_CAP * half, half, half, k)]
        + [pltpu.VMEM((16, bsize * bsize), bf16)]
        + [pltpu.VMEM(v.shape, v.dtype) for v in sources[1:]],
        name="prepare",
    )(counts, *(pltpu.with_memory_space_constraint(v, pltpu.HBM) for v in sources))

    home = full_part(tile, has_full, n_col // 2, part, chip, core)
    home = home.reshape(part, half, 128).transpose(1, 0, 2).reshape(half * part, 128)

    together = lax.optimization_barrier
    where = jnp.stack([row, chip, core]).astype(jnp.int32)
    home, smalls, where = together((home, along_rows(small), where))
    homes, smalls = along_rows(home), along_one_chip_axis(smalls)
    smalls, homes[1] = together((smalls, homes[1]))
    smalls = jnp.concatenate(smalls + along_other_chip_axis(smalls))
    homes, smalls = together((homes, smalls))
    others = swap(smalls, "core", 1)
    homes = along_one_chip_axis(homes)
    last = along_other_chip_axis(homes)

    height, width = 2 * n_col * bsize, 2 * n_row * bsize
    slots = n_dev * OFF_CAP + 2 * UNROLL
    f32, i32, vmem, smem = jnp.float32, jnp.int32, pltpu.VMEM, pltpu.SMEM
    pair, twice, mass = (n_dev, k, 128), (2 * n_dev, k, 128), (n_dev, 8, 128)
    smem_spec, vmem_spec, any_spec = (pl.BlockSpec(memory_space=m) for m in (smem, vmem, pl.ANY))
    arrays = [
        ((8, 128), f32), ((slots // 2, 128, 128), bf16), (mass, f32), (mass, f32),
        (pair, bf16), (twice, bf16), (twice, f32), (twice, f32),
    ]
    lists, *unpacked = pl.pallas_call(
        functools.partial(unpack, n_row, n_col),
        out_shape=[jax.ShapeDtypeStruct((2 * slots + 8,), i32)]
        + [vmem(*v) for v in arrays],
        in_specs=[smem_spec, any_spec, any_spec],
        out_specs=[smem_spec] + [vmem_spec] * len(arrays),
        scratch_shapes=[
            vmem((n_dev, 128), i32),
            smem((n_dev, 128), i32),
            pltpu.SemaphoreType.DMA((3,)),
            vmem((n_dev,) + small.shape, bf16),
        ],
        compiler_params=pltpu.CompilerParams(vmem_limit_bytes=VMEM_LIMIT // 2),
        cost_estimate=pl.CostEstimate(
            flops=0, bytes_accessed=4 * n_dev * small.size * 2, transcendentals=0
        ),
        name="unpack",
    )(where, smalls, others)
    last, lists = together((last, lists))
    mine = homes + last
    fulls = mine + [swap(v, "core", 1) for v in mine]
    return pl.pallas_call(
        functools.partial(iterate, n_row, n_col, n_cap, float(n_dev * own * bsize)),
        out_shape=jax.ShapeDtypeStruct((own, k * bsize), f32),
        in_specs=[smem_spec] * 2 + [vmem_spec] * len(arrays) + [any_spec] * len(fulls),
        out_specs=vmem_spec,
        scratch_shapes=[
            pltpu.SemaphoreType.DMA((len(fulls),)),
            vmem((n_dev,) + home.shape, bf16),
            vmem((n_row, height, 128), f32),
            vmem((n_row, height, 2 * width), bf16),
            *[vmem(*v) for v in arrays[4:]],
            vmem(pair, f32), vmem(pair, bf16), vmem(twice, bf16),
            vmem(pair, f32), vmem(twice, f32), vmem(twice, f32),
            vmem((n_dev, 2 * k, 128), bf16),
            vmem((k, k), f32),
        ],
        compiler_params=pltpu.CompilerParams(vmem_limit_bytes=VMEM_LIMIT),
        name="iterate",
    )(where, lists, *(pltpu.with_memory_space_constraint(v, vmem) for v in unpacked), *fulls)


def rotate(projected, gram):
    lower = jnp.linalg.cholesky(gram)
    inverse = lax.linalg.triangular_solve(
        lower, jnp.eye(gram.shape[0], dtype=jnp.float32), left_side=True, lower=True
    )
    return jnp.einsum(
        "kl,bli->bki",
        inverse,
        projected,
        precision=lax.Precision.HIGHEST,
        preferred_element_type=jnp.float32,
    )


def local_gram(projected):
    return jnp.einsum(
        "bki,bli->kl",
        projected,
        projected,
        precision=lax.Precision.HIGHEST,
        preferred_element_type=jnp.float32,
    )


def split_by_tile(blocks, block_row, block_col, counts, vectors, row_mass, col_mass):
    tile = blocks[0, 0]
    n_cap = tile.shape[0]
    bsize = row_mass.shape[1]
    vecs = vectors.shape[1] // bsize
    own = vectors.shape[0]
    n_row = lax.axis_size("row")
    n_col = lax.axis_size("col")
    row_panel = own * n_col
    col_panel = own * n_row
    total_boxes = float(own * bsize * n_row * n_col)
    rows_idx = block_row[0, 0]
    cols_idx = block_col[0, 0]
    live = jnp.arange(n_cap) < counts[0, 0]
    fwd_ids = jnp.where(live, rows_idx, row_panel)
    bwd_ids = jnp.where(live, cols_idx, col_panel)
    square = tile.reshape(n_cap, bsize, bsize)
    inv_col = 1.0 / jnp.sqrt(col_mass)
    current = vectors.reshape(own, vecs, bsize)
    for step in range(ITERS):
        scaled = (current * inv_col[:, None, :]).astype(jnp.bfloat16).reshape(own, vecs * bsize)
        panel = lax.all_gather(scaled, "row", axis=0, tiled=True)
        forward_taken = jnp.take(panel.reshape(col_panel, vecs, bsize), cols_idx, axis=0)
        forward_product = jnp.einsum(
            "bij,bkj->bki", square, forward_taken, preferred_element_type=jnp.float32
        )
        forward_summed = jax.ops.segment_sum(forward_product, fwd_ids, num_segments=row_panel + 1)
        rows_sum = lax.psum_scatter(
            forward_summed[:row_panel].reshape(row_panel, vecs * bsize),
            "col",
            scatter_dimension=0,
            tiled=True,
        )
        weighted = (rows_sum.reshape(own, vecs, bsize) * row_mass[:, None, :]).astype(jnp.bfloat16)
        whole_rows = lax.all_gather(weighted.reshape(own, vecs * bsize), "col", axis=0, tiled=True)
        taken = jnp.take(whole_rows.reshape(row_panel, vecs, bsize), rows_idx, axis=0)
        product = jnp.einsum("bij,bki->bkj", square, taken, preferred_element_type=jnp.float32)
        summed = jax.ops.segment_sum(product, bwd_ids, num_segments=col_panel + 1)
        cols_sum = lax.psum_scatter(
            summed[:col_panel].reshape(col_panel, vecs * bsize),
            "row",
            scatter_dimension=0,
            tiled=True,
        )
        projected = cols_sum.reshape(own, vecs, bsize) * inv_col[:, None, :]
        gram = lax.psum(local_gram(projected), ("row", "col")) / total_boxes
        current = rotate(projected, gram)
    return current.reshape(own, vecs * bsize)


def fits(n_row, n_col, blocks, vectors, row_mass):
    own, bsize = row_mass.shape[0] // (n_row * n_col), row_mass.shape[1]
    n_cap = blocks.shape[2]
    dense = n_row * (own * n_col * bsize) * (own * n_row * bsize) * 4
    shapes = own * bsize == 128 and vectors.shape[1] == bsize * bsize and n_cap == 128
    return dense <= VMEM_LIMIT // 4 and shapes and n_cap % (16 * n_col) == 0 and n_row == 4 and n_col == 8


def solution(mesh):
    n_row, n_col = mesh.shape["row"], mesh.shape["col"]

    def run(blocks, block_row, block_col, counts, vectors, row_mass, col_mass):
        args = (blocks, block_row, block_col, counts, vectors, row_mass, col_mass)
        if fits(n_row, n_col, blocks, vectors, row_mass):
            devices = mesh.devices.reshape(n_row, n_col // 2, 2)
            grid, col = jax.sharding.Mesh(devices, ("row", "chip", "core")), ("chip", "core")
            body = functools.partial(whole_on_each, n_row, n_col)
        else:
            grid, col, body = mesh, ("col",), split_by_tile
        by_row, by_col = P(("row",) + col, None), P(col + ("row",), None)
        in_specs = (
            P("row", col, None, None), P("row", col, None), P("row", col, None), P("row", col),
            by_col, by_row, by_col,
        )
        return jax.shard_map(
            body, mesh=grid, in_specs=in_specs, out_specs=by_col, check_vma=False
        )(*args)

    return run
```
